32 devices in a mesh: grp: 2 (over y), clu: 4 (over z), sub: 2 (over x), rep: 2 (over core).
Axes of the slice: x: 2, y: 2, z: 4, core: 2. Of those that a mesh axis runs over, the one named last changes fastest.
Arguments:
- charges: float32 [1024, 256], P(('grp', 'clu'), 'sub'), parts along dimension 0, may hold values from -0.6 to 0.6
- panel_mask: int32 [1024, 256], P(('grp', 'clu'), 'sub'), parts along dimension 0, may hold values from 0 to 1, as said below
- geometry: float32 [1024, 4, 256], P(('grp', 'clu')), parts along dimension 0
- remote_source: int32 [8, 4, 32], P(('grp', 'clu'), None, 'rep'), parts along dimension 0, may hold values from 0 to 127
- remote_target: int32 [8, 4, 32], P(('grp', 'clu'), None, 'rep'), parts along dimension 0, may hold values from 0 to 127
- remote_live: int32 [8, 4, 32], P(('grp', 'clu'), None, 'rep'), parts along dimension 0, may hold values from 0 to 1, as said below
- local_pairs: int32 [8, 256, 2], P(('grp', 'clu'), 'rep'), parts along dimension 0, may hold values from 0 to 127, as said below
- basis: float32 [1024, 256, 32], P(('grp', 'clu'), 'sub'), parts along dimension 0, may hold values from -0.9 to 0.9
- transfer: float32 [1024, 32, 32], P(('grp', 'clu')), parts along dimension 0, may hold values from -1 to 1
- parent_of: int32 [1024], P(('grp', 'clu')), parts along dimension 0, may hold values from 0 to 15, as said below
- far_list: int32 [128, 8], P(('grp', 'clu')), parts along dimension 0, may hold values from 0 to 63
- coupling: float32 [128, 8, 32, 32], P(('grp', 'clu')), parts along dimension 0, may hold values from -0.375 to 0.375
Outputs:
- potential: float32 [1024, 256], P(('grp', 'clu'), 'sub'), parts along dimension 0
The draws below stay inside these ranges and needn't reach their ends.
There are 2 independent parts, one for each index of `grp`. The reference program is written for one: setup_inputs(seed, part) draws one part's arguments, and reference() takes and returns one part's arrays. A program takes and returns all parts, laid end to end along the dimension named above; each array names one. Nothing has to cross between parts.
Inputs may be any that keep to these rules, and one draw needn't show every extreme that they name: `panel_mask`: within each cluster the real panels come first, and at least 128 are real. `remote_live`: live slots come first in each slot list [c, d]; the list [c, c] is empty; the lists between clu neighbours at cycle distance 1 are full (32 live). `local_pairs`: the two clusters of a local pair differ. `parent_of`: each of the 16 parents of a clu device has exactly 8 children on that device.
All inputs are finite; a program needn't handle non-finite values.
Results may differ from the reference program's by a relative error of at most 0.000064.
Values sent between devices are 32-bit elements; how exact they have to be, the bound alone decides.
No kernel may reach another device: no remote copies, remote signals or barrier semaphores. Data moves between devices by JAX's collectives and lax.ppermute only.
A program may use at most 64 MiB of HBM per device.

```python
import math
import jax
import jax.numpy as jnp
from jax import lax

P_SIZE = 256
R = 32
BRANCH = 8
CAP = 32
FAR_N = 8
CL_DEV = 128
OWNERS = 4
CLUSTERS = 512
PAR_DEV = 16
PARENTS = 64
LOCAL_PAIRS = 256


def draw_panel_mask(key, part):
    key = jax.random.fold_in(key, 5)
    counts = jax.random.randint(key, (CLUSTERS, 1), P_SIZE // 2, P_SIZE + 1)
    return (jnp.arange(P_SIZE, dtype=jnp.int32)[None, :] < counts).astype(jnp.int32)


def draw_geometry(key, part):
    key = jax.random.fold_in(key, 7)
    key_pos, key_rad = jax.random.split(key)
    points = jax.random.uniform(key_pos, (CLUSTERS, 3, P_SIZE), jnp.float32, -1.0, 1.0)
    log_rad = jax.random.uniform(key_rad, (CLUSTERS, 1, P_SIZE), jnp.float32, jnp.log(0.05), jnp.log(0.3))
    return jnp.concatenate([points, jnp.exp(log_rad)], axis=1).astype(jnp.float32)


def draw_remote_live(key, part):
    key = jax.random.fold_in(key, 11)
    key_mid, key_far = jax.random.split(key)
    rows = jnp.arange(OWNERS, dtype=jnp.int32)[:, None]
    cols = jnp.arange(OWNERS, dtype=jnp.int32)[None, :]
    spread = jnp.abs(rows - cols)
    cycle = jnp.minimum(spread, OWNERS - spread)
    middle = jax.random.randint(key_mid, (OWNERS, OWNERS), CAP // 4, CAP + 1)
    distant = jax.random.randint(key_far, (OWNERS, OWNERS), CAP // 4, CAP // 2 + 1)
    counts = jnp.where(cycle == 0, 0, jnp.where(cycle == 1, CAP, jnp.where(cycle == 2, middle, distant)))
    return (jnp.arange(CAP, dtype=jnp.int32)[None, None, :] < counts[:, :, None]).astype(jnp.int32)


def draw_local_pairs(key, part):
    key = jax.random.fold_in(key, 13)
    key_first, key_offset = jax.random.split(key)
    first = jax.random.randint(key_first, (OWNERS, LOCAL_PAIRS), 0, CL_DEV)
    offset = jax.random.randint(key_offset, (OWNERS, LOCAL_PAIRS), 1, 4)
    second = (first + offset) % CL_DEV
    return jnp.stack([first, second], axis=2).astype(jnp.int32)


def draw_parent_of(key, part):
    key = jax.random.fold_in(key, 17)
    keys = jax.random.split(key, OWNERS)
    orders = jax.vmap(lambda single_key: jax.random.permutation(single_key, CL_DEV))(keys)
    return (orders // BRANCH).reshape(CLUSTERS).astype(jnp.int32)


def with_ends(values, key, least, top_value):
    longest = values.shape.index(max(values.shape))
    spots = []
    for shift in (0, 1):
        where = [jax.random.randint(jax.random.fold_in(key, axis), (), 0, length) for axis, length in enumerate(values.shape)]
        where[longest] = (where[longest] + shift) % values.shape[longest]
        spots.append(tuple(where))
    return values.at[spots[0]].set(least).at[spots[1]].set(top_value)


def block_levels(stream_key, shape, cuts, least, top_value):
    factor_of = 1.0
    for position, blocks in cuts:
        steps = jax.random.uniform(jax.random.fold_in(jax.random.fold_in(stream_key, 6), position), (blocks,), jnp.float32, least / len(cuts), top_value / len(cuts))
        factor_of = factor_of * jnp.repeat(jnp.exp(steps), shape[position] // blocks).reshape((-1,) + (1,) * (len(shape) - 1 - position))
    return factor_of


def normal_values(key, extent, scale, reach, cuts=(), kind=jnp.bfloat16):
    drawn = scale * jax.random.normal(key, extent, jnp.float32)
    if cuts:
        drawn = drawn * block_levels(key, extent, cuts, -0.22, 0.18)
    return jnp.clip(drawn, -reach, reach).astype(kind)


def setup_inputs(seed: int = 0, part: int = 0) -> dict:
    key_of = jax.random.split(jax.random.key(seed), 13)
    own_keys = jax.random.split(jax.random.fold_in(key_of[12], part), 13)
    charges = normal_values(own_keys[0], (CLUSTERS, P_SIZE), 0.1, 0.6, ((0, 4), (1, 2)), jnp.float32)
    panel_mask = draw_panel_mask(jax.random.fold_in(jax.random.fold_in(key_of[12], part), 71), part)
    geometry = draw_geometry(jax.random.fold_in(jax.random.fold_in(key_of[12], part), 71), part)
    remote_source = with_ends(jax.random.randint(own_keys[3], (OWNERS, OWNERS, CAP), 0, CL_DEV), jax.random.fold_in(own_keys[3], 1), 0, CL_DEV - 1).astype(jnp.int32)
    remote_target = with_ends(jax.random.randint(own_keys[4], (OWNERS, OWNERS, CAP), 0, CL_DEV), jax.random.fold_in(own_keys[4], 1), 0, CL_DEV - 1).astype(jnp.int32)
    remote_live = draw_remote_live(jax.random.fold_in(jax.random.fold_in(key_of[12], part), 71), part)
    local_pairs = draw_local_pairs(jax.random.fold_in(jax.random.fold_in(key_of[12], part), 71), part)
    basis = normal_values(own_keys[7], (CLUSTERS, P_SIZE, R), 0.15, 0.9, ((0, 4), (1, 2)), jnp.float32)
    transfer = normal_values(own_keys[8], (CLUSTERS, R, R), R ** -0.5, 1.0, ((0, 4),), jnp.float32)
    parent_of = draw_parent_of(jax.random.fold_in(jax.random.fold_in(key_of[12], part), 71), part)
    far_list = with_ends(jax.random.randint(own_keys[10], (PARENTS, FAR_N), 0, PARENTS), jax.random.fold_in(own_keys[10], 1), 0, PARENTS - 1).astype(jnp.int32)
    coupling = normal_values(own_keys[11], (PARENTS, FAR_N, R, R), (R * FAR_N) ** -0.5, 0.375, ((0, 4),), jnp.float32)
    return {"charges": charges, "panel_mask": panel_mask, "geometry": geometry, "remote_source": remote_source, "remote_target": remote_target, "remote_live": remote_live, "local_pairs": local_pairs, "basis": basis, "transfer": transfer, "parent_of": parent_of, "far_list": far_list, "coupling": coupling}


def kernel_tile(rows_geo, cols_geo):
    delta = rows_geo[:, :3, :, None] - cols_geo[:, :3, None, :]
    dist_sq = lax.optimization_barrier(jnp.sum(delta * delta, axis=1))
    radius_sq = rows_geo[:, 3, :, None] * rows_geo[:, 3, :, None] + cols_geo[:, 3, None, :] * cols_geo[:, 3, None, :]
    return lax.rsqrt(dist_sq + radius_sq)

def pair_terms(rows_geo, rows_q, cols_geo, cols_q):
    tile = kernel_tile(rows_geo, cols_geo)
    return (lax.optimization_barrier(jnp.sum(tile * cols_q[:, None, :], axis=2)), lax.optimization_barrier(jnp.sum(tile * rows_q[:, :, None], axis=1)))

def reference(charges, panel_mask, geometry, remote_source, remote_target, remote_live, local_pairs, basis, transfer, parent_of, far_list, coupling):
    highest = lax.Precision.HIGHEST
    maskf = panel_mask.astype(jnp.float32)
    masked = charges * maskf
    owner_base = jnp.arange(OWNERS, dtype=jnp.int32) * CL_DEV
    self_idx = jnp.arange(CLUSTERS, dtype=jnp.int32)
    local_a = (local_pairs[:, :, 0] + owner_base[:, None]).reshape(-1)
    local_b = (local_pairs[:, :, 1] + owner_base[:, None]).reshape(-1)
    remote_a = (remote_target + owner_base[:, None, None]).reshape(-1)
    remote_b = (remote_source + owner_base[None, :, None]).reshape(-1)
    live_f = remote_live.reshape(-1).astype(jnp.float32)
    first = jnp.concatenate([self_idx, local_a, remote_a]).astype(jnp.int32)
    second = jnp.concatenate([self_idx, local_b, remote_b]).astype(jnp.int32)
    forward_w = jnp.concatenate([jnp.ones((CLUSTERS,), jnp.float32), jnp.ones(local_a.shape, jnp.float32), live_f])
    reverse_w = jnp.concatenate([jnp.zeros((CLUSTERS,), jnp.float32), jnp.ones(local_a.shape, jnp.float32), live_f])
    total = first.shape[0]
    step_len = math.gcd(total, 64)

    def single(args):
        first_blk, second_blk, fw_blk, rw_blk = args
        forward, backward = pair_terms(geometry[first_blk], masked[first_blk], geometry[second_blk], masked[second_blk])
        return (forward * fw_blk[:, None], backward * rw_blk[:, None])
    shaped = tuple((x.reshape((total // step_len, step_len)) for x in (first, second, forward_w, reverse_w)))
    forward, backward = lax.map(single, shaped)
    near = jnp.zeros((CLUSTERS, P_SIZE), jnp.float32)
    near = near.at[first].add(forward.reshape(total, P_SIZE))
    near = near.at[second].add(backward.reshape(total, P_SIZE))
    leaf = jnp.einsum('cpr,cp->cr', basis, masked, precision=highest)
    lifted = jnp.einsum('crs,cr->cs', transfer, leaf, precision=highest)
    parent_global = (parent_of + jnp.arange(CLUSTERS, dtype=jnp.int32) // CL_DEV * PAR_DEV).astype(jnp.int32)
    upward = jax.ops.segment_sum(lifted, parent_global, num_segments=PARENTS)
    field = jnp.einsum('pkrs,pks->pr', coupling, upward[far_list], precision=highest)
    leaf_field = jnp.einsum('crs,cs->cr', transfer, field[parent_global], precision=highest)
    far = jnp.einsum('cpr,cr->cp', basis, leaf_field, precision=highest)
    return maskf * (near + far)
```

```python
import functools

import jax
import jax.numpy as jnp
from jax import lax
from jax.experimental import pallas as pl
from jax.experimental.pallas import tpu as pltpu
from jax.sharding import PartitionSpec as P

F32 = jnp.float32
BF16 = jnp.bfloat16
HIGHEST = lax.Precision.HIGHEST
ROWS = 40
LANES = 128
PARAMS = pltpu.CompilerParams(vmem_limit_bytes=56 * 1024 * 1024)


def vmem():
    return pl.BlockSpec(memory_space=pltpu.VMEM)


def smem():
    return pl.BlockSpec(memory_space=pltpu.SMEM)


def whole(size):
    return -(-size // LANES) * LANES


def cut(v):
    return v.astype(BF16).astype(F32)


def powers(sign):
    lane = lax.broadcasted_iota(jnp.int32, (8, LANES), 1)
    out = jnp.full((8, LANES), 2.0 ** (-64 * sign), F32)
    for bit in range(7):
        out = out * jnp.where((lane >> bit) & 1 == 1, F32(2.0 ** (sign * 2**bit)), F32(1.0))
    return out


def frame(parts):
    low = [functools.reduce(jnp.minimum, [jnp.min(p[k]) for p in parts]) for k in range(3)]
    high = [functools.reduce(jnp.maximum, [jnp.max(p[k]) for p in parts]) for k in range(3)]
    width = functools.reduce(jnp.maximum, [jnp.max(jnp.abs(p[3])) for p in parts])
    for lo, hi in zip(low, high):
        width = jnp.maximum(width, 0.5 * (hi - lo))
    up, down = powers(1), powers(-1)
    size = jnp.min(jnp.where(up >= width, up, F32(2.0**63)))
    inv = jnp.max(jnp.where(up >= width, down, F32(2.0**-63)))
    magic = size * F32(1.5 * 2.0**20)
    centre = [(0.5 * (lo + hi) + magic) - magic for lo, hi in zip(low, high)]
    return centre, inv


def split_features(points, centre, inv):
    magic = F32(1.5 * 2.0**16)
    grid, rest = [], []
    for k in range(3):
        u = (points[k] - centre[k]) * inv
        h = (u + magic) - magic
        grid.append(h)
        rest.append(u - h)
    rad = points[3] * inv
    norm = grid[0] * grid[0] + grid[1] * grid[1] + grid[2] * grid[2]
    norm1 = cut(norm)
    norm2 = norm - norm1
    cross = grid[0] * rest[0] + grid[1] * rest[1] + grid[2] * rest[2]
    extra = 2.0 * cross + (rest[0] * rest[0] + rest[1] * rest[1] + rest[2] * rest[2]) + rad * rad
    extra1 = cut(extra)
    extra2 = cut(extra - extra1)
    extra3 = (extra - extra1) - extra2
    rest1 = [cut(v) for v in rest]
    rest2 = [v - w for v, w in zip(rest, rest1)]
    neg = lambda vs: [-2.0 * v for v in vs]
    one, zero = jnp.ones_like(rad), jnp.zeros_like(rad)
    left = grid + [norm1, norm2, one, one]
    right = neg(grid) + [one, one, norm1, norm2]
    left += [extra1, extra2, extra3, one, one, one]
    right += [one, one, one, extra1, extra2, extra3]
    left += grid + grid + rest1 + rest2 + rest1 + rest1 + rest2
    right += neg(rest1) + neg(rest2) + neg(grid) + neg(grid) + neg(rest1) + neg(rest2) + neg(rest1)
    left += [zero] * (ROWS - len(left))
    right += [zero] * (ROWS - len(right))
    return left, right, rad


def store_features(ref, rows):
    count = rows[0].shape[0]
    width = rows[0].shape[1]
    for k, row in enumerate(rows):
        for t, piece in enumerate(ref):
            piece[pl.ds(k, count, stride=ROWS), :] = row[:, t * LANES : min(width, (t + 1) * LANES)]


def load_features(ref, index):
    start = pl.multiple_of(index * ROWS, 8)
    return [piece[pl.ds(start, ROWS), :].astype(BF16) for piece in ref]


def contract(left, right):
    return lax.dot_general(left, right, (((0,), (0,)), ((), ())), preferred_element_type=F32)


def column(table, index):
    if table.shape[1] == LANES and table.shape[0] % 8 == 0:
        return jnp.take_along_axis(table, jnp.full(table.shape, index, jnp.int32), axis=1)
    lane = lax.broadcasted_iota(jnp.int32, table.shape, 1)
    picked = jnp.sum(jnp.where(lane == index, table, 0.0), axis=1, keepdims=True)
    return jnp.broadcast_to(picked, (table.shape[0], LANES))


def put_column(table_ref, first, value, second=None, other=None):
    lane = lax.broadcasted_iota(jnp.int32, table_ref.shape, 1)
    add = jnp.where(lane == first, value, 0.0)
    if second is not None:
        add = add + jnp.where(lane == second, other, 0.0)
    table_ref[...] += add


def pack_kernel(sizes, charges, mask, geo, targets, sources, live, masked, codes, *packs):
    C, S, L, slots = sizes
    me, sub = lax.axis_index("clu"), lax.axis_index("sub")
    masked[...] = charges[...] * mask[...].astype(F32)
    for shift in range(1, C):
        dest = lax.rem(me + shift, C)
        for j in range(slots):
            codes[shift - 1, j] = jnp.where(live[dest, j] > 0, sources[dest, j], -1)

    def fill(s):
        for shift in range(1, C):
            dest = lax.rem(me + shift, C)
            pack = packs[shift - 1]
            for j in range(slots):
                t = targets[dest, j]
                g = geo[t, :, s * L : (s + 1) * L]
                for k in range(4):
                    pack[k * slots + j : k * slots + j + 1, :] = g[k : k + 1]
                pack[4 * slots + j : 4 * slots + j + 1, :] = masked[pl.ds(t, 1), :]

    for s in range(S):
        pl.when(sub == s)(functools.partial(fill, s))


def local_kernel(sizes, geo, pairs, *rest):
    C, S, L, R, clusters, panels = sizes
    pieces = rest[:S]
    ups = rest[S : 2 * S]
    acc_out, up_sum = rest[2 * S : 2 * S + 2]
    q, qt, acc, acct, fa0, fa1, fb0, fb1, rads = rest[2 * S + 2 :]
    fa, fb = (fa0, fa1), (fb0, fb1)
    sub, rep = lax.axis_index("sub"), lax.axis_index("rep")
    total = ups[0][...]
    for u in ups[1:]:
        total = total + u[...]
    up_sum[...] = total

    def place(s):
        for shift in range(S):
            owner = (s - shift) % S
            q[:, owner * L : (owner + 1) * L] = pieces[shift][...]

    for s in range(S):
        pl.when(sub == s)(functools.partial(place, s))
    qt[...] = q[...].T
    acc[...] = jnp.zeros_like(acc)
    acct[...] = jnp.zeros_like(acct)
    points = [geo[:, k, :] for k in range(4)]
    centre, inv = frame([points])
    left, right, rad = split_features(points, centre, inv)
    store_features(fa, left)
    store_features(fb, right)
    rads[...] = rad

    half = panels // 2
    share = clusters // (S * R)
    first = (rep * S + sub) * share

    def self_tile(c):
        a = load_features(fa, c)
        b = load_features(fb, c)
        qrow = q[pl.ds(c, 1), :]
        radius = rads[pl.ds(c, 1), :]
        diag = lax.rsqrt(2.0 * (radius * radius))
        eye = lax.broadcasted_iota(jnp.int32, (half, half), 0) == lax.broadcasted_iota(
            jnp.int32, (half, half), 1
        )
        d00 = contract(a[0], b[0])
        d01 = contract(a[0], b[1])
        d11 = contract(a[1], b[1])
        g00 = jnp.where(eye, diag[:, :half], lax.rsqrt(d00))
        g11 = jnp.where(eye, diag[:, half:], lax.rsqrt(d11))
        g01 = lax.rsqrt(d01)
        qcol = column(qt[:half, :], c)
        top = jnp.sum(g00 * qrow[:, :half] + g01 * qrow[:, half:], axis=1, keepdims=True)
        bottom = jnp.sum(g11 * qrow[:, half:], axis=1, keepdims=True)
        back = jnp.sum(g01 * qcol, axis=0, keepdims=True)
        return top, bottom, jnp.concatenate([jnp.zeros_like(back), back], axis=1)

    def self_step(i, carry):
        c0 = first + 2 * i
        c1 = c0 + 1
        top0, bottom0, back0 = self_tile(c0)
        top1, bottom1, back1 = self_tile(c1)
        lane = lax.broadcasted_iota(jnp.int32, (half, clusters), 1)
        acct[:half, :] += jnp.where(lane == c0, top0, 0.0) + jnp.where(lane == c1, top1, 0.0)
        acct[half:, :] += jnp.where(lane == c0, bottom0, 0.0) + jnp.where(lane == c1, bottom1, 0.0)
        acc[pl.ds(c0, 1), :] += back0
        acc[pl.ds(c1, 1), :] += back1
        return carry

    lax.fori_loop(0, share // 2, self_step, 0)

    count = pairs.shape[1] // S
    begin = sub * count

    def pair_tile(p):
        ia, ib = pairs[0, p], pairs[1, p]
        a = load_features(fa, ia)
        b = load_features(fb, ib)
        left = jnp.concatenate(a, axis=1)
        g0 = lax.rsqrt(contract(left, b[0]))
        g1 = lax.rsqrt(contract(left, b[1]))
        qb = q[pl.ds(ib, 1), :]
        qcol = column(qt[...], ia)
        fwd = jnp.sum(g0 * qb[:, :LANES] + g1 * qb[:, LANES:], axis=1, keepdims=True)
        back = jnp.concatenate(
            [jnp.sum(g * qcol, axis=0, keepdims=True) for g in (g0, g1)], axis=1
        )
        return ia, ib, fwd, back

    def pair_step(i, carry):
        ia0, ib0, fwd0, back0 = pair_tile(begin + 2 * i)
        ia1, ib1, fwd1, back1 = pair_tile(begin + 2 * i + 1)
        put_column(acct, ia0, fwd0, ia1, fwd1)
        acc[pl.ds(ib0, 1), :] += back0
        acc[pl.ds(ib1, 1), :] += back1
        return carry

    lax.fori_loop(0, count // 2, pair_step, 0)
    acc_out[...] = (acc[...] + acct[...].T) * inv


def remote_kernel(sizes, geo, codes, acc_in, *rest):
    C, S, L, slots, clusters, panels = sizes
    pieces = rest[:S]
    packs = rest[S : S + C - 1]
    outs = rest[S + C - 1 : 2 * (S + C - 1)]
    parts, sends = outs[:S], outs[S:]
    q, tqt, acc, fwdt, sgeo, fa0, fb0, fb1, order = rest[2 * (S + C - 1) :]
    fa, fb = (fa0,), (fb0, fb1)
    sub = lax.axis_index("sub")
    n = (C - 1) * slots

    def place(s):
        for shift in range(S):
            owner = (s - shift) % S
            q[:, owner * L : (owner + 1) * L] = pieces[shift][...]

    for s in range(S):
        pl.when(sub == s)(functools.partial(place, s))
    acc[...] = jnp.zeros_like(acc)
    fwdt[...] = jnp.zeros_like(fwdt)
    found = jnp.int32(0)
    for shift in range(C - 1):
        for j in range(slots):
            code = codes[shift, j]
            order[found] = shift * slots + j
            found = found + (code >= 0).astype(jnp.int32)
            g = geo[jnp.maximum(code, 0)]
            for k in range(4):
                row = k * n + shift * slots + j
                sgeo[row : row + 1, :] = g[k : k + 1]
    tpoints = [
        jnp.concatenate([p[k * slots : (k + 1) * slots, :] for p in packs], axis=0) for k in range(5)
    ]
    spoints = [sgeo[k * n : (k + 1) * n, :] for k in range(4)]
    centre, inv = frame([tpoints, spoints])
    left, _, _ = split_features(tpoints, centre, inv)
    _, right, _ = split_features(spoints, centre, inv)
    store_features(fa, left)
    store_features(fb, right)
    wide = tqt.shape[1]
    tq = tpoints[4]
    if wide > n:
        tq = jnp.concatenate([tq, jnp.zeros((wide - n, L), F32)], axis=0)
    tqt[...] = tq.T

    def tile(i):
        ok = i < found
        slot = order[jnp.minimum(i, found - 1)]
        source = codes[slot // slots, lax.rem(slot, slots)]
        (a,) = load_features(fa, slot)
        b = load_features(fb, slot)
        g0 = lax.rsqrt(contract(a, b[0]))
        g1 = lax.rsqrt(contract(a, b[1]))
        qb = q[pl.ds(source, 1), :]
        qcol = column(tqt[...], slot)
        fwd = jnp.sum(g0 * qb[:, :LANES] + g1 * qb[:, LANES:], axis=1, keepdims=True)
        back = jnp.concatenate(
            [jnp.sum(g * qcol, axis=0, keepdims=True) for g in (g0, g1)], axis=1
        )
        return jnp.where(ok, slot, -1), source, fwd, jnp.where(ok, back, 0.0)

    def step(i, carry):
        slot0, source0, fwd0, back0 = tile(2 * i)
        slot1, source1, fwd1, back1 = tile(2 * i + 1)
        put_column(fwdt, slot0, fwd0, slot1, fwd1)
        acc[pl.ds(source0, 1), :] += back0
        acc[pl.ds(source1, 1), :] += back1
        return carry

    lax.fori_loop(0, (found + 1) // 2, step, 0)
    total = acc_in[...] + acc[...] * inv

    def give(s):
        for shift in range(S):
            other = (s + shift) % S
            parts[shift][...] = total[:, other * L : (other + 1) * L]

    for s in range(S):
        pl.when(sub == s)(functools.partial(give, s))
    fwd = (fwdt[...] * inv).T
    for shift in range(C - 1):
        sends[shift][...] = fwd[shift * slots : (shift + 1) * slots, :]


def up_kernel(basis, masked, transfer, parent, up):
    clusters = basis.shape[0]
    rank = basis.shape[1]
    lane = lax.broadcasted_iota(jnp.int32, (rank, clusters), 1)
    leaf = jnp.zeros((rank, clusters), F32)
    for c in range(clusters):
        part = jnp.sum(basis[c] * masked[c : c + 1, :], axis=1, keepdims=True)
        leaf = jnp.where(lane == c, part, leaf)
    lifted = jnp.zeros((rank, clusters), F32)
    for r in range(rank):
        lifted = lifted + transfer[r] * leaf[r : r + 1, :]
    which = lax.broadcasted_iota(jnp.int32, (up.shape[0], clusters), 0)
    onehot = (parent[...] == which).astype(F32)
    up[...] = lax.dot_general(
        onehot, lifted, (((1,), (1,)), ((), ())), precision=HIGHEST, preferred_element_type=F32
    )


def down_kernel(sizes, far_list, coupling, transfer, parent, basis, *rest):
    C = sizes
    ups = rest[:C]
    far, parents, leaf_field = rest[C:]
    me = lax.axis_index("clu")
    par_dev, far_n, rank = coupling.shape[0], coupling.shape[1], coupling.shape[2]
    clusters = basis.shape[0]
    for shift in range(C):
        owner = lax.rem(me + C - shift, C)
        parents[pl.ds(pl.multiple_of(owner * par_dev, 8), par_dev), :] = ups[shift][...]
    lane = lax.broadcasted_iota(jnp.int32, (rank, LANES), 1)
    field = jnp.zeros((rank, LANES), F32)
    for p in range(par_dev):
        part = jnp.zeros((rank, rank), F32)
        for k in range(far_n):
            part = part + coupling[p, k] * parents[pl.ds(far_list[p, k], 1), :]
        field = jnp.where(lane == p, jnp.sum(part, axis=1, keepdims=True), field)
    which = lax.broadcasted_iota(jnp.int32, (LANES, clusters), 0)
    onehot = (parent[...] == which).astype(F32)
    down = jnp.dot(field, onehot, precision=HIGHEST, preferred_element_type=F32)
    for r in range(rank):
        leaf_field[r : r + 1, :] = jnp.sum(transfer[r] * down, axis=0, keepdims=True)
    fields = leaf_field[...]
    for c in range(clusters):
        far[c : c + 1, :] = jnp.sum(basis[c] * fields[:, c : c + 1], axis=0, keepdims=True)


def final_kernel(sizes, *rest):
    C, S, R, slots = sizes
    lists = rest[:R]
    mask, far = rest[R : R + 2]
    near = rest[R + 2 : R + 2 + S * R]
    sums = rest[R + 2 + S * R : -1]
    out = rest[-1]
    me = lax.axis_index("clu")
    total = far[...]
    for part in near:
        total = total + part[...]
    out[...] = total
    for r in range(R):
        for shift in range(1, C):
            dest = lax.rem(me + shift, C)
            got = sums[r * (C - 1) + shift - 1]
            for j in range(slots):
                t = lists[r][dest, j]
                out[pl.ds(t, 1), :] += got[j : j + 1, :]
    out[...] = out[...] * mask[...].astype(F32)


def send(value, moves):
    names = tuple(name for name, _ in moves)
    steps = [step for _, step in moves]
    sizes = [lax.axis_size(name) for name in names]
    perm = []

    def flat(coords):
        index = 0
        for size, c in zip(sizes, coords):
            index = index * size + c
        return index

    total = 1
    for size in sizes:
        total *= size
    for index in range(total):
        coords, left = [], index
        for size in reversed(sizes):
            coords.append(left % size)
            left //= size
        coords.reverse()
        perm.append((index, flat([(c + s) % n for c, s, n in zip(coords, steps, sizes)])))
    return lax.ppermute(value, names if len(names) > 1 else names[0], perm)


def on_device(
    charges,
    panel_mask,
    geometry,
    remote_source,
    remote_target,
    remote_live,
    local_pairs,
    basis,
    transfer,
    parent_of,
    far_list,
    coupling,
):
    clusters, L = charges.shape
    panels = geometry.shape[2]
    C, S, R = lax.axis_size("clu"), lax.axis_size("sub"), lax.axis_size("rep")
    slots = remote_source.shape[2]
    par_dev, rank = far_list.shape[0], transfer.shape[1]
    n = (C - 1) * slots
    shape = jax.ShapeDtypeStruct
    targets = remote_target[0]
    basis_t = jnp.transpose(basis, (0, 2, 1))
    transfer_t = jnp.transpose(transfer, (1, 2, 0))
    parent = parent_of[None, :]

    made = pl.pallas_call(
        functools.partial(pack_kernel, (C, S, L, slots)),
        out_shape=[shape((clusters, L), F32), shape((C - 1, slots), jnp.int32)]
        + [shape((5 * slots, L), F32)] * (C - 1),
        in_specs=[vmem()] * 3 + [smem()] * 3,
        out_specs=[vmem(), smem()] + [vmem()] * (C - 1),
        compiler_params=PARAMS,
        name="packs",
    )(charges, panel_mask, geometry, targets, remote_source[0], remote_live[0])
    masked, codes, packs = made[0], made[1], made[2:]
    pieces = [masked] + [send(masked, (("sub", d),)) for d in range(1, S)]
    got_packs = [send(packs[d - 1], (("clu", d),)) for d in range(1, C)]
    got_codes = jnp.concatenate([send(codes[d - 1 : d], (("clu", d),)) for d in range(1, C)], axis=0)
    lists = [targets] + [send(targets, (("rep", d),)) for d in range(1, R)]

    up = pl.pallas_call(
        up_kernel,
        out_shape=shape((par_dev, rank), F32),
        in_specs=[vmem()] * 4,
        out_specs=vmem(),
        compiler_params=PARAMS,
        name="far_up",
    )(basis_t, masked, transfer_t, parent)
    ups = [up] + [send(up, (("sub", d),)) for d in range(1, S)]

    half = [pltpu.VMEM((clusters * ROWS, LANES), F32)] * 2
    acc, up_sum = pl.pallas_call(
        functools.partial(local_kernel, (C, S, L, R, clusters, panels)),
        out_shape=[shape((clusters, panels), F32), shape((par_dev, rank), F32)],
        in_specs=[vmem(), smem()] + [vmem()] * (2 * S),
        out_specs=[vmem(), vmem()],
        scratch_shapes=[
            pltpu.VMEM((clusters, panels), F32),
            pltpu.VMEM((panels, clusters), F32),
            pltpu.VMEM((clusters, panels), F32),
            pltpu.VMEM((panels, clusters), F32),
            *half,
            *half,
            pltpu.VMEM((clusters, panels), F32),
        ],
        compiler_params=PARAMS,
        name="near_local",
    )(geometry, local_pairs[0].T, *pieces, *ups)
    all_ups = [up_sum] + [send(up_sum, (("clu", d),)) for d in range(1, C)]

    made = pl.pallas_call(
        functools.partial(remote_kernel, (C, S, L, slots, clusters, panels)),
        out_shape=[shape((clusters, L), F32)] * S + [shape((slots, L), F32)] * (C - 1),
        in_specs=[vmem(), smem()] + [vmem()] * (1 + S + C - 1),
        out_specs=[vmem()] * (S + C - 1),
        scratch_shapes=[
            pltpu.VMEM((clusters, panels), F32),
            pltpu.VMEM((L, whole(n)), F32),
            pltpu.VMEM((clusters, panels), F32),
            pltpu.VMEM((L, whole(n)), F32),
            pltpu.VMEM((4 * n, panels), F32),
            pltpu.VMEM((n * ROWS, L), F32),
            pltpu.VMEM((n * ROWS, LANES), F32),
            pltpu.VMEM((n * ROWS, LANES), F32),
            pltpu.SMEM((n + 1,), jnp.int32),
        ],
        compiler_params=PARAMS,
        name="near_remote",
    )(geometry, got_codes, acc, *pieces, *got_packs)
    parts, sums = made[:S], made[S:]
    near = []
    for d in range(S):
        for e in range(R):
            near.append(send(parts[d], (("sub", d), ("rep", e))) if d or e else parts[0])
    back = []
    for e in range(R):
        for d in range(1, C):
            back.append(send(sums[d - 1], (("clu", C - d), ("rep", e))))

    far = pl.pallas_call(
        functools.partial(down_kernel, C),
        out_shape=shape((clusters, L), F32),
        in_specs=[smem()] + [vmem()] * (4 + C),
        out_specs=vmem(),
        scratch_shapes=[pltpu.VMEM((C * par_dev, rank), F32), pltpu.VMEM((rank, clusters), F32)],
        compiler_params=PARAMS,
        name="far_down",
    )(far_list, coupling, transfer_t, parent, basis_t, *all_ups)

    return pl.pallas_call(
        functools.partial(final_kernel, (C, S, R, slots)),
        out_shape=shape((clusters, L), F32),
        in_specs=[smem()] * R + [vmem()] * (2 + S * R + R * (C - 1)),
        out_specs=vmem(),
        compiler_params=PARAMS,
        name="combine",
    )(*lists, panel_mask, far, *near, *back)


def solution(mesh):
    placed = (
        P(("grp", "clu"), "sub"),
        P(("grp", "clu"), "sub"),
        P(("grp", "clu"), None, None),
        P(("grp", "clu"), None, "rep"),
        P(("grp", "clu"), None, "rep"),
        P(("grp", "clu"), None, "rep"),
        P(("grp", "clu"), "rep", None),
        P(("grp", "clu"), "sub", None),
        P(("grp", "clu"), None, None),
        P(("grp", "clu")),
        P(("grp", "clu"), None),
        P(("grp", "clu"), None, None, None),
    )
    return jax.shard_map(
        on_device, mesh=mesh, in_specs=placed, out_specs=P(("grp", "clu"), "sub"), check_vma=False
    )
```

```python
import functools

import jax
import jax.numpy as jnp
from jax import lax
from jax.experimental import pallas as pl
from jax.experimental.pallas import tpu as pltpu
from jax.sharding import PartitionSpec as P

F32 = jnp.float32
BF16 = jnp.bfloat16
HIGHEST = lax.Precision.HIGHEST
ROWS = 40
USED = 34
LANES = 128
PARAMS = pltpu.CompilerParams(vmem_limit_bytes=56 * 1024 * 1024)


def vmem():
    return pl.BlockSpec(memory_space=pltpu.VMEM)


def smem():
    return pl.BlockSpec(memory_space=pltpu.SMEM)


def whole(size):
    return -(-size // LANES) * LANES


def cut(v):
    return v.astype(BF16).astype(F32)


def powers(sign):
    lane = lax.broadcasted_iota(jnp.int32, (8, LANES), 1)
    out = jnp.full((8, LANES), 2.0 ** (-64 * sign), F32)
    for bit in range(7):
        out = out * jnp.where((lane >> bit) & 1 == 1, F32(2.0 ** (sign * 2**bit)), F32(1.0))
    return out


def frame(parts):
    low = [functools.reduce(jnp.minimum, [jnp.min(p[k]) for p in parts]) for k in range(3)]
    high = [functools.reduce(jnp.maximum, [jnp.max(p[k]) for p in parts]) for k in range(3)]
    width = functools.reduce(jnp.maximum, [jnp.max(jnp.abs(p[3])) for p in parts])
    for lo, hi in zip(low, high):
        width = jnp.maximum(width, 0.5 * (hi - lo))
    up, down = powers(1), powers(-1)
    size = jnp.min(jnp.where(up >= width, up, F32(2.0**63)))
    inv = jnp.max(jnp.where(up >= width, down, F32(2.0**-63)))
    magic = size * F32(1.5 * 2.0**20)
    centre = [(0.5 * (lo + hi) + magic) - magic for lo, hi in zip(low, high)]
    return centre, inv


def split_features(points, centre, inv):
    magic = F32(1.5 * 2.0**16)
    grid, rest = [], []
    for k in range(3):
        u = (points[k] - centre[k]) * inv
        h = (u + magic) - magic
        grid.append(h)
        rest.append(u - h)
    rad = points[3] * inv
    norm = grid[0] * grid[0] + grid[1] * grid[1] + grid[2] * grid[2]
    norm1 = cut(norm)
    norm2 = norm - norm1
    cross = grid[0] * rest[0] + grid[1] * rest[1] + grid[2] * rest[2]
    extra = 2.0 * cross + (rest[0] * rest[0] + rest[1] * rest[1] + rest[2] * rest[2]) + rad * rad
    extra1 = cut(extra)
    extra2 = cut(extra - extra1)
    extra3 = (extra - extra1) - extra2
    rest1 = [cut(v) for v in rest]
    rest2 = [v - w for v, w in zip(rest, rest1)]
    neg = lambda vs: [-2.0 * v for v in vs]
    one = jnp.ones_like(rad)
    left = grid + [norm1, norm2, one, one]
    right = neg(grid) + [one, one, norm1, norm2]
    left += [extra1, extra2, extra3, one, one, one]
    right += [one, one, one, extra1, extra2, extra3]
    left += grid + grid + rest1 + rest2 + rest1 + rest1 + rest2
    right += neg(rest1) + neg(rest2) + neg(grid) + neg(grid) + neg(rest1) + neg(rest2) + neg(rest1)
    return left, right, rad


def store_features(ref, rows):
    count = rows[0].shape[0]
    width = rows[0].shape[1]
    for k, row in enumerate(rows):
        for t, piece in enumerate(ref):
            piece[pl.ds(k, count, stride=ROWS), :] = row[:, t * LANES : min(width, (t + 1) * LANES)]


def load_features(ref, index):
    start = pl.multiple_of(index * ROWS, 8)
    return [piece[pl.ds(start, USED), :].astype(BF16) for piece in ref]


def contract(left, right):
    return lax.dot_general(left, right, (((0,), (0,)), ((), ())), preferred_element_type=F32)


def column(table, index):
    if table.shape[1] == LANES and table.shape[0] % 8 == 0:
        return jnp.take_along_axis(table, jnp.full(table.shape, index, jnp.int32), axis=1)
    lane = lax.broadcasted_iota(jnp.int32, table.shape, 1)
    picked = jnp.sum(jnp.where(lane == index, table, 0.0), axis=1, keepdims=True)
    return jnp.broadcast_to(picked, (table.shape[0], LANES))


def put_column(table_ref, rows, index, value):
    lane = lax.broadcasted_iota(jnp.int32, (rows.stop - rows.start, table_ref.shape[1]), 1)
    table_ref[rows, :] += jnp.where(lane == index, value, 0.0)


def fold(v):
    return jnp.sum(v.reshape(v.shape[0] // 8, 8, v.shape[1]), axis=0)


def distances(left, right, out):
    whole_left = jnp.concatenate(left, axis=1) if len(left) > 1 else left[0]
    for t, r in enumerate(right):
        out[:, t * LANES : (t + 1) * LANES] = contract(whole_left, r)


def tile_sums(dist, qrow, qtable, slot, table_ref, index, step=64):
    height = dist.shape[0]
    step = min(step, height)
    q0, q1 = qrow[:, :LANES], qrow[:, LANES:]
    back0 = back1 = jnp.zeros((8, LANES), F32)
    for r in range(0, height, step):
        rows = slice(r, r + step)
        g0 = lax.rsqrt(dist[rows, :LANES])
        g1 = lax.rsqrt(dist[rows, LANES:])
        qcol = column(qtable[rows, :], slot)
        put_column(table_ref, rows, index, jnp.sum(g0 * q0 + g1 * q1, axis=1, keepdims=True))
        back0 = back0 + fold(g0 * qcol)
        back1 = back1 + fold(g1 * qcol)
    return jnp.concatenate(
        [jnp.sum(back0, axis=0, keepdims=True), jnp.sum(back1, axis=0, keepdims=True)], axis=1
    )


def assemble(sub, S, L, q, pieces):
    def place(s):
        for shift in range(S):
            owner = (s - shift) % S
            q[:, owner * L : (owner + 1) * L] = pieces[shift][...]

    for s in range(S):
        pl.when(sub == s)(functools.partial(place, s))


def pack_kernel(sizes, charges, mask, geo, targets, sources, live, masked, *packs):
    C, S, L, slots = sizes
    me, sub = lax.axis_index("clu"), lax.axis_index("sub")
    masked[...] = charges[...] * mask[...].astype(F32)
    lane = lax.broadcasted_iota(jnp.int32, (8, L), 1)
    for shift in range(1, C):
        dest = lax.rem(me + shift, C)
        codes = jnp.full((8, L), -1.0, F32)
        for j in range(slots):
            code = jnp.where(live[dest, j] > 0, sources[dest, j], -1)
            codes = jnp.where(lane == j, code.astype(F32), codes)
        packs[shift - 1][5 * slots :, :] = codes

    def fill(s):
        for shift in range(1, C):
            dest = lax.rem(me + shift, C)
            pack = packs[shift - 1]
            for j in range(slots):
                t = targets[dest, j]
                g = geo[t, :, s * L : (s + 1) * L]
                for k in range(4):
                    pack[k * slots + j : k * slots + j + 1, :] = g[k : k + 1]
                pack[4 * slots + j : 4 * slots + j + 1, :] = masked[pl.ds(t, 1), :]

    for s in range(S):
        pl.when(sub == s)(functools.partial(fill, s))


def remote_kernel(sizes, geo, codes, up, *rest):
    C, S, L, slots, clusters, panels = sizes
    pieces = rest[:S]
    packs = rest[S : S + C - 1]
    acc_out = rest[S + C - 1]
    sends = rest[S + C : S + C + C - 1]
    q, tqt, acc, fwdt, sgeo, fa0, fb0, fb1, dist0, dist1, order = rest[S + C + C - 1 :]
    fa, fb = (fa0,), (fb0, fb1)
    n = (C - 1) * slots
    assemble(lax.axis_index("sub"), S, L, q, pieces)
    acc[...] = jnp.zeros_like(acc)
    fwdt[...] = jnp.zeros_like(fwdt)
    found = jnp.int32(0)
    for shift in range(C - 1):
        for j in range(slots):
            code = codes[shift, j]
            order[found] = shift * slots + j
            found = found + (code >= 0).astype(jnp.int32)
            g = geo[jnp.maximum(code, 0)]
            for k in range(4):
                row = k * n + shift * slots + j
                sgeo[row : row + 1, :] = g[k : k + 1]
    tpoints = [
        jnp.concatenate([p[k * slots : (k + 1) * slots, :] for p in packs], axis=0) for k in range(5)
    ]
    spoints = [sgeo[k * n : (k + 1) * n, :] for k in range(4)]
    centre, inv = frame([tpoints, spoints])
    left, _, _ = split_features(tpoints, centre, inv)
    _, right, _ = split_features(spoints, centre, inv)
    store_features(fa, left)
    store_features(fb, right)
    wide = tqt.shape[1]
    tq = tpoints[4]
    if wide > n:
        tq = jnp.concatenate([tq, jnp.zeros((wide - n, L), F32)], axis=0)
    tqt[...] = tq.T

    def begin(i, dist):
        slot = order[jnp.minimum(i, jnp.maximum(found - 1, 0))]
        distances(load_features(fa, slot), load_features(fb, slot), dist)

    def finish(i, dist):
        ok = i < found
        slot = order[jnp.minimum(i, jnp.maximum(found - 1, 0))]
        source = jnp.maximum(codes[slot // slots, lax.rem(slot, slots)], 0)
        back = tile_sums(
            dist, q[pl.ds(source, 1), :], tqt, slot, fwdt, jnp.where(ok, slot, -1)
        )
        acc[pl.ds(source, 1), :] += jnp.where(ok, back, 0.0)

    def step(i, carry):
        begin(2 * i + 1, dist1)
        finish(2 * i, dist0)
        begin(2 * i + 2, dist0)
        finish(2 * i + 1, dist1)
        return carry

    begin(0, dist0)
    lax.fori_loop(0, (found + 1) // 2, step, 0)
    acc_out[...] = acc[...] * inv
    fwd = (fwdt[...] * inv).T
    rank = up.shape[1]
    for shift in range(C - 1):
        sends[shift][:slots, :] = fwd[shift * slots : (shift + 1) * slots, :]
        sends[shift][slots:, :] = jnp.zeros((up.shape[0], L), F32)
        sends[shift][slots:, :rank] = up[...]


def local_kernel(
    sizes, geo, pairs, targets, far_list, coupling, transfer, parent, up, acc_in, *rest
):
    C, S, L, R, slots, clusters, panels = sizes
    pieces = rest[:S]
    sums = rest[S : S + C - 1]
    parts = rest[S + C - 1 : 2 * S + C - 1]
    q, qt, acc, acct, fa0, fa1, fb0, fb1, rads, dist0, dist1, got, parents = rest[2 * S + C - 1 :]
    fa, fb = (fa0, fa1), (fb0, fb1)
    me, sub, rep = lax.axis_index("clu"), lax.axis_index("sub"), lax.axis_index("rep")
    assemble(sub, S, L, q, pieces)
    qt[...] = q[...].T
    acc[...] = jnp.zeros_like(acc)
    acct[...] = jnp.zeros_like(acct)
    points = [geo[:, k, :] for k in range(4)]
    centre, inv = frame([points])
    left, right, rad = split_features(points, centre, inv)
    store_features(fa, left)
    store_features(fb, right)
    rads[...] = rad

    half = panels // 2
    share = clusters // (S * R)
    first = (rep * S + sub) * share

    def begin_self(i, dist):
        c = first + jnp.minimum(i, share - 1)
        a = load_features(fa, c)
        b = load_features(fb, c)
        dist[:half, :half] = contract(a[0], b[0])
        dist[:half, half:] = contract(a[0], b[1])
        dist[half:, half:] = contract(a[1], b[1])

    def finish_self(i, dist):
        c = first + i
        qrow = q[pl.ds(c, 1), :]
        radius = rads[pl.ds(c, 1), :]
        diag = lax.rsqrt(2.0 * (radius * radius))
        back = jnp.zeros((8, LANES), F32)
        step = 64
        for r in range(0, panels, step):
            rows = slice(r, r + step)
            base = r % half
            eye = lax.broadcasted_iota(jnp.int32, (step, half), 0) + base == lax.broadcasted_iota(
                jnp.int32, (step, half), 1
            )
            if r < half:
                g0 = jnp.where(eye, diag[:, :half], lax.rsqrt(dist[rows, :half]))
                g1 = lax.rsqrt(dist[rows, half:])
                qcol = column(qt[rows, :], c)
                back = back + fold(g1 * qcol)
                part = g0 * qrow[:, :half] + g1 * qrow[:, half:]
            else:
                part = jnp.where(eye, diag[:, half:], lax.rsqrt(dist[rows, half:])) * qrow[:, half:]
            put_column(acct, rows, c, jnp.sum(part, axis=1, keepdims=True))
        back = jnp.sum(back, axis=0, keepdims=True)
        acc[pl.ds(c, 1), :] += jnp.concatenate([jnp.zeros_like(back), back], axis=1)

    def self_step(i, carry):
        begin_self(2 * i + 1, dist1)
        finish_self(2 * i, dist0)
        begin_self(2 * i + 2, dist0)
        finish_self(2 * i + 1, dist1)
        return carry

    begin_self(0, dist0)
    lax.fori_loop(0, share // 2, self_step, 0)

    count = pairs.shape[1] // S
    start = sub * count

    def begin(i, dist):
        p = start + jnp.minimum(i, count - 1)
        distances(load_features(fa, pairs[0, p]), load_features(fb, pairs[1, p]), dist)

    def finish(i, dist):
        ia, ib = pairs[0, start + i], pairs[1, start + i]
        acc[pl.ds(ib, 1), :] += tile_sums(dist, q[pl.ds(ib, 1), :], qt, ia, acct, ia)

    def pair_step(i, carry):
        begin(2 * i + 1, dist1)
        finish(2 * i, dist0)
        begin(2 * i + 2, dist0)
        finish(2 * i + 1, dist1)
        return carry

    begin(0, dist0)
    lax.fori_loop(0, count // 2, pair_step, 0)
    total = acc_in[...] + (acc[...] + acct[...].T) * inv

    got[...] = jnp.zeros_like(got)
    for shift in range(1, C):
        dest = lax.rem(me + shift, C)
        for j in range(slots):
            got[pl.ds(targets[dest, j], 1), :] += sums[shift - 1][j : j + 1, :]

    par_dev, far_n, rank = coupling.shape[0], coupling.shape[1], coupling.shape[2]
    parents[pl.ds(pl.multiple_of(me * par_dev, 8), par_dev), :] = up[...]
    for shift in range(1, C):
        owner = lax.rem(me + shift, C)
        parents[pl.ds(pl.multiple_of(owner * par_dev, 8), par_dev), :] = sums[shift - 1][slots:, :rank]
    lane = lax.broadcasted_iota(jnp.int32, (rank, LANES), 1)
    field = jnp.zeros((rank, LANES), F32)
    for p in range(par_dev):
        part = jnp.zeros((rank, rank), F32)
        for k in range(far_n):
            part = part + coupling[p, k] * parents[pl.ds(far_list[p, k], 1), :]
        field = jnp.where(lane == p, jnp.sum(part, axis=1, keepdims=True), field)
    which = lax.broadcasted_iota(jnp.int32, (LANES, clusters), 0)
    onehot = (parent[...] == which).astype(F32)
    down = jnp.dot(field, onehot, precision=HIGHEST, preferred_element_type=F32)
    fields = jnp.concatenate(
        [jnp.sum(transfer[r] * down, axis=0, keepdims=True) for r in range(rank)], axis=0
    )

    def give(s):
        for shift in range(S):
            other = (s + shift) % S
            part = total[:, other * L : (other + 1) * L]
            parts[shift][:clusters, :] = part + got[...] if shift == 0 else part
            for t in range(clusters // L):
                at = clusters + t * rank
                parts[shift][at : at + rank, :] = fields[:, t * L : (t + 1) * L]

    for s in range(S):
        pl.when(sub == s)(functools.partial(give, s))


def up_kernel(basis, masked, transfer, parent, up):
    clusters = basis.shape[0]
    rank = basis.shape[1]
    lane = lax.broadcasted_iota(jnp.int32, (rank, clusters), 1)
    leaf = jnp.zeros((rank, clusters), F32)
    for c in range(clusters):
        part = jnp.sum(basis[c] * masked[c : c + 1, :], axis=1, keepdims=True)
        leaf = jnp.where(lane == c, part, leaf)
    lifted = jnp.zeros((rank, clusters), F32)
    for r in range(rank):
        lifted = lifted + transfer[r] * leaf[r : r + 1, :]
    which = lax.broadcasted_iota(jnp.int32, (up.shape[0], clusters), 0)
    onehot = (parent[...] == which).astype(F32)
    up[...] = lax.dot_general(
        onehot, lifted, (((1,), (1,)), ((), ())), precision=HIGHEST, preferred_element_type=F32
    )


def final_kernel(sizes, mask, basis, *rest):
    S, R, L = sizes
    near, out = rest[: S * R], rest[-1]
    clusters, rank = basis.shape[0], basis.shape[1]
    fields = []
    for t in range(clusters // L):
        rows = slice(clusters + t * rank, clusters + (t + 1) * rank)
        fields.append(sum(near[d * R][rows, :] for d in range(1, S)) + near[0][rows, :])
    fields = jnp.concatenate(fields, axis=1) if len(fields) > 1 else fields[0]
    for c in range(clusters):
        out[c : c + 1, :] = jnp.sum(basis[c] * fields[:, c : c + 1], axis=0, keepdims=True)
    total = out[...]
    for part in near:
        total = total + part[:clusters, :]
    out[...] = total * mask[...].astype(F32)


def send(value, moves):
    names = tuple(name for name, _ in moves)
    steps = [step for _, step in moves]
    sizes = [lax.axis_size(name) for name in names]
    perm = []

    def flat(coords):
        index = 0
        for size, c in zip(sizes, coords):
            index = index * size + c
        return index

    total = 1
    for size in sizes:
        total *= size
    for index in range(total):
        coords, left = [], index
        for size in reversed(sizes):
            coords.append(left % size)
            left //= size
        coords.reverse()
        perm.append((index, flat([(c + s) % n for c, s, n in zip(coords, steps, sizes)])))
    return lax.ppermute(value, names if len(names) > 1 else names[0], perm)


def on_device(
    charges,
    panel_mask,
    geometry,
    remote_source,
    remote_target,
    remote_live,
    local_pairs,
    basis,
    transfer,
    parent_of,
    far_list,
    coupling,
):
    clusters, L = charges.shape
    panels = geometry.shape[2]
    C, S, R = lax.axis_size("clu"), lax.axis_size("sub"), lax.axis_size("rep")
    slots = remote_source.shape[2]
    par_dev, rank = far_list.shape[0], transfer.shape[1]
    n = (C - 1) * slots
    shape = jax.ShapeDtypeStruct
    targets = remote_target[0]
    basis_t = jnp.transpose(basis, (0, 2, 1))
    transfer_t = jnp.transpose(transfer, (1, 2, 0))
    parent = parent_of[None, :]

    made = pl.pallas_call(
        functools.partial(pack_kernel, (C, S, L, slots)),
        out_shape=[shape((clusters, L), F32)] + [shape((5 * slots + 8, L), F32)] * (C - 1),
        in_specs=[vmem()] * 3 + [smem()] * 3,
        out_specs=[vmem()] * C,
        compiler_params=PARAMS,
        name="packs",
    )(charges, panel_mask, geometry, targets, remote_source[0], remote_live[0])
    masked, packs = made[0], made[1:]
    pieces = [masked] + [send(masked, (("sub", d),)) for d in range(1, S)]
    packs = [send(packs[d - 1], (("clu", d),)) for d in range(1, C)]
    codes = jnp.stack([p[5 * slots, :slots] for p in packs]).astype(jnp.int32)

    up = pl.pallas_call(
        up_kernel,
        out_shape=shape((par_dev, rank), F32),
        in_specs=[vmem()] * 4,
        out_specs=vmem(),
        compiler_params=PARAMS,
        name="far_up",
    )(basis_t, masked, transfer_t, parent)

    made = pl.pallas_call(
        functools.partial(remote_kernel, (C, S, L, slots, clusters, panels)),
        out_shape=[shape((clusters, panels), F32)] + [shape((slots + par_dev, L), F32)] * (C - 1),
        in_specs=[vmem(), smem()] + [vmem()] * (1 + S + C - 1),
        out_specs=[vmem()] * C,
        scratch_shapes=[
            pltpu.VMEM((clusters, panels), F32),
            pltpu.VMEM((L, whole(n)), F32),
            pltpu.VMEM((clusters, panels), F32),
            pltpu.VMEM((L, whole(n)), F32),
            pltpu.VMEM((4 * n, panels), F32),
            pltpu.VMEM((n * ROWS, L), F32),
            pltpu.VMEM((n * ROWS, LANES), F32),
            pltpu.VMEM((n * ROWS, LANES), F32),
            pltpu.VMEM((L, panels), F32),
            pltpu.VMEM((L, panels), F32),
            pltpu.SMEM((n + 1,), jnp.int32),
        ],
        compiler_params=PARAMS,
        name="near_remote",
    )(geometry, codes, up, *pieces, *packs)
    acc, sums = made[0], [send(made[d], (("clu", C - d),)) for d in range(1, C)]

    half = [pltpu.VMEM((clusters * ROWS, LANES), F32)] * 2
    parts = pl.pallas_call(
        functools.partial(local_kernel, (C, S, L, R, slots, clusters, panels)),
        out_shape=[shape((clusters + clusters // L * rank, L), F32)] * S,
        in_specs=[vmem()] + [smem()] * 3 + [vmem()] * (5 + S + C - 1),
        out_specs=[vmem()] * S,
        scratch_shapes=[
            pltpu.VMEM((clusters, panels), F32),
            pltpu.VMEM((panels, clusters), F32),
            pltpu.VMEM((clusters, panels), F32),
            pltpu.VMEM((panels, clusters), F32),
            *half,
            *half,
            pltpu.VMEM((clusters, panels), F32),
            pltpu.VMEM((panels, panels), F32),
            pltpu.VMEM((panels, panels), F32),
            pltpu.VMEM((clusters, L), F32),
            pltpu.VMEM((C * par_dev, rank), F32),
        ],
        compiler_params=PARAMS,
        name="near_local",
    )(geometry, local_pairs[0].T, targets, far_list, coupling, transfer_t, parent, up, acc, *pieces, *sums)
    near = []
    for d in range(S):
        for e in range(R):
            near.append(send(parts[d], (("sub", d), ("rep", e))) if d or e else parts[0])

    return pl.pallas_call(
        functools.partial(final_kernel, (S, R, L)),
        out_shape=shape((clusters, L), F32),
        in_specs=[vmem()] * (2 + S * R),
        out_specs=vmem(),
        compiler_params=PARAMS,
        name="combine",
    )(panel_mask, basis_t, *near)


def solution(mesh):
    placed = (
        P(("grp", "clu"), "sub"),
        P(("grp", "clu"), "sub"),
        P(("grp", "clu"), None, None),
        P(("grp", "clu"), None, "rep"),
        P(("grp", "clu"), None, "rep"),
        P(("grp", "clu"), None, "rep"),
        P(("grp", "clu"), "rep", None),
        P(("grp", "clu"), "sub", None),
        P(("grp", "clu"), None, None),
        P(("grp", "clu")),
        P(("grp", "clu"), None),
        P(("grp", "clu"), None, None, None),
    )
    return jax.shard_map(
        on_device, mesh=mesh, in_specs=placed, out_specs=P(("grp", "clu"), "sub"), check_vma=False
    )
```

```python
import functools

import jax
import jax.numpy as jnp
from jax import lax
from jax.experimental import pallas as pl
from jax.experimental.pallas import tpu as pltpu
from jax.sharding import PartitionSpec as P

F32 = jnp.float32
BF16 = jnp.bfloat16
HIGHEST = lax.Precision.HIGHEST
ROWS = 40
USED = 37
LANES = 128
PARAMS = pltpu.CompilerParams(vmem_limit_bytes=56 * 1024 * 1024)


def vmem():
    return pl.BlockSpec(memory_space=pltpu.VMEM)


def smem():
    return pl.BlockSpec(memory_space=pltpu.SMEM)


def whole(size):
    return -(-size // LANES) * LANES


def cut(v):
    return v.astype(BF16).astype(F32)


def powers(sign):
    lane = lax.broadcasted_iota(jnp.int32, (8, LANES), 1)
    out = jnp.full((8, LANES), 2.0 ** (-64 * sign), F32)
    for bit in range(7):
        out = out * jnp.where((lane >> bit) & 1 == 1, F32(2.0 ** (sign * 2**bit)), F32(1.0))
    return out


def frame(parts):
    low = [functools.reduce(jnp.minimum, [jnp.min(p[k]) for p in parts]) for k in range(3)]
    high = [functools.reduce(jnp.maximum, [jnp.max(p[k]) for p in parts]) for k in range(3)]
    width = functools.reduce(jnp.maximum, [jnp.max(jnp.abs(p[3])) for p in parts])
    for lo, hi in zip(low, high):
        width = jnp.maximum(width, 0.5 * (hi - lo))
    up, down = powers(1), powers(-1)
    size = jnp.min(jnp.where(up >= width, up, F32(2.0**63)))
    inv = jnp.max(jnp.where(up >= width, down, F32(2.0**-63)))
    magic = size * F32(1.5 * 2.0**20)
    centre = [(0.5 * (lo + hi) + magic) - magic for lo, hi in zip(low, high)]
    return centre, inv


def split_features(points, centre, inv, charge=None):
    magic = F32(1.5 * 2.0**16)
    grid, rest = [], []
    for k in range(3):
        u = (points[k] - centre[k]) * inv
        h = (u + magic) - magic
        grid.append(h)
        rest.append(u - h)
    rad = points[3] * inv
    norm = grid[0] * grid[0] + grid[1] * grid[1] + grid[2] * grid[2]
    norm1 = cut(norm)
    norm2 = norm - norm1
    cross = grid[0] * rest[0] + grid[1] * rest[1] + grid[2] * rest[2]
    extra = 2.0 * cross + (rest[0] * rest[0] + rest[1] * rest[1] + rest[2] * rest[2]) + rad * rad
    extra1 = cut(extra)
    extra2 = cut(extra - extra1)
    extra3 = (extra - extra1) - extra2
    rest1 = [cut(v) for v in rest]
    rest2 = [v - w for v, w in zip(rest, rest1)]
    neg = lambda vs: [-2.0 * v for v in vs]
    one = jnp.ones_like(rad)
    left = grid + [norm1, norm2, one, one]
    right = neg(grid) + [one, one, norm1, norm2]
    left += [extra1, extra2, extra3, one, one, one]
    right += [one, one, one, extra1, extra2, extra3]
    left += grid + grid + rest1 + rest2 + rest1 + rest1 + rest2
    right += neg(rest1) + neg(rest2) + neg(grid) + neg(grid) + neg(rest1) + neg(rest2) + neg(rest1)
    if charge is not None:
        charge1 = cut(charge)
        charge2 = cut(charge - charge1)
        left += [charge1, charge2, (charge - charge1) - charge2]
    right += [jnp.zeros_like(rad)] * 3
    return left, right, rad


def store_features(ref, rows):
    count = rows[0].shape[0]
    width = rows[0].shape[1]
    for k, row in enumerate(rows):
        for t, piece in enumerate(ref):
            piece[pl.ds(k, count, stride=ROWS), :] = row[:, t * LANES : min(width, (t + 1) * LANES)]


def load_features(ref, index):
    start = pl.multiple_of(index * ROWS, 8)
    return [piece[pl.ds(start, USED), :].astype(BF16) for piece in ref]


def contract(left, right):
    return lax.dot_general(left, right, (((0,), (0,)), ((), ())), preferred_element_type=F32)


def pick(rows, width, index):
    lane = lax.broadcasted_iota(jnp.int32, (rows, width), 1)
    return jnp.where(lane == index, 1.0, 0.0).astype(BF16)


def fold(v):
    return jnp.sum(v.reshape(v.shape[0] // 8, 8, v.shape[1]), axis=0)


def charge_rows():
    row = lax.broadcasted_iota(jnp.int32, (USED, LANES), 0)
    return jnp.where(row >= USED - 3, 1.0, 0.0).astype(BF16)


def distances(left, right, out):
    whole_left = jnp.concatenate(left, axis=1) if len(left) > 1 else left[0]
    for t, r in enumerate(list(right) + [charge_rows()]):
        out[:, t * LANES : (t + 1) * LANES] = contract(whole_left, r)


def keep(parts, rows, value):
    high = value.astype(BF16)
    parts[rows, :LANES] = high
    parts[rows, LANES:] = (value - high.astype(F32)).astype(BF16)


def add_columns(table, parts, indices):
    width = table.shape[1]
    left = jnp.concatenate([p[...] for p in parts], axis=1)
    right = jnp.concatenate([pick(2 * LANES, width, i) for i in indices], axis=0)
    table[...] += jnp.dot(left, right, preferred_element_type=F32)


def tile_sums(dist, qrow, parts, step=64):
    height = dist.shape[0]
    step = min(step, height)
    q0, q1 = qrow[:, :LANES], qrow[:, LANES:]
    back0 = back1 = jnp.zeros((8, LANES), F32)
    for r in range(0, height, step):
        rows = slice(r, r + step)
        g0 = lax.rsqrt(dist[rows, :LANES])
        g1 = lax.rsqrt(dist[rows, LANES : 2 * LANES])
        qcol = dist[rows, 2 * LANES :]
        keep(parts, rows, g0 * q0 + g1 * q1)
        back0 = back0 + fold(g0 * qcol)
        back1 = back1 + fold(g1 * qcol)
    return jnp.concatenate(
        [jnp.sum(back0, axis=0, keepdims=True), jnp.sum(back1, axis=0, keepdims=True)], axis=1
    )


def assemble(sub, S, L, q, pieces):
    def place(s):
        for shift in range(S):
            owner = (s - shift) % S
            q[:, owner * L : (owner + 1) * L] = pieces[shift][...]

    for s in range(S):
        pl.when(sub == s)(functools.partial(place, s))


def pack_kernel(sizes, charges, mask, geo, targets, sources, live, masked, *packs):
    C, S, L, slots = sizes
    me, sub = lax.axis_index("clu"), lax.axis_index("sub")
    masked[...] = charges[...] * mask[...].astype(F32)
    lane = lax.broadcasted_iota(jnp.int32, (8, L), 1)
    for shift in range(1, C):
        dest = lax.rem(me + shift, C)
        codes = jnp.full((8, L), -1.0, F32)
        for j in range(slots):
            code = jnp.where(live[dest, j] > 0, sources[dest, j], -1)
            codes = jnp.where(lane == j, code.astype(F32), codes)
        packs[shift - 1][5 * slots :, :] = codes

    def fill(s):
        for shift in range(1, C):
            dest = lax.rem(me + shift, C)
            pack = packs[shift - 1]
            for j in range(slots):
                t = targets[dest, j]
                g = geo[t, :, s * L : (s + 1) * L]
                for k in range(4):
                    pack[k * slots + j : k * slots + j + 1, :] = g[k : k + 1]
                pack[4 * slots + j : 4 * slots + j + 1, :] = masked[pl.ds(t, 1), :]

    for s in range(S):
        pl.when(sub == s)(functools.partial(fill, s))


def remote_kernel(sizes, geo, codes, up, *rest):
    C, S, L, slots, clusters, panels = sizes
    pieces = rest[:S]
    packs = rest[S : S + C - 1]
    acc_out = rest[S + C - 1]
    sends = rest[S + C : S + C + C - 1]
    q, acc, fwdt, sgeo, fa0, fb0, fb1, dist0, dist1, part0, part1, order = rest[S + C + C - 1 :]
    fa, fb = (fa0,), (fb0, fb1)
    n = (C - 1) * slots
    assemble(lax.axis_index("sub"), S, L, q, pieces)
    acc[...] = jnp.zeros_like(acc)
    fwdt[...] = jnp.zeros_like(fwdt)
    found = jnp.int32(0)
    for shift in range(C - 1):
        for j in range(slots):
            code = codes[shift, j]
            order[found] = shift * slots + j
            found = found + (code >= 0).astype(jnp.int32)
            g = geo[jnp.maximum(code, 0)]
            for k in range(4):
                row = k * n + shift * slots + j
                sgeo[row : row + 1, :] = g[k : k + 1]
    tpoints = [
        jnp.concatenate([p[k * slots : (k + 1) * slots, :] for p in packs], axis=0) for k in range(5)
    ]
    spoints = [sgeo[k * n : (k + 1) * n, :] for k in range(4)]
    centre, inv = frame([tpoints, spoints])
    left, _, _ = split_features(tpoints, centre, inv, tpoints[4])
    _, right, _ = split_features(spoints, centre, inv)
    store_features(fa, left)
    store_features(fb, right)
    def begin(i, dist):
        slot = order[jnp.minimum(i, jnp.maximum(found - 1, 0))]
        distances(load_features(fa, slot), load_features(fb, slot), dist)

    def finish(i, dist, part):
        ok = i < found
        slot = order[jnp.minimum(i, jnp.maximum(found - 1, 0))]
        source = jnp.maximum(codes[slot // slots, lax.rem(slot, slots)], 0)
        back = tile_sums(dist, q[pl.ds(source, 1), :], part)
        acc[pl.ds(source, 1), :] += jnp.where(ok, back, 0.0)
        return jnp.where(ok, slot, -1)

    def step(i, carry):
        begin(2 * i + 1, dist1)
        slot0 = finish(2 * i, dist0, part0)
        begin(2 * i + 2, dist0)
        slot1 = finish(2 * i + 1, dist1, part1)
        add_columns(fwdt, (part0, part1), (slot0, slot1))
        return carry

    begin(0, dist0)
    lax.fori_loop(0, (found + 1) // 2, step, 0)
    acc_out[...] = acc[...] * inv
    fwd = (fwdt[...] * inv).T
    rank = up.shape[1]
    for shift in range(C - 1):
        sends[shift][:slots, :] = fwd[shift * slots : (shift + 1) * slots, :]
        sends[shift][slots:, :] = jnp.zeros((up.shape[0], L), F32)
        sends[shift][slots:, :rank] = up[...]


def local_kernel(
    sizes, geo, pairs, targets, far_list, coupling, transfer, parent, up, acc_in, *rest
):
    C, S, L, R, slots, clusters, panels = sizes
    pieces = rest[:S]
    sums = rest[S : S + C - 1]
    parts = rest[S + C - 1 : 2 * S + C - 1]
    q, acc, acct, fa0, fa1, fb0, fb1, rads, dist0, dist1, part0, part1, got, parents = rest[2 * S + C - 1 :]
    fa, fb = (fa0, fa1), (fb0, fb1)
    me, sub, rep = lax.axis_index("clu"), lax.axis_index("sub"), lax.axis_index("rep")
    assemble(sub, S, L, q, pieces)
    acc[...] = jnp.zeros_like(acc)
    acct[...] = jnp.zeros_like(acct)
    points = [geo[:, k, :] for k in range(4)]
    centre, inv = frame([points])
    left, right, rad = split_features(points, centre, inv, q[...])
    store_features(fa, left)
    store_features(fb, right)
    rads[...] = rad

    half = panels // 2
    share = clusters // (S * R)
    first = (rep * S + sub) * share

    def begin_self(i, dist):
        c = first + jnp.minimum(i, share - 1)
        a = load_features(fa, c)
        b = load_features(fb, c)
        dist[:half, :half] = contract(a[0], b[0])
        dist[:half, half:panels] = contract(a[0], b[1])
        dist[:half, panels:] = contract(a[0], charge_rows())
        dist[half:, half:panels] = contract(a[1], b[1])

    def finish_self(i, dist, parts):
        c = first + i
        qrow = q[pl.ds(c, 1), :]
        radius = rads[pl.ds(c, 1), :]
        diag = lax.rsqrt(2.0 * (radius * radius))
        back = jnp.zeros((8, LANES), F32)
        step = 64
        for r in range(0, panels, step):
            rows = slice(r, r + step)
            base = r % half
            eye = lax.broadcasted_iota(jnp.int32, (step, half), 0) + base == lax.broadcasted_iota(
                jnp.int32, (step, half), 1
            )
            if r < half:
                g0 = jnp.where(eye, diag[:, :half], lax.rsqrt(dist[rows, :half]))
                g1 = lax.rsqrt(dist[rows, half:panels])
                qcol = dist[rows, panels:]
                back = back + fold(g1 * qcol)
                part = g0 * qrow[:, :half] + g1 * qrow[:, half:]
            else:
                part = jnp.where(eye, diag[:, half:], lax.rsqrt(dist[rows, half:panels])) * qrow[:, half:]
            keep(parts, rows, part)
        back = jnp.sum(back, axis=0, keepdims=True)
        acc[pl.ds(c, 1), :] += jnp.concatenate([jnp.zeros_like(back), back], axis=1)
        return c

    def self_step(i, carry):
        begin_self(2 * i + 1, dist1)
        c0 = finish_self(2 * i, dist0, part0)
        begin_self(2 * i + 2, dist0)
        c1 = finish_self(2 * i + 1, dist1, part1)
        add_columns(acct, (part0, part1), (c0, c1))
        return carry

    begin_self(0, dist0)
    lax.fori_loop(0, share // 2, self_step, 0)

    count = pairs.shape[1] // S
    start = sub * count

    def begin(i, dist):
        p = start + jnp.minimum(i, count - 1)
        distances(load_features(fa, pairs[0, p]), load_features(fb, pairs[1, p]), dist)

    def finish(i, dist, part):
        ia, ib = pairs[0, start + i], pairs[1, start + i]
        acc[pl.ds(ib, 1), :] += tile_sums(dist, q[pl.ds(ib, 1), :], part)
        return ia

    def pair_step(i, carry):
        begin(2 * i + 1, dist1)
        ia0 = finish(2 * i, dist0, part0)
        begin(2 * i + 2, dist0)
        ia1 = finish(2 * i + 1, dist1, part1)
        add_columns(acct, (part0, part1), (ia0, ia1))
        return carry

    begin(0, dist0)
    lax.fori_loop(0, count // 2, pair_step, 0)
    total = acc_in[...] + (acc[...] + acct[...].T) * inv

    got[...] = jnp.zeros_like(got)
    for shift in range(1, C):
        dest = lax.rem(me + shift, C)
        for j in range(slots):
            got[pl.ds(targets[dest, j], 1), :] += sums[shift - 1][j : j + 1, :]

    par_dev, far_n, rank = coupling.shape[0], coupling.shape[1], coupling.shape[2]
    parents[pl.ds(pl.multiple_of(me * par_dev, 8), par_dev), :] = up[...]
    for shift in range(1, C):
        owner = lax.rem(me + shift, C)
        parents[pl.ds(pl.multiple_of(owner * par_dev, 8), par_dev), :] = sums[shift - 1][slots:, :rank]
    lane = lax.broadcasted_iota(jnp.int32, (rank, LANES), 1)
    field = jnp.zeros((rank, LANES), F32)
    for p in range(par_dev):
        part = jnp.zeros((rank, rank), F32)
        for k in range(far_n):
            part = part + coupling[p, k] * parents[pl.ds(far_list[p, k], 1), :]
        field = jnp.where(lane == p, jnp.sum(part, axis=1, keepdims=True), field)
    which = lax.broadcasted_iota(jnp.int32, (LANES, clusters), 0)
    onehot = (parent[...] == which).astype(F32)
    down = jnp.dot(field, onehot, precision=HIGHEST, preferred_element_type=F32)
    fields = jnp.concatenate(
        [jnp.sum(transfer[r] * down, axis=0, keepdims=True) for r in range(rank)], axis=0
    )

    def give(s):
        for shift in range(S):
            other = (s + shift) % S
            part = total[:, other * L : (other + 1) * L]
            parts[shift][:clusters, :] = part + got[...] if shift == 0 else part
            for t in range(clusters // L):
                at = clusters + t * rank
                parts[shift][at : at + rank, :] = fields[:, t * L : (t + 1) * L]

    for s in range(S):
        pl.when(sub == s)(functools.partial(give, s))


def up_kernel(basis, masked, transfer, parent, up):
    clusters = basis.shape[0]
    rank = basis.shape[1]
    lane = lax.broadcasted_iota(jnp.int32, (rank, clusters), 1)
    leaf = jnp.zeros((rank, clusters), F32)
    for c in range(clusters):
        part = jnp.sum(basis[c] * masked[c : c + 1, :], axis=1, keepdims=True)
        leaf = jnp.where(lane == c, part, leaf)
    lifted = jnp.zeros((rank, clusters), F32)
    for r in range(rank):
        lifted = lifted + transfer[r] * leaf[r : r + 1, :]
    which = lax.broadcasted_iota(jnp.int32, (up.shape[0], clusters), 0)
    onehot = (parent[...] == which).astype(F32)
    up[...] = lax.dot_general(
        onehot, lifted, (((1,), (1,)), ((), ())), precision=HIGHEST, preferred_element_type=F32
    )


def final_kernel(sizes, mask, basis, *rest):
    S, R, L = sizes
    near, out = rest[: S * R], rest[-1]
    clusters, rank = basis.shape[0], basis.shape[1]
    fields = []
    for t in range(clusters // L):
        rows = slice(clusters + t * rank, clusters + (t + 1) * rank)
        fields.append(sum(near[d * R][rows, :] for d in range(1, S)) + near[0][rows, :])
    fields = jnp.concatenate(fields, axis=1) if len(fields) > 1 else fields[0]
    for c in range(clusters):
        out[c : c + 1, :] = jnp.sum(basis[c] * fields[:, c : c + 1], axis=0, keepdims=True)
    total = out[...]
    for part in near:
        total = total + part[:clusters, :]
    out[...] = total * mask[...].astype(F32)


def send(value, moves):
    names = tuple(name for name, _ in moves)
    steps = [step for _, step in moves]
    sizes = [lax.axis_size(name) for name in names]
    perm = []

    def flat(coords):
        index = 0
        for size, c in zip(sizes, coords):
            index = index * size + c
        return index

    total = 1
    for size in sizes:
        total *= size
    for index in range(total):
        coords, left = [], index
        for size in reversed(sizes):
            coords.append(left % size)
            left //= size
        coords.reverse()
        perm.append((index, flat([(c + s) % n for c, s, n in zip(coords, steps, sizes)])))
    return lax.ppermute(value, names if len(names) > 1 else names[0], perm)


def on_device(
    charges,
    panel_mask,
    geometry,
    remote_source,
    remote_target,
    remote_live,
    local_pairs,
    basis,
    transfer,
    parent_of,
    far_list,
    coupling,
):
    clusters, L = charges.shape
    panels = geometry.shape[2]
    C, S, R = lax.axis_size("clu"), lax.axis_size("sub"), lax.axis_size("rep")
    slots = remote_source.shape[2]
    par_dev, rank = far_list.shape[0], transfer.shape[1]
    n = (C - 1) * slots
    shape = jax.ShapeDtypeStruct
    targets = remote_target[0]
    basis_t = jnp.transpose(basis, (0, 2, 1))
    transfer_t = jnp.transpose(transfer, (1, 2, 0))
    parent = parent_of[None, :]

    made = pl.pallas_call(
        functools.partial(pack_kernel, (C, S, L, slots)),
        out_shape=[shape((clusters, L), F32)] + [shape((5 * slots + 8, L), F32)] * (C - 1),
        in_specs=[vmem()] * 3 + [smem()] * 3,
        out_specs=[vmem()] * C,
        compiler_params=PARAMS,
        name="packs",
    )(charges, panel_mask, geometry, targets, remote_source[0], remote_live[0])
    masked, packs = made[0], made[1:]
    pieces = [masked] + [send(masked, (("sub", d),)) for d in range(1, S)]
    packs = [send(packs[d - 1], (("clu", d),)) for d in range(1, C)]
    codes = jnp.stack([p[5 * slots, :slots] for p in packs]).astype(jnp.int32)

    up = pl.pallas_call(
        up_kernel,
        out_shape=shape((par_dev, rank), F32),
        in_specs=[vmem()] * 4,
        out_specs=vmem(),
        compiler_params=PARAMS,
        name="far_up",
    )(basis_t, masked, transfer_t, parent)

    made = pl.pallas_call(
        functools.partial(remote_kernel, (C, S, L, slots, clusters, panels)),
        out_shape=[shape((clusters, panels), F32)] + [shape((slots + par_dev, L), F32)] * (C - 1),
        in_specs=[vmem(), smem()] + [vmem()] * (1 + S + C - 1),
        out_specs=[vmem()] * C,
        scratch_shapes=[
            pltpu.VMEM((clusters, panels), F32),
            pltpu.VMEM((clusters, panels), F32),
            pltpu.VMEM((L, whole(n)), F32),
            pltpu.VMEM((4 * n, panels), F32),
            pltpu.VMEM((n * ROWS, L), F32),
            pltpu.VMEM((n * ROWS, LANES), F32),
            pltpu.VMEM((n * ROWS, LANES), F32),
            pltpu.VMEM((L, panels + LANES), F32),
            pltpu.VMEM((L, panels + LANES), F32),
            pltpu.VMEM((L, 2 * LANES), BF16),
            pltpu.VMEM((L, 2 * LANES), BF16),
            pltpu.SMEM((n + 1,), jnp.int32),
        ],
        compiler_params=PARAMS,
        name="near_remote",
    )(geometry, codes, up, *pieces, *packs)
    acc, sums = made[0], [send(made[d], (("clu", C - d),)) for d in range(1, C)]

    half = [pltpu.VMEM((clusters * ROWS, LANES), F32)] * 2
    parts = pl.pallas_call(
        functools.partial(local_kernel, (C, S, L, R, slots, clusters, panels)),
        out_shape=[shape((clusters + clusters // L * rank, L), F32)] * S,
        in_specs=[vmem()] + [smem()] * 3 + [vmem()] * (5 + S + C - 1),
        out_specs=[vmem()] * S,
        scratch_shapes=[
            pltpu.VMEM((clusters, panels), F32),
            pltpu.VMEM((clusters, panels), F32),
            pltpu.VMEM((panels, clusters), F32),
            *half,
            *half,
            pltpu.VMEM((clusters, panels), F32),
            pltpu.VMEM((panels, panels + LANES), F32),
            pltpu.VMEM((panels, panels + LANES), F32),
            pltpu.VMEM((panels, 2 * LANES), BF16),
            pltpu.VMEM((panels, 2 * LANES), BF16),
            pltpu.VMEM((clusters, L), F32),
            pltpu.VMEM((C * par_dev, rank), F32),
        ],
        compiler_params=PARAMS,
        name="near_local",
    )(geometry, local_pairs[0].T, targets, far_list, coupling, transfer_t, parent, up, acc, *pieces, *sums)
    near = []
    for d in range(S):
        for e in range(R):
            near.append(send(parts[d], (("sub", d), ("rep", e))) if d or e else parts[0])

    return pl.pallas_call(
        functools.partial(final_kernel, (S, R, L)),
        out_shape=shape((clusters, L), F32),
        in_specs=[vmem()] * (2 + S * R),
        out_specs=vmem(),
        compiler_params=PARAMS,
        name="combine",
    )(panel_mask, basis_t, *near)


def solution(mesh):
    placed = (
        P(("grp", "clu"), "sub"),
        P(("grp", "clu"), "sub"),
        P(("grp", "clu"), None, None),
        P(("grp", "clu"), None, "rep"),
        P(("grp", "clu"), None, "rep"),
        P(("grp", "clu"), None, "rep"),
        P(("grp", "clu"), "rep", None),
        P(("grp", "clu"), "sub", None),
        P(("grp", "clu"), None, None),
        P(("grp", "clu")),
        P(("grp", "clu"), None),
        P(("grp", "clu"), None, None, None),
    )
    return jax.shard_map(
        on_device, mesh=mesh, in_specs=placed, out_specs=P(("grp", "clu"), "sub"), check_vma=False
    )
```

```python
import functools

import jax
import jax.numpy as jnp
from jax import lax
from jax.experimental import pallas as pl
from jax.experimental.pallas import tpu as pltpu
from jax.sharding import PartitionSpec as P

F32 = jnp.float32
BF16 = jnp.bfloat16
HIGHEST = lax.Precision.HIGHEST
ROWS = 40
USED = 37
LANES = 128
PARAMS = pltpu.CompilerParams(vmem_limit_bytes=56 * 1024 * 1024)


def vmem():
    return pl.BlockSpec(memory_space=pltpu.VMEM)


def smem():
    return pl.BlockSpec(memory_space=pltpu.SMEM)


def whole(size):
    return -(-size // LANES) * LANES


def cut(v):
    return v.astype(BF16).astype(F32)


def powers(sign):
    lane = lax.broadcasted_iota(jnp.int32, (8, LANES), 1)
    out = jnp.full((8, LANES), 2.0 ** (-64 * sign), F32)
    for bit in range(7):
        out = out * jnp.where((lane >> bit) & 1 == 1, F32(2.0 ** (sign * 2**bit)), F32(1.0))
    return out


def frame(parts):
    low = [functools.reduce(jnp.minimum, [jnp.min(p[k]) for p in parts]) for k in range(3)]
    high = [functools.reduce(jnp.maximum, [jnp.max(p[k]) for p in parts]) for k in range(3)]
    width = functools.reduce(jnp.maximum, [jnp.max(jnp.abs(p[3])) for p in parts])
    for lo, hi in zip(low, high):
        width = jnp.maximum(width, 0.5 * (hi - lo))
    up, down = powers(1), powers(-1)
    size = jnp.min(jnp.where(up >= width, up, F32(2.0**63)))
    inv = jnp.max(jnp.where(up >= width, down, F32(2.0**-63)))
    magic = size * F32(1.5 * 2.0**20)
    centre = [(0.5 * (lo + hi) + magic) - magic for lo, hi in zip(low, high)]
    return centre, inv


def split_features(points, centre, inv, charge=None):
    magic = F32(1.5 * 2.0**16)
    grid, rest = [], []
    for k in range(3):
        u = (points[k] - centre[k]) * inv
        h = (u + magic) - magic
        grid.append(h)
        rest.append(u - h)
    rad = points[3] * inv
    norm = grid[0] * grid[0] + grid[1] * grid[1] + grid[2] * grid[2]
    norm1 = cut(norm)
    norm2 = norm - norm1
    cross = grid[0] * rest[0] + grid[1] * rest[1] + grid[2] * rest[2]
    extra = 2.0 * cross + (rest[0] * rest[0] + rest[1] * rest[1] + rest[2] * rest[2]) + rad * rad
    extra1 = cut(extra)
    extra2 = cut(extra - extra1)
    extra3 = (extra - extra1) - extra2
    rest1 = [cut(v) for v in rest]
    rest2 = [v - w for v, w in zip(rest, rest1)]
    neg = lambda vs: [-2.0 * v for v in vs]
    one = jnp.ones_like(rad)
    left = grid + [norm1, norm2, one, one]
    right = neg(grid) + [one, one, norm1, norm2]
    left += [extra1, extra2, extra3, one, one, one]
    right += [one, one, one, extra1, extra2, extra3]
    left += grid + grid + rest1 + rest2 + rest1 + rest1 + rest2
    right += neg(rest1) + neg(rest2) + neg(grid) + neg(grid) + neg(rest1) + neg(rest2) + neg(rest1)
    if charge is not None:
        charge1 = cut(charge)
        charge2 = cut(charge - charge1)
        left += [charge1, charge2, (charge - charge1) - charge2]
    right += [jnp.zeros_like(rad)] * 3
    return left, right, rad


def store_features(ref, rows):
    count = rows[0].shape[0]
    width = rows[0].shape[1]
    for k, row in enumerate(rows):
        for t, piece in enumerate(ref):
            piece[pl.ds(k, count, stride=ROWS), :] = row[:, t * LANES : min(width, (t + 1) * LANES)]


def load_features(ref, index):
    start = pl.multiple_of(index * ROWS, 8)
    return [piece[pl.ds(start, USED), :].astype(BF16) for piece in ref]


def contract(left, right):
    return lax.dot_general(left, right, (((0,), (0,)), ((), ())), preferred_element_type=F32)


def pick(rows, width, index):
    lane = lax.broadcasted_iota(jnp.int32, (rows, width), 1)
    return jnp.where(lane == index, 1.0, 0.0).astype(BF16)


def twice_rsqrt(d):
    y = lax.rsqrt(d.astype(BF16)).astype(F32)
    return y * (3.0 - (d * y) * y)


def fold(v):
    return jnp.sum(v.reshape(v.shape[0] // 8, 8, v.shape[1]), axis=0)


def charge_rows():
    row = lax.broadcasted_iota(jnp.int32, (USED, LANES), 0)
    return jnp.where(row >= USED - 3, 1.0, 0.0).astype(BF16)


def distances(left, right, out):
    whole_left = jnp.concatenate(left, axis=1) if len(left) > 1 else left[0]
    for t, r in enumerate(list(right) + [charge_rows()]):
        out[:, t * LANES : (t + 1) * LANES] = contract(whole_left, r)


def keep(parts, rows, value):
    high = value.astype(BF16)
    parts[rows, :LANES] = high
    parts[rows, LANES:] = (value - high.astype(F32)).astype(BF16)


def add_columns(table, parts, indices):
    width = table.shape[1]
    left = jnp.concatenate([p[...] for p in parts], axis=1)
    right = jnp.concatenate([pick(2 * LANES, width, i) for i in indices], axis=0)
    table[...] += jnp.dot(left, right, preferred_element_type=F32)


def tile_sums(dist, qrow, parts, step=64):
    height = dist.shape[0]
    step = min(step, height)
    q0, q1 = qrow[:, :LANES], qrow[:, LANES:]
    back0 = back1 = jnp.zeros((8, LANES), F32)
    for r in range(0, height, step):
        rows = slice(r, r + step)
        g0 = twice_rsqrt(dist[rows, :LANES])
        g1 = twice_rsqrt(dist[rows, LANES : 2 * LANES])
        qcol = dist[rows, 2 * LANES :]
        keep(parts, rows, g0 * q0 + g1 * q1)
        back0 = back0 + fold(g0 * qcol)
        back1 = back1 + fold(g1 * qcol)
    return jnp.concatenate(
        [jnp.sum(back0, axis=0, keepdims=True), jnp.sum(back1, axis=0, keepdims=True)], axis=1
    )


def assemble(sub, S, L, q, pieces):
    def place(s):
        for shift in range(S):
            owner = (s - shift) % S
            q[:, owner * L : (owner + 1) * L] = pieces[shift][...]

    for s in range(S):
        pl.when(sub == s)(functools.partial(place, s))


def pack_kernel(sizes, charges, mask, geo, targets, sources, live, masked, *packs):
    C, S, L, slots = sizes
    me, sub = lax.axis_index("clu"), lax.axis_index("sub")
    masked[...] = charges[...] * mask[...].astype(F32)
    lane = lax.broadcasted_iota(jnp.int32, (8, L), 1)
    for shift in range(1, C):
        dest = lax.rem(me + shift, C)
        codes = jnp.full((8, L), -1.0, F32)
        for j in range(slots):
            code = jnp.where(live[dest, j] > 0, sources[dest, j], -1)
            codes = jnp.where(lane == j, code.astype(F32), codes)
        packs[shift - 1][5 * slots :, :] = codes

    def fill(s):
        for shift in range(1, C):
            dest = lax.rem(me + shift, C)
            pack = packs[shift - 1]
            for j in range(slots):
                t = targets[dest, j]
                g = geo[t, :, s * L : (s + 1) * L]
                for k in range(4):
                    pack[k * slots + j : k * slots + j + 1, :] = g[k : k + 1]
                pack[4 * slots + j : 4 * slots + j + 1, :] = masked[pl.ds(t, 1), :]

    for s in range(S):
        pl.when(sub == s)(functools.partial(fill, s))


def remote_kernel(sizes, geo, codes, up, *rest):
    C, S, L, slots, clusters, panels = sizes
    pieces = rest[:S]
    packs = rest[S : S + C - 1]
    acc_out = rest[S + C - 1]
    sends = rest[S + C : S + C + C - 1]
    q, acc, fwdt, sgeo, fa0, fb0, fb1, dist0, dist1, part0, part1, order = rest[S + C + C - 1 :]
    fa, fb = (fa0,), (fb0, fb1)
    n = (C - 1) * slots
    assemble(lax.axis_index("sub"), S, L, q, pieces)
    acc[...] = jnp.zeros_like(acc)
    fwdt[...] = jnp.zeros_like(fwdt)
    found = jnp.int32(0)
    for shift in range(C - 1):
        for j in range(slots):
            code = codes[shift, j]
            order[found] = shift * slots + j
            found = found + (code >= 0).astype(jnp.int32)
            g = geo[jnp.maximum(code, 0)]
            for k in range(4):
                row = k * n + shift * slots + j
                sgeo[row : row + 1, :] = g[k : k + 1]
    tpoints = [
        jnp.concatenate([p[k * slots : (k + 1) * slots, :] for p in packs], axis=0) for k in range(5)
    ]
    spoints = [sgeo[k * n : (k + 1) * n, :] for k in range(4)]
    centre, inv = frame([tpoints, spoints])
    left, _, _ = split_features(tpoints, centre, inv, tpoints[4])
    _, right, _ = split_features(spoints, centre, inv)
    store_features(fa, left)
    store_features(fb, right)
    def begin(i, dist):
        slot = order[jnp.minimum(i, jnp.maximum(found - 1, 0))]
        distances(load_features(fa, slot), load_features(fb, slot), dist)

    def finish(i, dist, part):
        ok = i < found
        slot = order[jnp.minimum(i, jnp.maximum(found - 1, 0))]
        source = jnp.maximum(codes[slot // slots, lax.rem(slot, slots)], 0)
        back = tile_sums(dist, q[pl.ds(source, 1), :], part)
        acc[pl.ds(source, 1), :] += jnp.where(ok, back, 0.0)
        return jnp.where(ok, slot, -1)

    def step(i, carry):
        begin(2 * i + 1, dist1)
        slot0 = finish(2 * i, dist0, part0)
        begin(2 * i + 2, dist0)
        slot1 = finish(2 * i + 1, dist1, part1)
        add_columns(fwdt, (part0, part1), (slot0, slot1))
        return carry

    begin(0, dist0)
    lax.fori_loop(0, (found + 1) // 2, step, 0)
    acc_out[...] = acc[...] * (0.5 * inv)
    fwd = (fwdt[...] * (0.5 * inv)).T
    rank = up.shape[1]
    for shift in range(C - 1):
        sends[shift][:slots, :] = fwd[shift * slots : (shift + 1) * slots, :]
        sends[shift][slots:, :] = jnp.zeros((up.shape[0], L), F32)
        sends[shift][slots:, :rank] = up[...]


def local_kernel(
    sizes, geo, pairs, targets, far_list, coupling, transfer, parent, up, acc_in, *rest
):
    C, S, L, R, slots, clusters, panels = sizes
    pieces = rest[:S]
    sums = rest[S : S + C - 1]
    parts = rest[S + C - 1 : 2 * S + C - 1]
    q, acc, acct, fa0, fa1, fb0, fb1, rads, dist0, dist1, part0, part1, got, parents = rest[2 * S + C - 1 :]
    fa, fb = (fa0, fa1), (fb0, fb1)
    me, sub, rep = lax.axis_index("clu"), lax.axis_index("sub"), lax.axis_index("rep")
    assemble(sub, S, L, q, pieces)
    acc[...] = jnp.zeros_like(acc)
    acct[...] = jnp.zeros_like(acct)
    points = [geo[:, k, :] for k in range(4)]
    centre, inv = frame([points])
    left, right, rad = split_features(points, centre, inv, q[...])
    store_features(fa, left)
    store_features(fb, right)
    rads[...] = rad

    half = panels // 2
    share = clusters // (S * R)
    first = (rep * S + sub) * share

    def begin_self(i, dist):
        c = first + jnp.minimum(i, share - 1)
        a = load_features(fa, c)
        b = load_features(fb, c)
        dist[:half, :half] = contract(a[0], b[0])
        dist[:half, half:panels] = contract(a[0], b[1])
        dist[:half, panels:] = contract(a[0], charge_rows())
        dist[half:, half:panels] = contract(a[1], b[1])

    def finish_self(i, dist, parts):
        c = first + i
        qrow = q[pl.ds(c, 1), :]
        radius = rads[pl.ds(c, 1), :]
        diag = 2.0 * lax.rsqrt(2.0 * (radius * radius))
        back = jnp.zeros((8, LANES), F32)
        step = 64
        for r in range(0, panels, step):
            rows = slice(r, r + step)
            base = r % half
            eye = lax.broadcasted_iota(jnp.int32, (step, half), 0) + base == lax.broadcasted_iota(
                jnp.int32, (step, half), 1
            )
            if r < half:
                g0 = jnp.where(eye, diag[:, :half], twice_rsqrt(dist[rows, :half]))
                g1 = twice_rsqrt(dist[rows, half:panels])
                qcol = dist[rows, panels:]
                back = back + fold(g1 * qcol)
                part = g0 * qrow[:, :half] + g1 * qrow[:, half:]
            else:
                part = jnp.where(eye, diag[:, half:], twice_rsqrt(dist[rows, half:panels])) * qrow[:, half:]
            keep(parts, rows, part)
        back = jnp.sum(back, axis=0, keepdims=True)
        acc[pl.ds(c, 1), :] += jnp.concatenate([jnp.zeros_like(back), back], axis=1)
        return c

    def self_step(i, carry):
        begin_self(2 * i + 1, dist1)
        c0 = finish_self(2 * i, dist0, part0)
        begin_self(2 * i + 2, dist0)
        c1 = finish_self(2 * i + 1, dist1, part1)
        add_columns(acct, (part0, part1), (c0, c1))
        return carry

    begin_self(0, dist0)
    lax.fori_loop(0, share // 2, self_step, 0)

    count = pairs.shape[1] // S
    start = sub * count

    def begin(i, dist):
        p = start + jnp.minimum(i, count - 1)
        distances(load_features(fa, pairs[0, p]), load_features(fb, pairs[1, p]), dist)

    def finish(i, dist, part):
        ia, ib = pairs[0, start + i], pairs[1, start + i]
        acc[pl.ds(ib, 1), :] += tile_sums(dist, q[pl.ds(ib, 1), :], part)
        return ia

    def pair_step(i, carry):
        begin(2 * i + 1, dist1)
        ia0 = finish(2 * i, dist0, part0)
        begin(2 * i + 2, dist0)
        ia1 = finish(2 * i + 1, dist1, part1)
        add_columns(acct, (part0, part1), (ia0, ia1))
        return carry

    begin(0, dist0)
    lax.fori_loop(0, count // 2, pair_step, 0)
    total = acc_in[...] + (acc[...] + acct[...].T) * (0.5 * inv)

    got[...] = jnp.zeros_like(got)
    for shift in range(1, C):
        dest = lax.rem(me + shift, C)
        for j in range(slots):
            got[pl.ds(targets[dest, j], 1), :] += sums[shift - 1][j : j + 1, :]

    par_dev, far_n, rank = coupling.shape[0], coupling.shape[1], coupling.shape[2]
    parents[pl.ds(pl.multiple_of(me * par_dev, 8), par_dev), :] = up[...]
    for shift in range(1, C):
        owner = lax.rem(me + shift, C)
        parents[pl.ds(pl.multiple_of(owner * par_dev, 8), par_dev), :] = sums[shift - 1][slots:, :rank]
    lane = lax.broadcasted_iota(jnp.int32, (rank, LANES), 1)
    field = jnp.zeros((rank, LANES), F32)
    for p in range(par_dev):
        part = jnp.zeros((rank, rank), F32)
        for k in range(far_n):
            part = part + coupling[p, k] * parents[pl.ds(far_list[p, k], 1), :]
        field = jnp.where(lane == p, jnp.sum(part, axis=1, keepdims=True), field)
    which = lax.broadcasted_iota(jnp.int32, (LANES, clusters), 0)
    onehot = (parent[...] == which).astype(F32)
    down = jnp.dot(field, onehot, precision=HIGHEST, preferred_element_type=F32)
    fields = jnp.concatenate(
        [jnp.sum(transfer[r] * down, axis=0, keepdims=True) for r in range(rank)], axis=0
    )

    def give(s):
        for shift in range(S):
            other = (s + shift) % S
            part = total[:, other * L : (other + 1) * L]
            parts[shift][:clusters, :] = part + got[...] if shift == 0 else part
            for t in range(clusters // L):
                at = clusters + t * rank
                parts[shift][at : at + rank, :] = fields[:, t * L : (t + 1) * L]

    for s in range(S):
        pl.when(sub == s)(functools.partial(give, s))


def up_kernel(basis, masked, transfer, parent, up):
    clusters = basis.shape[0]
    rank = basis.shape[1]
    lane = lax.broadcasted_iota(jnp.int32, (rank, clusters), 1)
    leaf = jnp.zeros((rank, clusters), F32)
    for c in range(clusters):
        part = jnp.sum(basis[c] * masked[c : c + 1, :], axis=1, keepdims=True)
        leaf = jnp.where(lane == c, part, leaf)
    lifted = jnp.zeros((rank, clusters), F32)
    for r in range(rank):
        lifted = lifted + transfer[r] * leaf[r : r + 1, :]
    which = lax.broadcasted_iota(jnp.int32, (up.shape[0], clusters), 0)
    onehot = (parent[...] == which).astype(F32)
    up[...] = lax.dot_general(
        onehot, lifted, (((1,), (1,)), ((), ())), precision=HIGHEST, preferred_element_type=F32
    )


def final_kernel(sizes, mask, basis, *rest):
    S, R, L = sizes
    near, out = rest[: S * R], rest[-1]
    clusters, rank = basis.shape[0], basis.shape[1]
    fields = []
    for t in range(clusters // L):
        rows = slice(clusters + t * rank, clusters + (t + 1) * rank)
        fields.append(sum(near[d * R][rows, :] for d in range(1, S)) + near[0][rows, :])
    fields = jnp.concatenate(fields, axis=1) if len(fields) > 1 else fields[0]
    for c in range(clusters):
        out[c : c + 1, :] = jnp.sum(basis[c] * fields[:, c : c + 1], axis=0, keepdims=True)
    total = out[...]
    for part in near:
        total = total + part[:clusters, :]
    out[...] = total * mask[...].astype(F32)


def send(value, moves):
    names = tuple(name for name, _ in moves)
    steps = [step for _, step in moves]
    sizes = [lax.axis_size(name) for name in names]
    perm = []

    def flat(coords):
        index = 0
        for size, c in zip(sizes, coords):
            index = index * size + c
        return index

    total = 1
    for size in sizes:
        total *= size
    for index in range(total):
        coords, left = [], index
        for size in reversed(sizes):
            coords.append(left % size)
            left //= size
        coords.reverse()
        perm.append((index, flat([(c + s) % n for c, s, n in zip(coords, steps, sizes)])))
    return lax.ppermute(value, names if len(names) > 1 else names[0], perm)


def on_device(
    charges,
    panel_mask,
    geometry,
    remote_source,
    remote_target,
    remote_live,
    local_pairs,
    basis,
    transfer,
    parent_of,
    far_list,
    coupling,
):
    clusters, L = charges.shape
    panels = geometry.shape[2]
    C, S, R = lax.axis_size("clu"), lax.axis_size("sub"), lax.axis_size("rep")
    slots = remote_source.shape[2]
    par_dev, rank = far_list.shape[0], transfer.shape[1]
    n = (C - 1) * slots
    shape = jax.ShapeDtypeStruct
    targets = remote_target[0]
    basis_t = jnp.transpose(basis, (0, 2, 1))
    transfer_t = jnp.transpose(transfer, (1, 2, 0))
    parent = parent_of[None, :]

    made = pl.pallas_call(
        functools.partial(pack_kernel, (C, S, L, slots)),
        out_shape=[shape((clusters, L), F32)] + [shape((5 * slots + 8, L), F32)] * (C - 1),
        in_specs=[vmem()] * 3 + [smem()] * 3,
        out_specs=[vmem()] * C,
        compiler_params=PARAMS,
        name="packs",
    )(charges, panel_mask, geometry, targets, remote_source[0], remote_live[0])
    masked, packs = made[0], made[1:]
    pieces = [masked] + [send(masked, (("sub", d),)) for d in range(1, S)]
    packs = [send(packs[d - 1], (("clu", d),)) for d in range(1, C)]
    codes = jnp.stack([p[5 * slots, :slots] for p in packs]).astype(jnp.int32)

    up = pl.pallas_call(
        up_kernel,
        out_shape=shape((par_dev, rank), F32),
        in_specs=[vmem()] * 4,
        out_specs=vmem(),
        compiler_params=PARAMS,
        name="far_up",
    )(basis_t, masked, transfer_t, parent)

    made = pl.pallas_call(
        functools.partial(remote_kernel, (C, S, L, slots, clusters, panels)),
        out_shape=[shape((clusters, panels), F32)] + [shape((slots + par_dev, L), F32)] * (C - 1),
        in_specs=[vmem(), smem()] + [vmem()] * (1 + S + C - 1),
        out_specs=[vmem()] * C,
        scratch_shapes=[
            pltpu.VMEM((clusters, panels), F32),
            pltpu.VMEM((clusters, panels), F32),
            pltpu.VMEM((L, whole(n)), F32),
            pltpu.VMEM((4 * n, panels), F32),
            pltpu.VMEM((n * ROWS, L), F32),
            pltpu.VMEM((n * ROWS, LANES), F32),
            pltpu.VMEM((n * ROWS, LANES), F32),
            pltpu.VMEM((L, panels + LANES), F32),
            pltpu.VMEM((L, panels + LANES), F32),
            pltpu.VMEM((L, 2 * LANES), BF16),
            pltpu.VMEM((L, 2 * LANES), BF16),
            pltpu.SMEM((n + 1,), jnp.int32),
        ],
        compiler_params=PARAMS,
        name="near_remote",
    )(geometry, codes, up, *pieces, *packs)
    acc, sums = made[0], [send(made[d], (("clu", C - d),)) for d in range(1, C)]

    half = [pltpu.VMEM((clusters * ROWS, LANES), F32)] * 2
    parts = pl.pallas_call(
        functools.partial(local_kernel, (C, S, L, R, slots, clusters, panels)),
        out_shape=[shape((clusters + clusters // L * rank, L), F32)] * S,
        in_specs=[vmem()] + [smem()] * 3 + [vmem()] * (5 + S + C - 1),
        out_specs=[vmem()] * S,
        scratch_shapes=[
            pltpu.VMEM((clusters, panels), F32),
            pltpu.VMEM((clusters, panels), F32),
            pltpu.VMEM((panels, clusters), F32),
            *half,
            *half,
            pltpu.VMEM((clusters, panels), F32),
            pltpu.VMEM((panels, panels + LANES), F32),
            pltpu.VMEM((panels, panels + LANES), F32),
            pltpu.VMEM((panels, 2 * LANES), BF16),
            pltpu.VMEM((panels, 2 * LANES), BF16),
            pltpu.VMEM((clusters, L), F32),
            pltpu.VMEM((C * par_dev, rank), F32),
        ],
        compiler_params=PARAMS,
        name="near_local",
    )(geometry, local_pairs[0].T, targets, far_list, coupling, transfer_t, parent, up, acc, *pieces, *sums)
    near = []
    for d in range(S):
        for e in range(R):
            near.append(send(parts[d], (("sub", d), ("rep", e))) if d or e else parts[0])

    return pl.pallas_call(
        functools.partial(final_kernel, (S, R, L)),
        out_shape=shape((clusters, L), F32),
        in_specs=[vmem()] * (2 + S * R),
        out_specs=vmem(),
        compiler_params=PARAMS,
        name="combine",
    )(panel_mask, basis_t, *near)


def solution(mesh):
    placed = (
        P(("grp", "clu"), "sub"),
        P(("grp", "clu"), "sub"),
        P(("grp", "clu"), None, None),
        P(("grp", "clu"), None, "rep"),
        P(("grp", "clu"), None, "rep"),
        P(("grp", "clu"), None, "rep"),
        P(("grp", "clu"), "rep", None),
        P(("grp", "clu"), "sub", None),
        P(("grp", "clu"), None, None),
        P(("grp", "clu")),
        P(("grp", "clu"), None),
        P(("grp", "clu"), None, None, None),
    )
    return jax.shard_map(
        on_device, mesh=mesh, in_specs=placed, out_specs=P(("grp", "clu"), "sub"), check_vma=False
    )
```

```python
import functools

import jax
import jax.numpy as jnp
from jax import lax
from jax.experimental import pallas as pl
from jax.experimental.pallas import tpu as pltpu
from jax.sharding import PartitionSpec as P

F32 = jnp.float32
BF16 = jnp.bfloat16
HIGHEST = lax.Precision.HIGHEST
ROWS = 40
USED = 37
LANES = 128
PARAMS = pltpu.CompilerParams(vmem_limit_bytes=56 * 1024 * 1024)


def vmem():
    return pl.BlockSpec(memory_space=pltpu.VMEM)


def smem():
    return pl.BlockSpec(memory_space=pltpu.SMEM)


def whole(size):
    return -(-size // LANES) * LANES


def cut(v):
    return v.astype(BF16).astype(F32)


def powers(sign):
    lane = lax.broadcasted_iota(jnp.int32, (8, LANES), 1)
    out = jnp.full((8, LANES), 2.0 ** (-64 * sign), F32)
    for bit in range(7):
        out = out * jnp.where((lane >> bit) & 1 == 1, F32(2.0 ** (sign * 2**bit)), F32(1.0))
    return out


def frame(parts):
    low = [functools.reduce(jnp.minimum, [jnp.min(p[k]) for p in parts]) for k in range(3)]
    high = [functools.reduce(jnp.maximum, [jnp.max(p[k]) for p in parts]) for k in range(3)]
    width = functools.reduce(jnp.maximum, [jnp.max(jnp.abs(p[3])) for p in parts])
    for lo, hi in zip(low, high):
        width = jnp.maximum(width, 0.5 * (hi - lo))
    up, down = powers(1), powers(-1)
    size = jnp.min(jnp.where(up >= width, up, F32(2.0**63)))
    inv = jnp.max(jnp.where(up >= width, down, F32(2.0**-63)))
    magic = size * F32(1.5 * 2.0**20)
    centre = [(0.5 * (lo + hi) + magic) - magic for lo, hi in zip(low, high)]
    return centre, inv


def split_features(points, centre, inv, charge=None):
    magic = F32(1.5 * 2.0**16)
    grid, rest = [], []
    for k in range(3):
        u = (points[k] - centre[k]) * inv
        h = (u + magic) - magic
        grid.append(h)
        rest.append(u - h)
    rad = points[3] * inv
    norm = grid[0] * grid[0] + grid[1] * grid[1] + grid[2] * grid[2]
    norm1 = cut(norm)
    norm2 = norm - norm1
    cross = grid[0] * rest[0] + grid[1] * rest[1] + grid[2] * rest[2]
    extra = 2.0 * cross + (rest[0] * rest[0] + rest[1] * rest[1] + rest[2] * rest[2]) + rad * rad
    extra1 = cut(extra)
    extra2 = cut(extra - extra1)
    extra3 = (extra - extra1) - extra2
    rest1 = [cut(v) for v in rest]
    rest2 = [v - w for v, w in zip(rest, rest1)]
    neg = lambda vs: [-2.0 * v for v in vs]
    one = jnp.ones_like(rad)
    left = grid + [norm1, norm2, one, one]
    right = neg(grid) + [one, one, norm1, norm2]
    left += [extra1, extra2, extra3, one, one, one]
    right += [one, one, one, extra1, extra2, extra3]
    left += grid + grid + rest1 + rest2 + rest1 + rest1 + rest2
    right += neg(rest1) + neg(rest2) + neg(grid) + neg(grid) + neg(rest1) + neg(rest2) + neg(rest1)
    if charge is not None:
        charge1 = cut(charge)
        charge2 = cut(charge - charge1)
        left += [charge1, charge2, (charge - charge1) - charge2]
    right += [jnp.zeros_like(rad)] * 3
    return left, right, rad


def store_features(ref, rows):
    count = rows[0].shape[0]
    width = rows[0].shape[1]
    for k, row in enumerate(rows):
        for t, piece in enumerate(ref):
            piece[pl.ds(k, count, stride=ROWS), :] = row[:, t * LANES : min(width, (t + 1) * LANES)]


def load_features(ref, index):
    start = pl.multiple_of(index * ROWS, 8)
    return [piece[pl.ds(start, USED), :].astype(BF16) for piece in ref]


def contract(left, right):
    return jnp.dot(left, right, preferred_element_type=F32)


def pick(rows, width, index):
    lane = lax.broadcasted_iota(jnp.int32, (rows, width), 1)
    return jnp.where(lane == index, 1.0, 0.0).astype(BF16)


def fold(v):
    return jnp.sum(v.reshape(v.shape[0] // 8, 8, v.shape[1]), axis=0)


def charge_rows():
    row = lax.broadcasted_iota(jnp.int32, (USED, LANES), 0)
    return jnp.where(row >= USED - 3, 1.0, 0.0).astype(BF16)


def distances(left, right, out):
    whole_left = jnp.concatenate(left, axis=1) if len(left) > 1 else left[0]
    whole_right = jnp.concatenate(list(right) + [charge_rows()], axis=1)
    out[...] = contract(whole_left.T, whole_right)


def keep(parts, rows, value):
    high = value.astype(BF16)
    parts[rows, :LANES] = high
    parts[rows, LANES:] = (value - high.astype(F32)).astype(BF16)


def add_columns(table, parts, indices):
    width = table.shape[1]
    left = jnp.concatenate([p[...] for p in parts], axis=1)
    right = jnp.concatenate([pick(2 * LANES, width, i) for i in indices], axis=0)
    table[...] += jnp.dot(left, right, preferred_element_type=F32)


def tile_sums(dist, qrow, parts, step=64):
    height = dist.shape[0]
    step = min(step, height)
    q0, q1 = qrow[:, :LANES], qrow[:, LANES:]
    back0 = back1 = jnp.zeros((8, LANES), F32)
    for r in range(0, height, step):
        rows = slice(r, r + step)
        g0 = lax.rsqrt(dist[rows, :LANES])
        g1 = lax.rsqrt(dist[rows, LANES : 2 * LANES])
        qcol = dist[rows, 2 * LANES :]
        keep(parts, rows, g0 * q0 + g1 * q1)
        back0 = back0 + fold(g0 * qcol)
        back1 = back1 + fold(g1 * qcol)
    return jnp.concatenate(
        [jnp.sum(back0, axis=0, keepdims=True), jnp.sum(back1, axis=0, keepdims=True)], axis=1
    )


def assemble(sub, S, L, q, pieces):
    def place(s):
        for shift in range(S):
            owner = (s - shift) % S
            q[:, owner * L : (owner + 1) * L] = pieces[shift][...]

    for s in range(S):
        pl.when(sub == s)(functools.partial(place, s))


def pack_kernel(sizes, charges, mask, geo, targets, sources, live, masked, *packs):
    C, S, L, slots = sizes
    me, sub = lax.axis_index("clu"), lax.axis_index("sub")
    masked[...] = charges[...] * mask[...].astype(F32)
    lane = lax.broadcasted_iota(jnp.int32, (8, L), 1)
    for shift in range(1, C):
        dest = lax.rem(me + shift, C)
        codes = jnp.full((8, L), -1.0, F32)
        for j in range(slots):
            code = jnp.where(live[dest, j] > 0, sources[dest, j], -1)
            codes = jnp.where(lane == j, code.astype(F32), codes)
        packs[shift - 1][5 * slots :, :] = codes

    def fill(s):
        for shift in range(1, C):
            dest = lax.rem(me + shift, C)
            pack = packs[shift - 1]
            for j in range(slots):
                t = targets[dest, j]
                g = geo[t, :, s * L : (s + 1) * L]
                for k in range(4):
                    pack[k * slots + j : k * slots + j + 1, :] = g[k : k + 1]
                pack[4 * slots + j : 4 * slots + j + 1, :] = masked[pl.ds(t, 1), :]

    for s in range(S):
        pl.when(sub == s)(functools.partial(fill, s))


def remote_kernel(sizes, geo, codes, up, *rest):
    C, S, L, slots, clusters, panels = sizes
    pieces = rest[:S]
    packs = rest[S : S + C - 1]
    acc_out = rest[S + C - 1]
    sends = rest[S + C : S + C + C - 1]
    q, acc, fwdt, sgeo, fa0, fb0, fb1, dist0, dist1, part0, part1, order = rest[S + C + C - 1 :]
    fa, fb = (fa0,), (fb0, fb1)
    n = (C - 1) * slots
    assemble(lax.axis_index("sub"), S, L, q, pieces)
    acc[...] = jnp.zeros_like(acc)
    fwdt[...] = jnp.zeros_like(fwdt)
    found = jnp.int32(0)
    for shift in range(C - 1):
        for j in range(slots):
            code = codes[shift, j]
            order[found] = shift * slots + j
            found = found + (code >= 0).astype(jnp.int32)
            g = geo[jnp.maximum(code, 0)]
            for k in range(4):
                row = k * n + shift * slots + j
                sgeo[row : row + 1, :] = g[k : k + 1]
    tpoints = [
        jnp.concatenate([p[k * slots : (k + 1) * slots, :] for p in packs], axis=0) for k in range(5)
    ]
    spoints = [sgeo[k * n : (k + 1) * n, :] for k in range(4)]
    centre, inv = frame([tpoints, spoints])
    left, _, _ = split_features(tpoints, centre, inv, tpoints[4])
    _, right, _ = split_features(spoints, centre, inv)
    store_features(fa, left)
    store_features(fb, right)
    def begin(i, dist):
        slot = order[jnp.minimum(i, jnp.maximum(found - 1, 0))]
        distances(load_features(fa, slot), load_features(fb, slot), dist)

    def finish(i, dist, part):
        ok = i < found
        slot = order[jnp.minimum(i, jnp.maximum(found - 1, 0))]
        source = jnp.maximum(codes[slot // slots, lax.rem(slot, slots)], 0)
        back = tile_sums(dist, q[pl.ds(source, 1), :], part)
        acc[pl.ds(source, 1), :] += jnp.where(ok, back, 0.0)
        return jnp.where(ok, slot, -1)

    def step(i, carry):
        begin(2 * i + 1, dist1)
        slot0 = finish(2 * i, dist0, part0)
        begin(2 * i + 2, dist0)
        slot1 = finish(2 * i + 1, dist1, part1)
        add_columns(fwdt, (part0, part1), (slot0, slot1))
        return carry

    begin(0, dist0)
    lax.fori_loop(0, (found + 1) // 2, step, 0)
    acc_out[...] = acc[...] * inv
    fwd = (fwdt[...] * inv).T
    rank = up.shape[1]
    for shift in range(C - 1):
        sends[shift][:slots, :] = fwd[shift * slots : (shift + 1) * slots, :]
        sends[shift][slots:, :] = jnp.zeros((up.shape[0], L), F32)
        sends[shift][slots:, :rank] = up[...]


def local_kernel(
    sizes, geo, pairs, targets, far_list, coupling, transfer, parent, up, acc_in, *rest
):
    C, S, L, R, slots, clusters, panels = sizes
    pieces = rest[:S]
    sums = rest[S : S + C - 1]
    parts = rest[S + C - 1 : 2 * S + C - 1]
    q, acc, acct, fa0, fa1, fb0, fb1, rads, dist0, dist1, part0, part1, got, parents = rest[2 * S + C - 1 :]
    fa, fb = (fa0, fa1), (fb0, fb1)
    me, sub, rep = lax.axis_index("clu"), lax.axis_index("sub"), lax.axis_index("rep")
    assemble(sub, S, L, q, pieces)
    acc[...] = jnp.zeros_like(acc)
    acct[...] = jnp.zeros_like(acct)
    points = [geo[:, k, :] for k in range(4)]
    centre, inv = frame([points])
    left, right, rad = split_features(points, centre, inv, q[...])
    store_features(fa, left)
    store_features(fb, right)
    rads[...] = rad

    half = panels // 2
    share = clusters // (S * R)
    first = (rep * S + sub) * share

    def begin_self(i, dist):
        c = first + jnp.minimum(i, share - 1)
        a = load_features(fa, c)
        b = load_features(fb, c)
        dist[:half, :] = contract(a[0].T, jnp.concatenate([b[0], b[1], charge_rows()], axis=1))
        dist[half:, half:panels] = contract(a[1].T, b[1])

    def finish_self(i, dist, parts):
        c = first + i
        qrow = q[pl.ds(c, 1), :]
        radius = rads[pl.ds(c, 1), :]
        diag = lax.rsqrt(2.0 * (radius * radius))
        back = jnp.zeros((8, LANES), F32)
        step = 64
        for r in range(0, panels, step):
            rows = slice(r, r + step)
            base = r % half
            eye = lax.broadcasted_iota(jnp.int32, (step, half), 0) + base == lax.broadcasted_iota(
                jnp.int32, (step, half), 1
            )
            if r < half:
                g0 = jnp.where(eye, diag[:, :half], lax.rsqrt(dist[rows, :half]))
                g1 = lax.rsqrt(dist[rows, half:panels])
                qcol = dist[rows, panels:]
                back = back + fold(g1 * qcol)
                part = g0 * qrow[:, :half] + g1 * qrow[:, half:]
            else:
                part = jnp.where(eye, diag[:, half:], lax.rsqrt(dist[rows, half:panels])) * qrow[:, half:]
            keep(parts, rows, part)
        back = jnp.sum(back, axis=0, keepdims=True)
        acc[pl.ds(c, 1), :] += jnp.concatenate([jnp.zeros_like(back), back], axis=1)
        return c

    def self_step(i, carry):
        begin_self(2 * i + 1, dist1)
        c0 = finish_self(2 * i, dist0, part0)
        begin_self(2 * i + 2, dist0)
        c1 = finish_self(2 * i + 1, dist1, part1)
        add_columns(acct, (part0, part1), (c0, c1))
        return carry

    begin_self(0, dist0)
    lax.fori_loop(0, share // 2, self_step, 0)

    count = pairs.shape[1] // S
    start = sub * count

    def begin(i, dist):
        p = start + jnp.minimum(i, count - 1)
        distances(load_features(fa, pairs[0, p]), load_features(fb, pairs[1, p]), dist)

    def finish(i, dist, part):
        ia, ib = pairs[0, start + i], pairs[1, start + i]
        acc[pl.ds(ib, 1), :] += tile_sums(dist, q[pl.ds(ib, 1), :], part)
        return ia

    def pair_step(i, carry):
        begin(2 * i + 1, dist1)
        ia0 = finish(2 * i, dist0, part0)
        begin(2 * i + 2, dist0)
        ia1 = finish(2 * i + 1, dist1, part1)
        add_columns(acct, (part0, part1), (ia0, ia1))
        return carry

    begin(0, dist0)
    lax.fori_loop(0, count // 2, pair_step, 0)
    total = acc_in[...] + (acc[...] + acct[...].T) * inv

    got[...] = jnp.zeros_like(got)
    for shift in range(1, C):
        dest = lax.rem(me + shift, C)
        for j in range(slots):
            got[pl.ds(targets[dest, j], 1), :] += sums[shift - 1][j : j + 1, :]

    par_dev, far_n, rank = coupling.shape[0], coupling.shape[1], coupling.shape[2]
    parents[pl.ds(pl.multiple_of(me * par_dev, 8), par_dev), :] = up[...]
    for shift in range(1, C):
        owner = lax.rem(me + shift, C)
        parents[pl.ds(pl.multiple_of(owner * par_dev, 8), par_dev), :] = sums[shift - 1][slots:, :rank]
    lane = lax.broadcasted_iota(jnp.int32, (rank, LANES), 1)
    field = jnp.zeros((rank, LANES), F32)
    for p in range(par_dev):
        part = jnp.zeros((rank, rank), F32)
        for k in range(far_n):
            part = part + coupling[p, k] * parents[pl.ds(far_list[p, k], 1), :]
        field = jnp.where(lane == p, jnp.sum(part, axis=1, keepdims=True), field)
    which = lax.broadcasted_iota(jnp.int32, (LANES, clusters), 0)
    onehot = (parent[...] == which).astype(F32)
    down = jnp.dot(field, onehot, precision=HIGHEST, preferred_element_type=F32)
    fields = jnp.concatenate(
        [jnp.sum(transfer[r] * down, axis=0, keepdims=True) for r in range(rank)], axis=0
    )

    def give(s):
        for shift in range(S):
            other = (s + shift) % S
            part = total[:, other * L : (other + 1) * L]
            parts[shift][:clusters, :] = part + got[...] if shift == 0 else part
            for t in range(clusters // L):
                at = clusters + t * rank
                parts[shift][at : at + rank, :] = fields[:, t * L : (t + 1) * L]

    for s in range(S):
        pl.when(sub == s)(functools.partial(give, s))


def up_kernel(basis, masked, transfer, parent, up):
    clusters = basis.shape[0]
    rank = basis.shape[1]
    lane = lax.broadcasted_iota(jnp.int32, (rank, clusters), 1)
    leaf = jnp.zeros((rank, clusters), F32)
    for c in range(clusters):
        part = jnp.sum(basis[c] * masked[c : c + 1, :], axis=1, keepdims=True)
        leaf = jnp.where(lane == c, part, leaf)
    lifted = jnp.zeros((rank, clusters), F32)
    for r in range(rank):
        lifted = lifted + transfer[r] * leaf[r : r + 1, :]
    which = lax.broadcasted_iota(jnp.int32, (up.shape[0], clusters), 0)
    onehot = (parent[...] == which).astype(F32)
    up[...] = lax.dot_general(
        onehot, lifted, (((1,), (1,)), ((), ())), precision=HIGHEST, preferred_element_type=F32
    )


def final_kernel(sizes, mask, basis, *rest):
    S, R, L = sizes
    near, out = rest[: S * R], rest[-1]
    clusters, rank = basis.shape[0], basis.shape[1]
    fields = []
    for t in range(clusters // L):
        rows = slice(clusters + t * rank, clusters + (t + 1) * rank)
        fields.append(sum(near[d * R][rows, :] for d in range(1, S)) + near[0][rows, :])
    fields = jnp.concatenate(fields, axis=1) if len(fields) > 1 else fields[0]
    for c in range(clusters):
        out[c : c + 1, :] = jnp.sum(basis[c] * fields[:, c : c + 1], axis=0, keepdims=True)
    total = out[...]
    for part in near:
        total = total + part[:clusters, :]
    out[...] = total * mask[...].astype(F32)


def send(value, moves):
    names = tuple(name for name, _ in moves)
    steps = [step for _, step in moves]
    sizes = [lax.axis_size(name) for name in names]
    perm = []

    def flat(coords):
        index = 0
        for size, c in zip(sizes, coords):
            index = index * size + c
        return index

    total = 1
    for size in sizes:
        total *= size
    for index in range(total):
        coords, left = [], index
        for size in reversed(sizes):
            coords.append(left % size)
            left //= size
        coords.reverse()
        perm.append((index, flat([(c + s) % n for c, s, n in zip(coords, steps, sizes)])))
    return lax.ppermute(value, names if len(names) > 1 else names[0], perm)


def on_device(
    charges,
    panel_mask,
    geometry,
    remote_source,
    remote_target,
    remote_live,
    local_pairs,
    basis,
    transfer,
    parent_of,
    far_list,
    coupling,
):
    clusters, L = charges.shape
    panels = geometry.shape[2]
    C, S, R = lax.axis_size("clu"), lax.axis_size("sub"), lax.axis_size("rep")
    slots = remote_source.shape[2]
    par_dev, rank = far_list.shape[0], transfer.shape[1]
    n = (C - 1) * slots
    shape = jax.ShapeDtypeStruct
    targets = remote_target[0]
    basis_t = jnp.transpose(basis, (0, 2, 1))
    transfer_t = jnp.transpose(transfer, (1, 2, 0))
    parent = parent_of[None, :]

    made = pl.pallas_call(
        functools.partial(pack_kernel, (C, S, L, slots)),
        out_shape=[shape((clusters, L), F32)] + [shape((5 * slots + 8, L), F32)] * (C - 1),
        in_specs=[vmem()] * 3 + [smem()] * 3,
        out_specs=[vmem()] * C,
        compiler_params=PARAMS,
        name="packs",
    )(charges, panel_mask, geometry, targets, remote_source[0], remote_live[0])
    masked, packs = made[0], made[1:]
    pieces = [masked] + [send(masked, (("sub", d),)) for d in range(1, S)]
    packs = [send(packs[d - 1], (("clu", d),)) for d in range(1, C)]
    codes = jnp.stack([p[5 * slots, :slots] for p in packs]).astype(jnp.int32)

    up = pl.pallas_call(
        up_kernel,
        out_shape=shape((par_dev, rank), F32),
        in_specs=[vmem()] * 4,
        out_specs=vmem(),
        compiler_params=PARAMS,
        name="far_up",
    )(basis_t, masked, transfer_t, parent)

    made = pl.pallas_call(
        functools.partial(remote_kernel, (C, S, L, slots, clusters, panels)),
        out_shape=[shape((clusters, panels), F32)] + [shape((slots + par_dev, L), F32)] * (C - 1),
        in_specs=[vmem(), smem()] + [vmem()] * (1 + S + C - 1),
        out_specs=[vmem()] * C,
        scratch_shapes=[
            pltpu.VMEM((clusters, panels), F32),
            pltpu.VMEM((clusters, panels), F32),
            pltpu.VMEM((L, whole(n)), F32),
            pltpu.VMEM((4 * n, panels), F32),
            pltpu.VMEM((n * ROWS, L), F32),
            pltpu.VMEM((n * ROWS, LANES), F32),
            pltpu.VMEM((n * ROWS, LANES), F32),
            pltpu.VMEM((L, panels + LANES), F32),
            pltpu.VMEM((L, panels + LANES), F32),
            pltpu.VMEM((L, 2 * LANES), BF16),
            pltpu.VMEM((L, 2 * LANES), BF16),
            pltpu.SMEM((n + 1,), jnp.int32),
        ],
        compiler_params=PARAMS,
        name="near_remote",
    )(geometry, codes, up, *pieces, *packs)
    acc, sums = made[0], [send(made[d], (("clu", C - d),)) for d in range(1, C)]

    half = [pltpu.VMEM((clusters * ROWS, LANES), F32)] * 2
    parts = pl.pallas_call(
        functools.partial(local_kernel, (C, S, L, R, slots, clusters, panels)),
        out_shape=[shape((clusters + clusters // L * rank, L), F32)] * S,
        in_specs=[vmem()] + [smem()] * 3 + [vmem()] * (5 + S + C - 1),
        out_specs=[vmem()] * S,
        scratch_shapes=[
            pltpu.VMEM((clusters, panels), F32),
            pltpu.VMEM((clusters, panels), F32),
            pltpu.VMEM((panels, clusters), F32),
            *half,
            *half,
            pltpu.VMEM((clusters, panels), F32),
            pltpu.VMEM((panels, panels + LANES), F32),
            pltpu.VMEM((panels, panels + LANES), F32),
            pltpu.VMEM((panels, 2 * LANES), BF16),
            pltpu.VMEM((panels, 2 * LANES), BF16),
            pltpu.VMEM((clusters, L), F32),
            pltpu.VMEM((C * par_dev, rank), F32),
        ],
        compiler_params=PARAMS,
        name="near_local",
    )(geometry, local_pairs[0].T, targets, far_list, coupling, transfer_t, parent, up, acc, *pieces, *sums)
    near = []
    for d in range(S):
        for e in range(R):
            near.append(send(parts[d], (("sub", d), ("rep", e))) if d or e else parts[0])

    return pl.pallas_call(
        functools.partial(final_kernel, (S, R, L)),
        out_shape=shape((clusters, L), F32),
        in_specs=[vmem()] * (2 + S * R),
        out_specs=vmem(),
        compiler_params=PARAMS,
        name="combine",
    )(panel_mask, basis_t, *near)


def solution(mesh):
    placed = (
        P(("grp", "clu"), "sub"),
        P(("grp", "clu"), "sub"),
        P(("grp", "clu"), None, None),
        P(("grp", "clu"), None, "rep"),
        P(("grp", "clu"), None, "rep"),
        P(("grp", "clu"), None, "rep"),
        P(("grp", "clu"), "rep", None),
        P(("grp", "clu"), "sub", None),
        P(("grp", "clu"), None, None),
        P(("grp", "clu")),
        P(("grp", "clu"), None),
        P(("grp", "clu"), None, None, None),
    )
    return jax.shard_map(
        on_device, mesh=mesh, in_specs=placed, out_specs=P(("grp", "clu"), "sub"), check_vma=False
    )
```

```python
import functools

import jax
import jax.numpy as jnp
from jax import lax
from jax.experimental import pallas as pl
from jax.experimental.pallas import tpu as pltpu
from jax.sharding import PartitionSpec as P

F32 = jnp.float32
BF16 = jnp.bfloat16
HIGHEST = lax.Precision.HIGHEST
ROWS = 40
USED = 34
LANES = 128
PARAMS = pltpu.CompilerParams(vmem_limit_bytes=56 * 1024 * 1024)


def vmem():
    return pl.BlockSpec(memory_space=pltpu.VMEM)


def smem():
    return pl.BlockSpec(memory_space=pltpu.SMEM)


def whole(size):
    return -(-size // LANES) * LANES


def cut(v):
    return v.astype(BF16).astype(F32)


def powers(sign):
    lane = lax.broadcasted_iota(jnp.int32, (8, LANES), 1)
    out = jnp.full((8, LANES), 2.0 ** (-64 * sign), F32)
    for bit in range(7):
        out = out * jnp.where((lane >> bit) & 1 == 1, F32(2.0 ** (sign * 2**bit)), F32(1.0))
    return out


def frame(parts):
    low = [functools.reduce(jnp.minimum, [jnp.min(p[k]) for p in parts]) for k in range(3)]
    high = [functools.reduce(jnp.maximum, [jnp.max(p[k]) for p in parts]) for k in range(3)]
    width = functools.reduce(jnp.maximum, [jnp.max(jnp.abs(p[3])) for p in parts])
    for lo, hi in zip(low, high):
        width = jnp.maximum(width, 0.5 * (hi - lo))
    up, down = powers(1), powers(-1)
    size = jnp.min(jnp.where(up >= width, up, F32(2.0**63)))
    inv = jnp.max(jnp.where(up >= width, down, F32(2.0**-63)))
    magic = size * F32(1.5 * 2.0**20)
    centre = [(0.5 * (lo + hi) + magic) - magic for lo, hi in zip(low, high)]
    return centre, inv


def split_features(points, centre, inv):
    magic = F32(1.5 * 2.0**16)
    grid, rest = [], []
    for k in range(3):
        u = (points[k] - centre[k]) * inv
        h = (u + magic) - magic
        grid.append(h)
        rest.append(u - h)
    rad = points[3] * inv
    norm = grid[0] * grid[0] + grid[1] * grid[1] + grid[2] * grid[2]
    norm1 = cut(norm)
    norm2 = norm - norm1
    cross = grid[0] * rest[0] + grid[1] * rest[1] + grid[2] * rest[2]
    extra = 2.0 * cross + (rest[0] * rest[0] + rest[1] * rest[1] + rest[2] * rest[2]) + rad * rad
    extra1 = cut(extra)
    extra2 = cut(extra - extra1)
    extra3 = (extra - extra1) - extra2
    rest1 = [cut(v) for v in rest]
    rest2 = [v - w for v, w in zip(rest, rest1)]
    neg = lambda vs: [-2.0 * v for v in vs]
    one = jnp.ones_like(rad)
    left = grid + [norm1, norm2, one, one]
    right = neg(grid) + [one, one, norm1, norm2]
    left += [extra1, extra2, extra3, one, one, one]
    right += [one, one, one, extra1, extra2, extra3]
    left += grid + grid + rest1 + rest2 + rest1 + rest1 + rest2
    right += neg(rest1) + neg(rest2) + neg(grid) + neg(grid) + neg(rest1) + neg(rest2) + neg(rest1)
    return left, right, rad


def store_features(ref, rows):
    count = rows[0].shape[0]
    width = rows[0].shape[1]
    for k, row in enumerate(rows):
        for t, piece in enumerate(ref):
            piece[pl.ds(k, count, stride=ROWS), :] = row[:, t * LANES : min(width, (t + 1) * LANES)]


def load_features(ref, index):
    start = pl.multiple_of(index * ROWS, 8)
    return [piece[pl.ds(start, USED), :].astype(BF16) for piece in ref]


def contract(left, right):
    return lax.dot_general(left, right, (((0,), (0,)), ((), ())), preferred_element_type=F32)


def column(table, index):
    if table.shape[1] == LANES and table.shape[0] % 8 == 0:
        return jnp.take_along_axis(table, jnp.full(table.shape, index, jnp.int32), axis=1)
    lane = lax.broadcasted_iota(jnp.int32, table.shape, 1)
    picked = jnp.sum(jnp.where(lane == index, table, 0.0), axis=1, keepdims=True)
    return jnp.broadcast_to(picked, (table.shape[0], LANES))


def put_column(table, rows, index, value):
    shape = (rows.stop - rows.start, table.shape[1])
    lane = lax.broadcasted_iota(jnp.int32, shape, 1)
    pltpu.store(table.at[rows, :], jnp.broadcast_to(value, shape), mask=lane == index)


def inverse_root(d):
    return lax.exp2(-0.5 * lax.log2(d))


def fold(v):
    return jnp.sum(v.reshape(v.shape[0] // 8, 8, v.shape[1]), axis=0)


def distances(left, right, out):
    whole_left = jnp.concatenate(left, axis=1) if len(left) > 1 else left[0]
    for t, r in enumerate(right):
        out[:, t * LANES : (t + 1) * LANES] = contract(whole_left, r)


def tile_sums(dist, qrow, qtable, slot, table_ref, index, step=64):
    height = dist.shape[0]
    step = min(step, height)
    q0, q1 = qrow[:, :LANES], qrow[:, LANES:]
    back0 = back1 = jnp.zeros((8, LANES), F32)
    for r in range(0, height, step):
        rows = slice(r, r + step)
        g0 = inverse_root(dist[rows, :LANES])
        g1 = inverse_root(dist[rows, LANES:])
        qcol = column(qtable[rows, :], slot)
        put_column(table_ref, rows, index, jnp.sum(g0 * q0 + g1 * q1, axis=1, keepdims=True))
        back0 = back0 + fold(g0 * qcol)
        back1 = back1 + fold(g1 * qcol)
    return jnp.concatenate(
        [jnp.sum(back0, axis=0, keepdims=True), jnp.sum(back1, axis=0, keepdims=True)], axis=1
    )


def assemble(sub, S, L, q, pieces):
    def place(s):
        for shift in range(S):
            owner = (s - shift) % S
            q[:, owner * L : (owner + 1) * L] = pieces[shift][...]

    for s in range(S):
        pl.when(sub == s)(functools.partial(place, s))


def pack_kernel(sizes, charges, mask, geo, targets, sources, live, masked, *packs):
    C, S, L, slots = sizes
    me, sub = lax.axis_index("clu"), lax.axis_index("sub")
    masked[...] = charges[...] * mask[...].astype(F32)
    lane = lax.broadcasted_iota(jnp.int32, (8, L), 1)
    for shift in range(1, C):
        dest = lax.rem(me + shift, C)
        codes = jnp.full((8, L), -1.0, F32)
        for j in range(slots):
            code = jnp.where(live[dest, j] > 0, sources[dest, j], -1)
            codes = jnp.where(lane == j, code.astype(F32), codes)
        packs[shift - 1][5 * slots :, :] = codes

    def fill(s):
        for shift in range(1, C):
            dest = lax.rem(me + shift, C)
            pack = packs[shift - 1]
            for j in range(slots):
                t = targets[dest, j]
                g = geo[t, :, s * L : (s + 1) * L]
                for k in range(4):
                    pack[k * slots + j : k * slots + j + 1, :] = g[k : k + 1]
                pack[4 * slots + j : 4 * slots + j + 1, :] = masked[pl.ds(t, 1), :]

    for s in range(S):
        pl.when(sub == s)(functools.partial(fill, s))


def remote_kernel(sizes, geo, codes, up, *rest):
    C, S, L, slots, clusters, panels = sizes
    pieces = rest[:S]
    packs = rest[S : S + C - 1]
    acc_out = rest[S + C - 1]
    sends = rest[S + C : S + C + C - 1]
    q, tqt, acc, fwdt, sgeo, fa0, fb0, fb1, dist0, dist1, order = rest[S + C + C - 1 :]
    fa, fb = (fa0,), (fb0, fb1)
    n = (C - 1) * slots
    assemble(lax.axis_index("sub"), S, L, q, pieces)
    acc[...] = jnp.zeros_like(acc)
    fwdt[...] = jnp.zeros_like(fwdt)
    found = jnp.int32(0)
    for shift in range(C - 1):
        for j in range(slots):
            code = codes[shift, j]
            order[found] = shift * slots + j
            found = found + (code >= 0).astype(jnp.int32)
            g = geo[jnp.maximum(code, 0)]
            for k in range(4):
                row = k * n + shift * slots + j
                sgeo[row : row + 1, :] = g[k : k + 1]
    tpoints = [
        jnp.concatenate([p[k * slots : (k + 1) * slots, :] for p in packs], axis=0) for k in range(5)
    ]
    spoints = [sgeo[k * n : (k + 1) * n, :] for k in range(4)]
    centre, inv = frame([tpoints, spoints])
    left, _, _ = split_features(tpoints, centre, inv)
    _, right, _ = split_features(spoints, centre, inv)
    store_features(fa, left)
    store_features(fb, right)
    wide = tqt.shape[1]
    tq = tpoints[4]
    if wide > n:
        tq = jnp.concatenate([tq, jnp.zeros((wide - n, L), F32)], axis=0)
    tqt[...] = tq.T

    def begin(i, dist):
        slot = order[jnp.minimum(i, jnp.maximum(found - 1, 0))]
        distances(load_features(fa, slot), load_features(fb, slot), dist)

    def finish(i, dist):
        ok = i < found
        slot = order[jnp.minimum(i, jnp.maximum(found - 1, 0))]
        source = jnp.maximum(codes[slot // slots, lax.rem(slot, slots)], 0)
        back = tile_sums(
            dist, q[pl.ds(source, 1), :], tqt, slot, fwdt, jnp.where(ok, slot, -1)
        )
        acc[pl.ds(source, 1), :] += jnp.where(ok, back, 0.0)

    def step(i, carry):
        begin(2 * i + 1, dist1)
        finish(2 * i, dist0)
        begin(2 * i + 2, dist0)
        finish(2 * i + 1, dist1)
        return carry

    begin(0, dist0)
    lax.fori_loop(0, (found + 1) // 2, step, 0)
    acc_out[...] = acc[...] * inv
    fwd = (fwdt[...] * inv).T
    rank = up.shape[1]
    for shift in range(C - 1):
        sends[shift][:slots, :] = fwd[shift * slots : (shift + 1) * slots, :]
        sends[shift][slots:, :] = jnp.zeros((up.shape[0], L), F32)
        sends[shift][slots:, :rank] = up[...]


def local_kernel(
    sizes, geo, pairs, targets, far_list, coupling, transfer, parent, up, acc_in, *rest
):
    C, S, L, R, slots, clusters, panels = sizes
    pieces = rest[:S]
    sums = rest[S : S + C - 1]
    parts = rest[S + C - 1 : 2 * S + C - 1]
    q, qt, acc, acct, fa0, fa1, fb0, fb1, rads, dist0, dist1, got, parents, rows = rest[2 * S + C - 1 :]
    fa, fb = (fa0, fa1), (fb0, fb1)
    me, sub, rep = lax.axis_index("clu"), lax.axis_index("sub"), lax.axis_index("rep")
    assemble(sub, S, L, q, pieces)
    qt[...] = q[...].T
    acc[...] = jnp.zeros_like(acc)
    acct[...] = jnp.zeros_like(acct)
    points = [geo[:, k, :] for k in range(4)]
    centre, inv = frame([points])
    left, right, rad = split_features(points, centre, inv)
    store_features(fa, left)
    store_features(fb, right)
    rads[...] = rad

    half = panels // 2
    share = clusters // (S * R)
    first = (rep * S + sub) * share

    def begin_self(i, dist):
        c = first + jnp.minimum(i, share - 1)
        a = load_features(fa, c)
        b = load_features(fb, c)
        dist[:half, :half] = contract(a[0], b[0])
        dist[:half, half:] = contract(a[0], b[1])
        dist[half:, half:] = contract(a[1], b[1])

    def finish_self(i, dist):
        c = first + i
        qrow = q[pl.ds(c, 1), :]
        radius = rads[pl.ds(c, 1), :]
        diag = lax.rsqrt(2.0 * (radius * radius))
        back = jnp.zeros((8, LANES), F32)
        step = 64
        for r in range(0, panels, step):
            span = slice(r, r + step)
            base = r % half
            eye = lax.broadcasted_iota(jnp.int32, (step, half), 0) + base == lax.broadcasted_iota(
                jnp.int32, (step, half), 1
            )
            if r < half:
                g0 = jnp.where(eye, diag[:, :half], inverse_root(dist[span, :half]))
                g1 = inverse_root(dist[span, half:])
                qcol = column(qt[span, :], c)
                back = back + fold(g1 * qcol)
                part = g0 * qrow[:, :half] + g1 * qrow[:, half:]
            else:
                part = jnp.where(eye, diag[:, half:], inverse_root(dist[span, half:])) * qrow[:, half:]
            put_column(acct, span, i, jnp.sum(part, axis=1, keepdims=True))
        back = jnp.sum(back, axis=0, keepdims=True)
        acc[pl.ds(c, 1), :] += jnp.concatenate([jnp.zeros_like(back), back], axis=1)

    def self_step(i, carry):
        begin_self(2 * i + 1, dist1)
        finish_self(2 * i, dist0)
        begin_self(2 * i + 2, dist0)
        finish_self(2 * i + 1, dist1)
        return carry

    begin_self(0, dist0)
    lax.fori_loop(0, share // 2, self_step, 0)

    count = pairs.shape[1] // S
    start = sub * count

    def begin(i, dist):
        p = start + jnp.minimum(i, count - 1)
        distances(load_features(fa, pairs[0, p]), load_features(fb, pairs[1, p]), dist)

    def finish(i, dist):
        ia, ib = pairs[0, start + i], pairs[1, start + i]
        acc[pl.ds(ib, 1), :] += tile_sums(dist, q[pl.ds(ib, 1), :], qt, ia, acct, share + i)

    def pair_step(i, carry):
        begin(2 * i + 1, dist1)
        finish(2 * i, dist0)
        begin(2 * i + 2, dist0)
        finish(2 * i + 1, dist1)
        return carry

    begin(0, dist0)
    lax.fori_loop(0, count // 2, pair_step, 0)
    rows[...] = acct[...].T
    for i in range(share):
        acc[pl.ds(first + i, 1), :] += rows[i : i + 1, :]
    for i in range(count):
        acc[pl.ds(pairs[0, start + i], 1), :] += rows[share + i : share + i + 1, :]
    total = acc_in[...] + acc[...] * inv

    got[...] = jnp.zeros_like(got)
    for shift in range(1, C):
        dest = lax.rem(me + shift, C)
        for j in range(slots):
            got[pl.ds(targets[dest, j], 1), :] += sums[shift - 1][j : j + 1, :]

    par_dev, far_n, rank = coupling.shape[0], coupling.shape[1], coupling.shape[2]
    parents[pl.ds(pl.multiple_of(me * par_dev, 8), par_dev), :] = up[...]
    for shift in range(1, C):
        owner = lax.rem(me + shift, C)
        parents[pl.ds(pl.multiple_of(owner * par_dev, 8), par_dev), :] = sums[shift - 1][slots:, :rank]
    lane = lax.broadcasted_iota(jnp.int32, (rank, LANES), 1)
    field = jnp.zeros((rank, LANES), F32)
    for p in range(par_dev):
        part = jnp.zeros((rank, rank), F32)
        for k in range(far_n):
            part = part + coupling[p, k] * parents[pl.ds(far_list[p, k], 1), :]
        field = jnp.where(lane == p, jnp.sum(part, axis=1, keepdims=True), field)
    which = lax.broadcasted_iota(jnp.int32, (LANES, clusters), 0)
    onehot = (parent[...] == which).astype(F32)
    down = jnp.dot(field, onehot, precision=HIGHEST, preferred_element_type=F32)
    fields = jnp.concatenate(
        [jnp.sum(transfer[r] * down, axis=0, keepdims=True) for r in range(rank)], axis=0
    )

    def give(s):
        for shift in range(S):
            other = (s + shift) % S
            part = total[:, other * L : (other + 1) * L]
            parts[shift][:clusters, :] = part + got[...] if shift == 0 else part
            for t in range(clusters // L):
                at = clusters + t * rank
                parts[shift][at : at + rank, :] = fields[:, t * L : (t + 1) * L]

    for s in range(S):
        pl.when(sub == s)(functools.partial(give, s))


def up_kernel(basis, masked, transfer, parent, up):
    clusters = basis.shape[0]
    rank = basis.shape[1]
    lane = lax.broadcasted_iota(jnp.int32, (rank, clusters), 1)
    leaf = jnp.zeros((rank, clusters), F32)
    for c in range(clusters):
        part = jnp.sum(basis[c] * masked[c : c + 1, :], axis=1, keepdims=True)
        leaf = jnp.where(lane == c, part, leaf)
    lifted = jnp.zeros((rank, clusters), F32)
    for r in range(rank):
        lifted = lifted + transfer[r] * leaf[r : r + 1, :]
    which = lax.broadcasted_iota(jnp.int32, (up.shape[0], clusters), 0)
    onehot = (parent[...] == which).astype(F32)
    up[...] = lax.dot_general(
        onehot, lifted, (((1,), (1,)), ((), ())), precision=HIGHEST, preferred_element_type=F32
    )


def final_kernel(sizes, mask, basis, *rest):
    S, R, L = sizes
    near, out = rest[: S * R], rest[-1]
    clusters, rank = basis.shape[0], basis.shape[1]
    fields = []
    for t in range(clusters // L):
        rows = slice(clusters + t * rank, clusters + (t + 1) * rank)
        fields.append(sum(near[d * R][rows, :] for d in range(1, S)) + near[0][rows, :])
    fields = jnp.concatenate(fields, axis=1) if len(fields) > 1 else fields[0]
    for c in range(clusters):
        out[c : c + 1, :] = jnp.sum(basis[c] * fields[:, c : c + 1], axis=0, keepdims=True)
    total = out[...]
    for part in near:
        total = total + part[:clusters, :]
    out[...] = total * mask[...].astype(F32)


def send(value, moves):
    names = tuple(name for name, _ in moves)
    steps = [step for _, step in moves]
    sizes = [lax.axis_size(name) for name in names]
    perm = []

    def flat(coords):
        index = 0
        for size, c in zip(sizes, coords):
            index = index * size + c
        return index

    total = 1
    for size in sizes:
        total *= size
    for index in range(total):
        coords, left = [], index
        for size in reversed(sizes):
            coords.append(left % size)
            left //= size
        coords.reverse()
        perm.append((index, flat([(c + s) % n for c, s, n in zip(coords, steps, sizes)])))
    return lax.ppermute(value, names if len(names) > 1 else names[0], perm)


def on_device(
    charges,
    panel_mask,
    geometry,
    remote_source,
    remote_target,
    remote_live,
    local_pairs,
    basis,
    transfer,
    parent_of,
    far_list,
    coupling,
):
    clusters, L = charges.shape
    panels = geometry.shape[2]
    C, S, R = lax.axis_size("clu"), lax.axis_size("sub"), lax.axis_size("rep")
    slots = remote_source.shape[2]
    par_dev, rank = far_list.shape[0], transfer.shape[1]
    n = (C - 1) * slots
    shape = jax.ShapeDtypeStruct
    targets = remote_target[0]
    basis_t = jnp.transpose(basis, (0, 2, 1))
    transfer_t = jnp.transpose(transfer, (1, 2, 0))
    parent = parent_of[None, :]

    made = pl.pallas_call(
        functools.partial(pack_kernel, (C, S, L, slots)),
        out_shape=[shape((clusters, L), F32)] + [shape((5 * slots + 8, L), F32)] * (C - 1),
        in_specs=[vmem()] * 3 + [smem()] * 3,
        out_specs=[vmem()] * C,
        compiler_params=PARAMS,
        name="packs",
    )(charges, panel_mask, geometry, targets, remote_source[0], remote_live[0])
    masked, packs = made[0], made[1:]
    pieces = [masked] + [send(masked, (("sub", d),)) for d in range(1, S)]
    packs = [send(packs[d - 1], (("clu", d),)) for d in range(1, C)]
    codes = jnp.stack([p[5 * slots, :slots] for p in packs]).astype(jnp.int32)

    up = pl.pallas_call(
        up_kernel,
        out_shape=shape((par_dev, rank), F32),
        in_specs=[vmem()] * 4,
        out_specs=vmem(),
        compiler_params=PARAMS,
        name="far_up",
    )(basis_t, masked, transfer_t, parent)

    made = pl.pallas_call(
        functools.partial(remote_kernel, (C, S, L, slots, clusters, panels)),
        out_shape=[shape((clusters, panels), F32)] + [shape((slots + par_dev, L), F32)] * (C - 1),
        in_specs=[vmem(), smem()] + [vmem()] * (1 + S + C - 1),
        out_specs=[vmem()] * C,
        scratch_shapes=[
            pltpu.VMEM((clusters, panels), F32),
            pltpu.VMEM((L, whole(n)), F32),
            pltpu.VMEM((clusters, panels), F32),
            pltpu.VMEM((L, whole(n)), F32),
            pltpu.VMEM((4 * n, panels), F32),
            pltpu.VMEM((n * ROWS, L), F32),
            pltpu.VMEM((n * ROWS, LANES), F32),
            pltpu.VMEM((n * ROWS, LANES), F32),
            pltpu.VMEM((L, panels), F32),
            pltpu.VMEM((L, panels), F32),
            pltpu.SMEM((n + 1,), jnp.int32),
        ],
        compiler_params=PARAMS,
        name="near_remote",
    )(geometry, codes, up, *pieces, *packs)
    acc, sums = made[0], [send(made[d], (("clu", C - d),)) for d in range(1, C)]

    columns = whole(clusters // (S * R) + local_pairs.shape[1] // S)
    half = [pltpu.VMEM((clusters * ROWS, LANES), F32)] * 2
    parts = pl.pallas_call(
        functools.partial(local_kernel, (C, S, L, R, slots, clusters, panels)),
        out_shape=[shape((clusters + clusters // L * rank, L), F32)] * S,
        in_specs=[vmem()] + [smem()] * 3 + [vmem()] * (5 + S + C - 1),
        out_specs=[vmem()] * S,
        scratch_shapes=[
            pltpu.VMEM((clusters, panels), F32),
            pltpu.VMEM((panels, clusters), F32),
            pltpu.VMEM((clusters, panels), F32),
            pltpu.VMEM((panels, columns), F32),
            *half,
            *half,
            pltpu.VMEM((clusters, panels), F32),
            pltpu.VMEM((panels, panels), F32),
            pltpu.VMEM((panels, panels), F32),
            pltpu.VMEM((clusters, L), F32),
            pltpu.VMEM((C * par_dev, rank), F32),
            pltpu.VMEM((columns, panels), F32),
        ],
        compiler_params=PARAMS,
        name="near_local",
    )(geometry, local_pairs[0].T, targets, far_list, coupling, transfer_t, parent, up, acc, *pieces, *sums)
    near = []
    for d in range(S):
        for e in range(R):
            near.append(send(parts[d], (("sub", d), ("rep", e))) if d or e else parts[0])

    return pl.pallas_call(
        functools.partial(final_kernel, (S, R, L)),
        out_shape=shape((clusters, L), F32),
        in_specs=[vmem()] * (2 + S * R),
        out_specs=vmem(),
        compiler_params=PARAMS,
        name="combine",
    )(panel_mask, basis_t, *near)


def solution(mesh):
    placed = (
        P(("grp", "clu"), "sub"),
        P(("grp", "clu"), "sub"),
        P(("grp", "clu"), None, None),
        P(("grp", "clu"), None, "rep"),
        P(("grp", "clu"), None, "rep"),
        P(("grp", "clu"), None, "rep"),
        P(("grp", "clu"), "rep", None),
        P(("grp", "clu"), "sub", None),
        P(("grp", "clu"), None, None),
        P(("grp", "clu")),
        P(("grp", "clu"), None),
        P(("grp", "clu"), None, None, None),
    )
    return jax.shard_map(
        on_device, mesh=mesh, in_specs=placed, out_specs=P(("grp", "clu"), "sub"), check_vma=False
    )
```

```python
import functools

import jax
import jax.numpy as jnp
from jax import lax
from jax.experimental import pallas as pl
from jax.experimental.pallas import tpu as pltpu
from jax.sharding import PartitionSpec as P

F32 = jnp.float32
BF16 = jnp.bfloat16
HIGHEST = lax.Precision.HIGHEST
ROWS = 40
USED = 34
LANES = 128
PARAMS = pltpu.CompilerParams(vmem_limit_bytes=56 * 1024 * 1024)


def vmem():
    return pl.BlockSpec(memory_space=pltpu.VMEM)


def smem():
    return pl.BlockSpec(memory_space=pltpu.SMEM)


def whole(size):
    return -(-size // LANES) * LANES


def cut(v):
    return v.astype(BF16).astype(F32)


def powers(sign):
    lane = lax.broadcasted_iota(jnp.int32, (8, LANES), 1)
    out = jnp.full((8, LANES), 2.0 ** (-64 * sign), F32)
    for bit in range(7):
        out = out * jnp.where((lane >> bit) & 1 == 1, F32(2.0 ** (sign * 2**bit)), F32(1.0))
    return out


def frame(parts):
    low = [functools.reduce(jnp.minimum, [jnp.min(p[k]) for p in parts]) for k in range(3)]
    high = [functools.reduce(jnp.maximum, [jnp.max(p[k]) for p in parts]) for k in range(3)]
    width = functools.reduce(jnp.maximum, [jnp.max(jnp.abs(p[3])) for p in parts])
    for lo, hi in zip(low, high):
        width = jnp.maximum(width, 0.5 * (hi - lo))
    up, down = powers(1), powers(-1)
    size = jnp.min(jnp.where(up >= width, up, F32(2.0**63)))
    inv = jnp.max(jnp.where(up >= width, down, F32(2.0**-63)))
    magic = size * F32(1.5 * 2.0**20)
    centre = [(0.5 * (lo + hi) + magic) - magic for lo, hi in zip(low, high)]
    return centre, inv


def split_features(points, centre, inv):
    magic = F32(1.5 * 2.0**16)
    grid, rest = [], []
    for k in range(3):
        u = (points[k] - centre[k]) * inv
        h = (u + magic) - magic
        grid.append(h)
        rest.append(u - h)
    rad = points[3] * inv
    norm = grid[0] * grid[0] + grid[1] * grid[1] + grid[2] * grid[2]
    norm1 = cut(norm)
    norm2 = norm - norm1
    cross = grid[0] * rest[0] + grid[1] * rest[1] + grid[2] * rest[2]
    extra = 2.0 * cross + (rest[0] * rest[0] + rest[1] * rest[1] + rest[2] * rest[2]) + rad * rad
    extra1 = cut(extra)
    extra2 = cut(extra - extra1)
    extra3 = (extra - extra1) - extra2
    rest1 = [cut(v) for v in rest]
    rest2 = [v - w for v, w in zip(rest, rest1)]
    neg = lambda vs: [-2.0 * v for v in vs]
    one = jnp.ones_like(rad)
    left = grid + [norm1, norm2, one, one]
    right = neg(grid) + [one, one, norm1, norm2]
    left += [extra1, extra2, extra3, one, one, one]
    right += [one, one, one, extra1, extra2, extra3]
    left += grid + grid + rest1 + rest2 + rest1 + rest1 + rest2
    right += neg(rest1) + neg(rest2) + neg(grid) + neg(grid) + neg(rest1) + neg(rest2) + neg(rest1)
    return left, right, rad


def store_features(ref, rows):
    count = rows[0].shape[0]
    width = rows[0].shape[1]
    for k, row in enumerate(rows):
        for t, piece in enumerate(ref):
            piece[pl.ds(k, count, stride=ROWS), :] = row[:, t * LANES : min(width, (t + 1) * LANES)]


def load_features(ref, index):
    start = pl.multiple_of(index * ROWS, 8)
    return [piece[pl.ds(start, USED), :].astype(BF16) for piece in ref]


def contract(left, right):
    return lax.dot_general(left, right, (((0,), (0,)), ((), ())), preferred_element_type=F32)


def column(table, index):
    if table.shape[1] == LANES and table.shape[0] % 8 == 0:
        return jnp.take_along_axis(table, jnp.full(table.shape, index, jnp.int32), axis=1)
    lane = lax.broadcasted_iota(jnp.int32, table.shape, 1)
    picked = jnp.sum(jnp.where(lane == index, table, 0.0), axis=1, keepdims=True)
    return jnp.broadcast_to(picked, (table.shape[0], LANES))


def put_column(table, rows, index, value):
    shape = (rows.stop - rows.start, table.shape[1])
    lane = lax.broadcasted_iota(jnp.int32, shape, 1)
    pltpu.store(table.at[rows, :], jnp.broadcast_to(value, shape), mask=lane == index)


def inverse_root(d):
    return lax.exp2(-0.5 * lax.log2(d))


def fold(v):
    return jnp.sum(v.reshape(v.shape[0] // 8, 8, v.shape[1]), axis=0)


def distances(left, right, out):
    whole_left = jnp.concatenate(left, axis=1) if len(left) > 1 else left[0]
    for t, r in enumerate(right):
        out[:, t * LANES : (t + 1) * LANES] = contract(whole_left, r)


def tile_sums(dist, qrow, qtable, slot, table_ref, index, step=64):
    height = dist.shape[0]
    step = min(step, height)
    q0, q1 = qrow[:, :LANES], qrow[:, LANES:]
    back0 = back1 = jnp.zeros((8, LANES), F32)
    for r in range(0, height, step):
        rows = slice(r, r + step)
        g0 = inverse_root(dist[rows, :LANES])
        g1 = inverse_root(dist[rows, LANES:])
        qcol = column(qtable[rows, :], slot)
        put_column(table_ref, rows, index, jnp.sum(g0 * q0 + g1 * q1, axis=1, keepdims=True))
        back0 = back0 + fold(g0 * qcol)
        back1 = back1 + fold(g1 * qcol)
    return jnp.concatenate(
        [jnp.sum(back0, axis=0, keepdims=True), jnp.sum(back1, axis=0, keepdims=True)], axis=1
    )


def pipeline(total, begin, finish, ring):
    size = len(ring)
    ahead = min(2, size - 1)

    def body(i, carry):
        for k in range(size):
            begin(i * size + k + ahead, ring[(k + ahead) % size])
            finish(i * size + k, ring[k])
        return carry

    for k in range(ahead):
        begin(k, ring[k])
    lax.fori_loop(0, (total + size - 1) // size, body, 0)


def ring_size(total):
    return next(size for size in (8, 4, 2, 1) if total % size == 0)


def assemble(sub, S, L, q, pieces):
    def place(s):
        for shift in range(S):
            owner = (s - shift) % S
            q[:, owner * L : (owner + 1) * L] = pieces[shift][...]

    for s in range(S):
        pl.when(sub == s)(functools.partial(place, s))


def pack_kernel(sizes, charges, mask, geo, targets, sources, live, masked, *packs):
    C, S, L, slots = sizes
    me, sub = lax.axis_index("clu"), lax.axis_index("sub")
    masked[...] = charges[...] * mask[...].astype(F32)
    lane = lax.broadcasted_iota(jnp.int32, (8, L), 1)
    for shift in range(1, C):
        dest = lax.rem(me + shift, C)
        codes = jnp.full((8, L), -1.0, F32)
        for j in range(slots):
            code = jnp.where(live[dest, j] > 0, sources[dest, j], -1)
            codes = jnp.where(lane == j, code.astype(F32), codes)
        packs[shift - 1][5 * slots :, :] = codes

    def fill(s):
        for shift in range(1, C):
            dest = lax.rem(me + shift, C)
            pack = packs[shift - 1]
            for j in range(slots):
                t = targets[dest, j]
                g = geo[t, :, s * L : (s + 1) * L]
                for k in range(4):
                    pack[k * slots + j : k * slots + j + 1, :] = g[k : k + 1]
                pack[4 * slots + j : 4 * slots + j + 1, :] = masked[pl.ds(t, 1), :]

    for s in range(S):
        pl.when(sub == s)(functools.partial(fill, s))


def remote_kernel(sizes, geo, codes, up, *rest):
    C, S, L, slots, clusters, panels = sizes
    pieces = rest[:S]
    packs = rest[S : S + C - 1]
    acc_out = rest[S + C - 1]
    sends = rest[S + C : S + C + C - 1]
    q, tqt, acc, fwdt, sgeo, fa0, fb0, fb1, order, *ring = rest[S + C + C - 1 :]
    fa, fb = (fa0,), (fb0, fb1)
    n = (C - 1) * slots
    assemble(lax.axis_index("sub"), S, L, q, pieces)
    acc[...] = jnp.zeros_like(acc)
    fwdt[...] = jnp.zeros_like(fwdt)
    found = jnp.int32(0)
    for shift in range(C - 1):
        for j in range(slots):
            code = codes[shift, j]
            order[found] = shift * slots + j
            found = found + (code >= 0).astype(jnp.int32)
            g = geo[jnp.maximum(code, 0)]
            for k in range(4):
                row = k * n + shift * slots + j
                sgeo[row : row + 1, :] = g[k : k + 1]
    tpoints = [
        jnp.concatenate([p[k * slots : (k + 1) * slots, :] for p in packs], axis=0) for k in range(5)
    ]
    spoints = [sgeo[k * n : (k + 1) * n, :] for k in range(4)]
    centre, inv = frame([tpoints, spoints])
    left, _, _ = split_features(tpoints, centre, inv)
    _, right, _ = split_features(spoints, centre, inv)
    store_features(fa, left)
    store_features(fb, right)
    wide = tqt.shape[1]
    tq = tpoints[4]
    if wide > n:
        tq = jnp.concatenate([tq, jnp.zeros((wide - n, L), F32)], axis=0)
    tqt[...] = tq.T

    def begin(i, dist):
        slot = order[jnp.minimum(i, jnp.maximum(found - 1, 0))]
        distances(load_features(fa, slot), load_features(fb, slot), dist)

    def finish(i, dist):
        ok = i < found
        slot = order[jnp.minimum(i, jnp.maximum(found - 1, 0))]
        source = jnp.maximum(codes[slot // slots, lax.rem(slot, slots)], 0)
        back = tile_sums(
            dist, q[pl.ds(source, 1), :], tqt, slot, fwdt, jnp.where(ok, slot, -1)
        )
        acc[pl.ds(source, 1), :] += jnp.where(ok, back, 0.0)

    pipeline(found, begin, finish, ring)
    acc_out[...] = acc[...] * inv
    fwd = (fwdt[...] * inv).T
    rank = up.shape[1]
    for shift in range(C - 1):
        sends[shift][:slots, :] = fwd[shift * slots : (shift + 1) * slots, :]
        sends[shift][slots:, :] = jnp.zeros((up.shape[0], L), F32)
        sends[shift][slots:, :rank] = up[...]


def local_kernel(
    sizes, geo, pairs, targets, far_list, coupling, transfer, parent, up, acc_in, *rest
):
    C, S, L, R, slots, clusters, panels = sizes
    pieces = rest[:S]
    sums = rest[S : S + C - 1]
    parts = rest[S + C - 1 : 2 * S + C - 1]
    q, qt, acc, acct, fa0, fa1, fb0, fb1, rads, got, parents, rows, *ring = rest[2 * S + C - 1 :]
    fa, fb = (fa0, fa1), (fb0, fb1)
    me, sub, rep = lax.axis_index("clu"), lax.axis_index("sub"), lax.axis_index("rep")
    assemble(sub, S, L, q, pieces)
    qt[...] = q[...].T
    acc[...] = jnp.zeros_like(acc)
    acct[...] = jnp.zeros_like(acct)
    points = [geo[:, k, :] for k in range(4)]
    centre, inv = frame([points])
    left, right, rad = split_features(points, centre, inv)
    store_features(fa, left)
    store_features(fb, right)
    rads[...] = rad

    half = panels // 2
    share = clusters // (S * R)
    first = (rep * S + sub) * share

    def begin_self(i, dist):
        c = first + jnp.minimum(i, share - 1)
        a = load_features(fa, c)
        b = load_features(fb, c)
        dist[:half, :half] = contract(a[0], b[0])
        dist[:half, half:] = contract(a[0], b[1])
        dist[half:, half:] = contract(a[1], b[1])

    def finish_self(i, dist):
        c = first + i
        qrow = q[pl.ds(c, 1), :]
        radius = rads[pl.ds(c, 1), :]
        diag = lax.rsqrt(2.0 * (radius * radius))
        back = jnp.zeros((8, LANES), F32)
        step = 64
        for r in range(0, panels, step):
            span = slice(r, r + step)
            base = r % half
            eye = lax.broadcasted_iota(jnp.int32, (step, half), 0) + base == lax.broadcasted_iota(
                jnp.int32, (step, half), 1
            )
            if r < half:
                g0 = jnp.where(eye, diag[:, :half], inverse_root(dist[span, :half]))
                g1 = inverse_root(dist[span, half:])
                qcol = column(qt[span, :], c)
                back = back + fold(g1 * qcol)
                part = g0 * qrow[:, :half] + g1 * qrow[:, half:]
            else:
                part = jnp.where(eye, diag[:, half:], inverse_root(dist[span, half:])) * qrow[:, half:]
            put_column(acct, span, i, jnp.sum(part, axis=1, keepdims=True))
        back = jnp.sum(back, axis=0, keepdims=True)
        acc[pl.ds(c, 1), :] += jnp.concatenate([jnp.zeros_like(back), back], axis=1)

    pipeline(share, begin_self, finish_self, ring[: ring_size(share)])

    count = pairs.shape[1] // S
    start = sub * count

    def begin(i, dist):
        p = start + jnp.minimum(i, count - 1)
        distances(load_features(fa, pairs[0, p]), load_features(fb, pairs[1, p]), dist)

    def finish(i, dist):
        ia, ib = pairs[0, start + i], pairs[1, start + i]
        acc[pl.ds(ib, 1), :] += tile_sums(dist, q[pl.ds(ib, 1), :], qt, ia, acct, share + i)

    pipeline(count, begin, finish, ring[: ring_size(count)])
    rows[...] = acct[...].T
    for i in range(share):
        acc[pl.ds(first + i, 1), :] += rows[i : i + 1, :]
    for i in range(count):
        acc[pl.ds(pairs[0, start + i], 1), :] += rows[share + i : share + i + 1, :]
    total = acc_in[...] + acc[...] * inv

    got[...] = jnp.zeros_like(got)
    for shift in range(1, C):
        dest = lax.rem(me + shift, C)
        for j in range(slots):
            got[pl.ds(targets[dest, j], 1), :] += sums[shift - 1][j : j + 1, :]

    par_dev, far_n, rank = coupling.shape[0], coupling.shape[1], coupling.shape[2]
    parents[pl.ds(pl.multiple_of(me * par_dev, 8), par_dev), :] = up[...]
    for shift in range(1, C):
        owner = lax.rem(me + shift, C)
        parents[pl.ds(pl.multiple_of(owner * par_dev, 8), par_dev), :] = sums[shift - 1][slots:, :rank]
    lane = lax.broadcasted_iota(jnp.int32, (rank, LANES), 1)
    field = jnp.zeros((rank, LANES), F32)
    for p in range(par_dev):
        part = jnp.zeros((rank, rank), F32)
        for k in range(far_n):
            part = part + coupling[p, k] * parents[pl.ds(far_list[p, k], 1), :]
        field = jnp.where(lane == p, jnp.sum(part, axis=1, keepdims=True), field)
    which = lax.broadcasted_iota(jnp.int32, (LANES, clusters), 0)
    onehot = (parent[...] == which).astype(F32)
    down = jnp.dot(field, onehot, precision=HIGHEST, preferred_element_type=F32)
    fields = jnp.concatenate(
        [jnp.sum(transfer[r] * down, axis=0, keepdims=True) for r in range(rank)], axis=0
    )

    def give(s):
        for shift in range(S):
            other = (s + shift) % S
            part = total[:, other * L : (other + 1) * L]
            parts[shift][:clusters, :] = part + got[...] if shift == 0 else part
            for t in range(clusters // L):
                at = clusters + t * rank
                parts[shift][at : at + rank, :] = fields[:, t * L : (t + 1) * L]

    for s in range(S):
        pl.when(sub == s)(functools.partial(give, s))


def up_kernel(basis, masked, transfer, parent, up):
    clusters = basis.shape[0]
    rank = basis.shape[1]
    lane = lax.broadcasted_iota(jnp.int32, (rank, clusters), 1)
    leaf = jnp.zeros((rank, clusters), F32)
    for c in range(clusters):
        part = jnp.sum(basis[c] * masked[c : c + 1, :], axis=1, keepdims=True)
        leaf = jnp.where(lane == c, part, leaf)
    lifted = jnp.zeros((rank, clusters), F32)
    for r in range(rank):
        lifted = lifted + transfer[r] * leaf[r : r + 1, :]
    which = lax.broadcasted_iota(jnp.int32, (up.shape[0], clusters), 0)
    onehot = (parent[...] == which).astype(F32)
    up[...] = lax.dot_general(
        onehot, lifted, (((1,), (1,)), ((), ())), precision=HIGHEST, preferred_element_type=F32
    )


def final_kernel(sizes, mask, basis, *rest):
    S, R, L = sizes
    near, out = rest[: S * R], rest[-1]
    clusters, rank = basis.shape[0], basis.shape[1]
    fields = []
    for t in range(clusters // L):
        rows = slice(clusters + t * rank, clusters + (t + 1) * rank)
        fields.append(sum(near[d * R][rows, :] for d in range(1, S)) + near[0][rows, :])
    fields = jnp.concatenate(fields, axis=1) if len(fields) > 1 else fields[0]
    for c in range(clusters):
        out[c : c + 1, :] = jnp.sum(basis[c] * fields[:, c : c + 1], axis=0, keepdims=True)
    total = out[...]
    for part in near:
        total = total + part[:clusters, :]
    out[...] = total * mask[...].astype(F32)


def send(value, moves):
    names = tuple(name for name, _ in moves)
    steps = [step for _, step in moves]
    sizes = [lax.axis_size(name) for name in names]
    perm = []

    def flat(coords):
        index = 0
        for size, c in zip(sizes, coords):
            index = index * size + c
        return index

    total = 1
    for size in sizes:
        total *= size
    for index in range(total):
        coords, left = [], index
        for size in reversed(sizes):
            coords.append(left % size)
            left //= size
        coords.reverse()
        perm.append((index, flat([(c + s) % n for c, s, n in zip(coords, steps, sizes)])))
    return lax.ppermute(value, names if len(names) > 1 else names[0], perm)


def on_device(
    charges,
    panel_mask,
    geometry,
    remote_source,
    remote_target,
    remote_live,
    local_pairs,
    basis,
    transfer,
    parent_of,
    far_list,
    coupling,
):
    clusters, L = charges.shape
    panels = geometry.shape[2]
    C, S, R = lax.axis_size("clu"), lax.axis_size("sub"), lax.axis_size("rep")
    slots = remote_source.shape[2]
    par_dev, rank = far_list.shape[0], transfer.shape[1]
    n = (C - 1) * slots
    shape = jax.ShapeDtypeStruct
    targets = remote_target[0]
    basis_t = jnp.transpose(basis, (0, 2, 1))
    transfer_t = jnp.transpose(transfer, (1, 2, 0))
    parent = parent_of[None, :]

    made = pl.pallas_call(
        functools.partial(pack_kernel, (C, S, L, slots)),
        out_shape=[shape((clusters, L), F32)] + [shape((5 * slots + 8, L), F32)] * (C - 1),
        in_specs=[vmem()] * 3 + [smem()] * 3,
        out_specs=[vmem()] * C,
        compiler_params=PARAMS,
        name="packs",
    )(charges, panel_mask, geometry, targets, remote_source[0], remote_live[0])
    masked, packs = made[0], made[1:]
    pieces = [masked] + [send(masked, (("sub", d),)) for d in range(1, S)]
    packs = [send(packs[d - 1], (("clu", d),)) for d in range(1, C)]
    codes = jnp.stack([p[5 * slots, :slots] for p in packs]).astype(jnp.int32)

    up = pl.pallas_call(
        up_kernel,
        out_shape=shape((par_dev, rank), F32),
        in_specs=[vmem()] * 4,
        out_specs=vmem(),
        compiler_params=PARAMS,
        name="far_up",
    )(basis_t, masked, transfer_t, parent)

    made = pl.pallas_call(
        functools.partial(remote_kernel, (C, S, L, slots, clusters, panels)),
        out_shape=[shape((clusters, panels), F32)] + [shape((slots + par_dev, L), F32)] * (C - 1),
        in_specs=[vmem(), smem()] + [vmem()] * (1 + S + C - 1),
        out_specs=[vmem()] * C,
        scratch_shapes=[
            pltpu.VMEM((clusters, panels), F32),
            pltpu.VMEM((L, whole(n)), F32),
            pltpu.VMEM((clusters, panels), F32),
            pltpu.VMEM((L, whole(n)), F32),
            pltpu.VMEM((4 * n, panels), F32),
            pltpu.VMEM((n * ROWS, L), F32),
            pltpu.VMEM((n * ROWS, LANES), F32),
            pltpu.VMEM((n * ROWS, LANES), F32),
            pltpu.SMEM((n + 1,), jnp.int32),
        ]
        + [pltpu.VMEM((L, panels), F32)] * 4,
        compiler_params=PARAMS,
        name="near_remote",
    )(geometry, codes, up, *pieces, *packs)
    acc, sums = made[0], [send(made[d], (("clu", C - d),)) for d in range(1, C)]

    columns = whole(clusters // (S * R) + local_pairs.shape[1] // S)
    half = [pltpu.VMEM((clusters * ROWS, LANES), F32)] * 2
    parts = pl.pallas_call(
        functools.partial(local_kernel, (C, S, L, R, slots, clusters, panels)),
        out_shape=[shape((clusters + clusters // L * rank, L), F32)] * S,
        in_specs=[vmem()] + [smem()] * 3 + [vmem()] * (5 + S + C - 1),
        out_specs=[vmem()] * S,
        scratch_shapes=[
            pltpu.VMEM((clusters, panels), F32),
            pltpu.VMEM((panels, clusters), F32),
            pltpu.VMEM((clusters, panels), F32),
            pltpu.VMEM((panels, columns), F32),
            *half,
            *half,
            pltpu.VMEM((clusters, panels), F32),
            pltpu.VMEM((clusters, L), F32),
            pltpu.VMEM((C * par_dev, rank), F32),
            pltpu.VMEM((columns, panels), F32),
        ]
        + [pltpu.VMEM((panels, panels), F32)] * 8,
        compiler_params=PARAMS,
        name="near_local",
    )(geometry, local_pairs[0].T, targets, far_list, coupling, transfer_t, parent, up, acc, *pieces, *sums)
    near = []
    for d in range(S):
        for e in range(R):
            near.append(send(parts[d], (("sub", d), ("rep", e))) if d or e else parts[0])

    return pl.pallas_call(
        functools.partial(final_kernel, (S, R, L)),
        out_shape=shape((clusters, L), F32),
        in_specs=[vmem()] * (2 + S * R),
        out_specs=vmem(),
        compiler_params=PARAMS,
        name="combine",
    )(panel_mask, basis_t, *near)


def solution(mesh):
    placed = (
        P(("grp", "clu"), "sub"),
        P(("grp", "clu"), "sub"),
        P(("grp", "clu"), None, None),
        P(("grp", "clu"), None, "rep"),
        P(("grp", "clu"), None, "rep"),
        P(("grp", "clu"), None, "rep"),
        P(("grp", "clu"), "rep", None),
        P(("grp", "clu"), "sub", None),
        P(("grp", "clu"), None, None),
        P(("grp", "clu")),
        P(("grp", "clu"), None),
        P(("grp", "clu"), None, None, None),
    )
    return jax.shard_map(
        on_device, mesh=mesh, in_specs=placed, out_specs=P(("grp", "clu"), "sub"), check_vma=False
    )
```

```python
import functools

import jax
import jax.numpy as jnp
from jax import lax
from jax.experimental import pallas as pl
from jax.experimental.pallas import tpu as pltpu
from jax.sharding import PartitionSpec as P

F32 = jnp.float32
BF16 = jnp.bfloat16
HIGHEST = lax.Precision.HIGHEST
ROWS = 40
USED = 34
LANES = 128
PARAMS = pltpu.CompilerParams(vmem_limit_bytes=56 * 1024 * 1024)


def vmem():
    return pl.BlockSpec(memory_space=pltpu.VMEM)


def smem():
    return pl.BlockSpec(memory_space=pltpu.SMEM)


def whole(size):
    return -(-size // LANES) * LANES


def cut(v):
    return v.astype(BF16).astype(F32)


def powers(sign):
    lane = lax.broadcasted_iota(jnp.int32, (8, LANES), 1)
    out = jnp.full((8, LANES), 2.0 ** (-64 * sign), F32)
    for bit in range(7):
        out = out * jnp.where((lane >> bit) & 1 == 1, F32(2.0 ** (sign * 2**bit)), F32(1.0))
    return out


def frame(parts):
    low = [functools.reduce(jnp.minimum, [jnp.min(p[k]) for p in parts]) for k in range(3)]
    high = [functools.reduce(jnp.maximum, [jnp.max(p[k]) for p in parts]) for k in range(3)]
    width = functools.reduce(jnp.maximum, [jnp.max(jnp.abs(p[3])) for p in parts])
    for lo, hi in zip(low, high):
        width = jnp.maximum(width, 0.5 * (hi - lo))
    up, down = powers(1), powers(-1)
    size = jnp.min(jnp.where(up >= width, up, F32(2.0**63)))
    inv = jnp.max(jnp.where(up >= width, down, F32(2.0**-63)))
    magic = size * F32(1.5 * 2.0**20)
    centre = [(0.5 * (lo + hi) + magic) - magic for lo, hi in zip(low, high)]
    return centre, inv


def split_features(points, centre, inv):
    magic = F32(1.5 * 2.0**16)
    grid, rest = [], []
    for k in range(3):
        u = (points[k] - centre[k]) * inv
        h = (u + magic) - magic
        grid.append(h)
        rest.append(u - h)
    rad = points[3] * inv
    norm = grid[0] * grid[0] + grid[1] * grid[1] + grid[2] * grid[2]
    norm1 = cut(norm)
    norm2 = norm - norm1
    cross = grid[0] * rest[0] + grid[1] * rest[1] + grid[2] * rest[2]
    extra = 2.0 * cross + (rest[0] * rest[0] + rest[1] * rest[1] + rest[2] * rest[2]) + rad * rad
    extra1 = cut(extra)
    extra2 = cut(extra - extra1)
    extra3 = (extra - extra1) - extra2
    rest1 = [cut(v) for v in rest]
    rest2 = [v - w for v, w in zip(rest, rest1)]
    neg = lambda vs: [-2.0 * v for v in vs]
    one = jnp.ones_like(rad)
    left = grid + [norm1, norm2, one, one]
    right = neg(grid) + [one, one, norm1, norm2]
    left += [extra1, extra2, extra3, one, one, one]
    right += [one, one, one, extra1, extra2, extra3]
    left += grid + grid + rest1 + rest2 + rest1 + rest1 + rest2
    right += neg(rest1) + neg(rest2) + neg(grid) + neg(grid) + neg(rest1) + neg(rest2) + neg(rest1)
    return left, right, rad


def store_features(ref, rows):
    count = rows[0].shape[0]
    width = rows[0].shape[1]
    for k, row in enumerate(rows):
        for t, piece in enumerate(ref):
            piece[pl.ds(k, count, stride=ROWS), :] = row[:, t * LANES : min(width, (t + 1) * LANES)]


def load_features(ref, index):
    start = pl.multiple_of(index * ROWS, 8)
    return [piece[pl.ds(start, USED), :].astype(BF16) for piece in ref]


def contract(left, right):
    return lax.dot_general(left, right, (((0,), (0,)), ((), ())), preferred_element_type=F32)


def column(table, index):
    if table.shape[1] == LANES and table.shape[0] % 8 == 0:
        return jnp.take_along_axis(table, jnp.full(table.shape, index, jnp.int32), axis=1)
    lane = lax.broadcasted_iota(jnp.int32, table.shape, 1)
    picked = jnp.sum(jnp.where(lane == index, table, 0.0), axis=1, keepdims=True)
    return jnp.broadcast_to(picked, (table.shape[0], LANES))


def put_column(table, rows, index, value):
    shape = (rows.stop - rows.start, table.shape[1])
    lane = lax.broadcasted_iota(jnp.int32, shape, 1)
    pltpu.store(table.at[rows, :], jnp.broadcast_to(value, shape), mask=lane == index)


def inverse_root(d):
    return lax.rsqrt(d)


def fold(v):
    return jnp.sum(v.reshape(v.shape[0] // 8, 8, v.shape[1]), axis=0)


def distances(left, right, out):
    whole_left = jnp.concatenate(left, axis=1) if len(left) > 1 else left[0]
    for t, r in enumerate(right):
        out[:, t * LANES : (t + 1) * LANES] = contract(whole_left, r)


def staged(spans, *stages):
    held = {}
    for t in range(len(spans) + len(stages) - 1):
        for depth in reversed(range(len(stages))):
            k = t - depth
            if 0 <= k < len(spans):
                held[k] = stages[depth](spans[k], held.get(k))
                if depth == len(stages) - 1:
                    del held[k]


def spans_of(height, step=16):
    step = min(step, height)
    return [slice(r, r + step) for r in range(0, height, step)]


def tile_sums(dist, qrow, qtable, slot, table, index):
    q0, q1 = qrow[:, :LANES], qrow[:, LANES:]
    back = [jnp.zeros((8, LANES), F32), jnp.zeros((8, LANES), F32)]

    def root(rows, _):
        return (
            inverse_root(dist[rows, :LANES]),
            inverse_root(dist[rows, LANES:]),
            column(qtable[rows, :], slot),
        )

    def sums(rows, held):
        g0, g1, qcol = held
        back[0] = back[0] + fold(g0 * qcol)
        back[1] = back[1] + fold(g1 * qcol)
        return jnp.sum(g0 * q0 + g1 * q1, axis=1, keepdims=True)

    def store(rows, held):
        put_column(table, rows, index, held)

    staged(spans_of(dist.shape[0]), root, sums, store)
    return jnp.concatenate([jnp.sum(b, axis=0, keepdims=True) for b in back], axis=1)


def pipeline(total, begin, finish, ring):
    size = len(ring)
    ahead = min(2, size - 1)

    def body(i, carry):
        for k in range(size):
            begin(i * size + k + ahead, ring[(k + ahead) % size])
            finish(i * size + k, ring[k])
        return carry

    for k in range(ahead):
        begin(k, ring[k])
    lax.fori_loop(0, (total + size - 1) // size, body, 0)


def ring_size(total):
    return next(size for size in (8, 4, 2, 1) if total % size == 0)


def assemble(sub, S, L, q, pieces):
    def place(s):
        for shift in range(S):
            owner = (s - shift) % S
            q[:, owner * L : (owner + 1) * L] = pieces[shift][...]

    for s in range(S):
        pl.when(sub == s)(functools.partial(place, s))


def pack_kernel(sizes, charges, mask, geo, targets, sources, live, masked, *packs):
    C, S, L, slots = sizes
    me, sub = lax.axis_index("clu"), lax.axis_index("sub")
    masked[...] = charges[...] * mask[...].astype(F32)
    lane = lax.broadcasted_iota(jnp.int32, (8, L), 1)
    for shift in range(1, C):
        dest = lax.rem(me + shift, C)
        codes = jnp.full((8, L), -1.0, F32)
        for j in range(slots):
            code = jnp.where(live[dest, j] > 0, sources[dest, j], -1)
            codes = jnp.where(lane == j, code.astype(F32), codes)
        packs[shift - 1][5 * slots :, :] = codes

    def fill(s):
        for shift in range(1, C):
            dest = lax.rem(me + shift, C)
            pack = packs[shift - 1]
            for j in range(slots):
                t = targets[dest, j]
                g = geo[t, :, s * L : (s + 1) * L]
                for k in range(4):
                    pack[k * slots + j : k * slots + j + 1, :] = g[k : k + 1]
                pack[4 * slots + j : 4 * slots + j + 1, :] = masked[pl.ds(t, 1), :]

    for s in range(S):
        pl.when(sub == s)(functools.partial(fill, s))


def remote_kernel(sizes, geo, codes, up, *rest):
    C, S, L, slots, clusters, panels = sizes
    pieces = rest[:S]
    packs = rest[S : S + C - 1]
    acc_out = rest[S + C - 1]
    sends = rest[S + C : S + C + C - 1]
    q, tqt, acc, fwdt, sgeo, fa0, fb0, fb1, order, *ring = rest[S + C + C - 1 :]
    fa, fb = (fa0,), (fb0, fb1)
    n = (C - 1) * slots
    assemble(lax.axis_index("sub"), S, L, q, pieces)
    acc[...] = jnp.zeros_like(acc)
    fwdt[...] = jnp.zeros_like(fwdt)
    found = jnp.int32(0)
    for shift in range(C - 1):
        for j in range(slots):
            code = codes[shift, j]
            order[found] = shift * slots + j
            found = found + (code >= 0).astype(jnp.int32)
            g = geo[jnp.maximum(code, 0)]
            for k in range(4):
                row = k * n + shift * slots + j
                sgeo[row : row + 1, :] = g[k : k + 1]
    tpoints = [
        jnp.concatenate([p[k * slots : (k + 1) * slots, :] for p in packs], axis=0) for k in range(5)
    ]
    spoints = [sgeo[k * n : (k + 1) * n, :] for k in range(4)]
    centre, inv = frame([tpoints, spoints])
    left, _, _ = split_features(tpoints, centre, inv)
    _, right, _ = split_features(spoints, centre, inv)
    store_features(fa, left)
    store_features(fb, right)
    wide = tqt.shape[1]
    tq = tpoints[4]
    if wide > n:
        tq = jnp.concatenate([tq, jnp.zeros((wide - n, L), F32)], axis=0)
    tqt[...] = tq.T

    def begin(i, dist):
        slot = order[jnp.minimum(i, jnp.maximum(found - 1, 0))]
        distances(load_features(fa, slot), load_features(fb, slot), dist)

    def finish(i, dist):
        ok = i < found
        slot = order[jnp.minimum(i, jnp.maximum(found - 1, 0))]
        source = jnp.maximum(codes[slot // slots, lax.rem(slot, slots)], 0)
        back = tile_sums(
            dist, q[pl.ds(source, 1), :], tqt, slot, fwdt, jnp.where(ok, slot, -1)
        )
        acc[pl.ds(source, 1), :] += jnp.where(ok, back, 0.0)

    pipeline(found, begin, finish, ring)
    acc_out[...] = acc[...] * inv
    fwd = (fwdt[...] * inv).T
    rank = up.shape[1]
    for shift in range(C - 1):
        sends[shift][:slots, :] = fwd[shift * slots : (shift + 1) * slots, :]
        sends[shift][slots:, :] = jnp.zeros((up.shape[0], L), F32)
        sends[shift][slots:, :rank] = up[...]


def local_kernel(
    sizes, geo, pairs, targets, far_list, coupling, transfer, parent, up, acc_in, *rest
):
    C, S, L, R, slots, clusters, panels = sizes
    pieces = rest[:S]
    sums = rest[S : S + C - 1]
    parts = rest[S + C - 1 : 2 * S + C - 1]
    q, qt, acc, acct, fa0, fa1, fb0, fb1, rads, got, parents, rows, *ring = rest[2 * S + C - 1 :]
    fa, fb = (fa0, fa1), (fb0, fb1)
    me, sub, rep = lax.axis_index("clu"), lax.axis_index("sub"), lax.axis_index("rep")
    assemble(sub, S, L, q, pieces)
    qt[...] = q[...].T
    acc[...] = jnp.zeros_like(acc)
    acct[...] = jnp.zeros_like(acct)
    points = [geo[:, k, :] for k in range(4)]
    centre, inv = frame([points])
    left, right, rad = split_features(points, centre, inv)
    store_features(fa, left)
    store_features(fb, right)
    rads[...] = rad

    half = panels // 2
    share = clusters // (S * R)
    first = (rep * S + sub) * share

    def begin_self(i, dist):
        c = first + jnp.minimum(i, share - 1)
        a = load_features(fa, c)
        b = load_features(fb, c)
        dist[:half, :half] = contract(a[0], b[0])
        dist[:half, half:] = contract(a[0], b[1])
        dist[half:, half:] = contract(a[1], b[1])

    def finish_self(i, dist):
        c = first + i
        qrow = q[pl.ds(c, 1), :]
        radius = rads[pl.ds(c, 1), :]
        diag = lax.rsqrt(2.0 * (radius * radius))
        back = [jnp.zeros((8, LANES), F32)]

        def eye(span):
            shape = (span.stop - span.start, half)
            row = lax.broadcasted_iota(jnp.int32, shape, 0) + span.start % half
            return row == lax.broadcasted_iota(jnp.int32, shape, 1)

        def root(span, _):
            if span.start < half:
                return (
                    jnp.where(eye(span), diag[:, :half], inverse_root(dist[span, :half])),
                    inverse_root(dist[span, half:]),
                    column(qt[span, :], c),
                )
            return (jnp.where(eye(span), diag[:, half:], inverse_root(dist[span, half:])),)

        def sums(span, held):
            if span.start < half:
                g0, g1, qcol = held
                back[0] = back[0] + fold(g1 * qcol)
                part = g0 * qrow[:, :half] + g1 * qrow[:, half:]
            else:
                part = held[0] * qrow[:, half:]
            return jnp.sum(part, axis=1, keepdims=True)

        def store(span, held):
            put_column(acct, span, i, held)

        staged(spans_of(panels), root, sums, store)
        back = jnp.sum(back[0], axis=0, keepdims=True)
        acc[pl.ds(c, 1), :] += jnp.concatenate([jnp.zeros_like(back), back], axis=1)

    pipeline(share, begin_self, finish_self, ring[: ring_size(share)])

    count = pairs.shape[1] // S
    start = sub * count

    def begin(i, dist):
        p = start + jnp.minimum(i, count - 1)
        distances(load_features(fa, pairs[0, p]), load_features(fb, pairs[1, p]), dist)

    def finish(i, dist):
        ia, ib = pairs[0, start + i], pairs[1, start + i]
        acc[pl.ds(ib, 1), :] += tile_sums(dist, q[pl.ds(ib, 1), :], qt, ia, acct, share + i)

    pipeline(count, begin, finish, ring[: ring_size(count)])
    rows[...] = acct[...].T
    for i in range(share):
        acc[pl.ds(first + i, 1), :] += rows[i : i + 1, :]
    for i in range(count):
        acc[pl.ds(pairs[0, start + i], 1), :] += rows[share + i : share + i + 1, :]
    total = acc_in[...] + acc[...] * inv

    got[...] = jnp.zeros_like(got)
    for shift in range(1, C):
        dest = lax.rem(me + shift, C)
        for j in range(slots):
            got[pl.ds(targets[dest, j], 1), :] += sums[shift - 1][j : j + 1, :]

    par_dev, far_n, rank = coupling.shape[0], coupling.shape[1], coupling.shape[2]
    parents[pl.ds(pl.multiple_of(me * par_dev, 8), par_dev), :] = up[...]
    for shift in range(1, C):
        owner = lax.rem(me + shift, C)
        parents[pl.ds(pl.multiple_of(owner * par_dev, 8), par_dev), :] = sums[shift - 1][slots:, :rank]
    lane = lax.broadcasted_iota(jnp.int32, (rank, LANES), 1)
    field = jnp.zeros((rank, LANES), F32)
    for p in range(par_dev):
        part = jnp.zeros((rank, rank), F32)
        for k in range(far_n):
            part = part + coupling[p, k] * parents[pl.ds(far_list[p, k], 1), :]
        field = jnp.where(lane == p, jnp.sum(part, axis=1, keepdims=True), field)
    which = lax.broadcasted_iota(jnp.int32, (LANES, clusters), 0)
    onehot = (parent[...] == which).astype(F32)
    down = jnp.dot(field, onehot, precision=HIGHEST, preferred_element_type=F32)
    fields = jnp.concatenate(
        [jnp.sum(transfer[r] * down, axis=0, keepdims=True) for r in range(rank)], axis=0
    )

    def give(s):
        for shift in range(S):
            other = (s + shift) % S
            part = total[:, other * L : (other + 1) * L]
            parts[shift][:clusters, :] = part + got[...] if shift == 0 else part
            for t in range(clusters // L):
                at = clusters + t * rank
                parts[shift][at : at + rank, :] = fields[:, t * L : (t + 1) * L]

    for s in range(S):
        pl.when(sub == s)(functools.partial(give, s))


def up_kernel(basis, masked, transfer, parent, up):
    clusters = basis.shape[0]
    rank = basis.shape[1]
    lane = lax.broadcasted_iota(jnp.int32, (rank, clusters), 1)
    leaf = jnp.zeros((rank, clusters), F32)
    for c in range(clusters):
        part = jnp.sum(basis[c] * masked[c : c + 1, :], axis=1, keepdims=True)
        leaf = jnp.where(lane == c, part, leaf)
    lifted = jnp.zeros((rank, clusters), F32)
    for r in range(rank):
        lifted = lifted + transfer[r] * leaf[r : r + 1, :]
    which = lax.broadcasted_iota(jnp.int32, (up.shape[0], clusters), 0)
    onehot = (parent[...] == which).astype(F32)
    up[...] = lax.dot_general(
        onehot, lifted, (((1,), (1,)), ((), ())), precision=HIGHEST, preferred_element_type=F32
    )


def final_kernel(sizes, mask, basis, *rest):
    S, R, L = sizes
    near, out = rest[: S * R], rest[-1]
    clusters, rank = basis.shape[0], basis.shape[1]
    fields = []
    for t in range(clusters // L):
        rows = slice(clusters + t * rank, clusters + (t + 1) * rank)
        fields.append(sum(near[d * R][rows, :] for d in range(1, S)) + near[0][rows, :])
    fields = jnp.concatenate(fields, axis=1) if len(fields) > 1 else fields[0]
    for c in range(clusters):
        out[c : c + 1, :] = jnp.sum(basis[c] * fields[:, c : c + 1], axis=0, keepdims=True)
    total = out[...]
    for part in near:
        total = total + part[:clusters, :]
    out[...] = total * mask[...].astype(F32)


def send(value, moves):
    names = tuple(name for name, _ in moves)
    steps = [step for _, step in moves]
    sizes = [lax.axis_size(name) for name in names]
    perm = []

    def flat(coords):
        index = 0
        for size, c in zip(sizes, coords):
            index = index * size + c
        return index

    total = 1
    for size in sizes:
        total *= size
    for index in range(total):
        coords, left = [], index
        for size in reversed(sizes):
            coords.append(left % size)
            left //= size
        coords.reverse()
        perm.append((index, flat([(c + s) % n for c, s, n in zip(coords, steps, sizes)])))
    return lax.ppermute(value, names if len(names) > 1 else names[0], perm)


def on_device(
    charges,
    panel_mask,
    geometry,
    remote_source,
    remote_target,
    remote_live,
    local_pairs,
    basis,
    transfer,
    parent_of,
    far_list,
    coupling,
):
    clusters, L = charges.shape
    panels = geometry.shape[2]
    C, S, R = lax.axis_size("clu"), lax.axis_size("sub"), lax.axis_size("rep")
    slots = remote_source.shape[2]
    par_dev, rank = far_list.shape[0], transfer.shape[1]
    n = (C - 1) * slots
    shape = jax.ShapeDtypeStruct
    targets = remote_target[0]
    basis_t = jnp.transpose(basis, (0, 2, 1))
    transfer_t = jnp.transpose(transfer, (1, 2, 0))
    parent = parent_of[None, :]

    made = pl.pallas_call(
        functools.partial(pack_kernel, (C, S, L, slots)),
        out_shape=[shape((clusters, L), F32)] + [shape((5 * slots + 8, L), F32)] * (C - 1),
        in_specs=[vmem()] * 3 + [smem()] * 3,
        out_specs=[vmem()] * C,
        compiler_params=PARAMS,
        name="packs",
    )(charges, panel_mask, geometry, targets, remote_source[0], remote_live[0])
    masked, packs = made[0], made[1:]
    pieces = [masked] + [send(masked, (("sub", d),)) for d in range(1, S)]
    packs = [send(packs[d - 1], (("clu", d),)) for d in range(1, C)]
    codes = jnp.stack([p[5 * slots, :slots] for p in packs]).astype(jnp.int32)

    up = pl.pallas_call(
        up_kernel,
        out_shape=shape((par_dev, rank), F32),
        in_specs=[vmem()] * 4,
        out_specs=vmem(),
        compiler_params=PARAMS,
        name="far_up",
    )(basis_t, masked, transfer_t, parent)

    made = pl.pallas_call(
        functools.partial(remote_kernel, (C, S, L, slots, clusters, panels)),
        out_shape=[shape((clusters, panels), F32)] + [shape((slots + par_dev, L), F32)] * (C - 1),
        in_specs=[vmem(), smem()] + [vmem()] * (1 + S + C - 1),
        out_specs=[vmem()] * C,
        scratch_shapes=[
            pltpu.VMEM((clusters, panels), F32),
            pltpu.VMEM((L, whole(n)), F32),
            pltpu.VMEM((clusters, panels), F32),
            pltpu.VMEM((L, whole(n)), F32),
            pltpu.VMEM((4 * n, panels), F32),
            pltpu.VMEM((n * ROWS, L), F32),
            pltpu.VMEM((n * ROWS, LANES), F32),
            pltpu.VMEM((n * ROWS, LANES), F32),
            pltpu.SMEM((n + 1,), jnp.int32),
        ]
        + [pltpu.VMEM((L, panels), F32)] * 4,
        compiler_params=PARAMS,
        name="near_remote",
    )(geometry, codes, up, *pieces, *packs)
    acc, sums = made[0], [send(made[d], (("clu", C - d),)) for d in range(1, C)]

    columns = whole(clusters // (S * R) + local_pairs.shape[1] // S)
    half = [pltpu.VMEM((clusters * ROWS, LANES), F32)] * 2
    parts = pl.pallas_call(
        functools.partial(local_kernel, (C, S, L, R, slots, clusters, panels)),
        out_shape=[shape((clusters + clusters // L * rank, L), F32)] * S,
        in_specs=[vmem()] + [smem()] * 3 + [vmem()] * (5 + S + C - 1),
        out_specs=[vmem()] * S,
        scratch_shapes=[
            pltpu.VMEM((clusters, panels), F32),
            pltpu.VMEM((panels, clusters), F32),
            pltpu.VMEM((clusters, panels), F32),
            pltpu.VMEM((panels, columns), F32),
            *half,
            *half,
            pltpu.VMEM((clusters, panels), F32),
            pltpu.VMEM((clusters, L), F32),
            pltpu.VMEM((C * par_dev, rank), F32),
            pltpu.VMEM((columns, panels), F32),
        ]
        + [pltpu.VMEM((panels, panels), F32)] * 8,
        compiler_params=PARAMS,
        name="near_local",
    )(geometry, local_pairs[0].T, targets, far_list, coupling, transfer_t, parent, up, acc, *pieces, *sums)
    near = []
    for d in range(S):
        for e in range(R):
            near.append(send(parts[d], (("sub", d), ("rep", e))) if d or e else parts[0])

    return pl.pallas_call(
        functools.partial(final_kernel, (S, R, L)),
        out_shape=shape((clusters, L), F32),
        in_specs=[vmem()] * (2 + S * R),
        out_specs=vmem(),
        compiler_params=PARAMS,
        name="combine",
    )(panel_mask, basis_t, *near)


def solution(mesh):
    placed = (
        P(("grp", "clu"), "sub"),
        P(("grp", "clu"), "sub"),
        P(("grp", "clu"), None, None),
        P(("grp", "clu"), None, "rep"),
        P(("grp", "clu"), None, "rep"),
        P(("grp", "clu"), None, "rep"),
        P(("grp", "clu"), "rep", None),
        P(("grp", "clu"), "sub", None),
        P(("grp", "clu"), None, None),
        P(("grp", "clu")),
        P(("grp", "clu"), None),
        P(("grp", "clu"), None, None, None),
    )
    return jax.shard_map(
        on_device, mesh=mesh, in_specs=placed, out_specs=P(("grp", "clu"), "sub"), check_vma=False
    )
```

```python
import functools

import jax
import jax.numpy as jnp
from jax import lax
from jax.experimental import pallas as pl
from jax.experimental.pallas import tpu as pltpu
from jax.sharding import PartitionSpec as P

F32 = jnp.float32
HIGHEST = lax.Precision.HIGHEST
LANES = 128
PARAMS = pltpu.CompilerParams(vmem_limit_bytes=56 * 1024 * 1024)


def vmem():
    return pl.BlockSpec(memory_space=pltpu.VMEM)


def smem():
    return pl.BlockSpec(memory_space=pltpu.SMEM)


def whole(size):
    return -(-size // LANES) * LANES


def column(table, index):
    if table.shape[1] == LANES and table.shape[0] % 8 == 0:
        return jnp.take_along_axis(table, jnp.full(table.shape, index, jnp.int32), axis=1)
    lane = lax.broadcasted_iota(jnp.int32, table.shape, 1)
    picked = jnp.sum(jnp.where(lane == index, table, 0.0), axis=1, keepdims=True)
    return jnp.broadcast_to(picked, (table.shape[0], LANES))


def put_column(table, rows, index, value):
    shape = (rows.stop - rows.start, table.shape[1])
    lane = lax.broadcasted_iota(jnp.int32, shape, 1)
    pltpu.store(table.at[rows, :], jnp.broadcast_to(value, shape), mask=lane == index)


def inverse_root(d):
    return lax.rsqrt(d)


def fold(v):
    return jnp.sum(v.reshape(v.shape[0] // 8, 8, v.shape[1]), axis=0)


def staged(spans, *stages):
    held = {}
    for t in range(len(spans) + len(stages) - 1):
        for depth in reversed(range(len(stages))):
            k = t - depth
            if 0 <= k < len(spans):
                held[k] = stages[depth](spans[k], held.get(k))
                if depth == len(stages) - 1:
                    del held[k]


def spans_of(height, step=16):
    step = min(step, height)
    return [slice(r, r + step) for r in range(0, height, step)]


def kernel_values(columns, row):
    x, y, z, rr = columns
    dx, dy, dz = x - row[0], y - row[1], z - row[2]
    return lax.rsqrt((dx * dx + dy * dy + dz * dz) + (rr + row[3]))


def panel_rows(points):
    rows = [points[0:1, :], points[1:2, :], points[2:3, :], points[3:4, :] * points[3:4, :]]
    return [[r[:, t : t + LANES] for r in rows] for t in range(0, points.shape[1], LANES)]


def tile_sums(tables, slot, points, qrow, table, index):
    blocks = panel_rows(points)
    q = [qrow[:, :LANES], qrow[:, LANES:]]
    back = [jnp.zeros((8, LANES), F32), jnp.zeros((8, LANES), F32)]

    def root(rows, _):
        *place, qcol = [column(t[rows, :], slot) for t in tables]
        return [kernel_values(place, b) for b in blocks] + [qcol]

    def sums(rows, held):
        g0, g1, qcol = held
        back[0] = back[0] + fold(g0 * qcol)
        back[1] = back[1] + fold(g1 * qcol)
        return jnp.sum(g0 * q[0] + g1 * q[1], axis=1, keepdims=True)

    def store(rows, held):
        put_column(table, rows, index, held)

    staged(spans_of(tables[0].shape[0]), root, sums, store)
    return jnp.concatenate([jnp.sum(b, axis=0, keepdims=True) for b in back], axis=1)


def pipeline(total, tile, size):
    def body(i, carry):
        for k in range(size):
            tile(i * size + k)
        return carry

    lax.fori_loop(0, (total + size - 1) // size, body, 0)


def ring_size(total):
    return next(size for size in (4, 2, 1) if total % size == 0)


def assemble(sub, S, L, q, pieces):
    def place(s):
        for shift in range(S):
            owner = (s - shift) % S
            q[:, owner * L : (owner + 1) * L] = pieces[shift][...]

    for s in range(S):
        pl.when(sub == s)(functools.partial(place, s))


def pack_kernel(sizes, charges, mask, geo, targets, sources, live, masked, *packs):
    C, S, L, slots = sizes
    me, sub = lax.axis_index("clu"), lax.axis_index("sub")
    masked[...] = charges[...] * mask[...].astype(F32)
    lane = lax.broadcasted_iota(jnp.int32, (8, L), 1)
    for shift in range(1, C):
        dest = lax.rem(me + shift, C)
        codes = jnp.full((8, L), -1.0, F32)
        for j in range(slots):
            code = jnp.where(live[dest, j] > 0, sources[dest, j], -1)
            codes = jnp.where(lane == j, code.astype(F32), codes)
        packs[shift - 1][5 * slots :, :] = codes

    def fill(s):
        for shift in range(1, C):
            dest = lax.rem(me + shift, C)
            pack = packs[shift - 1]
            for j in range(slots):
                t = targets[dest, j]
                g = geo[t, :, s * L : (s + 1) * L]
                for k in range(4):
                    pack[k * slots + j : k * slots + j + 1, :] = g[k : k + 1]
                pack[4 * slots + j : 4 * slots + j + 1, :] = masked[pl.ds(t, 1), :]

    for s in range(S):
        pl.when(sub == s)(functools.partial(fill, s))


def remote_kernel(sizes, geo, codes, up, *rest):
    C, S, L, slots, clusters, panels = sizes
    pieces = rest[:S]
    packs = rest[S : S + C - 1]
    acc_out = rest[S + C - 1]
    sends = rest[S + C : S + C + C - 1]
    q, acc, fwdt, order, *tables = rest[S + C + C - 1 :]
    n = (C - 1) * slots
    assemble(lax.axis_index("sub"), S, L, q, pieces)
    acc[...] = jnp.zeros_like(acc)
    fwdt[...] = jnp.zeros_like(fwdt)
    found = jnp.int32(0)
    for shift in range(C - 1):
        for j in range(slots):
            order[found] = shift * slots + j
            found = found + (codes[shift, j] >= 0).astype(jnp.int32)
    wide = fwdt.shape[1]
    for k in range(5):
        rows = [p[k * slots : (k + 1) * slots, :] for p in packs]
        if wide > n:
            rows.append(jnp.zeros((wide - n, L), F32))
        value = jnp.concatenate(rows, axis=0).T
        tables[k][...] = value * value if k == 3 else value

    def tile(i):
        ok = i < found
        slot = order[jnp.minimum(i, jnp.maximum(found - 1, 0))]
        source = jnp.maximum(codes[slot // slots, lax.rem(slot, slots)], 0)
        back = tile_sums(
            tables, slot, geo[source], q[pl.ds(source, 1), :], fwdt, jnp.where(ok, slot, -1)
        )
        acc[pl.ds(source, 1), :] += jnp.where(ok, back, 0.0)

    pipeline(found, tile, 4)
    acc_out[...] = acc[...]
    fwd = fwdt[...].T
    rank = up.shape[1]
    for shift in range(C - 1):
        sends[shift][:slots, :] = fwd[shift * slots : (shift + 1) * slots, :]
        sends[shift][slots:, :] = jnp.zeros((up.shape[0], L), F32)
        sends[shift][slots:, :rank] = up[...]


def local_kernel(
    sizes, geo, pairs, targets, far_list, coupling, transfer, parent, up, acc_in, *rest
):
    C, S, L, R, slots, clusters, panels = sizes
    pieces = rest[:S]
    sums = rest[S : S + C - 1]
    parts = rest[S + C - 1 : 2 * S + C - 1]
    q, acc, acct, got, parents, rows, *tables = rest[2 * S + C - 1 :]
    me, sub, rep = lax.axis_index("clu"), lax.axis_index("sub"), lax.axis_index("rep")
    assemble(sub, S, L, q, pieces)
    acc[...] = jnp.zeros_like(acc)
    acct[...] = jnp.zeros_like(acct)
    for k in range(4):
        value = geo[:, k, :].T
        tables[k][...] = value * value if k == 3 else value
    tables[4][...] = q[...].T

    half = panels // 2
    share = clusters // (S * R)
    first = (rep * S + sub) * share

    def self_tile(i):
        c = first + i
        blocks = panel_rows(geo[c])
        qrow = q[pl.ds(c, 1), :]
        back = [jnp.zeros((8, LANES), F32)]

        def root(span, _):
            *place, qcol = [column(t[span, :], c) for t in tables]
            if span.start < half:
                return [kernel_values(place, b) for b in blocks] + [qcol]
            return [kernel_values(place, blocks[1])]

        def sums(span, held):
            if span.start < half:
                g0, g1, qcol = held
                back[0] = back[0] + fold(g1 * qcol)
                part = g0 * qrow[:, :half] + g1 * qrow[:, half:]
            else:
                part = held[0] * qrow[:, half:]
            return jnp.sum(part, axis=1, keepdims=True)

        def store(span, held):
            put_column(acct, span, i, held)

        staged(spans_of(panels), root, sums, store)
        total = jnp.sum(back[0], axis=0, keepdims=True)
        acc[pl.ds(c, 1), :] += jnp.concatenate([jnp.zeros_like(total), total], axis=1)

    pipeline(share, self_tile, ring_size(share))

    count = pairs.shape[1] // S
    start = sub * count

    def pair_tile(i):
        ia, ib = pairs[0, start + i], pairs[1, start + i]
        acc[pl.ds(ib, 1), :] += tile_sums(
            tables, ia, geo[ib], q[pl.ds(ib, 1), :], acct, share + i
        )

    pipeline(count, pair_tile, ring_size(count))
    rows[...] = acct[...].T
    for i in range(share):
        acc[pl.ds(first + i, 1), :] += rows[i : i + 1, :]
    for i in range(count):
        acc[pl.ds(pairs[0, start + i], 1), :] += rows[share + i : share + i + 1, :]
    total = acc_in[...] + acc[...]

    got[...] = jnp.zeros_like(got)
    for shift in range(1, C):
        dest = lax.rem(me + shift, C)
        for j in range(slots):
            got[pl.ds(targets[dest, j], 1), :] += sums[shift - 1][j : j + 1, :]

    par_dev, far_n, rank = coupling.shape[0], coupling.shape[1], coupling.shape[2]
    parents[pl.ds(pl.multiple_of(me * par_dev, 8), par_dev), :] = up[...]
    for shift in range(1, C):
        owner = lax.rem(me + shift, C)
        parents[pl.ds(pl.multiple_of(owner * par_dev, 8), par_dev), :] = sums[shift - 1][slots:, :rank]
    lane = lax.broadcasted_iota(jnp.int32, (rank, LANES), 1)
    field = jnp.zeros((rank, LANES), F32)
    for p in range(par_dev):
        part = jnp.zeros((rank, rank), F32)
        for k in range(far_n):
            part = part + coupling[p, k] * parents[pl.ds(far_list[p, k], 1), :]
        field = jnp.where(lane == p, jnp.sum(part, axis=1, keepdims=True), field)
    which = lax.broadcasted_iota(jnp.int32, (LANES, clusters), 0)
    onehot = (parent[...] == which).astype(F32)
    down = jnp.dot(field, onehot, precision=HIGHEST, preferred_element_type=F32)
    fields = jnp.concatenate(
        [jnp.sum(transfer[r] * down, axis=0, keepdims=True) for r in range(rank)], axis=0
    )

    def give(s):
        for shift in range(S):
            other = (s + shift) % S
            part = total[:, other * L : (other + 1) * L]
            parts[shift][:clusters, :] = part + got[...] if shift == 0 else part
            for t in range(clusters // L):
                at = clusters + t * rank
                parts[shift][at : at + rank, :] = fields[:, t * L : (t + 1) * L]

    for s in range(S):
        pl.when(sub == s)(functools.partial(give, s))


def up_kernel(basis, masked, transfer, parent, up):
    clusters = basis.shape[0]
    rank = basis.shape[1]
    lane = lax.broadcasted_iota(jnp.int32, (rank, clusters), 1)
    leaf = jnp.zeros((rank, clusters), F32)
    for c in range(clusters):
        part = jnp.sum(basis[c] * masked[c : c + 1, :], axis=1, keepdims=True)
        leaf = jnp.where(lane == c, part, leaf)
    lifted = jnp.zeros((rank, clusters), F32)
    for r in range(rank):
        lifted = lifted + transfer[r] * leaf[r : r + 1, :]
    which = lax.broadcasted_iota(jnp.int32, (up.shape[0], clusters), 0)
    onehot = (parent[...] == which).astype(F32)
    up[...] = lax.dot_general(
        onehot, lifted, (((1,), (1,)), ((), ())), precision=HIGHEST, preferred_element_type=F32
    )


def final_kernel(sizes, mask, basis, *rest):
    S, R, L = sizes
    near, out = rest[: S * R], rest[-1]
    clusters, rank = basis.shape[0], basis.shape[1]
    fields = []
    for t in range(clusters // L):
        rows = slice(clusters + t * rank, clusters + (t + 1) * rank)
        fields.append(sum(near[d * R][rows, :] for d in range(1, S)) + near[0][rows, :])
    fields = jnp.concatenate(fields, axis=1) if len(fields) > 1 else fields[0]
    for c in range(clusters):
        out[c : c + 1, :] = jnp.sum(basis[c] * fields[:, c : c + 1], axis=0, keepdims=True)
    total = out[...]
    for part in near:
        total = total + part[:clusters, :]
    out[...] = total * mask[...].astype(F32)


def send(value, moves):
    names = tuple(name for name, _ in moves)
    steps = [step for _, step in moves]
    sizes = [lax.axis_size(name) for name in names]
    perm = []

    def flat(coords):
        index = 0
        for size, c in zip(sizes, coords):
            index = index * size + c
        return index

    total = 1
    for size in sizes:
        total *= size
    for index in range(total):
        coords, left = [], index
        for size in reversed(sizes):
            coords.append(left % size)
            left //= size
        coords.reverse()
        perm.append((index, flat([(c + s) % n for c, s, n in zip(coords, steps, sizes)])))
    return lax.ppermute(value, names if len(names) > 1 else names[0], perm)


def on_device(
    charges,
    panel_mask,
    geometry,
    remote_source,
    remote_target,
    remote_live,
    local_pairs,
    basis,
    transfer,
    parent_of,
    far_list,
    coupling,
):
    clusters, L = charges.shape
    panels = geometry.shape[2]
    C, S, R = lax.axis_size("clu"), lax.axis_size("sub"), lax.axis_size("rep")
    slots = remote_source.shape[2]
    par_dev, rank = far_list.shape[0], transfer.shape[1]
    n = (C - 1) * slots
    shape = jax.ShapeDtypeStruct
    targets = remote_target[0]
    basis_t = jnp.transpose(basis, (0, 2, 1))
    transfer_t = jnp.transpose(transfer, (1, 2, 0))
    parent = parent_of[None, :]

    made = pl.pallas_call(
        functools.partial(pack_kernel, (C, S, L, slots)),
        out_shape=[shape((clusters, L), F32)] + [shape((5 * slots + 8, L), F32)] * (C - 1),
        in_specs=[vmem()] * 3 + [smem()] * 3,
        out_specs=[vmem()] * C,
        compiler_params=PARAMS,
        name="packs",
    )(charges, panel_mask, geometry, targets, remote_source[0], remote_live[0])
    masked, packs = made[0], made[1:]
    pieces = [masked] + [send(masked, (("sub", d),)) for d in range(1, S)]
    packs = [send(packs[d - 1], (("clu", d),)) for d in range(1, C)]
    codes = jnp.stack([p[5 * slots, :slots] for p in packs]).astype(jnp.int32)

    up = pl.pallas_call(
        up_kernel,
        out_shape=shape((par_dev, rank), F32),
        in_specs=[vmem()] * 4,
        out_specs=vmem(),
        compiler_params=PARAMS,
        name="far_up",
    )(basis_t, masked, transfer_t, parent)

    made = pl.pallas_call(
        functools.partial(remote_kernel, (C, S, L, slots, clusters, panels)),
        out_shape=[shape((clusters, panels), F32)] + [shape((slots + par_dev, L), F32)] * (C - 1),
        in_specs=[vmem(), smem()] + [vmem()] * (1 + S + C - 1),
        out_specs=[vmem()] * C,
        scratch_shapes=[
            pltpu.VMEM((clusters, panels), F32),
            pltpu.VMEM((clusters, panels), F32),
            pltpu.VMEM((L, whole(n)), F32),
            pltpu.SMEM((n + 1,), jnp.int32),
        ]
        + [pltpu.VMEM((L, whole(n)), F32)] * 5,
        compiler_params=PARAMS,
        name="near_remote",
    )(geometry, codes, up, *pieces, *packs)
    acc, sums = made[0], [send(made[d], (("clu", C - d),)) for d in range(1, C)]

    columns = whole(clusters // (S * R) + local_pairs.shape[1] // S)
    parts = pl.pallas_call(
        functools.partial(local_kernel, (C, S, L, R, slots, clusters, panels)),
        out_shape=[shape((clusters + clusters // L * rank, L), F32)] * S,
        in_specs=[vmem()] + [smem()] * 3 + [vmem()] * (5 + S + C - 1),
        out_specs=[vmem()] * S,
        scratch_shapes=[
            pltpu.VMEM((clusters, panels), F32),
            pltpu.VMEM((clusters, panels), F32),
            pltpu.VMEM((panels, columns), F32),
            pltpu.VMEM((clusters, L), F32),
            pltpu.VMEM((C * par_dev, rank), F32),
            pltpu.VMEM((columns, panels), F32),
        ]
        + [pltpu.VMEM((panels, clusters), F32)] * 5,
        compiler_params=PARAMS,
        name="near_local",
    )(geometry, local_pairs[0].T, targets, far_list, coupling, transfer_t, parent, up, acc, *pieces, *sums)
    near = []
    for d in range(S):
        for e in range(R):
            near.append(send(parts[d], (("sub", d), ("rep", e))) if d or e else parts[0])

    return pl.pallas_call(
        functools.partial(final_kernel, (S, R, L)),
        out_shape=shape((clusters, L), F32),
        in_specs=[vmem()] * (2 + S * R),
        out_specs=vmem(),
        compiler_params=PARAMS,
        name="combine",
    )(panel_mask, basis_t, *near)


def solution(mesh):
    placed = (
        P(("grp", "clu"), "sub"),
        P(("grp", "clu"), "sub"),
        P(("grp", "clu"), None, None),
        P(("grp", "clu"), None, "rep"),
        P(("grp", "clu"), None, "rep"),
        P(("grp", "clu"), None, "rep"),
        P(("grp", "clu"), "rep", None),
        P(("grp", "clu"), "sub", None),
        P(("grp", "clu"), None, None),
        P(("grp", "clu")),
        P(("grp", "clu"), None),
        P(("grp", "clu"), None, None, None),
    )
    return jax.shard_map(
        on_device, mesh=mesh, in_specs=placed, out_specs=P(("grp", "clu"), "sub"), check_vma=False
    )
```

```python
import functools

import jax
import jax.numpy as jnp
from jax import lax
from jax.experimental import pallas as pl
from jax.experimental.pallas import tpu as pltpu
from jax.sharding import PartitionSpec as P

F32 = jnp.float32
BF16 = jnp.bfloat16
HIGHEST = lax.Precision.HIGHEST
ROWS = 40
USED = 34
LANES = 128
PARAMS = pltpu.CompilerParams(vmem_limit_bytes=56 * 1024 * 1024)


def vmem():
    return pl.BlockSpec(memory_space=pltpu.VMEM)


def smem():
    return pl.BlockSpec(memory_space=pltpu.SMEM)


def whole(size):
    return -(-size // LANES) * LANES


def cut(v):
    return v.astype(BF16).astype(F32)


def powers(sign):
    lane = lax.broadcasted_iota(jnp.int32, (8, LANES), 1)
    out = jnp.full((8, LANES), 2.0 ** (-64 * sign), F32)
    for bit in range(7):
        out = out * jnp.where((lane >> bit) & 1 == 1, F32(2.0 ** (sign * 2**bit)), F32(1.0))
    return out


def frame(parts):
    low = [functools.reduce(jnp.minimum, [jnp.min(p[k]) for p in parts]) for k in range(3)]
    high = [functools.reduce(jnp.maximum, [jnp.max(p[k]) for p in parts]) for k in range(3)]
    width = functools.reduce(jnp.maximum, [jnp.max(jnp.abs(p[3])) for p in parts])
    for lo, hi in zip(low, high):
        width = jnp.maximum(width, 0.5 * (hi - lo))
    up, down = powers(1), powers(-1)
    size = jnp.min(jnp.where(up >= width, up, F32(2.0**63)))
    inv = jnp.max(jnp.where(up >= width, down, F32(2.0**-63)))
    magic = size * F32(1.5 * 2.0**20)
    centre = [(0.5 * (lo + hi) + magic) - magic for lo, hi in zip(low, high)]
    return centre, inv


def split_features(points, centre, inv):
    magic = F32(1.5 * 2.0**16)
    grid, rest = [], []
    for k in range(3):
        u = (points[k] - centre[k]) * inv
        h = (u + magic) - magic
        grid.append(h)
        rest.append(u - h)
    rad = points[3] * inv
    norm = grid[0] * grid[0] + grid[1] * grid[1] + grid[2] * grid[2]
    norm1 = cut(norm)
    norm2 = norm - norm1
    cross = grid[0] * rest[0] + grid[1] * rest[1] + grid[2] * rest[2]
    extra = 2.0 * cross + (rest[0] * rest[0] + rest[1] * rest[1] + rest[2] * rest[2]) + rad * rad
    extra1 = cut(extra)
    extra2 = cut(extra - extra1)
    extra3 = (extra - extra1) - extra2
    rest1 = [cut(v) for v in rest]
    rest2 = [v - w for v, w in zip(rest, rest1)]
    neg = lambda vs: [-2.0 * v for v in vs]
    one = jnp.ones_like(rad)
    left = grid + [norm1, norm2, one, one]
    right = neg(grid) + [one, one, norm1, norm2]
    left += [extra1, extra2, extra3, one, one, one]
    right += [one, one, one, extra1, extra2, extra3]
    left += grid + grid + rest1 + rest2 + rest1 + rest1 + rest2
    right += neg(rest1) + neg(rest2) + neg(grid) + neg(grid) + neg(rest1) + neg(rest2) + neg(rest1)
    return left, right, rad


def store_features(ref, rows):
    count = rows[0].shape[0]
    width = rows[0].shape[1]
    for k, row in enumerate(rows):
        for t, piece in enumerate(ref):
            piece[pl.ds(k, count, stride=ROWS), :] = row[:, t * LANES : min(width, (t + 1) * LANES)]


def load_features(ref, index):
    start = pl.multiple_of(index * ROWS, 8)
    return [piece[pl.ds(start, USED), :].astype(BF16) for piece in ref]


def contract(left, right):
    return jnp.dot(left, right, preferred_element_type=F32)


def upright(row):
    return jnp.broadcast_to(row, (8, row.shape[1])).T[:, :1]


def put_column(table, rows, index, value):
    shape = (rows.stop - rows.start, table.shape[1])
    lane = lax.broadcasted_iota(jnp.int32, shape, 1)
    pltpu.store(table.at[rows, :], jnp.broadcast_to(value, shape), mask=lane == index)


def inverse_root(d):
    return lax.rsqrt(d)


def fold(v):
    return jnp.sum(v.reshape(v.shape[0] // 8, 8, v.shape[1]), axis=0)


def distances(left, right, out):
    whole_left = jnp.concatenate(left, axis=1) if len(left) > 1 else left[0]
    out[...] = contract(whole_left.T, jnp.concatenate(right, axis=1))


def staged(spans, *stages):
    held = {}
    for t in range(len(spans) + len(stages) - 1):
        for depth in reversed(range(len(stages))):
            k = t - depth
            if 0 <= k < len(spans):
                held[k] = stages[depth](spans[k], held.get(k))
                if depth == len(stages) - 1:
                    del held[k]


def spans_of(height, step=32):
    step = min(step, height)
    return [slice(r, r + step) for r in range(0, height, step)]


def tile_sums(dist, qrow, qleft, table, index):
    q0, q1 = qrow[:, :LANES], qrow[:, LANES:]
    qcol = upright(qleft)
    back = [jnp.zeros((8, LANES), F32), jnp.zeros((8, LANES), F32)]

    def root(rows, _):
        return (
            inverse_root(dist[rows, :LANES]),
            inverse_root(dist[rows, LANES:]),
        )

    def sums(rows, held):
        g0, g1 = held
        back[0] = back[0] + fold(g0 * qcol[rows, :])
        back[1] = back[1] + fold(g1 * qcol[rows, :])
        return jnp.sum(g0 * q0 + g1 * q1, axis=1, keepdims=True)

    def store(rows, held):
        put_column(table, rows, index, held)

    staged(spans_of(dist.shape[0]), root, sums, store)
    return jnp.concatenate([jnp.sum(b, axis=0, keepdims=True) for b in back], axis=1)


def pipeline(total, begin, finish, ring):
    size = len(ring)
    ahead = min(2, size - 1)

    def body(i, carry):
        for k in range(size):
            begin(i * size + k + ahead, ring[(k + ahead) % size])
            finish(i * size + k, ring[k])
        return carry

    for k in range(ahead):
        begin(k, ring[k])
    lax.fori_loop(0, (total + size - 1) // size, body, 0)


def ring_size(total):
    return next(size for size in (8, 4, 2, 1) if total % size == 0)


def assemble(sub, S, L, q, pieces):
    def place(s):
        for shift in range(S):
            owner = (s - shift) % S
            q[:, owner * L : (owner + 1) * L] = pieces[shift][...]

    for s in range(S):
        pl.when(sub == s)(functools.partial(place, s))


def pack_kernel(sizes, charges, mask, geo, targets, sources, live, masked, *packs):
    C, S, L, slots = sizes
    me, sub = lax.axis_index("clu"), lax.axis_index("sub")
    masked[...] = charges[...] * mask[...].astype(F32)
    lane = lax.broadcasted_iota(jnp.int32, (8, L), 1)
    for shift in range(1, C):
        dest = lax.rem(me + shift, C)
        codes = jnp.full((8, L), -1.0, F32)
        for j in range(slots):
            code = jnp.where(live[dest, j] > 0, sources[dest, j], -1)
            codes = jnp.where(lane == j, code.astype(F32), codes)
        packs[shift - 1][5 * slots :, :] = codes

    def fill(s):
        for shift in range(1, C):
            dest = lax.rem(me + shift, C)
            pack = packs[shift - 1]
            for j in range(slots):
                t = targets[dest, j]
                g = geo[t, :, s * L : (s + 1) * L]
                for k in range(4):
                    pack[k * slots + j : k * slots + j + 1, :] = g[k : k + 1]
                pack[4 * slots + j : 4 * slots + j + 1, :] = masked[pl.ds(t, 1), :]

    for s in range(S):
        pl.when(sub == s)(functools.partial(fill, s))


def remote_kernel(sizes, geo, codes, up, *rest):
    C, S, L, slots, clusters, panels = sizes
    pieces = rest[:S]
    packs = rest[S : S + C - 1]
    acc_out = rest[S + C - 1]
    sends = rest[S + C : S + C + C - 1]
    q, tq, acc, fwdt, sgeo, fa0, fb0, fb1, order, *ring = rest[S + C + C - 1 :]
    fa, fb = (fa0,), (fb0, fb1)
    n = (C - 1) * slots
    assemble(lax.axis_index("sub"), S, L, q, pieces)
    acc[...] = jnp.zeros_like(acc)
    fwdt[...] = jnp.zeros_like(fwdt)
    found = jnp.int32(0)
    for shift in range(C - 1):
        for j in range(slots):
            code = codes[shift, j]
            order[found] = shift * slots + j
            found = found + (code >= 0).astype(jnp.int32)
            g = geo[jnp.maximum(code, 0)]
            for k in range(4):
                row = k * n + shift * slots + j
                sgeo[row : row + 1, :] = g[k : k + 1]
    tpoints = [
        jnp.concatenate([p[k * slots : (k + 1) * slots, :] for p in packs], axis=0) for k in range(5)
    ]
    spoints = [sgeo[k * n : (k + 1) * n, :] for k in range(4)]
    centre, inv = frame([tpoints, spoints])
    left, _, _ = split_features(tpoints, centre, inv)
    _, right, _ = split_features(spoints, centre, inv)
    store_features(fa, left)
    store_features(fb, right)
    tq[...] = tpoints[4]

    def begin(i, dist):
        slot = order[jnp.minimum(i, jnp.maximum(found - 1, 0))]
        distances(load_features(fa, slot), load_features(fb, slot), dist)

    def finish(i, dist):
        ok = i < found
        slot = order[jnp.minimum(i, jnp.maximum(found - 1, 0))]
        source = jnp.maximum(codes[slot // slots, lax.rem(slot, slots)], 0)
        back = tile_sums(
            dist, q[pl.ds(source, 1), :], tq[pl.ds(slot, 1), :], fwdt, jnp.where(ok, slot, -1)
        )
        acc[pl.ds(source, 1), :] += jnp.where(ok, back, 0.0)

    pipeline(found, begin, finish, ring)
    acc_out[...] = acc[...] * inv
    fwd = (fwdt[...] * inv).T
    rank = up.shape[1]
    for shift in range(C - 1):
        sends[shift][:slots, :] = fwd[shift * slots : (shift + 1) * slots, :]
        sends[shift][slots:, :] = jnp.zeros((up.shape[0], L), F32)
        sends[shift][slots:, :rank] = up[...]


def local_kernel(
    sizes, geo, pairs, targets, far_list, coupling, transfer, parent, up, acc_in, *rest
):
    C, S, L, R, slots, clusters, panels = sizes
    pieces = rest[:S]
    sums = rest[S : S + C - 1]
    parts = rest[S + C - 1 : 2 * S + C - 1]
    q, acc, acct, fa0, fa1, fb0, fb1, rads, got, parents, rows, *ring = rest[2 * S + C - 1 :]
    fa, fb = (fa0, fa1), (fb0, fb1)
    me, sub, rep = lax.axis_index("clu"), lax.axis_index("sub"), lax.axis_index("rep")
    assemble(sub, S, L, q, pieces)
    acc[...] = jnp.zeros_like(acc)
    acct[...] = jnp.zeros_like(acct)
    points = [geo[:, k, :] for k in range(4)]
    centre, inv = frame([points])
    left, right, rad = split_features(points, centre, inv)
    store_features(fa, left)
    store_features(fb, right)
    rads[...] = rad

    half = panels // 2
    share = clusters // (S * R)
    first = (rep * S + sub) * share

    def begin_self(i, dist):
        c = first + jnp.minimum(i, share - 1)
        a = load_features(fa, c)
        b = load_features(fb, c)
        dist[:half, :] = contract(a[0].T, jnp.concatenate(b, axis=1))
        dist[half:, half:] = contract(a[1].T, b[1])

    def finish_self(i, dist):
        c = first + i
        qrow = q[pl.ds(c, 1), :]
        qcol = upright(qrow[:, :half])
        radius = rads[pl.ds(c, 1), :]
        diag = lax.rsqrt(2.0 * (radius * radius))
        back = [jnp.zeros((8, LANES), F32)]

        def eye(span):
            shape = (span.stop - span.start, half)
            row = lax.broadcasted_iota(jnp.int32, shape, 0) + span.start % half
            return row == lax.broadcasted_iota(jnp.int32, shape, 1)

        def root(span, _):
            if span.start < half:
                return (
                    jnp.where(eye(span), diag[:, :half], inverse_root(dist[span, :half])),
                    inverse_root(dist[span, half:]),
                )
            return (jnp.where(eye(span), diag[:, half:], inverse_root(dist[span, half:])),)

        def sums(span, held):
            if span.start < half:
                g0, g1 = held
                back[0] = back[0] + fold(g1 * qcol[span, :])
                part = g0 * qrow[:, :half] + g1 * qrow[:, half:]
            else:
                part = held[0] * qrow[:, half:]
            return jnp.sum(part, axis=1, keepdims=True)

        def store(span, held):
            put_column(acct, span, i, held)

        staged(spans_of(panels), root, sums, store)
        back = jnp.sum(back[0], axis=0, keepdims=True)
        acc[pl.ds(c, 1), :] += jnp.concatenate([jnp.zeros_like(back), back], axis=1)

    pipeline(share, begin_self, finish_self, ring[: ring_size(share)])

    count = pairs.shape[1] // S
    start = sub * count

    def begin(i, dist):
        p = start + jnp.minimum(i, count - 1)
        distances(load_features(fa, pairs[0, p]), load_features(fb, pairs[1, p]), dist)

    def finish(i, dist):
        ia, ib = pairs[0, start + i], pairs[1, start + i]
        acc[pl.ds(ib, 1), :] += tile_sums(
            dist, q[pl.ds(ib, 1), :], q[pl.ds(ia, 1), :], acct, share + i
        )

    pipeline(count, begin, finish, ring[: ring_size(count)])
    rows[...] = acct[...].T
    for i in range(share):
        acc[pl.ds(first + i, 1), :] += rows[i : i + 1, :]
    for i in range(count):
        acc[pl.ds(pairs[0, start + i], 1), :] += rows[share + i : share + i + 1, :]
    total = acc_in[...] + acc[...] * inv

    got[...] = jnp.zeros_like(got)
    for shift in range(1, C):
        dest = lax.rem(me + shift, C)
        for j in range(slots):
            got[pl.ds(targets[dest, j], 1), :] += sums[shift - 1][j : j + 1, :]

    par_dev, far_n, rank = coupling.shape[0], coupling.shape[1], coupling.shape[2]
    parents[pl.ds(pl.multiple_of(me * par_dev, 8), par_dev), :] = up[...]
    for shift in range(1, C):
        owner = lax.rem(me + shift, C)
        parents[pl.ds(pl.multiple_of(owner * par_dev, 8), par_dev), :] = sums[shift - 1][slots:, :rank]
    lane = lax.broadcasted_iota(jnp.int32, (rank, LANES), 1)
    field = jnp.zeros((rank, LANES), F32)
    for p in range(par_dev):
        part = jnp.zeros((rank, rank), F32)
        for k in range(far_n):
            part = part + coupling[p, k] * parents[pl.ds(far_list[p, k], 1), :]
        field = jnp.where(lane == p, jnp.sum(part, axis=1, keepdims=True), field)
    which = lax.broadcasted_iota(jnp.int32, (LANES, clusters), 0)
    onehot = (parent[...] == which).astype(F32)
    down = jnp.dot(field, onehot, precision=HIGHEST, preferred_element_type=F32)
    fields = jnp.concatenate(
        [jnp.sum(transfer[r] * down, axis=0, keepdims=True) for r in range(rank)], axis=0
    )

    def give(s):
        for shift in range(S):
            other = (s + shift) % S
            part = total[:, other * L : (other + 1) * L]
            parts[shift][:clusters, :] = part + got[...] if shift == 0 else part
            for t in range(clusters // L):
                at = clusters + t * rank
                parts[shift][at : at + rank, :] = fields[:, t * L : (t + 1) * L]

    for s in range(S):
        pl.when(sub == s)(functools.partial(give, s))


def up_kernel(basis, masked, transfer, parent, up):
    clusters = basis.shape[0]
    rank = basis.shape[1]
    lane = lax.broadcasted_iota(jnp.int32, (rank, clusters), 1)
    leaf = jnp.zeros((rank, clusters), F32)
    for c in range(clusters):
        part = jnp.sum(basis[c] * masked[c : c + 1, :], axis=1, keepdims=True)
        leaf = jnp.where(lane == c, part, leaf)
    lifted = jnp.zeros((rank, clusters), F32)
    for r in range(rank):
        lifted = lifted + transfer[r] * leaf[r : r + 1, :]
    which = lax.broadcasted_iota(jnp.int32, (up.shape[0], clusters), 0)
    onehot = (parent[...] == which).astype(F32)
    up[...] = lax.dot_general(
        onehot, lifted, (((1,), (1,)), ((), ())), precision=HIGHEST, preferred_element_type=F32
    )


def final_kernel(sizes, mask, basis, *rest):
    S, R, L = sizes
    near, out = rest[: S * R], rest[-1]
    clusters, rank = basis.shape[0], basis.shape[1]
    fields = []
    for t in range(clusters // L):
        rows = slice(clusters + t * rank, clusters + (t + 1) * rank)
        fields.append(sum(near[d * R][rows, :] for d in range(1, S)) + near[0][rows, :])
    fields = jnp.concatenate(fields, axis=1) if len(fields) > 1 else fields[0]
    for c in range(clusters):
        out[c : c + 1, :] = jnp.sum(basis[c] * fields[:, c : c + 1], axis=0, keepdims=True)
    total = out[...]
    for part in near:
        total = total + part[:clusters, :]
    out[...] = total * mask[...].astype(F32)


def send(value, moves):
    names = tuple(name for name, _ in moves)
    steps = [step for _, step in moves]
    sizes = [lax.axis_size(name) for name in names]
    perm = []

    def flat(coords):
        index = 0
        for size, c in zip(sizes, coords):
            index = index * size + c
        return index

    total = 1
    for size in sizes:
        total *= size
    for index in range(total):
        coords, left = [], index
        for size in reversed(sizes):
            coords.append(left % size)
            left //= size
        coords.reverse()
        perm.append((index, flat([(c + s) % n for c, s, n in zip(coords, steps, sizes)])))
    return lax.ppermute(value, names if len(names) > 1 else names[0], perm)


def on_device(
    charges,
    panel_mask,
    geometry,
    remote_source,
    remote_target,
    remote_live,
    local_pairs,
    basis,
    transfer,
    parent_of,
    far_list,
    coupling,
):
    clusters, L = charges.shape
    panels = geometry.shape[2]
    C, S, R = lax.axis_size("clu"), lax.axis_size("sub"), lax.axis_size("rep")
    slots = remote_source.shape[2]
    par_dev, rank = far_list.shape[0], transfer.shape[1]
    n = (C - 1) * slots
    shape = jax.ShapeDtypeStruct
    targets = remote_target[0]
    basis_t = jnp.transpose(basis, (0, 2, 1))
    transfer_t = jnp.transpose(transfer, (1, 2, 0))
    parent = parent_of[None, :]

    made = pl.pallas_call(
        functools.partial(pack_kernel, (C, S, L, slots)),
        out_shape=[shape((clusters, L), F32)] + [shape((5 * slots + 8, L), F32)] * (C - 1),
        in_specs=[vmem()] * 3 + [smem()] * 3,
        out_specs=[vmem()] * C,
        compiler_params=PARAMS,
        name="packs",
    )(charges, panel_mask, geometry, targets, remote_source[0], remote_live[0])
    masked, packs = made[0], made[1:]
    pieces = [masked] + [send(masked, (("sub", d),)) for d in range(1, S)]
    packs = [send(packs[d - 1], (("clu", d),)) for d in range(1, C)]
    codes = jnp.stack([p[5 * slots, :slots] for p in packs]).astype(jnp.int32)

    up = pl.pallas_call(
        up_kernel,
        out_shape=shape((par_dev, rank), F32),
        in_specs=[vmem()] * 4,
        out_specs=vmem(),
        compiler_params=PARAMS,
        name="far_up",
    )(basis_t, masked, transfer_t, parent)

    made = pl.pallas_call(
        functools.partial(remote_kernel, (C, S, L, slots, clusters, panels)),
        out_shape=[shape((clusters, panels), F32)] + [shape((slots + par_dev, L), F32)] * (C - 1),
        in_specs=[vmem(), smem()] + [vmem()] * (1 + S + C - 1),
        out_specs=[vmem()] * C,
        scratch_shapes=[
            pltpu.VMEM((clusters, panels), F32),
            pltpu.VMEM((n, L), F32),
            pltpu.VMEM((clusters, panels), F32),
            pltpu.VMEM((L, whole(n)), F32),
            pltpu.VMEM((4 * n, panels), F32),
            pltpu.VMEM((n * ROWS, L), F32),
            pltpu.VMEM((n * ROWS, LANES), F32),
            pltpu.VMEM((n * ROWS, LANES), F32),
            pltpu.SMEM((n + 1,), jnp.int32),
        ]
        + [pltpu.VMEM((L, panels), F32)] * 4,
        compiler_params=PARAMS,
        name="near_remote",
    )(geometry, codes, up, *pieces, *packs)
    acc, sums = made[0], [send(made[d], (("clu", C - d),)) for d in range(1, C)]

    columns = whole(clusters // (S * R) + local_pairs.shape[1] // S)
    half = [pltpu.VMEM((clusters * ROWS, LANES), F32)] * 2
    parts = pl.pallas_call(
        functools.partial(local_kernel, (C, S, L, R, slots, clusters, panels)),
        out_shape=[shape((clusters + clusters // L * rank, L), F32)] * S,
        in_specs=[vmem()] + [smem()] * 3 + [vmem()] * (5 + S + C - 1),
        out_specs=[vmem()] * S,
        scratch_shapes=[
            pltpu.VMEM((clusters, panels), F32),
            pltpu.VMEM((clusters, panels), F32),
            pltpu.VMEM((panels, columns), F32),
            *half,
            *half,
            pltpu.VMEM((clusters, panels), F32),
            pltpu.VMEM((clusters, L), F32),
            pltpu.VMEM((C * par_dev, rank), F32),
            pltpu.VMEM((columns, panels), F32),
        ]
        + [pltpu.VMEM((panels, panels), F32)] * 8,
        compiler_params=PARAMS,
        name="near_local",
    )(geometry, local_pairs[0].T, targets, far_list, coupling, transfer_t, parent, up, acc, *pieces, *sums)
    near = []
    for d in range(S):
        for e in range(R):
            near.append(send(parts[d], (("sub", d), ("rep", e))) if d or e else parts[0])

    return pl.pallas_call(
        functools.partial(final_kernel, (S, R, L)),
        out_shape=shape((clusters, L), F32),
        in_specs=[vmem()] * (2 + S * R),
        out_specs=vmem(),
        compiler_params=PARAMS,
        name="combine",
    )(panel_mask, basis_t, *near)


def solution(mesh):
    placed = (
        P(("grp", "clu"), "sub"),
        P(("grp", "clu"), "sub"),
        P(("grp", "clu"), None, None),
        P(("grp", "clu"), None, "rep"),
        P(("grp", "clu"), None, "rep"),
        P(("grp", "clu"), None, "rep"),
        P(("grp", "clu"), "rep", None),
        P(("grp", "clu"), "sub", None),
        P(("grp", "clu"), None, None),
        P(("grp", "clu")),
        P(("grp", "clu"), None),
        P(("grp", "clu"), None, None, None),
    )
    return jax.shard_map(
        on_device, mesh=mesh, in_specs=placed, out_specs=P(("grp", "clu"), "sub"), check_vma=False
    )
```

```python
import functools

import jax
import jax.numpy as jnp
from jax import lax
from jax.experimental import pallas as pl
from jax.experimental.pallas import tpu as pltpu
from jax.sharding import PartitionSpec as P

F32 = jnp.float32
BF16 = jnp.bfloat16
HIGHEST = lax.Precision.HIGHEST
ROWS = 40
USED = 34
LANES = 128
PARAMS = pltpu.CompilerParams(vmem_limit_bytes=56 * 1024 * 1024)


def vmem():
    return pl.BlockSpec(memory_space=pltpu.VMEM)


def smem():
    return pl.BlockSpec(memory_space=pltpu.SMEM)


def whole(size):
    return -(-size // LANES) * LANES


def cut(v):
    return v.astype(BF16).astype(F32)


def powers(sign):
    lane = lax.broadcasted_iota(jnp.int32, (8, LANES), 1)
    out = jnp.full((8, LANES), 2.0 ** (-64 * sign), F32)
    for bit in range(7):
        out = out * jnp.where((lane >> bit) & 1 == 1, F32(2.0 ** (sign * 2**bit)), F32(1.0))
    return out


def frame(parts):
    low = [functools.reduce(jnp.minimum, [jnp.min(p[k]) for p in parts]) for k in range(3)]
    high = [functools.reduce(jnp.maximum, [jnp.max(p[k]) for p in parts]) for k in range(3)]
    width = functools.reduce(jnp.maximum, [jnp.max(jnp.abs(p[3])) for p in parts])
    for lo, hi in zip(low, high):
        width = jnp.maximum(width, 0.5 * (hi - lo))
    up, down = powers(1), powers(-1)
    size = jnp.min(jnp.where(up >= width, up, F32(2.0**63)))
    inv = jnp.max(jnp.where(up >= width, down, F32(2.0**-63)))
    magic = size * F32(1.5 * 2.0**20)
    centre = [(0.5 * (lo + hi) + magic) - magic for lo, hi in zip(low, high)]
    return centre, inv


def split_features(points, centre, inv):
    magic = F32(1.5 * 2.0**16)
    grid, rest = [], []
    for k in range(3):
        u = (points[k] - centre[k]) * inv
        h = (u + magic) - magic
        grid.append(h)
        rest.append(u - h)
    rad = points[3] * inv
    norm = grid[0] * grid[0] + grid[1] * grid[1] + grid[2] * grid[2]
    norm1 = cut(norm)
    norm2 = norm - norm1
    cross = grid[0] * rest[0] + grid[1] * rest[1] + grid[2] * rest[2]
    extra = 2.0 * cross + (rest[0] * rest[0] + rest[1] * rest[1] + rest[2] * rest[2]) + rad * rad
    extra1 = cut(extra)
    extra2 = cut(extra - extra1)
    extra3 = (extra - extra1) - extra2
    rest1 = [cut(v) for v in rest]
    rest2 = [v - w for v, w in zip(rest, rest1)]
    neg = lambda vs: [-2.0 * v for v in vs]
    one = jnp.ones_like(rad)
    left = grid + [norm1, norm2, one, one]
    right = neg(grid) + [one, one, norm1, norm2]
    left += [extra1, extra2, extra3, one, one, one]
    right += [one, one, one, extra1, extra2, extra3]
    left += grid + grid + rest1 + rest2 + rest1 + rest1 + rest2
    right += neg(rest1) + neg(rest2) + neg(grid) + neg(grid) + neg(rest1) + neg(rest2) + neg(rest1)
    return left, right, rad


def store_features(ref, rows):
    count = rows[0].shape[0]
    width = rows[0].shape[1]
    for k, row in enumerate(rows):
        for t, piece in enumerate(ref):
            piece[pl.ds(k, count, stride=ROWS), :] = row[:, t * LANES : min(width, (t + 1) * LANES)]


def load_features(ref, index):
    start = pl.multiple_of(index * ROWS, 8)
    return [piece[pl.ds(start, USED), :].astype(BF16) for piece in ref]


def contract(left, right):
    return jnp.dot(left, right, preferred_element_type=F32)


def upright(row):
    return jnp.broadcast_to(row, (8, row.shape[1])).T[:, :1]


def put_column(table, rows, index, value):
    shape = (rows.stop - rows.start, table.shape[1])
    lane = lax.broadcasted_iota(jnp.int32, shape, 1)
    pltpu.store(table.at[rows, :], jnp.broadcast_to(value, shape), mask=lane == index)


def inverse_root(d):
    return lax.rsqrt(d)


def fold(v):
    return jnp.sum(v.reshape(v.shape[0] // 8, 8, v.shape[1]), axis=0)


def distances(left, right, out):
    whole_left = jnp.concatenate(left, axis=1) if len(left) > 1 else left[0]
    out[...] = contract(whole_left.T, jnp.concatenate(right, axis=1))


def staged(spans, *stages):
    held = {}
    for t in range(len(spans) + len(stages) - 1):
        for depth in reversed(range(len(stages))):
            k = t - depth
            if 0 <= k < len(spans):
                held[k] = stages[depth](spans[k], held.get(k))
                if depth == len(stages) - 1:
                    del held[k]


def spans_of(height, step=32):
    step = min(step, height)
    return [slice(r, r + step) for r in range(0, height, step)]


def tile_sums(dist, qrow, qleft, table, index):
    q0, q1 = qrow[:, :LANES], qrow[:, LANES:]
    qcol = upright(qleft)
    back = [jnp.zeros((8, LANES), F32), jnp.zeros((8, LANES), F32)]

    def root(rows, _):
        return (
            inverse_root(dist[rows, :LANES]),
            inverse_root(dist[rows, LANES:]),
        )

    def sums(rows, held):
        g0, g1 = held
        back[0] = back[0] + fold(g0 * qcol[rows, :])
        back[1] = back[1] + fold(g1 * qcol[rows, :])
        return jnp.sum(g0 * q0 + g1 * q1, axis=1, keepdims=True)

    def store(rows, held):
        put_column(table, rows, index, held)

    staged(spans_of(dist.shape[0]), root, sums, store)
    return jnp.concatenate([jnp.sum(b, axis=0, keepdims=True) for b in back], axis=1)


def pipeline(total, begin, finish, ring):
    size = len(ring)
    ahead = min(2, size - 1)

    def body(i, carry):
        for k in range(size):
            begin(i * size + k + ahead, ring[(k + ahead) % size])
            finish(i * size + k, ring[k])
        return carry

    for k in range(ahead):
        begin(k, ring[k])
    lax.fori_loop(0, (total + size - 1) // size, body, 0)


def ring_size(total):
    return next(size for size in (4, 2, 1) if total % size == 0)


def assemble(sub, S, L, q, pieces):
    def place(s):
        for shift in range(S):
            owner = (s - shift) % S
            q[:, owner * L : (owner + 1) * L] = pieces[shift][...]

    for s in range(S):
        pl.when(sub == s)(functools.partial(place, s))


def pack_kernel(sizes, charges, mask, geo, targets, sources, live, masked, *packs):
    C, S, L, slots = sizes
    me, sub = lax.axis_index("clu"), lax.axis_index("sub")
    masked[...] = charges[...] * mask[...].astype(F32)
    lane = lax.broadcasted_iota(jnp.int32, (8, L), 1)

    def fill(s):
        for shift in range(1, C):
            dest = lax.rem(me + shift, C)
            pack = packs[shift - 1]

            def slot(j, codes):
                t = targets[dest, j]
                g = geo[t, :, s * L : (s + 1) * L]
                for k in range(4):
                    pack[pl.ds(k * slots + j, 1), :] = g[k : k + 1]
                pack[pl.ds(4 * slots + j, 1), :] = masked[pl.ds(t, 1), :]
                code = jnp.where(live[dest, j] > 0, sources[dest, j], -1)
                return jnp.where(lane == j, code.astype(F32), codes)

            pack[5 * slots :, :] = lax.fori_loop(0, slots, slot, jnp.full((8, L), -1.0, F32))

    for s in range(S):
        pl.when(sub == s)(functools.partial(fill, s))


def remote_kernel(sizes, geo, codes, up, *rest):
    C, S, L, slots, clusters, panels = sizes
    pieces = rest[:S]
    packs = rest[S : S + C - 1]
    acc_out = rest[S + C - 1]
    sends = rest[S + C : S + C + C - 1]
    q, tq, acc, fwdt, sgeo, fa0, fb0, fb1, order, *ring = rest[S + C + C - 1 :]
    fa, fb = (fa0,), (fb0, fb1)
    n = (C - 1) * slots
    assemble(lax.axis_index("sub"), S, L, q, pieces)
    acc[...] = jnp.zeros_like(acc)
    fwdt[...] = jnp.zeros_like(fwdt)
    found = jnp.int32(0)
    for shift in range(C - 1):
        for j in range(slots):
            code = codes[shift, j]
            order[found] = shift * slots + j
            found = found + (code >= 0).astype(jnp.int32)
            g = geo[jnp.maximum(code, 0)]
            for k in range(4):
                row = k * n + shift * slots + j
                sgeo[row : row + 1, :] = g[k : k + 1]
    tpoints = [
        jnp.concatenate([p[k * slots : (k + 1) * slots, :] for p in packs], axis=0) for k in range(5)
    ]
    spoints = [sgeo[k * n : (k + 1) * n, :] for k in range(4)]
    centre, inv = frame([tpoints, spoints])
    left, _, _ = split_features(tpoints, centre, inv)
    _, right, _ = split_features(spoints, centre, inv)
    store_features(fa, left)
    store_features(fb, right)
    tq[...] = tpoints[4]

    def begin(i, dist):
        slot = order[jnp.minimum(i, jnp.maximum(found - 1, 0))]
        distances(load_features(fa, slot), load_features(fb, slot), dist)

    def finish(i, dist):
        ok = i < found
        slot = order[jnp.minimum(i, jnp.maximum(found - 1, 0))]
        source = jnp.maximum(codes[slot // slots, lax.rem(slot, slots)], 0)
        back = tile_sums(
            dist, q[pl.ds(source, 1), :], tq[pl.ds(slot, 1), :], fwdt, jnp.where(ok, slot, -1)
        )
        acc[pl.ds(source, 1), :] += jnp.where(ok, back, 0.0)

    pipeline(found, begin, finish, ring)
    acc_out[...] = acc[...] * inv
    fwd = (fwdt[...] * inv).T
    rank = up.shape[1]
    for shift in range(C - 1):
        sends[shift][:slots, :] = fwd[shift * slots : (shift + 1) * slots, :]
        sends[shift][slots:, :] = jnp.zeros((up.shape[0], L), F32)
        sends[shift][slots:, :rank] = up[...]


def local_kernel(
    sizes, geo, pairs, targets, far_list, coupling, transfer, parent, up, acc_in, *rest
):
    C, S, L, R, slots, clusters, panels = sizes
    pieces = rest[:S]
    sums = rest[S : S + C - 1]
    parts = rest[S + C - 1 : 2 * S + C - 1]
    q, acc, acct, fa0, fa1, fb0, fb1, rads, got, parents, rows, *ring = rest[2 * S + C - 1 :]
    fa, fb = (fa0, fa1), (fb0, fb1)
    me, sub, rep = lax.axis_index("clu"), lax.axis_index("sub"), lax.axis_index("rep")
    assemble(sub, S, L, q, pieces)
    acc[...] = jnp.zeros_like(acc)
    acct[...] = jnp.zeros_like(acct)
    points = [geo[:, k, :] for k in range(4)]
    centre, inv = frame([points])
    left, right, rad = split_features(points, centre, inv)
    store_features(fa, left)
    store_features(fb, right)
    rads[...] = rad

    half = panels // 2
    share = clusters // (S * R)
    first = (rep * S + sub) * share

    def begin_self(i, dist):
        c = first + jnp.minimum(i, share - 1)
        a = load_features(fa, c)
        b = load_features(fb, c)
        dist[:half, :] = contract(a[0].T, jnp.concatenate(b, axis=1))
        dist[half:, half:] = contract(a[1].T, b[1])

    def finish_self(i, dist):
        c = first + i
        qrow = q[pl.ds(c, 1), :]
        qcol = upright(qrow[:, :half])
        radius = rads[pl.ds(c, 1), :]
        diag = lax.rsqrt(2.0 * (radius * radius))
        back = [jnp.zeros((8, LANES), F32)]

        def eye(span):
            shape = (span.stop - span.start, half)
            row = lax.broadcasted_iota(jnp.int32, shape, 0) + span.start % half
            return row == lax.broadcasted_iota(jnp.int32, shape, 1)

        def root(span, _):
            if span.start < half:
                return (
                    jnp.where(eye(span), diag[:, :half], inverse_root(dist[span, :half])),
                    inverse_root(dist[span, half:]),
                )
            return (jnp.where(eye(span), diag[:, half:], inverse_root(dist[span, half:])),)

        def sums(span, held):
            if span.start < half:
                g0, g1 = held
                back[0] = back[0] + fold(g1 * qcol[span, :])
                part = g0 * qrow[:, :half] + g1 * qrow[:, half:]
            else:
                part = held[0] * qrow[:, half:]
            return jnp.sum(part, axis=1, keepdims=True)

        def store(span, held):
            put_column(acct, span, i, held)

        staged(spans_of(panels), root, sums, store)
        back = jnp.sum(back[0], axis=0, keepdims=True)
        acc[pl.ds(c, 1), :] += jnp.concatenate([jnp.zeros_like(back), back], axis=1)

    pipeline(share, begin_self, finish_self, ring[: ring_size(share)])

    count = pairs.shape[1] // S
    start = sub * count

    def begin(i, dist):
        p = start + jnp.minimum(i, count - 1)
        distances(load_features(fa, pairs[0, p]), load_features(fb, pairs[1, p]), dist)

    def finish(i, dist):
        ia, ib = pairs[0, start + i], pairs[1, start + i]
        acc[pl.ds(ib, 1), :] += tile_sums(
            dist, q[pl.ds(ib, 1), :], q[pl.ds(ia, 1), :], acct, share + i
        )

    pipeline(count, begin, finish, ring[: ring_size(count)])
    rows[...] = acct[...].T
    for i in range(share):
        acc[pl.ds(first + i, 1), :] += rows[i : i + 1, :]
    for i in range(count):
        acc[pl.ds(pairs[0, start + i], 1), :] += rows[share + i : share + i + 1, :]
    total = acc_in[...] + acc[...] * inv

    got[...] = jnp.zeros_like(got)
    for shift in range(1, C):
        dest = lax.rem(me + shift, C)
        for j in range(slots):
            got[pl.ds(targets[dest, j], 1), :] += sums[shift - 1][j : j + 1, :]

    par_dev, far_n, rank = coupling.shape[0], coupling.shape[1], coupling.shape[2]
    parents[pl.ds(pl.multiple_of(me * par_dev, 8), par_dev), :] = up[...]
    for shift in range(1, C):
        owner = lax.rem(me + shift, C)
        parents[pl.ds(pl.multiple_of(owner * par_dev, 8), par_dev), :] = sums[shift - 1][slots:, :rank]
    lane = lax.broadcasted_iota(jnp.int32, (rank, LANES), 1)
    field = jnp.zeros((rank, LANES), F32)
    for p in range(par_dev):
        part = jnp.zeros((rank, rank), F32)
        for k in range(far_n):
            part = part + coupling[p, k] * parents[pl.ds(far_list[p, k], 1), :]
        field = jnp.where(lane == p, jnp.sum(part, axis=1, keepdims=True), field)
    which = lax.broadcasted_iota(jnp.int32, (LANES, clusters), 0)
    onehot = (parent[...] == which).astype(F32)
    down = jnp.dot(field, onehot, precision=HIGHEST, preferred_element_type=F32)
    fields = jnp.concatenate(
        [jnp.sum(transfer[r] * down, axis=0, keepdims=True) for r in range(rank)], axis=0
    )

    def give(s):
        for shift in range(S):
            other = (s + shift) % S
            part = total[:, other * L : (other + 1) * L]
            parts[shift][:clusters, :] = part + got[...] if shift == 0 else part
            for t in range(clusters // L):
                at = clusters + t * rank
                parts[shift][at : at + rank, :] = fields[:, t * L : (t + 1) * L]

    for s in range(S):
        pl.when(sub == s)(functools.partial(give, s))


def up_kernel(basis, masked, transfer, parent, up, groups):
    clusters = basis.shape[0]
    rank = basis.shape[1]
    lane = lax.broadcasted_iota(jnp.int32, (rank, LANES), 1)

    def group(g, carry):
        rows = masked[pl.ds(pl.multiple_of(g * 8, 8), 8), :]
        leaf = jnp.zeros((rank, LANES), F32)
        for j in range(8):
            part = jnp.sum(basis[g * 8 + j] * rows[j : j + 1, :], axis=1, keepdims=True)
            leaf = jnp.where(lane == j, part, leaf)
        groups[g] = leaf
        return carry

    lax.fori_loop(0, clusters // 8, group, 0)
    leaf = jnp.concatenate([groups[g][:, :8] for g in range(clusters // 8)], axis=1)
    lifted = jnp.zeros((rank, clusters), F32)
    for r in range(rank):
        lifted = lifted + transfer[r] * leaf[r : r + 1, :]
    which = lax.broadcasted_iota(jnp.int32, (up.shape[0], clusters), 0)
    onehot = (parent[...] == which).astype(F32)
    up[...] = lax.dot_general(
        onehot, lifted, (((1,), (1,)), ((), ())), precision=HIGHEST, preferred_element_type=F32
    )


def final_kernel(sizes, mask, basis, *rest):
    S, R, L = sizes
    near, out, groups = rest[: S * R], rest[-2], rest[-1]
    clusters, rank = basis.shape[0], basis.shape[1]
    fields = []
    for t in range(clusters // L):
        rows = slice(clusters + t * rank, clusters + (t + 1) * rank)
        fields.append(sum(near[d * R][rows, :] for d in range(1, S)) + near[0][rows, :])
    fields = jnp.concatenate(fields, axis=1) if len(fields) > 1 else fields[0]
    for g in range(clusters // 8):
        groups[g, :, :8] = fields[:, g * 8 : (g + 1) * 8]

    def group(g, carry):
        span = pl.ds(pl.multiple_of(g * 8, 8), 8)
        field = groups[g]
        far = [
            jnp.sum(basis[g * 8 + j] * field[:, j : j + 1], axis=0, keepdims=True)
            for j in range(8)
        ]
        total = jnp.concatenate(far, axis=0)
        for part in near:
            total = total + part[span, :]
        out[span, :] = total * mask[span, :].astype(F32)
        return carry

    lax.fori_loop(0, clusters // 8, group, 0)


def send(value, moves):
    names = tuple(name for name, _ in moves)
    steps = [step for _, step in moves]
    sizes = [lax.axis_size(name) for name in names]
    perm = []

    def flat(coords):
        index = 0
        for size, c in zip(sizes, coords):
            index = index * size + c
        return index

    total = 1
    for size in sizes:
        total *= size
    for index in range(total):
        coords, left = [], index
        for size in reversed(sizes):
            coords.append(left % size)
            left //= size
        coords.reverse()
        perm.append((index, flat([(c + s) % n for c, s, n in zip(coords, steps, sizes)])))
    return lax.ppermute(value, names if len(names) > 1 else names[0], perm)


def on_device(
    charges,
    panel_mask,
    geometry,
    remote_source,
    remote_target,
    remote_live,
    local_pairs,
    basis,
    transfer,
    parent_of,
    far_list,
    coupling,
):
    clusters, L = charges.shape
    panels = geometry.shape[2]
    C, S, R = lax.axis_size("clu"), lax.axis_size("sub"), lax.axis_size("rep")
    slots = remote_source.shape[2]
    par_dev, rank = far_list.shape[0], transfer.shape[1]
    n = (C - 1) * slots
    shape = jax.ShapeDtypeStruct
    targets = remote_target[0]
    basis_t = jnp.transpose(basis, (0, 2, 1))
    transfer_t = jnp.transpose(transfer, (1, 2, 0))
    parent = parent_of[None, :]

    made = pl.pallas_call(
        functools.partial(pack_kernel, (C, S, L, slots)),
        out_shape=[shape((clusters, L), F32)] + [shape((5 * slots + 8, L), F32)] * (C - 1),
        in_specs=[vmem()] * 3 + [smem()] * 3,
        out_specs=[vmem()] * C,
        compiler_params=PARAMS,
        name="packs",
    )(charges, panel_mask, geometry, targets, remote_source[0], remote_live[0])
    masked, packs = made[0], made[1:]
    pieces = [masked] + [send(masked, (("sub", d),)) for d in range(1, S)]
    packs = [send(packs[d - 1], (("clu", d),)) for d in range(1, C)]
    codes = jnp.stack([p[5 * slots, :slots] for p in packs]).astype(jnp.int32)

    up = pl.pallas_call(
        up_kernel,
        out_shape=shape((par_dev, rank), F32),
        in_specs=[vmem()] * 4,
        out_specs=vmem(),
        scratch_shapes=[pltpu.VMEM((clusters // 8, rank, LANES), F32)],
        compiler_params=PARAMS,
        name="far_up",
    )(basis_t, masked, transfer_t, parent)

    made = pl.pallas_call(
        functools.partial(remote_kernel, (C, S, L, slots, clusters, panels)),
        out_shape=[shape((clusters, panels), F32)] + [shape((slots + par_dev, L), F32)] * (C - 1),
        in_specs=[vmem(), smem()] + [vmem()] * (1 + S + C - 1),
        out_specs=[vmem()] * C,
        scratch_shapes=[
            pltpu.VMEM((clusters, panels), F32),
            pltpu.VMEM((n, L), F32),
            pltpu.VMEM((clusters, panels), F32),
            pltpu.VMEM((L, whole(n)), F32),
            pltpu.VMEM((4 * n, panels), F32),
            pltpu.VMEM((n * ROWS, L), F32),
            pltpu.VMEM((n * ROWS, LANES), F32),
            pltpu.VMEM((n * ROWS, LANES), F32),
            pltpu.SMEM((n + 1,), jnp.int32),
        ]
        + [pltpu.VMEM((L, panels), F32)] * 4,
        compiler_params=PARAMS,
        name="near_remote",
    )(geometry, codes, up, *pieces, *packs)
    acc, sums = made[0], [send(made[d], (("clu", C - d),)) for d in range(1, C)]

    columns = whole(clusters // (S * R) + local_pairs.shape[1] // S)
    half = [pltpu.VMEM((clusters * ROWS, LANES), F32)] * 2
    parts = pl.pallas_call(
        functools.partial(local_kernel, (C, S, L, R, slots, clusters, panels)),
        out_shape=[shape((clusters + clusters // L * rank, L), F32)] * S,
        in_specs=[vmem()] + [smem()] * 3 + [vmem()] * (5 + S + C - 1),
        out_specs=[vmem()] * S,
        scratch_shapes=[
            pltpu.VMEM((clusters, panels), F32),
            pltpu.VMEM((clusters, panels), F32),
            pltpu.VMEM((panels, columns), F32),
            *half,
            *half,
            pltpu.VMEM((clusters, panels), F32),
            pltpu.VMEM((clusters, L), F32),
            pltpu.VMEM((C * par_dev, rank), F32),
            pltpu.VMEM((columns, panels), F32),
        ]
        + [pltpu.VMEM((panels, panels), F32)] * 4,
        compiler_params=PARAMS,
        name="near_local",
    )(geometry, local_pairs[0].T, targets, far_list, coupling, transfer_t, parent, up, acc, *pieces, *sums)
    near = []
    for d in range(S):
        for e in range(R):
            near.append(send(parts[d], (("sub", d), ("rep", e))) if d or e else parts[0])

    return pl.pallas_call(
        functools.partial(final_kernel, (S, R, L)),
        out_shape=shape((clusters, L), F32),
        in_specs=[vmem()] * (2 + S * R),
        out_specs=vmem(),
        scratch_shapes=[pltpu.VMEM((clusters // 8, rank, LANES), F32)],
        compiler_params=PARAMS,
        name="combine",
    )(panel_mask, basis_t, *near)


def solution(mesh):
    placed = (
        P(("grp", "clu"), "sub"),
        P(("grp", "clu"), "sub"),
        P(("grp", "clu"), None, None),
        P(("grp", "clu"), None, "rep"),
        P(("grp", "clu"), None, "rep"),
        P(("grp", "clu"), None, "rep"),
        P(("grp", "clu"), "rep", None),
        P(("grp", "clu"), "sub", None),
        P(("grp", "clu"), None, None),
        P(("grp", "clu")),
        P(("grp", "clu"), None),
        P(("grp", "clu"), None, None, None),
    )
    return jax.shard_map(
        on_device, mesh=mesh, in_specs=placed, out_specs=P(("grp", "clu"), "sub"), check_vma=False
    )
```

```python
import functools

import jax
import jax.numpy as jnp
from jax import lax
from jax.experimental import pallas as pl
from jax.experimental.pallas import tpu as pltpu
from jax.sharding import PartitionSpec as P

F32 = jnp.float32
BF16 = jnp.bfloat16
HIGHEST = lax.Precision.HIGHEST
ROWS = 40
USED = 34
LANES = 128
PARAMS = pltpu.CompilerParams(vmem_limit_bytes=44 * 1024 * 1024)


def vmem():
    return pl.BlockSpec(memory_space=pltpu.VMEM)


def near_by(*arrays):
    return [pltpu.with_memory_space_constraint(x, pltpu.VMEM) for x in arrays]


def smem():
    return pl.BlockSpec(memory_space=pltpu.SMEM)


def whole(size):
    return -(-size // LANES) * LANES


def cut(v):
    return v.astype(BF16).astype(F32)


def powers(sign):
    lane = lax.broadcasted_iota(jnp.int32, (8, LANES), 1)
    out = jnp.full((8, LANES), 2.0 ** (-64 * sign), F32)
    for bit in range(7):
        out = out * jnp.where((lane >> bit) & 1 == 1, F32(2.0 ** (sign * 2**bit)), F32(1.0))
    return out


def frame(parts):
    low = [functools.reduce(jnp.minimum, [jnp.min(p[k]) for p in parts]) for k in range(3)]
    high = [functools.reduce(jnp.maximum, [jnp.max(p[k]) for p in parts]) for k in range(3)]
    width = functools.reduce(jnp.maximum, [jnp.max(jnp.abs(p[3])) for p in parts])
    for lo, hi in zip(low, high):
        width = jnp.maximum(width, 0.5 * (hi - lo))
    up, down = powers(1), powers(-1)
    size = jnp.min(jnp.where(up >= width, up, F32(2.0**63)))
    inv = jnp.max(jnp.where(up >= width, down, F32(2.0**-63)))
    magic = size * F32(1.5 * 2.0**20)
    centre = [(0.5 * (lo + hi) + magic) - magic for lo, hi in zip(low, high)]
    return centre, inv


def split_features(points, centre, inv):
    magic = F32(1.5 * 2.0**16)
    grid, rest = [], []
    for k in range(3):
        u = (points[k] - centre[k]) * inv
        h = (u + magic) - magic
        grid.append(h)
        rest.append(u - h)
    rad = points[3] * inv
    norm = grid[0] * grid[0] + grid[1] * grid[1] + grid[2] * grid[2]
    norm1 = cut(norm)
    norm2 = norm - norm1
    cross = grid[0] * rest[0] + grid[1] * rest[1] + grid[2] * rest[2]
    extra = 2.0 * cross + (rest[0] * rest[0] + rest[1] * rest[1] + rest[2] * rest[2]) + rad * rad
    extra1 = cut(extra)
    extra2 = cut(extra - extra1)
    extra3 = (extra - extra1) - extra2
    rest1 = [cut(v) for v in rest]
    rest2 = [v - w for v, w in zip(rest, rest1)]
    neg = lambda vs: [-2.0 * v for v in vs]
    one = jnp.ones_like(rad)
    left = grid + [norm1, norm2, one, one]
    right = neg(grid) + [one, one, norm1, norm2]
    left += [extra1, extra2, extra3, one, one, one]
    right += [one, one, one, extra1, extra2, extra3]
    left += grid + grid + rest1 + rest2 + rest1 + rest1 + rest2
    right += neg(rest1) + neg(rest2) + neg(grid) + neg(grid) + neg(rest1) + neg(rest2) + neg(rest1)
    return left, right, rad


def store_features(ref, rows):
    count = rows[0].shape[0]
    width = rows[0].shape[1]
    for k, row in enumerate(rows):
        for t, piece in enumerate(ref):
            piece[pl.ds(k, count, stride=ROWS), :] = row[:, t * LANES : min(width, (t + 1) * LANES)]


def load_features(ref, index):
    start = pl.multiple_of(index * ROWS, 8)
    return [piece[pl.ds(start, USED), :].astype(BF16) for piece in ref]


def contract(left, right):
    return jnp.dot(left, right, preferred_element_type=F32)


def upright(row):
    return jnp.broadcast_to(row, (8, row.shape[1])).T[:, :1]


def put_column(table, rows, index, value):
    shape = (rows.stop - rows.start, table.shape[1])
    lane = lax.broadcasted_iota(jnp.int32, shape, 1)
    pltpu.store(table.at[rows, :], jnp.broadcast_to(value, shape), mask=lane == index)


def inverse_root(d):
    return lax.rsqrt(d)


def fold(v):
    return jnp.sum(v.reshape(v.shape[0] // 8, 8, v.shape[1]), axis=0)


def distances(left, right, out):
    whole_left = jnp.concatenate(left, axis=1) if len(left) > 1 else left[0]
    out[...] = contract(whole_left.T, jnp.concatenate(right, axis=1))


def staged(spans, *stages):
    held = {}
    for t in range(len(spans) + len(stages) - 1):
        for depth in reversed(range(len(stages))):
            k = t - depth
            if 0 <= k < len(spans):
                held[k] = stages[depth](spans[k], held.get(k))
                if depth == len(stages) - 1:
                    del held[k]


def spans_of(height, step=32):
    step = min(step, height)
    return [slice(r, r + step) for r in range(0, height, step)]


def tile_sums(dist, qrow, qleft, table, index):
    q0, q1 = qrow[:, :LANES], qrow[:, LANES:]
    qcol = upright(qleft)
    back = [jnp.zeros((8, LANES), F32), jnp.zeros((8, LANES), F32)]

    def root(rows, _):
        return (
            inverse_root(dist[rows, :LANES]),
            inverse_root(dist[rows, LANES:]),
        )

    def sums(rows, held):
        g0, g1 = held
        back[0] = back[0] + fold(g0 * qcol[rows, :])
        back[1] = back[1] + fold(g1 * qcol[rows, :])
        return jnp.sum(g0 * q0 + g1 * q1, axis=1, keepdims=True)

    def store(rows, held):
        put_column(table, rows, index, held)

    staged(spans_of(dist.shape[0]), root, sums, store)
    return jnp.concatenate([jnp.sum(b, axis=0, keepdims=True) for b in back], axis=1)


def pipeline(total, begin, finish, ring):
    size = len(ring)
    ahead = min(2, size - 1)

    def body(i, carry):
        for k in range(size):
            begin(i * size + k + ahead, ring[(k + ahead) % size])
            finish(i * size + k, ring[k])
        return carry

    for k in range(ahead):
        begin(k, ring[k])
    lax.fori_loop(0, (total + size - 1) // size, body, 0)


def ring_size(total):
    return next(size for size in (16, 8, 4, 2, 1) if total % size == 0)


def assemble(sub, S, L, q, pieces):
    def place(s):
        for shift in range(S):
            owner = (s - shift) % S
            q[:, owner * L : (owner + 1) * L] = pieces[shift][...]

    for s in range(S):
        pl.when(sub == s)(functools.partial(place, s))


def pack_kernel(sizes, charges, mask, geo, targets, sources, live, masked, *packs):
    C, S, L, slots = sizes
    me, sub = lax.axis_index("clu"), lax.axis_index("sub")
    masked[...] = charges[...] * mask[...].astype(F32)
    lane = lax.broadcasted_iota(jnp.int32, (8, L), 1)
    for shift in range(1, C):
        dest = lax.rem(me + shift, C)
        codes = jnp.full((8, L), -1.0, F32)
        for j in range(slots):
            code = jnp.where(live[dest, j] > 0, sources[dest, j], -1)
            codes = jnp.where(lane == j, code.astype(F32), codes)
        packs[shift - 1][5 * slots :, :] = codes

    def fill(s):
        for shift in range(1, C):
            dest = lax.rem(me + shift, C)
            pack = packs[shift - 1]
            for j in range(slots):
                t = targets[dest, j]
                g = geo[t, :, s * L : (s + 1) * L]
                for k in range(4):
                    pack[k * slots + j : k * slots + j + 1, :] = g[k : k + 1]
                pack[4 * slots + j : 4 * slots + j + 1, :] = masked[pl.ds(t, 1), :]

    for s in range(S):
        pl.when(sub == s)(functools.partial(fill, s))


def remote_kernel(sizes, geo, up, *rest):
    C, S, L, slots, clusters, panels = sizes
    pieces = rest[:S]
    packs = rest[S : S + C - 1]
    acc_out = rest[S + C - 1]
    sends = rest[S + C : S + C + C - 1]
    q, tq, acc, fwdt, sgeo, fa0, fb0, fb1, order, codes, sems, *ring = rest[S + C + C - 1 :]
    fa, fb = (fa0,), (fb0, fb1)
    n = (C - 1) * slots
    copies = [
        pltpu.make_async_copy(packs[k].at[pl.ds(5 * slots, 8), :], codes.at[k], sems.at[k])
        for k in range(C - 1)
    ]
    for copy in copies:
        copy.start()
    assemble(lax.axis_index("sub"), S, L, q, pieces)
    acc[...] = jnp.zeros_like(acc)
    fwdt[...] = jnp.zeros_like(fwdt)
    for copy in copies:
        copy.wait()
    found = jnp.int32(0)
    for shift in range(C - 1):
        for j in range(slots):
            code = codes[shift, 0, j].astype(jnp.int32)
            order[n + 1 + shift * slots + j] = jnp.maximum(code, 0)
            order[found] = shift * slots + j
            found = found + (code >= 0).astype(jnp.int32)
            g = geo[jnp.maximum(code, 0)]
            for k in range(4):
                row = k * n + shift * slots + j
                sgeo[row : row + 1, :] = g[k : k + 1]
    tpoints = [
        jnp.concatenate([p[k * slots : (k + 1) * slots, :] for p in packs], axis=0) for k in range(5)
    ]
    spoints = [sgeo[k * n : (k + 1) * n, :] for k in range(4)]
    centre, inv = frame([tpoints, spoints])
    left, _, _ = split_features(tpoints, centre, inv)
    _, right, _ = split_features(spoints, centre, inv)
    store_features(fa, left)
    store_features(fb, right)
    tq[...] = tpoints[4]

    def begin(i, dist):
        slot = order[jnp.minimum(i, jnp.maximum(found - 1, 0))]
        distances(load_features(fa, slot), load_features(fb, slot), dist)

    def finish(i, dist):
        ok = i < found
        slot = order[jnp.minimum(i, jnp.maximum(found - 1, 0))]
        source = order[n + 1 + slot]
        back = tile_sums(
            dist, q[pl.ds(source, 1), :], tq[pl.ds(slot, 1), :], fwdt, jnp.where(ok, slot, -1)
        )
        acc[pl.ds(source, 1), :] += jnp.where(ok, back, 0.0)

    pipeline(found, begin, finish, ring)
    acc_out[...] = acc[...] * inv
    fwd = (fwdt[...] * inv).T
    rank = up.shape[1]
    for shift in range(C - 1):
        sends[shift][:slots, :] = fwd[shift * slots : (shift + 1) * slots, :]
        sends[shift][slots:, :] = jnp.zeros((up.shape[0], L), F32)
        sends[shift][slots:, :rank] = up[...]


def local_kernel(
    sizes, geo, pairs, targets, far_list, coupling, transfer, parent, up, acc_in, *rest
):
    C, S, L, R, slots, clusters, panels = sizes
    pieces = rest[:S]
    sums = rest[S : S + C - 1]
    parts = rest[S + C - 1 : 2 * S + C - 1]
    q, acc, acct, fa0, fa1, fb0, fb1, rads, got, parents, rows, *ring = rest[2 * S + C - 1 :]
    fa, fb = (fa0, fa1), (fb0, fb1)
    me, sub, rep = lax.axis_index("clu"), lax.axis_index("sub"), lax.axis_index("rep")
    assemble(sub, S, L, q, pieces)
    acc[...] = jnp.zeros_like(acc)
    acct[...] = jnp.zeros_like(acct)
    points = [geo[:, k, :] for k in range(4)]
    centre, inv = frame([points])
    left, right, rad = split_features(points, centre, inv)
    store_features(fa, left)
    store_features(fb, right)
    rads[...] = rad

    half = panels // 2
    share = clusters // (S * R)
    first = (rep * S + sub) * share

    def begin_self(i, dist):
        c = first + jnp.minimum(i, share - 1)
        a = load_features(fa, c)
        b = load_features(fb, c)
        dist[:half, :] = contract(a[0].T, jnp.concatenate(b, axis=1))
        dist[half:, half:] = contract(a[1].T, b[1])

    def finish_self(i, dist):
        c = first + i
        qrow = q[pl.ds(c, 1), :]
        qcol = upright(qrow[:, :half])
        radius = rads[pl.ds(c, 1), :]
        diag = lax.rsqrt(2.0 * (radius * radius))
        back = [jnp.zeros((8, LANES), F32)]

        def eye(span):
            shape = (span.stop - span.start, half)
            row = lax.broadcasted_iota(jnp.int32, shape, 0) + span.start % half
            return row == lax.broadcasted_iota(jnp.int32, shape, 1)

        def root(span, _):
            if span.start < half:
                return (
                    jnp.where(eye(span), diag[:, :half], inverse_root(dist[span, :half])),
                    inverse_root(dist[span, half:]),
                )
            return (jnp.where(eye(span), diag[:, half:], inverse_root(dist[span, half:])),)

        def sums(span, held):
            if span.start < half:
                g0, g1 = held
                back[0] = back[0] + fold(g1 * qcol[span, :])
                part = g0 * qrow[:, :half] + g1 * qrow[:, half:]
            else:
                part = held[0] * qrow[:, half:]
            return jnp.sum(part, axis=1, keepdims=True)

        def store(span, held):
            put_column(acct, span, i, held)

        staged(spans_of(panels), root, sums, store)
        back = jnp.sum(back[0], axis=0, keepdims=True)
        acc[pl.ds(c, 1), :] += jnp.concatenate([jnp.zeros_like(back), back], axis=1)

    pipeline(share, begin_self, finish_self, ring[: ring_size(share)])

    count = pairs.shape[1] // S
    start = sub * count

    def begin(i, dist):
        p = start + jnp.minimum(i, count - 1)
        distances(load_features(fa, pairs[0, p]), load_features(fb, pairs[1, p]), dist)

    def finish(i, dist):
        ia, ib = pairs[0, start + i], pairs[1, start + i]
        acc[pl.ds(ib, 1), :] += tile_sums(
            dist, q[pl.ds(ib, 1), :], q[pl.ds(ia, 1), :], acct, share + i
        )

    pipeline(count, begin, finish, ring[: ring_size(count)])
    rows[...] = acct[...].T
    for i in range(share):
        acc[pl.ds(first + i, 1), :] += rows[i : i + 1, :]
    for i in range(count):
        acc[pl.ds(pairs[0, start + i], 1), :] += rows[share + i : share + i + 1, :]
    total = acc_in[...] + acc[...] * inv

    got[...] = jnp.zeros_like(got)
    for shift in range(1, C):
        dest = lax.rem(me + shift, C)
        for j in range(slots):
            got[pl.ds(targets[dest, j], 1), :] += sums[shift - 1][j : j + 1, :]

    par_dev, far_n, rank = coupling.shape[0], coupling.shape[1], coupling.shape[2]
    parents[pl.ds(pl.multiple_of(me * par_dev, 8), par_dev), :] = up[...]
    for shift in range(1, C):
        owner = lax.rem(me + shift, C)
        parents[pl.ds(pl.multiple_of(owner * par_dev, 8), par_dev), :] = sums[shift - 1][slots:, :rank]
    lane = lax.broadcasted_iota(jnp.int32, (rank, LANES), 1)
    field = jnp.zeros((rank, LANES), F32)
    for p in range(par_dev):
        part = jnp.zeros((rank, rank), F32)
        for k in range(far_n):
            part = part + coupling[p, k] * parents[pl.ds(far_list[k, p], 1), :]
        field = jnp.where(lane == p, jnp.sum(part, axis=1, keepdims=True), field)
    which = lax.broadcasted_iota(jnp.int32, (LANES, clusters), 0)
    onehot = (parent[...] == which).astype(F32)
    down = jnp.dot(field, onehot, precision=HIGHEST, preferred_element_type=F32)
    fields = jnp.concatenate(
        [jnp.sum(transfer[r] * down, axis=0, keepdims=True) for r in range(rank)], axis=0
    )

    def give(s):
        for shift in range(S):
            other = (s + shift) % S
            part = total[:, other * L : (other + 1) * L]
            parts[shift][:clusters, :] = part + got[...] if shift == 0 else part
            for t in range(clusters // L):
                at = clusters + t * rank
                parts[shift][at : at + rank, :] = fields[:, t * L : (t + 1) * L]

    for s in range(S):
        pl.when(sub == s)(functools.partial(give, s))


def up_kernel(basis, masked, transfer, parent, up):
    clusters = basis.shape[0]
    rank = basis.shape[1]
    lane = lax.broadcasted_iota(jnp.int32, (rank, clusters), 1)
    leaf = jnp.zeros((rank, clusters), F32)
    for c in range(clusters):
        part = jnp.sum(basis[c] * masked[c : c + 1, :], axis=1, keepdims=True)
        leaf = jnp.where(lane == c, part, leaf)
    lifted = jnp.zeros((rank, clusters), F32)
    for r in range(rank):
        lifted = lifted + transfer[r] * leaf[r : r + 1, :]
    which = lax.broadcasted_iota(jnp.int32, (up.shape[0], clusters), 0)
    onehot = (parent[...] == which).astype(F32)
    up[...] = lax.dot_general(
        onehot, lifted, (((1,), (1,)), ((), ())), precision=HIGHEST, preferred_element_type=F32
    )


def final_kernel(sizes, mask, basis, *rest):
    S, R, L = sizes
    near, out = rest[: S * R], rest[-1]
    clusters, rank = basis.shape[0], basis.shape[1]
    fields = []
    for t in range(clusters // L):
        rows = slice(clusters + t * rank, clusters + (t + 1) * rank)
        fields.append(sum(near[d * R][rows, :] for d in range(1, S)) + near[0][rows, :])
    fields = jnp.concatenate(fields, axis=1) if len(fields) > 1 else fields[0]
    for c in range(clusters):
        out[c : c + 1, :] = jnp.sum(basis[c] * fields[:, c : c + 1], axis=0, keepdims=True)
    total = out[...]
    for part in near:
        total = total + part[:clusters, :]
    out[...] = total * mask[...].astype(F32)


def send(value, moves):
    names = tuple(name for name, _ in moves)
    steps = [step for _, step in moves]
    sizes = [lax.axis_size(name) for name in names]
    perm = []

    def flat(coords):
        index = 0
        for size, c in zip(sizes, coords):
            index = index * size + c
        return index

    total = 1
    for size in sizes:
        total *= size
    for index in range(total):
        coords, left = [], index
        for size in reversed(sizes):
            coords.append(left % size)
            left //= size
        coords.reverse()
        perm.append((index, flat([(c + s) % n for c, s, n in zip(coords, steps, sizes)])))
    return lax.ppermute(value, names if len(names) > 1 else names[0], perm)


def on_device(
    charges,
    panel_mask,
    geometry,
    remote_source,
    remote_target,
    remote_live,
    local_pairs,
    basis,
    transfer,
    parent_of,
    far_list,
    coupling,
):
    clusters, L = charges.shape
    panels = geometry.shape[2]
    C, S, R = lax.axis_size("clu"), lax.axis_size("sub"), lax.axis_size("rep")
    slots = remote_source.shape[2]
    par_dev, rank = far_list.shape[0], transfer.shape[1]
    n = (C - 1) * slots
    shape = jax.ShapeDtypeStruct
    targets = remote_target[0]
    basis_t = jnp.transpose(basis, (0, 2, 1))
    transfer_t = jnp.transpose(transfer, (1, 2, 0))
    parent = parent_of[None, :]

    made = pl.pallas_call(
        functools.partial(pack_kernel, (C, S, L, slots)),
        out_shape=[pltpu.VMEM((clusters, L), F32)] + [pltpu.VMEM((5 * slots + 8, L), F32)] * (C - 1),
        in_specs=[vmem()] * 3 + [smem()] * 3,
        out_specs=[vmem()] * C,
        compiler_params=PARAMS,
        name="packs",
    )(*near_by(charges, panel_mask, geometry), targets, remote_source[0], remote_live[0])
    masked, packs = made[0], made[1:]
    pieces = [masked] + [send(masked, (("sub", d),)) for d in range(1, S)]
    packs = [send(packs[d - 1], (("clu", d),)) for d in range(1, C)]

    up = pl.pallas_call(
        up_kernel,
        out_shape=pltpu.VMEM((par_dev, rank), F32),
        in_specs=[vmem()] * 4,
        out_specs=vmem(),
        compiler_params=PARAMS,
        name="far_up",
    )(*near_by(basis_t, masked, transfer_t, parent))

    made = pl.pallas_call(
        functools.partial(remote_kernel, (C, S, L, slots, clusters, panels)),
        out_shape=[pltpu.VMEM((clusters, panels), F32)]
        + [pltpu.VMEM((slots + par_dev, L), F32)] * (C - 1),
        in_specs=[vmem()] * (2 + S + C - 1),
        out_specs=[vmem()] * C,
        scratch_shapes=[
            pltpu.VMEM((clusters, panels), F32),
            pltpu.VMEM((n, L), F32),
            pltpu.VMEM((clusters, panels), F32),
            pltpu.VMEM((L, whole(n)), F32),
            pltpu.VMEM((4 * n, panels), F32),
            pltpu.VMEM((n * ROWS, L), F32),
            pltpu.VMEM((n * ROWS, LANES), F32),
            pltpu.VMEM((n * ROWS, LANES), F32),
            pltpu.SMEM((2 * n + 1,), jnp.int32),
            pltpu.SMEM((C - 1, 8, L), F32),
            pltpu.SemaphoreType.DMA((C - 1,)),
        ]
        + [pltpu.VMEM((L, panels), F32)] * 8,
        compiler_params=PARAMS,
        name="near_remote",
    )(*near_by(geometry, up, *pieces, *packs))
    acc, sums = made[0], [send(made[d], (("clu", C - d),)) for d in range(1, C)]

    columns = whole(clusters // (S * R) + local_pairs.shape[1] // S)
    half = [pltpu.VMEM((clusters * ROWS, LANES), F32)] * 2
    parts = pl.pallas_call(
        functools.partial(local_kernel, (C, S, L, R, slots, clusters, panels)),
        out_shape=[pltpu.VMEM((clusters + clusters // L * rank, L), F32)] * S,
        in_specs=[vmem()] + [smem()] * 3 + [vmem()] * (5 + S + C - 1),
        out_specs=[vmem()] * S,
        scratch_shapes=[
            pltpu.VMEM((clusters, panels), F32),
            pltpu.VMEM((clusters, panels), F32),
            pltpu.VMEM((panels, columns), F32),
            *half,
            *half,
            pltpu.VMEM((clusters, panels), F32),
            pltpu.VMEM((clusters, L), F32),
            pltpu.VMEM((C * par_dev, rank), F32),
            pltpu.VMEM((columns, panels), F32),
        ]
        + [pltpu.VMEM((panels, panels), F32)] * 16,
        compiler_params=PARAMS,
        name="near_local",
    )(
        *near_by(geometry),
        local_pairs[0].T,
        targets,
        far_list.T,
        *near_by(coupling, transfer_t, parent, up, acc, *pieces, *sums),
    )
    near = []
    for d in range(S):
        for e in range(R):
            near.append(send(parts[d], (("sub", d), ("rep", e))) if d or e else parts[0])

    return pl.pallas_call(
        functools.partial(final_kernel, (S, R, L)),
        out_shape=shape((clusters, L), F32),
        in_specs=[vmem()] * (2 + S * R),
        out_specs=vmem(),
        compiler_params=PARAMS,
        name="combine",
    )(*near_by(panel_mask, basis_t, *near))


def solution(mesh):
    placed = (
        P(("grp", "clu"), "sub"),
        P(("grp", "clu"), "sub"),
        P(("grp", "clu"), None, None),
        P(("grp", "clu"), None, "rep"),
        P(("grp", "clu"), None, "rep"),
        P(("grp", "clu"), None, "rep"),
        P(("grp", "clu"), "rep", None),
        P(("grp", "clu"), "sub", None),
        P(("grp", "clu"), None, None),
        P(("grp", "clu")),
        P(("grp", "clu"), None),
        P(("grp", "clu"), None, None, None),
    )
    return jax.shard_map(
        on_device, mesh=mesh, in_specs=placed, out_specs=P(("grp", "clu"), "sub"), check_vma=False
    )
```

```python
import functools

import jax
import jax.numpy as jnp
from jax import lax
from jax.experimental import pallas as pl
from jax.experimental.pallas import tpu as pltpu
from jax.sharding import PartitionSpec as P

F32 = jnp.float32
BF16 = jnp.bfloat16
HIGHEST = lax.Precision.HIGHEST
ROWS = 40
USED = 34
LANES = 128


def limit(mib):
    return pltpu.CompilerParams(vmem_limit_bytes=mib * 1024 * 1024)


def about(us):
    return pl.CostEstimate(flops=0, bytes_accessed=int(us * 3.5e6), transcendentals=0)


def vmem():
    return pl.BlockSpec(memory_space=pltpu.VMEM)


def near_by(*arrays):
    return [pltpu.with_memory_space_constraint(x, pltpu.VMEM) for x in arrays]


def smem():
    return pl.BlockSpec(memory_space=pltpu.SMEM)


def whole(size):
    return -(-size // LANES) * LANES


def cut(v):
    return v.astype(BF16).astype(F32)


def powers(sign):
    lane = lax.broadcasted_iota(jnp.int32, (8, LANES), 1)
    out = jnp.full((8, LANES), 2.0 ** (-64 * sign), F32)
    for bit in range(7):
        out = out * jnp.where((lane >> bit) & 1 == 1, F32(2.0 ** (sign * 2**bit)), F32(1.0))
    return out


def frame(parts):
    low = [functools.reduce(jnp.minimum, [jnp.min(p[k]) for p in parts]) for k in range(3)]
    high = [functools.reduce(jnp.maximum, [jnp.max(p[k]) for p in parts]) for k in range(3)]
    width = functools.reduce(jnp.maximum, [jnp.max(jnp.abs(p[3])) for p in parts])
    for lo, hi in zip(low, high):
        width = jnp.maximum(width, 0.5 * (hi - lo))
    up, down = powers(1), powers(-1)
    size = jnp.min(jnp.where(up >= width, up, F32(2.0**63)))
    inv = jnp.max(jnp.where(up >= width, down, F32(2.0**-63)))
    magic = size * F32(1.5 * 2.0**20)
    centre = [(0.5 * (lo + hi) + magic) - magic for lo, hi in zip(low, high)]
    return centre, inv


def split_features(points, centre, inv):
    magic = F32(1.5 * 2.0**16)
    grid, rest = [], []
    for k in range(3):
        u = (points[k] - centre[k]) * inv
        h = (u + magic) - magic
        grid.append(h)
        rest.append(u - h)
    rad = points[3] * inv
    norm = grid[0] * grid[0] + grid[1] * grid[1] + grid[2] * grid[2]
    norm1 = cut(norm)
    norm2 = norm - norm1
    cross = grid[0] * rest[0] + grid[1] * rest[1] + grid[2] * rest[2]
    extra = 2.0 * cross + (rest[0] * rest[0] + rest[1] * rest[1] + rest[2] * rest[2]) + rad * rad
    extra1 = cut(extra)
    extra2 = cut(extra - extra1)
    extra3 = (extra - extra1) - extra2
    rest1 = [cut(v) for v in rest]
    rest2 = [v - w for v, w in zip(rest, rest1)]
    neg = lambda vs: [-2.0 * v for v in vs]
    one = jnp.ones_like(rad)
    left = grid + [norm1, norm2, one, one]
    right = neg(grid) + [one, one, norm1, norm2]
    left += [extra1, extra2, extra3, one, one, one]
    right += [one, one, one, extra1, extra2, extra3]
    left += grid + grid + rest1 + rest2 + rest1 + rest1 + rest2
    right += neg(rest1) + neg(rest2) + neg(grid) + neg(grid) + neg(rest1) + neg(rest2) + neg(rest1)
    return left, right, rad


def store_features(ref, rows):
    count = rows[0].shape[0]
    width = rows[0].shape[1]
    for k, row in enumerate(rows):
        for t, piece in enumerate(ref):
            piece[pl.ds(k, count, stride=ROWS), :] = row[:, t * LANES : min(width, (t + 1) * LANES)]


def load_features(ref, index):
    start = pl.multiple_of(index * ROWS, 8)
    return [piece[pl.ds(start, USED), :].astype(BF16) for piece in ref]


def contract(left, right):
    return jnp.dot(left, right, preferred_element_type=F32)


def select_rows(index, value, count):
    row = lax.broadcasted_iota(jnp.int32, (count, index.shape[1]), 0)
    left = jnp.where(row == index, 1.0, 0.0).astype(BF16)
    high = value.astype(BF16)
    rest = value - high.astype(F32)
    mid = rest.astype(BF16)
    low = (rest - mid.astype(F32)).astype(BF16)
    return jnp.dot(
        jnp.concatenate([left] * 3, axis=1),
        jnp.concatenate([high, mid, low], axis=0),
        preferred_element_type=F32,
    )


def upright(row):
    return jnp.broadcast_to(row, (8, row.shape[1])).T[:, :1]


def put_column(table, rows, index, value):
    shape = (rows.stop - rows.start, table.shape[1])
    lane = lax.broadcasted_iota(jnp.int32, shape, 1)
    pltpu.store(table.at[rows, :], jnp.broadcast_to(value, shape), mask=lane == index)


def inverse_root(d):
    return lax.rsqrt(d)


def fold(v):
    return jnp.sum(v.reshape(v.shape[0] // 8, 8, v.shape[1]), axis=0)


def distances(left, right, out):
    whole_left = jnp.concatenate(left, axis=1) if len(left) > 1 else left[0]
    out[...] = contract(whole_left.T, jnp.concatenate(right, axis=1))


def staged(spans, *stages):
    held = {}
    for t in range(len(spans) + len(stages) - 1):
        for depth in reversed(range(len(stages))):
            k = t - depth
            if 0 <= k < len(spans):
                held[k] = stages[depth](spans[k], held.get(k))
                if depth == len(stages) - 1:
                    del held[k]


def spans_of(height, step=32):
    step = min(step, height)
    return [slice(r, r + step) for r in range(0, height, step)]


def tile_sums(dist, qrow, qleft, table, index):
    q0, q1 = qrow[:, :LANES], qrow[:, LANES:]
    qcol = upright(qleft)
    back = [jnp.zeros((8, LANES), F32), jnp.zeros((8, LANES), F32)]

    def root(rows, _):
        return (
            inverse_root(dist[rows, :LANES]),
            inverse_root(dist[rows, LANES:]),
        )

    def sums(rows, held):
        g0, g1 = held
        back[0] = back[0] + fold(g0 * qcol[rows, :])
        back[1] = back[1] + fold(g1 * qcol[rows, :])
        return jnp.sum(g0 * q0 + g1 * q1, axis=1, keepdims=True)

    def store(rows, held):
        put_column(table, rows, index, held)

    staged(spans_of(dist.shape[0]), root, sums, store)
    return jnp.concatenate([jnp.sum(b, axis=0, keepdims=True) for b in back], axis=1)


def pipeline(total, begin, finish, ring):
    size = len(ring)
    ahead = min(2, size - 1)

    def body(i, carry):
        for k in range(size):
            begin(i * size + k + ahead, ring[(k + ahead) % size])
            finish(i * size + k, ring[k])
        return carry

    for k in range(ahead):
        begin(k, ring[k])
    lax.fori_loop(0, (total + size - 1) // size, body, 0)


def ring_size(total):
    return next(size for size in (16, 8, 4, 2, 1) if total % size == 0)


def assemble(sub, S, L, q, pieces):
    def place(s):
        for shift in range(S):
            owner = (s - shift) % S
            q[:, owner * L : (owner + 1) * L] = pieces[shift][...]

    for s in range(S):
        pl.when(sub == s)(functools.partial(place, s))


def pack_kernel(sizes, charges, mask, geo, targets, sources, live, masked, *packs):
    C, S, L, slots = sizes
    me, sub = lax.axis_index("clu"), lax.axis_index("sub")
    masked[...] = charges[...] * mask[...].astype(F32)
    lane = lax.broadcasted_iota(jnp.int32, (8, L), 1)
    for shift in range(1, C):
        dest = lax.rem(me + shift, C)
        codes = jnp.full((8, L), -1.0, F32)
        for j in range(slots):
            code = jnp.where(live[dest, j] > 0, sources[dest, j], -1)
            codes = jnp.where(lane == j, code.astype(F32), codes)
        packs[shift - 1][5 * slots :, :] = codes

    def fill(s):
        for shift in range(1, C):
            dest = lax.rem(me + shift, C)
            pack = packs[shift - 1]
            for j in range(slots):
                t = targets[dest, j]
                g = geo[t, :, s * L : (s + 1) * L]
                for k in range(4):
                    pack[k * slots + j : k * slots + j + 1, :] = g[k : k + 1]
                pack[4 * slots + j : 4 * slots + j + 1, :] = masked[pl.ds(t, 1), :]

    for s in range(S):
        pl.when(sub == s)(functools.partial(fill, s))


def remote_kernel(sizes, geo, up, *rest):
    C, S, L, slots, clusters, panels = sizes
    pieces = rest[:S]
    packs = rest[S : S + C - 1]
    acc_out = rest[S + C - 1]
    sends = rest[S + C : S + C + C - 1]
    q, tq, acc, fwdt, sgeo, fa0, fb0, fb1, order, codes, sems, *ring = rest[S + C + C - 1 :]
    fa, fb = (fa0,), (fb0, fb1)
    n = (C - 1) * slots
    copies = [
        pltpu.make_async_copy(packs[k].at[pl.ds(5 * slots, 8), :], codes.at[k], sems.at[k])
        for k in range(C - 1)
    ]
    for copy in copies:
        copy.start()
    assemble(lax.axis_index("sub"), S, L, q, pieces)
    acc[...] = jnp.zeros_like(acc)
    fwdt[...] = jnp.zeros_like(fwdt)
    for copy in copies:
        copy.wait()
    found = jnp.int32(0)
    for shift in range(C - 1):
        for j in range(slots):
            code = codes[shift, 0, j].astype(jnp.int32)
            order[n + 1 + shift * slots + j] = jnp.maximum(code, 0)
            order[found] = shift * slots + j
            found = found + (code >= 0).astype(jnp.int32)
            g = geo[jnp.maximum(code, 0)]
            for k in range(4):
                row = k * n + shift * slots + j
                sgeo[row : row + 1, :] = g[k : k + 1]
    tpoints = [
        jnp.concatenate([p[k * slots : (k + 1) * slots, :] for p in packs], axis=0) for k in range(5)
    ]
    spoints = [sgeo[k * n : (k + 1) * n, :] for k in range(4)]
    centre, inv = frame([tpoints, spoints])
    left, _, _ = split_features(tpoints, centre, inv)
    _, right, _ = split_features(spoints, centre, inv)
    store_features(fa, left)
    store_features(fb, right)
    tq[...] = tpoints[4]

    def begin(i, dist):
        slot = order[jnp.minimum(i, jnp.maximum(found - 1, 0))]
        distances(load_features(fa, slot), load_features(fb, slot), dist)

    def finish(i, dist):
        ok = i < found
        slot = order[jnp.minimum(i, jnp.maximum(found - 1, 0))]
        source = order[n + 1 + slot]
        back = tile_sums(
            dist, q[pl.ds(source, 1), :], tq[pl.ds(slot, 1), :], fwdt, jnp.where(ok, slot, -1)
        )
        acc[pl.ds(source, 1), :] += jnp.where(ok, back, 0.0)

    pipeline(found, begin, finish, ring)
    acc_out[...] = acc[...] * inv
    fwd = (fwdt[...] * inv).T
    rank = up.shape[1]
    for shift in range(C - 1):
        sends[shift][:slots, :] = fwd[shift * slots : (shift + 1) * slots, :]
        sends[shift][slots:, :] = jnp.zeros((up.shape[0], L), F32)
        sends[shift][slots:, :rank] = up[...]


def feature_kernel(geo, fa0, fa1, fb0, fb1, diag, scale):
    points = [geo[:, k, :] for k in range(4)]
    centre, inv = frame([points])
    left, right, rad = split_features(points, centre, inv)
    store_features((fa0, fa1), left)
    store_features((fb0, fb1), right)
    diag[...] = lax.rsqrt(2.0 * (rad * rad))
    scale[...] = jnp.full(scale.shape, inv, F32)


def local_kernel(sizes, geo_pairs, pairs, fa0, fa1, fb0, fb1, diags, scale, acc_in, *rest):
    S, L, R, clusters, panels = sizes
    pieces = rest[:S]
    acc_out, q, acc, self_sums, pair_sums, *ring = rest[S:]
    fa, fb = (fa0, fa1), (fb0, fb1)
    sub, rep = lax.axis_index("sub"), lax.axis_index("rep")
    assemble(sub, S, L, q, pieces)
    acc[...] = jnp.zeros_like(acc)
    self_sums[...] = jnp.zeros_like(self_sums)
    pair_sums[...] = jnp.zeros_like(pair_sums)

    half = panels // 2
    share = clusters // (S * R)
    first = (rep * S + sub) * share

    def begin_self(i, dist):
        c = first + jnp.minimum(i, share - 1)
        a = load_features(fa, c)
        b = load_features(fb, c)
        dist[:half, :] = contract(a[0].T, jnp.concatenate(b, axis=1))
        dist[half:, half:] = contract(a[1].T, b[1])

    def finish_self(i, dist):
        c = first + i
        qrow = q[pl.ds(c, 1), :]
        qcol = upright(qrow[:, :half])
        diag = diags[pl.ds(c, 1), :]
        back = [jnp.zeros((8, LANES), F32)]

        def eye(span):
            shape = (span.stop - span.start, half)
            row = lax.broadcasted_iota(jnp.int32, shape, 0) + span.start % half
            return row == lax.broadcasted_iota(jnp.int32, shape, 1)

        def root(span, _):
            if span.start < half:
                return (
                    jnp.where(eye(span), diag[:, :half], inverse_root(dist[span, :half])),
                    inverse_root(dist[span, half:]),
                )
            return (jnp.where(eye(span), diag[:, half:], inverse_root(dist[span, half:])),)

        def sums(span, held):
            if span.start < half:
                g0, g1 = held
                back[0] = back[0] + fold(g1 * qcol[span, :])
                part = g0 * qrow[:, :half] + g1 * qrow[:, half:]
            else:
                part = held[0] * qrow[:, half:]
            return jnp.sum(part, axis=1, keepdims=True)

        def store(span, held):
            put_column(self_sums, span, c, held)

        staged(spans_of(panels), root, sums, store)
        back = jnp.sum(back[0], axis=0, keepdims=True)
        acc[pl.ds(c, 1), :] += jnp.concatenate([jnp.zeros_like(back), back], axis=1)

    pipeline(share, begin_self, finish_self, ring[: ring_size(share)])

    count = pairs.shape[1] // S
    start = sub * count

    def begin(i, dist):
        p = start + jnp.minimum(i, count - 1)
        distances(load_features(fa, pairs[0, p]), load_features(fb, pairs[1, p]), dist)

    def finish(i, dist):
        ia, ib = pairs[0, start + i], pairs[1, start + i]
        acc[pl.ds(ib, 1), :] += tile_sums(
            dist, q[pl.ds(ib, 1), :], q[pl.ds(ia, 1), :], pair_sums, start + i
        )

    pipeline(count, begin, finish, ring[: ring_size(count)])
    total = acc[...] + self_sums[...].T
    width = geo_pairs.shape[1]
    total = total + select_rows(geo_pairs[0:1, :], pair_sums[...].T[:width, :], clusters)
    acc_out[...] = acc_in[...] + total * scale[0:1, 0:1]


def merge_kernel(sizes, far_list, targets, near, coupling, transfer, parent, up, *rest):
    C, S, L, slots, clusters = sizes
    sums = rest[: C - 1]
    parts = rest[C - 1 : C - 1 + S]
    parents = rest[-1]
    me, sub = lax.axis_index("clu"), lax.axis_index("sub")
    index = [targets[pl.ds(lax.rem(me + shift, C), 1), :] for shift in range(1, C)]
    got = select_rows(
        jnp.concatenate(index, axis=1), jnp.concatenate([v[:slots, :] for v in sums], axis=0), clusters
    )

    par_dev, far_n, rank = coupling.shape[0], coupling.shape[1], coupling.shape[2]
    parents[pl.ds(pl.multiple_of(me * par_dev, 8), par_dev), :] = up[...]
    for shift in range(1, C):
        owner = lax.rem(me + shift, C)
        parents[pl.ds(pl.multiple_of(owner * par_dev, 8), par_dev), :] = sums[shift - 1][slots:, :rank]
    lane = lax.broadcasted_iota(jnp.int32, (rank, LANES), 1)
    field = jnp.zeros((rank, LANES), F32)
    for p in range(par_dev):
        part = jnp.zeros((rank, rank), F32)
        for k in range(far_n):
            part = part + coupling[p, k] * parents[pl.ds(far_list[k, p], 1), :]
        field = jnp.where(lane == p, jnp.sum(part, axis=1, keepdims=True), field)
    which = lax.broadcasted_iota(jnp.int32, (LANES, clusters), 0)
    onehot = (parent[...] == which).astype(F32)
    down = jnp.dot(field, onehot, precision=HIGHEST, preferred_element_type=F32)
    fields = jnp.concatenate(
        [jnp.sum(transfer[r] * down, axis=0, keepdims=True) for r in range(rank)], axis=0
    )

    def give(s):
        for shift in range(S):
            other = (s + shift) % S
            part = near[:, other * L : (other + 1) * L]
            parts[shift][:clusters, :] = part + got if shift == 0 else part
            for t in range(clusters // L):
                at = clusters + t * rank
                parts[shift][at : at + rank, :] = fields[:, t * L : (t + 1) * L]

    for s in range(S):
        pl.when(sub == s)(functools.partial(give, s))


def up_kernel(basis, masked, transfer, parent, after, up):
    del after
    clusters = basis.shape[0]
    rank = basis.shape[1]
    lane = lax.broadcasted_iota(jnp.int32, (rank, clusters), 1)
    leaf = jnp.zeros((rank, clusters), F32)
    for c in range(clusters):
        part = jnp.sum(basis[c] * masked[c : c + 1, :], axis=1, keepdims=True)
        leaf = jnp.where(lane == c, part, leaf)
    lifted = jnp.zeros((rank, clusters), F32)
    for r in range(rank):
        lifted = lifted + transfer[r] * leaf[r : r + 1, :]
    which = lax.broadcasted_iota(jnp.int32, (up.shape[0], clusters), 0)
    onehot = (parent[...] == which).astype(F32)
    up[...] = lax.dot_general(
        onehot, lifted, (((1,), (1,)), ((), ())), precision=HIGHEST, preferred_element_type=F32
    )


def far_kernel(basis, near, out):
    clusters, rank = basis.shape[0], basis.shape[1]
    L = out.shape[1]
    fields = [near[clusters + t * rank : clusters + (t + 1) * rank, :] for t in range(clusters // L)]
    fields = jnp.concatenate(fields, axis=1) if len(fields) > 1 else fields[0]
    for c in range(clusters):
        far = jnp.sum(basis[c] * fields[:, c : c + 1], axis=0, keepdims=True)
        out[c : c + 1, :] = far + near[c : c + 1, :]


def send(value, moves):
    names = tuple(name for name, _ in moves)
    steps = [step for _, step in moves]
    sizes = [lax.axis_size(name) for name in names]
    perm = []

    def flat(coords):
        index = 0
        for size, c in zip(sizes, coords):
            index = index * size + c
        return index

    total = 1
    for size in sizes:
        total *= size
    for index in range(total):
        coords, left = [], index
        for size in reversed(sizes):
            coords.append(left % size)
            left //= size
        coords.reverse()
        perm.append((index, flat([(c + s) % n for c, s, n in zip(coords, steps, sizes)])))
    return lax.ppermute(value, names if len(names) > 1 else names[0], perm)


def on_device(
    charges,
    panel_mask,
    geometry,
    remote_source,
    remote_target,
    remote_live,
    local_pairs,
    basis,
    transfer,
    parent_of,
    far_list,
    coupling,
):
    clusters, L = charges.shape
    panels = geometry.shape[2]
    C, S, R = lax.axis_size("clu"), lax.axis_size("sub"), lax.axis_size("rep")
    slots = remote_source.shape[2]
    par_dev, rank = far_list.shape[0], transfer.shape[1]
    n = (C - 1) * slots
    shape = jax.ShapeDtypeStruct
    targets = remote_target[0]
    basis_t = jnp.transpose(basis, (0, 2, 1))
    transfer_t = jnp.transpose(transfer, (1, 2, 0))
    parent = parent_of[None, :]

    made = pl.pallas_call(
        functools.partial(pack_kernel, (C, S, L, slots)),
        out_shape=[pltpu.VMEM((clusters, L), F32)] + [pltpu.VMEM((5 * slots + 8, L), F32)] * (C - 1),
        in_specs=[vmem()] * 3 + [smem()] * 3,
        out_specs=[vmem()] * C,
        compiler_params=limit(60),
        cost_estimate=about(2),
        name="packs",
    )(charges, panel_mask, geometry, targets, remote_source[0], remote_live[0])
    masked, packs = made[0], made[1:]
    pieces = [masked] + [send(masked, (("sub", d),)) for d in range(1, S)]
    packs = [send(packs[d - 1], (("clu", d),)) for d in range(1, C)]

    features = pl.pallas_call(
        feature_kernel,
        out_shape=[pltpu.VMEM((clusters * ROWS, LANES), F32)] * 4
        + [pltpu.VMEM((clusters, panels), F32), pltpu.VMEM((8, LANES), F32)],
        in_specs=[vmem()],
        out_specs=[vmem()] * 6,
        compiler_params=limit(32),
        cost_estimate=about(4),
        name="features",
    )(*near_by(geometry))

    up = pl.pallas_call(
        up_kernel,
        out_shape=pltpu.VMEM((par_dev, rank), F32),
        in_specs=[vmem()] * 5,
        out_specs=vmem(),
        compiler_params=limit(16),
        cost_estimate=about(1),
        name="far_up",
    )(*near_by(basis_t, masked, transfer_t, parent, features[5]))

    made = pl.pallas_call(
        functools.partial(remote_kernel, (C, S, L, slots, clusters, panels)),
        out_shape=[pltpu.VMEM((clusters, panels), F32)]
        + [pltpu.VMEM((slots + par_dev, L), F32)] * (C - 1),
        in_specs=[vmem()] * (2 + S + C - 1),
        out_specs=[vmem()] * C,
        scratch_shapes=[
            pltpu.VMEM((clusters, panels), F32),
            pltpu.VMEM((n, L), F32),
            pltpu.VMEM((clusters, panels), F32),
            pltpu.VMEM((L, whole(n)), F32),
            pltpu.VMEM((4 * n, panels), F32),
            pltpu.VMEM((n * ROWS, L), F32),
            pltpu.VMEM((n * ROWS, LANES), F32),
            pltpu.VMEM((n * ROWS, LANES), F32),
            pltpu.SMEM((2 * n + 1,), jnp.int32),
            pltpu.SMEM((C - 1, 8, L), F32),
            pltpu.SemaphoreType.DMA((C - 1,)),
        ]
        + [pltpu.VMEM((L, panels), F32)] * 8,
        compiler_params=limit(24),
        cost_estimate=about(6),
        name="near_remote",
    )(*near_by(geometry, up, *pieces, *packs))
    acc, sums = made[0], [send(made[d], (("clu", C - d),)) for d in range(1, C)]

    wide = whole(local_pairs.shape[1])
    acc = pl.pallas_call(
        functools.partial(local_kernel, (S, L, R, clusters, panels)),
        out_shape=pltpu.VMEM((clusters, panels), F32),
        in_specs=[vmem(), smem()] + [vmem()] * (7 + S),
        out_specs=vmem(),
        scratch_shapes=[
            pltpu.VMEM((clusters, panels), F32),
            pltpu.VMEM((clusters, panels), F32),
            pltpu.VMEM((panels, clusters), F32),
            pltpu.VMEM((panels, wide), F32),
        ]
        + [pltpu.VMEM((panels, panels), F32)] * 16,
        compiler_params=limit(24),
        cost_estimate=about(15),
        name="near_local",
    )(*near_by(local_pairs[0].T), local_pairs[0].T, *near_by(*features, acc, *pieces))

    parts = pl.pallas_call(
        functools.partial(merge_kernel, (C, S, L, slots, clusters)),
        out_shape=[pltpu.VMEM((clusters + clusters // L * rank, L), F32)] * S,
        in_specs=[smem()] + [vmem()] * (6 + C - 1),
        out_specs=[vmem()] * S,
        scratch_shapes=[pltpu.VMEM((C * par_dev, rank), F32)],
        compiler_params=limit(16),
        cost_estimate=about(2),
        name="merge",
    )(far_list.T, *near_by(targets, acc, coupling, transfer_t, parent, up, *sums))
    near = parts[0]
    for d in range(1, S):
        near = near + send(parts[d], (("sub", d),))
    others = [send(near, (("rep", e),)) for e in range(1, R)]

    total = pl.pallas_call(
        far_kernel,
        out_shape=pltpu.VMEM((clusters, L), F32),
        in_specs=[vmem()] * 2,
        out_specs=vmem(),
        compiler_params=limit(16),
        cost_estimate=about(1),
        name="far_down",
    )(*near_by(basis_t, near))
    for other in others:
        total = total + other[:clusters]
    return total * panel_mask.astype(F32)


def solution(mesh):
    placed = (
        P(("grp", "clu"), "sub"),
        P(("grp", "clu"), "sub"),
        P(("grp", "clu"), None, None),
        P(("grp", "clu"), None, "rep"),
        P(("grp", "clu"), None, "rep"),
        P(("grp", "clu"), None, "rep"),
        P(("grp", "clu"), "rep", None),
        P(("grp", "clu"), "sub", None),
        P(("grp", "clu"), None, None),
        P(("grp", "clu")),
        P(("grp", "clu"), None),
        P(("grp", "clu"), None, None, None),
    )
    return jax.shard_map(
        on_device, mesh=mesh, in_specs=placed, out_specs=P(("grp", "clu"), "sub"), check_vma=False
    )
```

```python
import functools

import jax
import jax.numpy as jnp
from jax import lax
from jax.experimental import pallas as pl
from jax.experimental.pallas import tpu as pltpu
from jax.sharding import PartitionSpec as P

F32 = jnp.float32
BF16 = jnp.bfloat16
HIGHEST = lax.Precision.HIGHEST
ROWS = 24
LANES = 128


def limit(mib):
    return pltpu.CompilerParams(vmem_limit_bytes=mib * 1024 * 1024)


def about(us):
    return pl.CostEstimate(flops=0, bytes_accessed=int(us * 3.5e6), transcendentals=0)


def vmem():
    return pl.BlockSpec(memory_space=pltpu.VMEM)


def near_by(*arrays):
    return [pltpu.with_memory_space_constraint(x, pltpu.VMEM) for x in arrays]


def smem():
    return pl.BlockSpec(memory_space=pltpu.SMEM)


def whole(size):
    return -(-size // LANES) * LANES


def cut(v):
    return v.astype(BF16).astype(F32)


def powers(sign):
    lane = lax.broadcasted_iota(jnp.int32, (8, LANES), 1)
    out = jnp.full((8, LANES), 2.0 ** (-64 * sign), F32)
    for bit in range(7):
        out = out * jnp.where((lane >> bit) & 1 == 1, F32(2.0 ** (sign * 2**bit)), F32(1.0))
    return out


def frame(parts):
    low = [functools.reduce(jnp.minimum, [jnp.min(p[k]) for p in parts]) for k in range(3)]
    high = [functools.reduce(jnp.maximum, [jnp.max(p[k]) for p in parts]) for k in range(3)]
    width = functools.reduce(jnp.maximum, [jnp.max(jnp.abs(p[3])) for p in parts])
    for lo, hi in zip(low, high):
        width = jnp.maximum(width, 0.5 * (hi - lo))
    up, down = powers(1), powers(-1)
    size = jnp.min(jnp.where(up >= width, up, F32(2.0**63)))
    inv = jnp.max(jnp.where(up >= width, down, F32(2.0**-63)))
    magic = size * F32(1.5 * 2.0**20)
    centre = [(0.5 * (lo + hi) + magic) - magic for lo, hi in zip(low, high)]
    return centre, inv


def split_features(points, centre, inv):
    magic = F32(1.5 * 2.0**16)
    grid, rest = [], []
    for k in range(3):
        u = (points[k] - centre[k]) * inv
        h = (u + magic) - magic
        grid.append(h)
        rest.append(u - h)
    rad = points[3] * inv
    norm = grid[0] * grid[0] + grid[1] * grid[1] + grid[2] * grid[2]
    norm1 = cut(norm)
    norm2 = norm - norm1
    cross = grid[0] * rest[0] + grid[1] * rest[1] + grid[2] * rest[2]
    extra = 2.0 * cross + (rest[0] * rest[0] + rest[1] * rest[1] + rest[2] * rest[2]) + rad * rad
    extra1 = cut(extra)
    extra2 = cut(extra - extra1)
    extra3 = (extra - extra1) - extra2
    rest1 = [cut(v) for v in rest]
    rest2 = [v - w for v, w in zip(rest, rest1)]
    neg = lambda vs: [-2.0 * v for v in vs]
    one, zero = jnp.ones_like(rad), jnp.zeros_like(rad)
    left = grid + [norm1, norm2, one, one, zero]
    left += rest1 + [extra1, extra2, zero, zero, zero]
    left += rest2 + [extra3, zero, zero, zero, zero]
    right = neg(grid) + [one, one, norm1, norm2, zero]
    right += neg(rest1) + [zero, zero, extra1, extra2, zero]
    right += neg(rest2) + [zero, zero, extra3, zero, zero]
    return left, right, rad


def products(left, right):
    a, b, c = [left[k : k + 8, :] for k in (0, 8, 16)]
    x, y, z = [right[k : k + 8, :] for k in (0, 8, 16)]
    pairs = [(a, x), (b, x), (a, y), (c, x), (a, z), (b, y), (b, z), (c, y)]
    return [jnp.concatenate(v, axis=0).astype(BF16) for v in zip(*pairs)]


def store_features(ref, rows):
    count = rows[0].shape[0]
    width = rows[0].shape[1]
    for k, row in enumerate(rows):
        for t, piece in enumerate(ref):
            piece[pl.ds(k, count, stride=ROWS), :] = row[:, t * LANES : min(width, (t + 1) * LANES)]


def load_features(ref, index):
    start = pl.multiple_of(index * ROWS, 8)
    blocks = [piece[pl.ds(start, ROWS), :] for piece in ref]
    return jnp.concatenate(blocks, axis=1) if len(blocks) > 1 else blocks[0]


def contract(left, right):
    return jnp.dot(left, right, preferred_element_type=F32)


def select_rows(index, value, count):
    row = lax.broadcasted_iota(jnp.int32, (count, index.shape[1]), 0)
    left = jnp.where(row == index, 1.0, 0.0).astype(BF16)
    high = value.astype(BF16)
    rest = value - high.astype(F32)
    mid = rest.astype(BF16)
    low = (rest - mid.astype(F32)).astype(BF16)
    return jnp.dot(
        jnp.concatenate([left] * 3, axis=1),
        jnp.concatenate([high, mid, low], axis=0),
        preferred_element_type=F32,
    )


def upright(row):
    return jnp.broadcast_to(row, (8, row.shape[1])).T[:, :1]


def keep(parts, rows, value):
    high = value.astype(BF16)
    parts[rows, :LANES] = high
    parts[rows, LANES:] = (value - high.astype(F32)).astype(BF16)


def add_columns(table, parts, indices):
    shape = (2 * LANES, table.shape[1])
    lane = lax.broadcasted_iota(jnp.int32, shape, 1)
    picks = [jnp.where(lane == index, 1.0, 0.0).astype(BF16) for index in indices]
    table[...] += jnp.dot(
        jnp.concatenate([p[...] for p in parts], axis=1),
        jnp.concatenate(picks, axis=0),
        preferred_element_type=F32,
    )


def inverse_root(d):
    return lax.rsqrt(d)


def fold(v):
    return jnp.sum(v.reshape(v.shape[0] // 8, 8, v.shape[1]), axis=0)


def distances(left, right, out):
    left, right = products(left, right)
    out[...] = contract(left.T, right)


def staged(spans, *stages):
    held = {}
    for t in range(len(spans) + len(stages) - 1):
        for depth in reversed(range(len(stages))):
            k = t - depth
            if 0 <= k < len(spans):
                held[k] = stages[depth](spans[k], held.get(k))
                if depth == len(stages) - 1:
                    del held[k]


def spans_of(height, step=32):
    step = min(step, height)
    return [slice(r, r + step) for r in range(0, height, step)]


def tile_sums(dist, qrow, qleft, parts):
    q0, q1 = qrow[:, :LANES], qrow[:, LANES:]
    qcol = upright(qleft)
    back = [jnp.zeros((8, LANES), F32), jnp.zeros((8, LANES), F32)]

    def root(rows, _):
        return (
            inverse_root(dist[rows, :LANES]),
            inverse_root(dist[rows, LANES:]),
        )

    def sums(rows, held):
        g0, g1 = held
        back[0] = back[0] + fold(g0 * qcol[rows, :])
        back[1] = back[1] + fold(g1 * qcol[rows, :])
        keep(parts, rows, g0 * q0 + g1 * q1)

    staged(spans_of(dist.shape[0]), root, sums)
    return jnp.concatenate([jnp.sum(b, axis=0, keepdims=True) for b in back], axis=1)


def pipeline(total, begin, finish, table, ring, parts):
    size = len(ring)
    ahead = min(2, size - 1)
    group = min(2, size)

    def body(i, carry):
        indices = []
        for k in range(size):
            begin(i * size + k + ahead, ring[(k + ahead) % size])
            indices.append(finish(i * size + k, ring[k], parts[k % len(parts)]))
            if len(indices) == group:
                done = [parts[(k - n) % len(parts)] for n in reversed(range(group))]
                add_columns(table, done, indices)
                indices = []
        return carry

    for k in range(ahead):
        begin(k, ring[k])
    lax.fori_loop(0, (total + size - 1) // size, body, 0)


def ring_size(total):
    return next(size for size in (16, 8, 4, 2, 1) if total % size == 0)


def assemble(sub, S, L, q, pieces):
    def place(s):
        for shift in range(S):
            owner = (s - shift) % S
            q[:, owner * L : (owner + 1) * L] = pieces[shift][...]

    for s in range(S):
        pl.when(sub == s)(functools.partial(place, s))


def pack_kernel(sizes, charges, mask, geo, targets, sources, live, masked, geo_out, *packs):
    C, S, L, slots = sizes
    me, sub = lax.axis_index("clu"), lax.axis_index("sub")
    masked[...] = charges[...] * mask[...].astype(F32)
    geo_out[...] = geo[...]
    lane = lax.broadcasted_iota(jnp.int32, (8, L), 1)
    for shift in range(1, C):
        dest = lax.rem(me + shift, C)
        codes = jnp.full((8, L), -1.0, F32)
        for j in range(slots):
            code = jnp.where(live[dest, j] > 0, sources[dest, j], -1)
            codes = jnp.where(lane == j, code.astype(F32), codes)
        packs[shift - 1][5 * slots :, :] = codes

    def fill(s):
        for shift in range(1, C):
            dest = lax.rem(me + shift, C)
            pack = packs[shift - 1]
            for j in range(slots):
                t = targets[dest, j]
                g = geo[t, :, s * L : (s + 1) * L]
                for k in range(4):
                    pack[k * slots + j : k * slots + j + 1, :] = g[k : k + 1]
                pack[4 * slots + j : 4 * slots + j + 1, :] = masked[pl.ds(t, 1), :]

    for s in range(S):
        pl.when(sub == s)(functools.partial(fill, s))


def remote_kernel(sizes, geo, up, *rest):
    C, S, L, slots, clusters, panels = sizes
    pieces = rest[:S]
    packs = rest[S : S + C - 1]
    acc_out = rest[S + C - 1]
    sends = rest[S + C : S + C + C - 1]
    q, tq, acc, fwdt, sgeo, fa0, fb0, fb1, order, codes, sems, *work = rest[S + C + C - 1 :]
    fa, fb = (fa0,), (fb0, fb1)
    n = (C - 1) * slots
    copies = [
        pltpu.make_async_copy(packs[k].at[pl.ds(5 * slots, 8), :], codes.at[k], sems.at[k])
        for k in range(C - 1)
    ]
    for copy in copies:
        copy.start()
    assemble(lax.axis_index("sub"), S, L, q, pieces)
    acc[...] = jnp.zeros_like(acc)
    fwdt[...] = jnp.zeros_like(fwdt)
    for copy in copies:
        copy.wait()
    found = jnp.int32(0)
    for shift in range(C - 1):
        for j in range(slots):
            code = codes[shift, 0, j].astype(jnp.int32)
            order[n + 1 + shift * slots + j] = jnp.maximum(code, 0)
            order[found] = shift * slots + j
            found = found + (code >= 0).astype(jnp.int32)
            g = geo[jnp.maximum(code, 0)]
            for k in range(4):
                row = k * n + shift * slots + j
                sgeo[row : row + 1, :] = g[k : k + 1]
    tpoints = [
        jnp.concatenate([p[k * slots : (k + 1) * slots, :] for p in packs], axis=0) for k in range(5)
    ]
    spoints = [sgeo[k * n : (k + 1) * n, :] for k in range(4)]
    centre, inv = frame([tpoints, spoints])
    left, _, _ = split_features(tpoints, centre, inv)
    _, right, _ = split_features(spoints, centre, inv)
    store_features(fa, left)
    store_features(fb, right)
    tq[...] = tpoints[4]

    def begin(i, dist):
        slot = order[jnp.minimum(i, jnp.maximum(found - 1, 0))]
        distances(load_features(fa, slot), load_features(fb, slot), dist)

    def finish(i, dist, part):
        ok = i < found
        slot = order[jnp.minimum(i, jnp.maximum(found - 1, 0))]
        source = order[n + 1 + slot]
        back = tile_sums(
            dist, q[pl.ds(source, 1), :], tq[pl.ds(slot, 1), :], part
        )
        acc[pl.ds(source, 1), :] += jnp.where(ok, back, 0.0)
        return jnp.where(ok, slot, -1)

    pipeline(found, begin, finish, fwdt, work[:8], work[8:])
    acc_out[...] = acc[...] * inv
    fwd = (fwdt[...] * inv).T
    rank = up.shape[1]
    for shift in range(C - 1):
        sends[shift][:slots, :] = fwd[shift * slots : (shift + 1) * slots, :]
        sends[shift][slots:, :] = jnp.zeros((up.shape[0], L), F32)
        sends[shift][slots:, :rank] = up[...]


def prepare_kernel(
    geo, masked, basis_far, transfer_far, parent_far,
    fa0, fa1, fb0, fb1, diag, scale, up, basis, transfer, parent, sems
):
    copies = [
        pltpu.make_async_copy(src, dst, sems.at[k])
        for k, (src, dst) in enumerate(
            [(basis_far, basis), (transfer_far, transfer), (parent_far, parent)]
        )
    ]
    for copy in copies:
        copy.start()
    points = [geo[:, k, :] for k in range(4)]
    centre, inv = frame([points])
    left, right, rad = split_features(points, centre, inv)
    store_features((fa0, fa1), left)
    store_features((fb0, fb1), right)
    diag[...] = lax.rsqrt(2.0 * (rad * rad))
    scale[...] = jnp.full(scale.shape, inv, F32)
    for copy in copies:
        copy.wait()
    up_sums(basis, masked, transfer, parent, up)


def local_kernel(sizes, geo_pairs, pairs, fa0, fa1, fb0, fb1, diags, scale, acc_in, *rest):
    S, L, R, clusters, panels = sizes
    pieces = rest[:S]
    acc_out, q, acc, self_sums, pair_sums, *work = rest[S:]
    ring, sums = work[:16], work[16:]
    fa, fb = (fa0, fa1), (fb0, fb1)
    sub, rep = lax.axis_index("sub"), lax.axis_index("rep")
    assemble(sub, S, L, q, pieces)
    acc[...] = jnp.zeros_like(acc)
    self_sums[...] = jnp.zeros_like(self_sums)
    pair_sums[...] = jnp.zeros_like(pair_sums)

    half = panels // 2
    share = clusters // (S * R)
    first = (rep * S + sub) * share

    def begin_self(i, dist):
        c = first + jnp.minimum(i, share - 1)
        left, right = products(load_features(fa, c), load_features(fb, c))
        left = left.T
        dist[:half, :] = contract(left[:half, :], right)
        dist[half:, half:] = contract(left[half:, :], right[:, half:])

    def finish_self(i, dist, parts):
        c = first + i
        qrow = q[pl.ds(c, 1), :]
        qcol = upright(qrow[:, :half])
        diag = diags[pl.ds(c, 1), :]
        back = [jnp.zeros((8, LANES), F32)]

        def eye(span):
            shape = (span.stop - span.start, half)
            row = lax.broadcasted_iota(jnp.int32, shape, 0) + span.start % half
            return row == lax.broadcasted_iota(jnp.int32, shape, 1)

        def root(span, _):
            if span.start < half:
                return (
                    jnp.where(eye(span), diag[:, :half], inverse_root(dist[span, :half])),
                    inverse_root(dist[span, half:]),
                )
            return (jnp.where(eye(span), diag[:, half:], inverse_root(dist[span, half:])),)

        def partial(span, held):
            if span.start < half:
                g0, g1 = held
                back[0] = back[0] + fold(g1 * qcol[span, :])
                keep(parts, span, g0 * qrow[:, :half] + g1 * qrow[:, half:])
            else:
                keep(parts, span, held[0] * qrow[:, half:])

        staged(spans_of(panels), root, partial)
        back = jnp.sum(back[0], axis=0, keepdims=True)
        acc[pl.ds(c, 1), :] += jnp.concatenate([jnp.zeros_like(back), back], axis=1)
        return c

    pipeline(share, begin_self, finish_self, self_sums, ring[: ring_size(share)], sums)

    count = pairs.shape[1] // S
    start = sub * count

    def begin(i, dist):
        p = start + jnp.minimum(i, count - 1)
        distances(load_features(fa, pairs[0, p]), load_features(fb, pairs[1, p]), dist)

    def finish(i, dist, part):
        ia, ib = pairs[0, start + i], pairs[1, start + i]
        acc[pl.ds(ib, 1), :] += tile_sums(
            dist, q[pl.ds(ib, 1), :], q[pl.ds(ia, 1), :], part
        )
        return start + i

    pipeline(count, begin, finish, pair_sums, ring[: ring_size(count)], sums)
    total = acc[...] + self_sums[...].T
    width = geo_pairs.shape[1]
    total = total + select_rows(geo_pairs[0:1, :], pair_sums[...].T[:width, :], clusters)
    acc_out[...] = acc_in[...] + total * scale[0:1, 0:1]


def merge_kernel(sizes, far_list, targets, near, coupling, transfer, parent, up, *rest):
    C, S, L, slots, clusters = sizes
    sums = rest[: C - 1]
    parts = rest[C - 1 : C - 1 + S]
    parents = rest[-1]
    me, sub = lax.axis_index("clu"), lax.axis_index("sub")
    index = [targets[pl.ds(lax.rem(me + shift, C), 1), :] for shift in range(1, C)]
    got = select_rows(
        jnp.concatenate(index, axis=1), jnp.concatenate([v[:slots, :] for v in sums], axis=0), clusters
    )

    par_dev, far_n, rank = coupling.shape[0], coupling.shape[1], coupling.shape[2]
    parents[pl.ds(pl.multiple_of(me * par_dev, 8), par_dev), :] = up[...]
    for shift in range(1, C):
        owner = lax.rem(me + shift, C)
        parents[pl.ds(pl.multiple_of(owner * par_dev, 8), par_dev), :] = sums[shift - 1][slots:, :rank]
    lane = lax.broadcasted_iota(jnp.int32, (rank, LANES), 1)
    field = jnp.zeros((rank, LANES), F32)
    for p in range(par_dev):
        part = jnp.zeros((rank, rank), F32)
        for k in range(far_n):
            part = part + coupling[p, k] * parents[pl.ds(far_list[k, p], 1), :]
        field = jnp.where(lane == p, jnp.sum(part, axis=1, keepdims=True), field)
    which = lax.broadcasted_iota(jnp.int32, (LANES, clusters), 0)
    onehot = (parent[...] == which).astype(F32)
    down = jnp.dot(field, onehot, precision=HIGHEST, preferred_element_type=F32)
    fields = jnp.concatenate(
        [jnp.sum(transfer[r] * down, axis=0, keepdims=True) for r in range(rank)], axis=0
    )

    def give(s):
        for shift in range(S):
            other = (s + shift) % S
            part = near[:, other * L : (other + 1) * L]
            parts[shift][:clusters, :] = part + got if shift == 0 else part
            for t in range(clusters // L):
                at = clusters + t * rank
                parts[shift][at : at + rank, :] = fields[:, t * L : (t + 1) * L]

    for s in range(S):
        pl.when(sub == s)(functools.partial(give, s))


def up_sums(basis, masked, transfer, parent, up):
    clusters = basis.shape[0]
    rank = basis.shape[1]
    lane = lax.broadcasted_iota(jnp.int32, (rank, clusters), 1)
    leaf = jnp.zeros((rank, clusters), F32)
    for c in range(clusters):
        part = jnp.sum(basis[c] * masked[c : c + 1, :], axis=1, keepdims=True)
        leaf = jnp.where(lane == c, part, leaf)
    lifted = jnp.zeros((rank, clusters), F32)
    for r in range(rank):
        lifted = lifted + transfer[r] * leaf[r : r + 1, :]
    which = lax.broadcasted_iota(jnp.int32, (up.shape[0], clusters), 0)
    onehot = (parent[...] == which).astype(F32)
    up[...] = lax.dot_general(
        onehot, lifted, (((1,), (1,)), ((), ())), precision=HIGHEST, preferred_element_type=F32
    )


def far_kernel(basis, near, out):
    clusters, rank = basis.shape[0], basis.shape[1]
    L = out.shape[1]
    fields = [near[clusters + t * rank : clusters + (t + 1) * rank, :] for t in range(clusters // L)]
    fields = jnp.concatenate(fields, axis=1) if len(fields) > 1 else fields[0]
    for c in range(clusters):
        far = jnp.sum(basis[c] * fields[:, c : c + 1], axis=0, keepdims=True)
        out[c : c + 1, :] = far + near[c : c + 1, :]


def send(value, moves):
    names = tuple(name for name, _ in moves)
    steps = [step for _, step in moves]
    sizes = [lax.axis_size(name) for name in names]
    perm = []

    def flat(coords):
        index = 0
        for size, c in zip(sizes, coords):
            index = index * size + c
        return index

    total = 1
    for size in sizes:
        total *= size
    for index in range(total):
        coords, left = [], index
        for size in reversed(sizes):
            coords.append(left % size)
            left //= size
        coords.reverse()
        perm.append((index, flat([(c + s) % n for c, s, n in zip(coords, steps, sizes)])))
    return lax.ppermute(value, names if len(names) > 1 else names[0], perm)


def on_device(
    charges,
    panel_mask,
    geometry,
    remote_source,
    remote_target,
    remote_live,
    local_pairs,
    basis,
    transfer,
    parent_of,
    far_list,
    coupling,
):
    clusters, L = charges.shape
    panels = geometry.shape[2]
    C, S, R = lax.axis_size("clu"), lax.axis_size("sub"), lax.axis_size("rep")
    slots = remote_source.shape[2]
    par_dev, rank = far_list.shape[0], transfer.shape[1]
    n = (C - 1) * slots
    shape = jax.ShapeDtypeStruct
    targets = remote_target[0]
    basis_t = jnp.transpose(basis, (0, 2, 1))
    transfer_t = jnp.transpose(transfer, (1, 2, 0))
    parent = parent_of[None, :]

    made = pl.pallas_call(
        functools.partial(pack_kernel, (C, S, L, slots)),
        out_shape=[pltpu.VMEM((clusters, L), F32), pltpu.VMEM(geometry.shape, F32)]
        + [pltpu.VMEM((5 * slots + 8, L), F32)] * (C - 1),
        in_specs=[vmem()] * 3 + [smem()] * 3,
        out_specs=[vmem()] * (C + 1),
        compiler_params=limit(60),
        cost_estimate=about(2),
        name="packs",
    )(charges, panel_mask, geometry, targets, remote_source[0], remote_live[0])
    masked, geo, packs = made[0], made[1], made[2:]
    pieces = [masked] + [send(masked, (("sub", d),)) for d in range(1, S)]
    packs = [send(packs[d - 1], (("clu", d),)) for d in range(1, C)]

    *features, up = pl.pallas_call(
        prepare_kernel,
        out_shape=[pltpu.VMEM((clusters * ROWS, LANES), F32)] * 4
        + [
            pltpu.VMEM((clusters, panels), F32),
            pltpu.VMEM((8, LANES), F32),
            pltpu.VMEM((par_dev, rank), F32),
        ],
        in_specs=[vmem()] * 2 + [pl.BlockSpec(memory_space=pl.ANY)] * 3,
        out_specs=[vmem()] * 7,
        scratch_shapes=[
            pltpu.VMEM(basis_t.shape, F32),
            pltpu.VMEM(transfer_t.shape, F32),
            pltpu.VMEM(parent.shape, jnp.int32),
            pltpu.SemaphoreType.DMA((3,)),
        ],
        compiler_params=limit(32),
        cost_estimate=about(4),
        name="prepare",
    )(*near_by(geo, masked), basis_t, transfer_t, parent)

    made = pl.pallas_call(
        functools.partial(remote_kernel, (C, S, L, slots, clusters, panels)),
        out_shape=[pltpu.VMEM((clusters, panels), F32)]
        + [pltpu.VMEM((slots + par_dev, L), F32)] * (C - 1),
        in_specs=[vmem()] * (2 + S + C - 1),
        out_specs=[vmem()] * C,
        scratch_shapes=[
            pltpu.VMEM((clusters, panels), F32),
            pltpu.VMEM((n, L), F32),
            pltpu.VMEM((clusters, panels), F32),
            pltpu.VMEM((L, whole(n)), F32),
            pltpu.VMEM((4 * n, panels), F32),
            pltpu.VMEM((n * ROWS, L), F32),
            pltpu.VMEM((n * ROWS, LANES), F32),
            pltpu.VMEM((n * ROWS, LANES), F32),
            pltpu.SMEM((2 * n + 1,), jnp.int32),
            pltpu.SMEM((C - 1, 8, L), F32),
            pltpu.SemaphoreType.DMA((C - 1,)),
        ]
        + [pltpu.VMEM((L, panels), F32)] * 8
        + [pltpu.VMEM((L, 2 * LANES), BF16)] * 4,
        compiler_params=limit(24),
        cost_estimate=about(6),
        name="near_remote",
    )(*near_by(geo, up, *pieces, *packs))
    acc, sums = made[0], [send(made[d], (("clu", C - d),)) for d in range(1, C)]

    wide = whole(local_pairs.shape[1])
    acc = pl.pallas_call(
        functools.partial(local_kernel, (S, L, R, clusters, panels)),
        out_shape=pltpu.VMEM((clusters, panels), F32),
        in_specs=[vmem(), smem()] + [vmem()] * (7 + S),
        out_specs=vmem(),
        scratch_shapes=[
            pltpu.VMEM((clusters, panels), F32),
            pltpu.VMEM((clusters, panels), F32),
            pltpu.VMEM((panels, clusters), F32),
            pltpu.VMEM((panels, wide), F32),
        ]
        + [pltpu.VMEM((panels, panels), F32)] * 16
        + [pltpu.VMEM((panels, 2 * LANES), BF16)] * 4,
        compiler_params=limit(24),
        cost_estimate=about(15),
        name="near_local",
    )(*near_by(local_pairs[0].T), local_pairs[0].T, *near_by(*features, acc, *pieces))

    parts = pl.pallas_call(
        functools.partial(merge_kernel, (C, S, L, slots, clusters)),
        out_shape=[pltpu.VMEM((clusters + clusters // L * rank, L), F32)] * S,
        in_specs=[smem()] + [vmem()] * (6 + C - 1),
        out_specs=[vmem()] * S,
        scratch_shapes=[pltpu.VMEM((C * par_dev, rank), F32)],
        compiler_params=limit(16),
        cost_estimate=about(2),
        name="merge",
    )(far_list.T, *near_by(targets, acc, coupling, transfer_t, parent, up, *sums))
    near = parts[0]
    for d in range(1, S):
        near = near + send(parts[d], (("sub", d),))
    others = [send(near, (("rep", e),)) for e in range(1, R)]

    total = pl.pallas_call(
        far_kernel,
        out_shape=pltpu.VMEM((clusters, L), F32),
        in_specs=[vmem()] * 2,
        out_specs=vmem(),
        compiler_params=limit(16),
        cost_estimate=about(1),
        name="far_down",
    )(*near_by(basis_t, near))
    for other in others:
        total = total + other[:clusters]
    return total * panel_mask.astype(F32)


def solution(mesh):
    placed = (
        P(("grp", "clu"), "sub"),
        P(("grp", "clu"), "sub"),
        P(("grp", "clu"), None, None),
        P(("grp", "clu"), None, "rep"),
        P(("grp", "clu"), None, "rep"),
        P(("grp", "clu"), None, "rep"),
        P(("grp", "clu"), "rep", None),
        P(("grp", "clu"), "sub", None),
        P(("grp", "clu"), None, None),
        P(("grp", "clu")),
        P(("grp", "clu"), None),
        P(("grp", "clu"), None, None, None),
    )
    return jax.shard_map(
        on_device, mesh=mesh, in_specs=placed, out_specs=P(("grp", "clu"), "sub"), check_vma=False
    )
```

```python
import functools

import jax
import jax.numpy as jnp
from jax import lax
from jax.experimental import pallas as pl
from jax.experimental.pallas import tpu as pltpu
from jax.sharding import PartitionSpec as P

F32 = jnp.float32
BF16 = jnp.bfloat16
HIGHEST = lax.Precision.HIGHEST
ROWS = 24
LANES = 128


def limit(mib):
    return pltpu.CompilerParams(vmem_limit_bytes=mib * 1024 * 1024)


def about(us):
    return pl.CostEstimate(flops=0, bytes_accessed=int(us * 3.5e6), transcendentals=0)


def vmem():
    return pl.BlockSpec(memory_space=pltpu.VMEM)


def near_by(*arrays):
    return [pltpu.with_memory_space_constraint(x, pltpu.VMEM) for x in arrays]


def far_off(*arrays):
    return [pltpu.with_memory_space_constraint(x, pltpu.HBM) for x in arrays]


def smem():
    return pl.BlockSpec(memory_space=pltpu.SMEM)


def whole(size):
    return -(-size // LANES) * LANES


def cut(v):
    return v.astype(BF16).astype(F32)


def powers(sign):
    lane = lax.broadcasted_iota(jnp.int32, (8, LANES), 1)
    out = jnp.full((8, LANES), 2.0 ** (-64 * sign), F32)
    for bit in range(7):
        out = out * jnp.where((lane >> bit) & 1 == 1, F32(2.0 ** (sign * 2**bit)), F32(1.0))
    return out


def frame(parts):
    low = [functools.reduce(jnp.minimum, [jnp.min(p[k]) for p in parts]) for k in range(3)]
    high = [functools.reduce(jnp.maximum, [jnp.max(p[k]) for p in parts]) for k in range(3)]
    width = functools.reduce(jnp.maximum, [jnp.max(jnp.abs(p[3])) for p in parts])
    for lo, hi in zip(low, high):
        width = jnp.maximum(width, 0.5 * (hi - lo))
    up, down = powers(1), powers(-1)
    size = jnp.min(jnp.where(up >= width, up, F32(2.0**63)))
    inv = jnp.max(jnp.where(up >= width, down, F32(2.0**-63)))
    magic = size * F32(1.5 * 2.0**20)
    centre = [(0.5 * (lo + hi) + magic) - magic for lo, hi in zip(low, high)]
    return centre, inv


def split_features(points, centre, inv):
    magic = F32(1.5 * 2.0**16)
    grid, rest = [], []
    for k in range(3):
        u = (points[k] - centre[k]) * inv
        h = (u + magic) - magic
        grid.append(h)
        rest.append(u - h)
    rad = points[3] * inv
    norm = grid[0] * grid[0] + grid[1] * grid[1] + grid[2] * grid[2]
    norm1 = cut(norm)
    norm2 = norm - norm1
    cross = grid[0] * rest[0] + grid[1] * rest[1] + grid[2] * rest[2]
    extra = 2.0 * cross + (rest[0] * rest[0] + rest[1] * rest[1] + rest[2] * rest[2]) + rad * rad
    extra1 = cut(extra)
    extra2 = cut(extra - extra1)
    extra3 = (extra - extra1) - extra2
    rest1 = [cut(v) for v in rest]
    rest2 = [v - w for v, w in zip(rest, rest1)]
    neg = lambda vs: [-2.0 * v for v in vs]
    one, zero = jnp.ones_like(rad), jnp.zeros_like(rad)
    left = grid + [norm1, norm2, one, one, zero]
    left += rest1 + [extra1, extra2, zero, zero, zero]
    left += rest2 + [extra3, zero, zero, zero, zero]
    right = neg(grid) + [one, one, norm1, norm2, zero]
    right += neg(rest1) + [zero, zero, extra1, extra2, zero]
    right += neg(rest2) + [zero, zero, extra3, zero, zero]
    return left, right, rad


def products(left, right):
    a, b, c = [left[k : k + 8, :] for k in (0, 8, 16)]
    x, y, z = [right[k : k + 8, :] for k in (0, 8, 16)]
    pairs = [(a, x), (b, x), (a, y), (c, x), (a, z), (b, y), (b, z), (c, y)]
    return [jnp.concatenate(v, axis=0).astype(BF16) for v in zip(*pairs)]


def store_features(ref, rows, first):
    width = rows[0].shape[1]
    for k, row in enumerate(rows):
        for t, piece in enumerate(ref):
            at = pl.ds(first * ROWS + k, 8, stride=ROWS)
            piece[at, :] = row[:, t * LANES : min(width, (t + 1) * LANES)]


def load_features(ref, index):
    start = pl.multiple_of(index * ROWS, 8)
    blocks = [piece[pl.ds(start, ROWS), :] for piece in ref]
    return jnp.concatenate(blocks, axis=1) if len(blocks) > 1 else blocks[0]


def contract(left, right):
    return jnp.dot(left, right, preferred_element_type=F32)


def select_rows(index, value, count):
    row = lax.broadcasted_iota(jnp.int32, (count, index.shape[1]), 0)
    left = jnp.where(row == index, 1.0, 0.0).astype(BF16)
    high = value.astype(BF16)
    rest = value - high.astype(F32)
    mid = rest.astype(BF16)
    low = (rest - mid.astype(F32)).astype(BF16)
    return jnp.dot(
        jnp.concatenate([left] * 3, axis=1),
        jnp.concatenate([high, mid, low], axis=0),
        preferred_element_type=F32,
    )


def upright(row):
    return jnp.broadcast_to(row, (8, row.shape[1])).T[:, :1]


def keep(parts, rows, value):
    high = value.astype(BF16)
    parts[rows, :LANES] = high
    parts[rows, LANES:] = (value - high.astype(F32)).astype(BF16)


def add_columns(table, parts, indices):
    shape = (2 * LANES, table.shape[1])
    lane = lax.broadcasted_iota(jnp.int32, shape, 1)
    picks = [jnp.where(lane == index, 1.0, 0.0).astype(BF16) for index in indices]
    table[...] += jnp.dot(
        jnp.concatenate([p[...] for p in parts], axis=1),
        jnp.concatenate(picks, axis=0),
        preferred_element_type=F32,
    )


def inverse_root(d):
    return lax.exp2(-0.5 * lax.log2(d))


def fold(v):
    return jnp.sum(v.reshape(v.shape[0] // 8, 8, v.shape[1]), axis=0)


def distances(left, right, out):
    left, right = products(left, right)
    out[...] = contract(left.T, right)


def staged(spans, *stages):
    held = {}
    for t in range(len(spans) + len(stages) - 1):
        for depth in reversed(range(len(stages))):
            k = t - depth
            if 0 <= k < len(spans):
                held[k] = stages[depth](spans[k], held.get(k))
                if depth == len(stages) - 1:
                    del held[k]


def spans_of(height, step=32):
    step = min(step, height)
    return [slice(r, r + step) for r in range(0, height, step)]


def tile_sums(dist, qrow, qleft, parts):
    q0, q1 = qrow[:, :LANES], qrow[:, LANES:]
    qcol = upright(qleft)
    back = [jnp.zeros((8, LANES), F32), jnp.zeros((8, LANES), F32)]

    def root(rows, _):
        return (
            inverse_root(dist[rows, :LANES]),
            inverse_root(dist[rows, LANES:]),
        )

    def sums(rows, held):
        g0, g1 = held
        back[0] = back[0] + fold(g0 * qcol[rows, :])
        back[1] = back[1] + fold(g1 * qcol[rows, :])
        keep(parts, rows, g0 * q0 + g1 * q1)

    staged(spans_of(dist.shape[0]), root, sums)
    return jnp.concatenate([jnp.sum(b, axis=0, keepdims=True) for b in back], axis=1)


def pipeline(total, begin, finish, table, ring, parts):
    size = len(ring)
    ahead = min(2, size - 1)
    group = min(2, size)

    def body(i, carry):
        indices = []
        for k in range(size):
            begin(i * size + k + ahead, ring[(k + ahead) % size])
            indices.append(finish(i * size + k, ring[k], parts[k % len(parts)]))
            if len(indices) == group:
                done = [parts[(k - n) % len(parts)] for n in reversed(range(group))]
                add_columns(table, done, indices)
                indices = []
        return carry

    for k in range(ahead):
        begin(k, ring[k])
    lax.fori_loop(0, (total + size - 1) // size, body, 0)


def ring_size(total):
    return next(size for size in (16, 8, 4, 2, 1) if total % size == 0)


def assemble(sub, S, L, q, pieces):
    def place(s):
        for shift in range(S):
            owner = (s - shift) % S
            q[:, owner * L : (owner + 1) * L] = pieces[shift][...]

    for s in range(S):
        pl.when(sub == s)(functools.partial(place, s))


def pack_kernel(sizes, charges, mask, geo, targets, sources, live, masked, geo_out, *packs):
    C, S, L, slots = sizes
    me, sub = lax.axis_index("clu"), lax.axis_index("sub")
    masked[...] = charges[...] * mask[...].astype(F32)
    geo_out[...] = geo[...]
    lane = lax.broadcasted_iota(jnp.int32, (8, L), 1)
    for shift in range(1, C):
        dest = lax.rem(me + shift, C)
        codes = jnp.full((8, L), -1.0, F32)
        for j in range(slots):
            code = jnp.where(live[dest, j] > 0, sources[dest, j], -1)
            codes = jnp.where(lane == j, code.astype(F32), codes)
        packs[shift - 1][5 * slots :, :] = codes

    def fill(s):
        for shift in range(1, C):
            dest = lax.rem(me + shift, C)
            pack = packs[shift - 1]
            for j in range(slots):
                t = targets[dest, j]
                g = geo[t, :, s * L : (s + 1) * L]
                for k in range(4):
                    pack[k * slots + j : k * slots + j + 1, :] = g[k : k + 1]
                pack[4 * slots + j : 4 * slots + j + 1, :] = masked[pl.ds(t, 1), :]

    for s in range(S):
        pl.when(sub == s)(functools.partial(fill, s))


def remote_kernel(sizes, geo, up, *rest):
    C, S, L, slots, clusters, panels = sizes
    pieces = rest[:S]
    packs = rest[S : S + C - 1]
    acc_out = rest[S + C - 1]
    sends = rest[S + C : S + C + C - 1]
    q, tq, acc, fwdt, sgeo, fa0, fb0, fb1, order, codes, sems, *work = rest[S + C + C - 1 :]
    fa, fb = (fa0,), (fb0, fb1)
    n = (C - 1) * slots
    copies = [
        pltpu.make_async_copy(packs[k].at[pl.ds(5 * slots, 8), :], codes.at[k], sems.at[k])
        for k in range(C - 1)
    ]
    for copy in copies:
        copy.start()
    assemble(lax.axis_index("sub"), S, L, q, pieces)
    acc[...] = jnp.zeros_like(acc)
    fwdt[...] = jnp.zeros_like(fwdt)
    for copy in copies:
        copy.wait()
    found = jnp.int32(0)
    for shift in range(C - 1):
        for j in range(slots):
            code = codes[shift, 0, j].astype(jnp.int32)
            order[n + 1 + shift * slots + j] = jnp.maximum(code, 0)
            order[found] = shift * slots + j
            found = found + (code >= 0).astype(jnp.int32)
            g = geo[jnp.maximum(code, 0)]
            for k in range(4):
                row = k * n + shift * slots + j
                sgeo[row : row + 1, :] = g[k : k + 1]
    tpoints = [
        jnp.concatenate([p[k * slots : (k + 1) * slots, :] for p in packs], axis=0) for k in range(5)
    ]
    spoints = [sgeo[k * n : (k + 1) * n, :] for k in range(4)]
    centre, inv = frame([tpoints, spoints])
    for first in range(0, n, 8):
        left, _, _ = split_features([v[first : first + 8, :] for v in tpoints], centre, inv)
        store_features(fa, left, first)
        _, right, _ = split_features([v[first : first + 8, :] for v in spoints], centre, inv)
        store_features(fb, right, first)
    tq[...] = tpoints[4]

    def begin(i, dist):
        slot = order[jnp.minimum(i, jnp.maximum(found - 1, 0))]
        distances(load_features(fa, slot), load_features(fb, slot), dist)

    def finish(i, dist, part):
        ok = i < found
        slot = order[jnp.minimum(i, jnp.maximum(found - 1, 0))]
        source = order[n + 1 + slot]
        back = tile_sums(
            dist, q[pl.ds(source, 1), :], tq[pl.ds(slot, 1), :], part
        )
        acc[pl.ds(source, 1), :] += jnp.where(ok, back, 0.0)
        return jnp.where(ok, slot, -1)

    pipeline(found, begin, finish, fwdt, work[:8], work[8:])
    acc_out[...] = acc[...] * inv
    fwd = (fwdt[...] * inv).T
    rank = up.shape[1]
    for shift in range(C - 1):
        sends[shift][:slots, :] = fwd[shift * slots : (shift + 1) * slots, :]
        sends[shift][slots:, :] = jnp.zeros((up.shape[0], L), F32)
        sends[shift][slots:, :rank] = up[...]


def prepare_kernel(
    geo, masked, basis_far, transfer_far, parent_far,
    fa0, fa1, fb0, fb1, diag, scale, up, basis, transfer, parent, sems
):
    copies = [
        pltpu.make_async_copy(src, dst, sems.at[k])
        for k, (src, dst) in enumerate(
            [(basis_far, basis), (transfer_far, transfer), (parent_far, parent)]
        )
    ]
    for copy in copies:
        copy.start()
    centre, inv = frame([[geo[:, k, :] for k in range(4)]])
    for first in range(0, geo.shape[0], 8):
        points = [geo[first : first + 8, k, :] for k in range(4)]
        left, right, rad = split_features(points, centre, inv)
        store_features((fa0, fa1), left, first)
        store_features((fb0, fb1), right, first)
        diag[first : first + 8, :] = lax.rsqrt(2.0 * (rad * rad))
    scale[...] = jnp.full(scale.shape, inv, F32)
    for copy in copies:
        copy.wait()
    up_sums(basis, masked, transfer, parent, up)


def local_kernel(sizes, geo_pairs, pairs, fa0, fa1, fb0, fb1, diags, scale, acc_in, *rest):
    S, L, R, clusters, panels = sizes
    pieces = rest[:S]
    acc_out, q, acc, self_sums, pair_sums, *work = rest[S:]
    ring, sums = work[:16], work[16:]
    fa, fb = (fa0, fa1), (fb0, fb1)
    sub, rep = lax.axis_index("sub"), lax.axis_index("rep")
    assemble(sub, S, L, q, pieces)
    acc[...] = jnp.zeros_like(acc)
    self_sums[...] = jnp.zeros_like(self_sums)
    pair_sums[...] = jnp.zeros_like(pair_sums)

    half = panels // 2
    share = clusters // (S * R)
    first = (rep * S + sub) * share

    def begin_self(i, dist):
        c = first + jnp.minimum(i, share - 1)
        left, right = products(load_features(fa, c), load_features(fb, c))
        left = left.T
        dist[:half, :] = contract(left[:half, :], right)
        dist[half:, half:] = contract(left[half:, :], right[:, half:])

    def finish_self(i, dist, parts):
        c = first + i
        qrow = q[pl.ds(c, 1), :]
        qcol = upright(qrow[:, :half])
        diag = diags[pl.ds(c, 1), :]
        back = [jnp.zeros((8, LANES), F32)]

        def eye(span):
            shape = (span.stop - span.start, half)
            row = lax.broadcasted_iota(jnp.int32, shape, 0) + span.start % half
            return row == lax.broadcasted_iota(jnp.int32, shape, 1)

        def root(span, _):
            if span.start < half:
                return (
                    jnp.where(eye(span), diag[:, :half], inverse_root(dist[span, :half])),
                    inverse_root(dist[span, half:]),
                )
            return (jnp.where(eye(span), diag[:, half:], inverse_root(dist[span, half:])),)

        def partial(span, held):
            if span.start < half:
                g0, g1 = held
                back[0] = back[0] + fold(g1 * qcol[span, :])
                keep(parts, span, g0 * qrow[:, :half] + g1 * qrow[:, half:])
            else:
                keep(parts, span, held[0] * qrow[:, half:])

        staged(spans_of(panels), root, partial)
        back = jnp.sum(back[0], axis=0, keepdims=True)
        acc[pl.ds(c, 1), :] += jnp.concatenate([jnp.zeros_like(back), back], axis=1)
        return c

    pipeline(share, begin_self, finish_self, self_sums, ring[: ring_size(share)], sums)

    count = pairs.shape[1] // S
    start = sub * count

    def begin(i, dist):
        p = start + jnp.minimum(i, count - 1)
        distances(load_features(fa, pairs[0, p]), load_features(fb, pairs[1, p]), dist)

    def finish(i, dist, part):
        ia, ib = pairs[0, start + i], pairs[1, start + i]
        acc[pl.ds(ib, 1), :] += tile_sums(
            dist, q[pl.ds(ib, 1), :], q[pl.ds(ia, 1), :], part
        )
        return start + i

    pipeline(count, begin, finish, pair_sums, ring[: ring_size(count)], sums)
    total = acc[...] + self_sums[...].T
    width = geo_pairs.shape[1]
    total = total + select_rows(geo_pairs[0:1, :], pair_sums[...].T[:width, :], clusters)
    acc_out[...] = acc_in[...] + total * scale[0:1, 0:1]


def merge_kernel(sizes, far_list, targets, near, coupling, transfer, parent, up, *rest):
    C, S, L, slots, clusters = sizes
    sums = rest[: C - 1]
    parts = rest[C - 1 : C - 1 + S]
    parents = rest[-1]
    me, sub = lax.axis_index("clu"), lax.axis_index("sub")
    index = [targets[pl.ds(lax.rem(me + shift, C), 1), :] for shift in range(1, C)]
    got = select_rows(
        jnp.concatenate(index, axis=1), jnp.concatenate([v[:slots, :] for v in sums], axis=0), clusters
    )

    par_dev, far_n, rank = coupling.shape[0], coupling.shape[1], coupling.shape[2]
    parents[pl.ds(pl.multiple_of(me * par_dev, 8), par_dev), :] = up[...]
    for shift in range(1, C):
        owner = lax.rem(me + shift, C)
        parents[pl.ds(pl.multiple_of(owner * par_dev, 8), par_dev), :] = sums[shift - 1][slots:, :rank]
    lane = lax.broadcasted_iota(jnp.int32, (rank, LANES), 1)
    field = jnp.zeros((rank, LANES), F32)
    for p in range(par_dev):
        part = jnp.zeros((rank, rank), F32)
        for k in range(far_n):
            part = part + coupling[p, k] * parents[pl.ds(far_list[k, p], 1), :]
        field = jnp.where(lane == p, jnp.sum(part, axis=1, keepdims=True), field)
    which = lax.broadcasted_iota(jnp.int32, (LANES, clusters), 0)
    onehot = (parent[...] == which).astype(F32)
    down = jnp.dot(field, onehot, precision=HIGHEST, preferred_element_type=F32)
    fields = jnp.concatenate(
        [jnp.sum(transfer[r] * down, axis=0, keepdims=True) for r in range(rank)], axis=0
    )

    def give(s):
        for shift in range(S):
            other = (s + shift) % S
            part = near[:, other * L : (other + 1) * L]
            parts[shift][:clusters, :] = part + got if shift == 0 else part
            for t in range(clusters // L):
                at = clusters + t * rank
                parts[shift][at : at + rank, :] = fields[:, t * L : (t + 1) * L]

    for s in range(S):
        pl.when(sub == s)(functools.partial(give, s))


def up_sums(basis, masked, transfer, parent, up):
    clusters = basis.shape[0]
    rank = basis.shape[1]
    lane = lax.broadcasted_iota(jnp.int32, (rank, clusters), 1)
    leaf = jnp.zeros((rank, clusters), F32)
    for c in range(clusters):
        part = jnp.sum(basis[c] * masked[c : c + 1, :], axis=1, keepdims=True)
        leaf = jnp.where(lane == c, part, leaf)
    lifted = jnp.zeros((rank, clusters), F32)
    for r in range(rank):
        lifted = lifted + transfer[r] * leaf[r : r + 1, :]
    which = lax.broadcasted_iota(jnp.int32, (up.shape[0], clusters), 0)
    onehot = (parent[...] == which).astype(F32)
    up[...] = lax.dot_general(
        onehot, lifted, (((1,), (1,)), ((), ())), precision=HIGHEST, preferred_element_type=F32
    )


def far_kernel(basis, near, out):
    clusters, rank = basis.shape[0], basis.shape[1]
    L = out.shape[1]
    fields = [near[clusters + t * rank : clusters + (t + 1) * rank, :] for t in range(clusters // L)]
    fields = jnp.concatenate(fields, axis=1) if len(fields) > 1 else fields[0]
    for c in range(clusters):
        far = jnp.sum(basis[c] * fields[:, c : c + 1], axis=0, keepdims=True)
        out[c : c + 1, :] = far + near[c : c + 1, :]


def send(value, moves):
    names = tuple(name for name, _ in moves)
    steps = [step for _, step in moves]
    sizes = [lax.axis_size(name) for name in names]
    perm = []

    def flat(coords):
        index = 0
        for size, c in zip(sizes, coords):
            index = index * size + c
        return index

    total = 1
    for size in sizes:
        total *= size
    for index in range(total):
        coords, left = [], index
        for size in reversed(sizes):
            coords.append(left % size)
            left //= size
        coords.reverse()
        perm.append((index, flat([(c + s) % n for c, s, n in zip(coords, steps, sizes)])))
    return lax.ppermute(value, names if len(names) > 1 else names[0], perm)


def on_device(
    charges,
    panel_mask,
    geometry,
    remote_source,
    remote_target,
    remote_live,
    local_pairs,
    basis,
    transfer,
    parent_of,
    far_list,
    coupling,
):
    clusters, L = charges.shape
    panels = geometry.shape[2]
    C, S, R = lax.axis_size("clu"), lax.axis_size("sub"), lax.axis_size("rep")
    slots = remote_source.shape[2]
    par_dev, rank = far_list.shape[0], transfer.shape[1]
    n = (C - 1) * slots
    shape = jax.ShapeDtypeStruct
    targets = remote_target[0]
    basis_t = jnp.transpose(basis, (0, 2, 1))
    transfer_t = jnp.transpose(transfer, (1, 2, 0))
    parent = parent_of[None, :]

    made = pl.pallas_call(
        functools.partial(pack_kernel, (C, S, L, slots)),
        out_shape=[pltpu.VMEM((clusters, L), F32), pltpu.VMEM(geometry.shape, F32)]
        + [pltpu.VMEM((5 * slots + 8, L), F32)] * (C - 1),
        in_specs=[vmem()] * 3 + [smem()] * 3,
        out_specs=[vmem()] * (C + 1),
        compiler_params=limit(60),
        cost_estimate=about(2),
        name="packs",
    )(charges, panel_mask, geometry, targets, remote_source[0], remote_live[0])
    masked, geo, packs = made[0], made[1], made[2:]
    pieces = [masked] + [send(masked, (("sub", d),)) for d in range(1, S)]
    packs = [send(packs[d - 1], (("clu", d),)) for d in range(1, C)]

    *features, up = pl.pallas_call(
        prepare_kernel,
        out_shape=[pltpu.VMEM((clusters * ROWS, LANES), F32)] * 4
        + [
            pltpu.VMEM((clusters, panels), F32),
            pltpu.VMEM((8, LANES), F32),
            pltpu.VMEM((par_dev, rank), F32),
        ],
        in_specs=[vmem()] * 2 + [pl.BlockSpec(memory_space=pltpu.HBM)] * 3,
        out_specs=[vmem()] * 7,
        scratch_shapes=[
            pltpu.VMEM(basis_t.shape, F32),
            pltpu.VMEM(transfer_t.shape, F32),
            pltpu.VMEM(parent.shape, jnp.int32),
            pltpu.SemaphoreType.DMA((3,)),
        ],
        compiler_params=limit(32),
        cost_estimate=about(4),
        name="prepare",
    )(*near_by(geo, masked), *far_off(basis_t, transfer_t, parent))

    made = pl.pallas_call(
        functools.partial(remote_kernel, (C, S, L, slots, clusters, panels)),
        out_shape=[pltpu.VMEM((clusters, panels), F32)]
        + [pltpu.VMEM((slots + par_dev, L), F32)] * (C - 1),
        in_specs=[vmem()] * (2 + S + C - 1),
        out_specs=[vmem()] * C,
        scratch_shapes=[
            pltpu.VMEM((clusters, panels), F32),
            pltpu.VMEM((n, L), F32),
            pltpu.VMEM((clusters, panels), F32),
            pltpu.VMEM((L, whole(n)), F32),
            pltpu.VMEM((4 * n, panels), F32),
            pltpu.VMEM((n * ROWS, L), F32),
            pltpu.VMEM((n * ROWS, LANES), F32),
            pltpu.VMEM((n * ROWS, LANES), F32),
            pltpu.SMEM((2 * n + 1,), jnp.int32),
            pltpu.SMEM((C - 1, 8, L), F32),
            pltpu.SemaphoreType.DMA((C - 1,)),
        ]
        + [pltpu.VMEM((L, panels), F32)] * 8
        + [pltpu.VMEM((L, 2 * LANES), BF16)] * 4,
        compiler_params=limit(24),
        cost_estimate=about(6),
        name="near_remote",
    )(*near_by(geo, up, *pieces, *packs))
    acc, sums = made[0], [send(made[d], (("clu", C - d),)) for d in range(1, C)]

    wide = whole(local_pairs.shape[1])
    acc = pl.pallas_call(
        functools.partial(local_kernel, (S, L, R, clusters, panels)),
        out_shape=pltpu.VMEM((clusters, panels), F32),
        in_specs=[vmem(), smem()] + [vmem()] * (7 + S),
        out_specs=vmem(),
        scratch_shapes=[
            pltpu.VMEM((clusters, panels), F32),
            pltpu.VMEM((clusters, panels), F32),
            pltpu.VMEM((panels, clusters), F32),
            pltpu.VMEM((panels, wide), F32),
        ]
        + [pltpu.VMEM((panels, panels), F32)] * 16
        + [pltpu.VMEM((panels, 2 * LANES), BF16)] * 4,
        compiler_params=limit(24),
        cost_estimate=about(15),
        name="near_local",
    )(*near_by(local_pairs[0].T), local_pairs[0].T, *near_by(*features, acc, *pieces))

    parts = pl.pallas_call(
        functools.partial(merge_kernel, (C, S, L, slots, clusters)),
        out_shape=[pltpu.VMEM((clusters + clusters // L * rank, L), F32)] * S,
        in_specs=[smem()] + [vmem()] * (6 + C - 1),
        out_specs=[vmem()] * S,
        scratch_shapes=[pltpu.VMEM((C * par_dev, rank), F32)],
        compiler_params=limit(16),
        cost_estimate=about(2),
        name="merge",
    )(far_list.T, *near_by(targets, acc, coupling, transfer_t, parent, up, *sums))
    near = parts[0]
    for d in range(1, S):
        near = near + send(parts[d], (("sub", d),))
    others = [send(near, (("rep", e),)) for e in range(1, R)]

    total = pl.pallas_call(
        far_kernel,
        out_shape=pltpu.VMEM((clusters, L), F32),
        in_specs=[vmem()] * 2,
        out_specs=vmem(),
        compiler_params=limit(16),
        cost_estimate=about(1),
        name="far_down",
    )(*near_by(basis_t, near))
    for other in others:
        total = total + other[:clusters]
    return total * panel_mask.astype(F32)


def solution(mesh):
    placed = (
        P(("grp", "clu"), "sub"),
        P(("grp", "clu"), "sub"),
        P(("grp", "clu"), None, None),
        P(("grp", "clu"), None, "rep"),
        P(("grp", "clu"), None, "rep"),
        P(("grp", "clu"), None, "rep"),
        P(("grp", "clu"), "rep", None),
        P(("grp", "clu"), "sub", None),
        P(("grp", "clu"), None, None),
        P(("grp", "clu")),
        P(("grp", "clu"), None),
        P(("grp", "clu"), None, None, None),
    )
    return jax.shard_map(
        on_device, mesh=mesh, in_specs=placed, out_specs=P(("grp", "clu"), "sub"), check_vma=False
    )
```

```python
import functools

import jax
import jax.numpy as jnp
from jax import lax
from jax.experimental import pallas as pl
from jax.experimental.pallas import tpu as pltpu
from jax.sharding import PartitionSpec as P

F32 = jnp.float32
BF16 = jnp.bfloat16
HIGHEST = lax.Precision.HIGHEST
ROWS = 24
LANES = 128


def limit(mib):
    return pltpu.CompilerParams(vmem_limit_bytes=mib * 1024 * 1024)


def about(us):
    return pl.CostEstimate(flops=0, bytes_accessed=int(us * 3.5e6), transcendentals=0)


def vmem():
    return pl.BlockSpec(memory_space=pltpu.VMEM)


def near_by(*arrays):
    return [pltpu.with_memory_space_constraint(x, pltpu.VMEM) for x in arrays]


def far_off(*arrays):
    return [pltpu.with_memory_space_constraint(x, pltpu.HBM) for x in arrays]


def smem():
    return pl.BlockSpec(memory_space=pltpu.SMEM)


def whole(size):
    return -(-size // LANES) * LANES


def cut(v):
    return v.astype(BF16).astype(F32)


def powers(sign):
    lane = lax.broadcasted_iota(jnp.int32, (8, LANES), 1)
    out = jnp.full((8, LANES), 2.0 ** (-64 * sign), F32)
    for bit in range(7):
        out = out * jnp.where((lane >> bit) & 1 == 1, F32(2.0 ** (sign * 2**bit)), F32(1.0))
    return out


def frame(geo):
    low, high = [None] * 8, [None] * 8
    for c in range(geo.shape[0]):
        g, k = geo[c], c % 8
        low[k] = g if low[k] is None else jnp.minimum(low[k], g)
        high[k] = g if high[k] is None else jnp.maximum(high[k], g)
    low = jnp.min(functools.reduce(jnp.minimum, low), axis=1, keepdims=True)
    high = jnp.max(functools.reduce(jnp.maximum, high), axis=1, keepdims=True)
    row = lax.broadcasted_iota(jnp.int32, low.shape, 0)
    radius = jnp.maximum(jnp.abs(low), jnp.abs(high))
    width = jnp.max(jnp.where(row == 3, radius, 0.5 * (high - low)), axis=0, keepdims=True)

    def over(table, least):
        return least(least(table, axis=1, keepdims=True), axis=0, keepdims=True)

    up, down = powers(1), powers(-1)
    size = over(jnp.where(up >= width, up, F32(2.0**63)), jnp.min)
    inv = over(jnp.where(up >= width, down, F32(2.0**-63)), jnp.max)
    magic = size * F32(1.5 * 2.0**20)
    return inv, (0.5 * (low + high) + magic) - magic


def split_frame(scale):
    return scale[0:1, 0:1], [scale[k : k + 1, 0:1] for k in range(1, 4)]


def split_features(points, centre, inv):
    magic = F32(1.5 * 2.0**16)
    grid, rest = [], []
    for k in range(3):
        u = (points[k] - centre[k]) * inv
        h = cut((u + magic) - magic)
        grid.append(h)
        rest.append(u - h)
    rad = points[3] * inv
    norm = grid[0] * grid[0] + grid[1] * grid[1] + grid[2] * grid[2]
    norm1 = cut(norm)
    norm2 = cut(norm - norm1)
    cross = grid[0] * rest[0] + grid[1] * rest[1] + grid[2] * rest[2]
    extra = 2.0 * cross + (rest[0] * rest[0] + rest[1] * rest[1] + rest[2] * rest[2]) + rad * rad
    extra = extra + ((norm - norm1) - norm2)
    extra1 = cut(extra)
    extra2 = cut(extra - extra1)
    extra3 = (extra - extra1) - extra2
    rest1 = [cut(v) for v in rest]
    rest2 = [v - w for v, w in zip(rest, rest1)]
    neg = lambda vs: [-2.0 * v for v in vs]
    one, zero = jnp.ones_like(rad), jnp.zeros_like(rad)
    left = grid + [norm1, norm2, one, one, zero]
    left += rest1 + [extra1, extra2, zero, zero, zero]
    left += rest2 + [extra3, zero, zero, zero, zero]
    right = neg(grid) + [one, one, norm1, norm2, zero]
    right += neg(rest1) + [zero, zero, extra1, extra2, zero]
    right += neg(rest2) + [zero, zero, extra3, zero, zero]
    return left, right, rad


def products(left, right):
    a, b, c = [left[k : k + 8, :] for k in (0, 8, 16)]
    x, y, z = [right[k : k + 8, :] for k in (0, 8, 16)]
    pairs = [(a, x), (b, x), (a, y), (c, x), (a, z), (b, y), (b, z), (c, y)]
    return [jnp.concatenate(v, axis=0).astype(BF16) for v in zip(*pairs)]


def store_features(ref, rows, first):
    width = rows[0].shape[1]
    for k, row in enumerate(rows):
        for t, piece in enumerate(ref):
            at = pl.ds(first * ROWS + k, 8, stride=ROWS)
            piece[at, :] = row[:, t * LANES : min(width, (t + 1) * LANES)]


def load_features(ref, index):
    start = pl.multiple_of(index * ROWS, 8)
    blocks = [piece[pl.ds(start, ROWS), :] for piece in ref]
    return jnp.concatenate(blocks, axis=1) if len(blocks) > 1 else blocks[0]


def contract(left, right):
    return jnp.dot(left, right, preferred_element_type=F32)


def select_rows(index, value, count):
    row = lax.broadcasted_iota(jnp.int32, (count, index.shape[1]), 0)
    left = jnp.where(row == index, 1.0, 0.0).astype(BF16)
    high = value.astype(BF16)
    rest = value - high.astype(F32)
    mid = rest.astype(BF16)
    low = (rest - mid.astype(F32)).astype(BF16)
    return jnp.dot(
        jnp.concatenate([left] * 3, axis=1),
        jnp.concatenate([high, mid, low], axis=0),
        preferred_element_type=F32,
    )


def upright(row):
    return jnp.broadcast_to(row, (8, row.shape[1])).T[:, :1]


def keep(parts, rows, value):
    high = value.astype(BF16)
    parts[rows, :LANES] = high
    parts[rows, LANES:] = (value - high.astype(F32)).astype(BF16)


def add_columns(table, parts, indices):
    shape = (2 * LANES, table.shape[1])
    lane = lax.broadcasted_iota(jnp.int32, shape, 1)
    picks = [jnp.where(lane == index, 1.0, 0.0).astype(BF16) for index in indices]
    table[...] += jnp.dot(
        jnp.concatenate([p[...] for p in parts], axis=1),
        jnp.concatenate(picks, axis=0),
        preferred_element_type=F32,
    )


def inverse_root(d):
    return lax.rsqrt(d)


def fold(v):
    return jnp.sum(v.reshape(v.shape[0] // 8, 8, v.shape[1]), axis=0)


def distances(left, right, out):
    left, right = products(left, right)
    out[...] = contract(left.T, right)


def staged(spans, *stages):
    held = {}
    for t in range(len(spans) + len(stages) - 1):
        for depth in reversed(range(len(stages))):
            k = t - depth
            if 0 <= k < len(spans):
                held[k] = stages[depth](spans[k], held.get(k))
                if depth == len(stages) - 1:
                    del held[k]


def spans_of(height, step=32):
    step = min(step, height)
    return [slice(r, r + step) for r in range(0, height, step)]


def tile_sums(dist, qrow, qleft, parts):
    q0, q1 = qrow[:, :LANES], qrow[:, LANES:]
    qcol = upright(qleft)
    back = [jnp.zeros((8, LANES), F32), jnp.zeros((8, LANES), F32)]

    def root(rows, _):
        return (
            inverse_root(dist[rows, :LANES]),
            inverse_root(dist[rows, LANES:]),
        )

    def sums(rows, held):
        g0, g1 = held
        back[0] = back[0] + fold(g0 * qcol[rows, :])
        back[1] = back[1] + fold(g1 * qcol[rows, :])
        keep(parts, rows, g0 * q0 + g1 * q1)

    staged(spans_of(dist.shape[0]), root, sums)
    return jnp.concatenate([jnp.sum(b, axis=0, keepdims=True) for b in back], axis=1)


def pipeline(total, begin, finish, table, ring, parts):
    size = len(ring)
    ahead = min(2, size - 1)
    group = min(2, size)

    def body(i, carry):
        indices = []
        for k in range(size):
            begin(i * size + k + ahead, ring[(k + ahead) % size])
            indices.append(finish(i * size + k, ring[k], parts[k % len(parts)]))
            if len(indices) == group:
                done = [parts[(k - n) % len(parts)] for n in reversed(range(group))]
                add_columns(table, done, indices)
                indices = []
        return carry

    for k in range(ahead):
        begin(k, ring[k])
    lax.fori_loop(0, (total + size - 1) // size, body, 0)


def ring_size(total):
    return next(size for size in (16, 8, 4, 2, 1) if total % size == 0)


def assemble(sub, S, L, q, pieces):
    def place(s):
        for shift in range(S):
            owner = (s - shift) % S
            q[:, owner * L : (owner + 1) * L] = pieces[shift][: q.shape[0], :]

    for s in range(S):
        pl.when(sub == s)(functools.partial(place, s))


def pack_kernel(
    sizes, charges, mask, geo, basis_far, transfer_far, parent_far, targets, sources, live, masked, geo_out, *rest
):
    C, S, L, slots = sizes
    clusters = charges.shape[0]
    *packs, basis, transfer, parent, sems = rest
    copies = [
        pltpu.make_async_copy(src, dst, sems.at[k])
        for k, (src, dst) in enumerate(
            [(basis_far, basis), (transfer_far, transfer), (parent_far, parent)]
        )
    ]
    for copy in copies:
        copy.start()
    me, sub = lax.axis_index("clu"), lax.axis_index("sub")
    masked[:clusters, :] = charges[...] * mask[...].astype(F32)
    geo_out[...] = geo[...]
    lane = lax.broadcasted_iota(jnp.int32, (8, L), 1)
    for shift in range(1, C):
        dest = lax.rem(me + shift, C)
        codes = jnp.full((8, L), -1.0, F32)
        for j in range(slots):
            code = jnp.where(live[dest, j] > 0, sources[dest, j], -1)
            codes = jnp.where(lane == j, code.astype(F32), codes)
        packs[shift - 1][5 * slots :, :] = codes

    def fill(s):
        for shift in range(1, C):
            dest = lax.rem(me + shift, C)
            pack = packs[shift - 1]
            for j in range(slots):
                t = targets[dest, j]
                g = geo[t, :, s * L : (s + 1) * L]
                for k in range(4):
                    pack[k * slots + j : k * slots + j + 1, :] = g[k : k + 1]
                pack[4 * slots + j : 4 * slots + j + 1, :] = masked[pl.ds(t, 1), :]

    for s in range(S):
        pl.when(sub == s)(functools.partial(fill, s))
    for copy in copies:
        copy.wait()
    up = up_sums(basis, masked, transfer, parent, masked.shape[0] - clusters)
    masked[clusters:, :] = jnp.zeros((up.shape[0], L), F32)
    masked[clusters:, : up.shape[1]] = up


def remote_kernel(sizes, fb0, fb1, scale, *rest):
    C, S, L, slots, clusters, panels = sizes
    pieces = rest[:S]
    packs = rest[S : S + C - 1]
    acc_out = rest[S + C - 1]
    sends = rest[S + C : S + C + C - 1]
    q, tq, acc, fwdt, fa0, order, codes, sems, *work = rest[S + C + C - 1 :]
    fa, fb = (fa0,), (fb0, fb1)
    n = (C - 1) * slots
    copies = [
        pltpu.make_async_copy(packs[k].at[pl.ds(5 * slots, 8), :], codes.at[k], sems.at[k])
        for k in range(C - 1)
    ]
    for copy in copies:
        copy.start()
    assemble(lax.axis_index("sub"), S, L, q, pieces)
    acc[...] = jnp.zeros_like(acc)
    fwdt[...] = jnp.zeros_like(fwdt)
    for copy in copies:
        copy.wait()
    found = jnp.int32(0)
    for shift in range(C - 1):
        for j in range(slots):
            code = codes[shift, 0, j].astype(jnp.int32)
            order[n + 1 + shift * slots + j] = jnp.maximum(code, 0)
            order[found] = shift * slots + j
            found = found + (code >= 0).astype(jnp.int32)
    inv, centre = split_frame(scale)
    for shift in range(C - 1):
        for first in range(0, slots, 8):
            points = [packs[shift][k * slots + first : k * slots + first + 8, :] for k in range(5)]
            left, _, _ = split_features(points, centre, inv)
            store_features(fa, left, shift * slots + first)
            at = shift * slots + first
            tq[at : at + 8, :] = points[4]

    def begin(i, dist):
        slot = order[jnp.minimum(i, jnp.maximum(found - 1, 0))]
        distances(load_features(fa, slot), load_features(fb, order[n + 1 + slot]), dist)

    def finish(i, dist, part):
        ok = i < found
        slot = order[jnp.minimum(i, jnp.maximum(found - 1, 0))]
        source = order[n + 1 + slot]
        back = tile_sums(
            dist, q[pl.ds(source, 1), :], tq[pl.ds(slot, 1), :], part
        )
        acc[pl.ds(source, 1), :] += jnp.where(ok, back, 0.0)
        return jnp.where(ok, slot, -1)

    pipeline(found, begin, finish, fwdt, work[:8], work[8:])
    acc_out[...] = acc[...] * inv
    fwd = (fwdt[...] * inv).T
    up = sum(p[clusters:, :] for p in pieces)
    for shift in range(C - 1):
        sends[shift][:slots, :] = fwd[shift * slots : (shift + 1) * slots, :]
        sends[shift][slots:, :] = up


def prepare_kernel(geo, fa0, fa1, fb0, fb1, diag, scale):
    inv, centre = frame(geo)
    scale[...] = jnp.zeros_like(scale)
    scale[0:1, :] = jnp.broadcast_to(inv, (1, LANES))
    for k in range(3):
        scale[k + 1 : k + 2, :] = jnp.broadcast_to(centre[k : k + 1, :], (1, LANES))
    inv, centre = split_frame(scale)
    for first in range(0, geo.shape[0], 8):
        points = [geo[first : first + 8, k, :] for k in range(4)]
        left, right, rad = split_features(points, centre, inv)
        store_features((fa0, fa1), left, first)
        store_features((fb0, fb1), right, first)
        diag[first : first + 8, :] = lax.rsqrt(2.0 * (rad * rad))


def local_kernel(sizes, geo_pairs, pairs, fa0, fa1, fb0, fb1, diags, scale, acc_in, *rest):
    S, L, R, clusters, panels = sizes
    pieces = rest[:S]
    parts = rest[S : 2 * S]
    q, acc, self_sums, pair_sums, *work = rest[2 * S :]
    ring, sums = work[:16], work[16:]
    fa, fb = (fa0, fa1), (fb0, fb1)
    sub, rep = lax.axis_index("sub"), lax.axis_index("rep")
    assemble(sub, S, L, q, pieces)
    acc[...] = jnp.zeros_like(acc)
    self_sums[...] = jnp.zeros_like(self_sums)
    pair_sums[...] = jnp.zeros_like(pair_sums)

    half = panels // 2
    share = clusters // (S * R)
    first = (rep * S + sub) * share

    def begin_self(i, dist):
        c = first + jnp.minimum(i, share - 1)
        left, right = products(load_features(fa, c), load_features(fb, c))
        left = left.T
        dist[:half, :] = contract(left[:half, :], right)
        dist[half:, half:] = contract(left[half:, :], right[:, half:])

    def finish_self(i, dist, parts):
        c = first + i
        qrow = q[pl.ds(c, 1), :]
        qcol = upright(qrow[:, :half])
        diag = diags[pl.ds(c, 1), :]
        back = [jnp.zeros((8, LANES), F32)]

        def eye(span):
            shape = (span.stop - span.start, half)
            row = lax.broadcasted_iota(jnp.int32, shape, 0) + span.start % half
            return row == lax.broadcasted_iota(jnp.int32, shape, 1)

        def root(span, _):
            if span.start < half:
                return (
                    jnp.where(eye(span), diag[:, :half], inverse_root(dist[span, :half])),
                    inverse_root(dist[span, half:]),
                )
            return (jnp.where(eye(span), diag[:, half:], inverse_root(dist[span, half:])),)

        def partial(span, held):
            if span.start < half:
                g0, g1 = held
                back[0] = back[0] + fold(g1 * qcol[span, :])
                keep(parts, span, g0 * qrow[:, :half] + g1 * qrow[:, half:])
            else:
                keep(parts, span, held[0] * qrow[:, half:])

        staged(spans_of(panels), root, partial)
        back = jnp.sum(back[0], axis=0, keepdims=True)
        acc[pl.ds(c, 1), :] += jnp.concatenate([jnp.zeros_like(back), back], axis=1)
        return c

    pipeline(share, begin_self, finish_self, self_sums, ring[: ring_size(share)], sums)

    count = pairs.shape[1] // S
    start = sub * count

    def begin(i, dist):
        p = start + jnp.minimum(i, count - 1)
        distances(load_features(fa, pairs[0, p]), load_features(fb, pairs[1, p]), dist)

    def finish(i, dist, part):
        ia, ib = pairs[0, start + i], pairs[1, start + i]
        acc[pl.ds(ib, 1), :] += tile_sums(
            dist, q[pl.ds(ib, 1), :], q[pl.ds(ia, 1), :], part
        )
        return start + i

    pipeline(count, begin, finish, pair_sums, ring[: ring_size(count)], sums)
    total = acc[...] + self_sums[...].T
    width = geo_pairs.shape[1]
    total = total + select_rows(geo_pairs[0:1, :], pair_sums[...].T[:width, :], clusters)
    total = acc_in[...] + total * scale[0:1, 0:1]

    def give(s):
        for shift in range(S):
            other = (s + shift) % S
            parts[shift][...] = total[:, other * L : (other + 1) * L]

    for s in range(S):
        pl.when(sub == s)(functools.partial(give, s))


def merge_kernel(sizes, far_list, targets, coupling, transfer, parent, *rest):
    C, S, L, slots, clusters = sizes
    near = rest[:S]
    pieces = rest[S : 2 * S]
    sums = rest[2 * S : 2 * S + C - 1]
    near_out, field_out, parents = rest[2 * S + C - 1 :]
    me = lax.axis_index("clu")
    index = [targets[pl.ds(lax.rem(me + shift, C), 1), :] for shift in range(1, C)]
    got = select_rows(
        jnp.concatenate(index, axis=1), jnp.concatenate([v[:slots, :] for v in sums], axis=0), clusters
    )

    near_out[...] = got + sum(v[...] for v in near)

    par_dev, far_n, rank = coupling.shape[0], coupling.shape[1], coupling.shape[2]
    own = sum(p[clusters:, :rank] for p in pieces)
    parents[pl.ds(pl.multiple_of(me * par_dev, 8), par_dev), :] = own
    for shift in range(1, C):
        owner = lax.rem(me + shift, C)
        parents[pl.ds(pl.multiple_of(owner * par_dev, 8), par_dev), :] = sums[shift - 1][slots:, :rank]
    lane = lax.broadcasted_iota(jnp.int32, (rank, LANES), 1)
    field = jnp.zeros((rank, LANES), F32)
    for p in range(par_dev):
        part = jnp.zeros((rank, rank), F32)
        for k in range(far_n):
            part = part + coupling[p, k] * parents[pl.ds(far_list[k, p], 1), :]
        field = jnp.where(lane == p, jnp.sum(part, axis=1, keepdims=True), field)
    which = lax.broadcasted_iota(jnp.int32, (LANES, clusters), 0)
    onehot = (parent[...] == which).astype(F32)
    down = jnp.dot(field, onehot, precision=HIGHEST, preferred_element_type=F32)
    for r in range(rank):
        field_out[r : r + 1, :] = jnp.sum(transfer[r] * down, axis=0, keepdims=True)


def up_sums(basis, masked, transfer, parent, count):
    clusters = basis.shape[0]
    rank = basis.shape[1]
    lane = lax.broadcasted_iota(jnp.int32, (rank, clusters), 1)
    leaf = jnp.zeros((rank, clusters), F32)
    for c in range(clusters):
        part = jnp.sum(basis[c] * masked[c : c + 1, :], axis=1, keepdims=True)
        leaf = jnp.where(lane == c, part, leaf)
    lifted = jnp.zeros((rank, clusters), F32)
    for r in range(rank):
        lifted = lifted + transfer[r] * leaf[r : r + 1, :]
    which = lax.broadcasted_iota(jnp.int32, (count, clusters), 0)
    onehot = (parent[...] == which).astype(F32)
    return lax.dot_general(
        onehot, lifted, (((1,), (1,)), ((), ())), precision=HIGHEST, preferred_element_type=F32
    )


def far_kernel(basis, field, near, out):
    for c in range(basis.shape[0]):
        far = jnp.sum(basis[c] * field[:, c : c + 1], axis=0, keepdims=True)
        out[c : c + 1, :] = far + near[c : c + 1, :]


def send(value, moves):
    names = tuple(name for name, _ in moves)
    steps = [step for _, step in moves]
    sizes = [lax.axis_size(name) for name in names]
    perm = []

    def flat(coords):
        index = 0
        for size, c in zip(sizes, coords):
            index = index * size + c
        return index

    total = 1
    for size in sizes:
        total *= size
    for index in range(total):
        coords, left = [], index
        for size in reversed(sizes):
            coords.append(left % size)
            left //= size
        coords.reverse()
        perm.append((index, flat([(c + s) % n for c, s, n in zip(coords, steps, sizes)])))
    return lax.ppermute(value, names if len(names) > 1 else names[0], perm)


def on_device(
    charges,
    panel_mask,
    geometry,
    remote_source,
    remote_target,
    remote_live,
    local_pairs,
    basis,
    transfer,
    parent_of,
    far_list,
    coupling,
):
    clusters, L = charges.shape
    panels = geometry.shape[2]
    C, S, R = lax.axis_size("clu"), lax.axis_size("sub"), lax.axis_size("rep")
    slots = remote_source.shape[2]
    par_dev, rank = far_list.shape[0], transfer.shape[1]
    n = (C - 1) * slots
    shape = jax.ShapeDtypeStruct
    targets = remote_target[0]
    basis_t = jnp.transpose(basis, (0, 2, 1))
    transfer_t = jnp.transpose(transfer, (1, 2, 0))
    parent = parent_of[None, :]

    made = pl.pallas_call(
        functools.partial(pack_kernel, (C, S, L, slots)),
        out_shape=[pltpu.VMEM((clusters + par_dev, L), F32), pltpu.VMEM(geometry.shape, F32)]
        + [pltpu.VMEM((5 * slots + 8, L), F32)] * (C - 1),
        in_specs=[vmem()] * 3 + [pl.BlockSpec(memory_space=pltpu.HBM)] * 3 + [smem()] * 3,
        out_specs=[vmem()] * (C + 1),
        scratch_shapes=[
            pltpu.VMEM(basis_t.shape, F32),
            pltpu.VMEM(transfer_t.shape, F32),
            pltpu.VMEM(parent.shape, jnp.int32),
            pltpu.SemaphoreType.DMA((3,)),
        ],
        compiler_params=limit(60),
        cost_estimate=about(3),
        name="packs",
    )(
        charges,
        panel_mask,
        geometry,
        *far_off(basis_t, transfer_t, parent),
        targets,
        remote_source[0],
        remote_live[0],
    )
    masked, geo, packs = made[0], made[1], made[2:]
    pieces = [masked] + [send(masked, (("sub", d),)) for d in range(1, S)]
    packs = [send(packs[d - 1], (("clu", d),)) for d in range(1, C)]

    features = pl.pallas_call(
        prepare_kernel,
        out_shape=[pltpu.VMEM((clusters * ROWS, LANES), F32)] * 4
        + [pltpu.VMEM((clusters, panels), F32), pltpu.VMEM((8, LANES), F32)],
        in_specs=[vmem()],
        out_specs=[vmem()] * 6,
        compiler_params=limit(24),
        cost_estimate=about(4),
        name="prepare",
    )(*near_by(geo))
    fb0, fb1, scale = features[2], features[3], features[5]

    made = pl.pallas_call(
        functools.partial(remote_kernel, (C, S, L, slots, clusters, panels)),
        out_shape=[pltpu.VMEM((clusters, panels), F32)]
        + [pltpu.VMEM((slots + par_dev, L), F32)] * (C - 1),
        in_specs=[vmem()] * (3 + S + C - 1),
        out_specs=[vmem()] * C,
        scratch_shapes=[
            pltpu.VMEM((clusters, panels), F32),
            pltpu.VMEM((n, L), F32),
            pltpu.VMEM((clusters, panels), F32),
            pltpu.VMEM((L, whole(n)), F32),
            pltpu.VMEM((n * ROWS, L), F32),
            pltpu.SMEM((2 * n + 1,), jnp.int32),
            pltpu.SMEM((C - 1, 8, L), F32),
            pltpu.SemaphoreType.DMA((C - 1,)),
        ]
        + [pltpu.VMEM((L, panels), F32)] * 8
        + [pltpu.VMEM((L, 2 * LANES), BF16)] * 4,
        compiler_params=limit(24),
        cost_estimate=about(6),
        name="near_remote",
    )(*near_by(fb0, fb1, scale, *pieces, *packs))
    acc, sums = made[0], made[1:]

    wide = whole(local_pairs.shape[1])
    parts = pl.pallas_call(
        functools.partial(local_kernel, (S, L, R, clusters, panels)),
        out_shape=[pltpu.VMEM((clusters, L), F32)] * S,
        in_specs=[vmem(), smem()] + [vmem()] * (7 + S),
        out_specs=[vmem()] * S,
        scratch_shapes=[
            pltpu.VMEM((clusters, panels), F32),
            pltpu.VMEM((clusters, panels), F32),
            pltpu.VMEM((panels, clusters), F32),
            pltpu.VMEM((panels, wide), F32),
        ]
        + [pltpu.VMEM((panels, panels), F32)] * 16
        + [pltpu.VMEM((panels, 2 * LANES), BF16)] * 4,
        compiler_params=limit(24),
        cost_estimate=about(12),
        name="near_local",
    )(*near_by(local_pairs[0].T), local_pairs[0].T, *near_by(*features, acc, *pieces))
    near = [parts[0]] + [send(parts[d], (("sub", d),)) for d in range(1, S)]
    sums = [send(sums[d - 1], (("clu", C - d),)) for d in range(1, C)]

    near, field = pl.pallas_call(
        functools.partial(merge_kernel, (C, S, L, slots, clusters)),
        out_shape=[pltpu.VMEM((clusters, L), F32), pltpu.VMEM((rank, clusters), F32)],
        in_specs=[smem()] + [vmem()] * (4 + 2 * S + C - 1),
        out_specs=[vmem()] * 2,
        scratch_shapes=[pltpu.VMEM((C * par_dev, rank), F32)],
        compiler_params=limit(16),
        cost_estimate=about(2),
        name="merge",
    )(far_list.T, *near_by(targets, coupling, transfer_t, parent, *near, *pieces, *sums))
    others = [send(near, (("rep", e),)) for e in range(1, R)]

    total = pl.pallas_call(
        far_kernel,
        out_shape=pltpu.VMEM((clusters, L), F32),
        in_specs=[vmem()] * 3,
        out_specs=vmem(),
        compiler_params=limit(16),
        cost_estimate=about(1),
        name="far_down",
    )(*near_by(basis_t, field, near))
    for other in others:
        total = total + other
    return total * panel_mask.astype(F32)


def solution(mesh):
    placed = (
        P(("grp", "clu"), "sub"),
        P(("grp", "clu"), "sub"),
        P(("grp", "clu"), None, None),
        P(("grp", "clu"), None, "rep"),
        P(("grp", "clu"), None, "rep"),
        P(("grp", "clu"), None, "rep"),
        P(("grp", "clu"), "rep", None),
        P(("grp", "clu"), "sub", None),
        P(("grp", "clu"), None, None),
        P(("grp", "clu")),
        P(("grp", "clu"), None),
        P(("grp", "clu"), None, None, None),
    )
    return jax.shard_map(
        on_device, mesh=mesh, in_specs=placed, out_specs=P(("grp", "clu"), "sub"), check_vma=False
    )
```

```python
import functools

import jax
import jax.numpy as jnp
from jax import lax
from jax.experimental import pallas as pl
from jax.experimental.pallas import tpu as pltpu
from jax.sharding import PartitionSpec as P

F32 = jnp.float32
BF16 = jnp.bfloat16
HIGHEST = lax.Precision.HIGHEST
ROWS = 24
LANES = 128


def limit(mib):
    return pltpu.CompilerParams(vmem_limit_bytes=mib * 1024 * 1024)


def about(us):
    return pl.CostEstimate(flops=0, bytes_accessed=int(us * 3.5e6), transcendentals=0)


def vmem():
    return pl.BlockSpec(memory_space=pltpu.VMEM)


def near_by(*arrays):
    return [pltpu.with_memory_space_constraint(x, pltpu.VMEM) for x in arrays]


def far_off(*arrays):
    return [pltpu.with_memory_space_constraint(x, pltpu.HBM) for x in arrays]


def smem():
    return pl.BlockSpec(memory_space=pltpu.SMEM)


def whole(size):
    return -(-size // LANES) * LANES


def cut(v):
    return v.astype(BF16).astype(F32)


def powers(sign):
    lane = lax.broadcasted_iota(jnp.int32, (8, LANES), 1)
    out = jnp.full((8, LANES), 2.0 ** (-64 * sign), F32)
    for bit in range(7):
        out = out * jnp.where((lane >> bit) & 1 == 1, F32(2.0 ** (sign * 2**bit)), F32(1.0))
    return out


def frame(geo):
    low, high = [None] * 8, [None] * 8
    for c in range(geo.shape[0]):
        g, k = geo[c], c % 8
        low[k] = g if low[k] is None else jnp.minimum(low[k], g)
        high[k] = g if high[k] is None else jnp.maximum(high[k], g)
    low = jnp.min(functools.reduce(jnp.minimum, low), axis=1, keepdims=True)
    high = jnp.max(functools.reduce(jnp.maximum, high), axis=1, keepdims=True)
    row = lax.broadcasted_iota(jnp.int32, low.shape, 0)
    radius = jnp.maximum(jnp.abs(low), jnp.abs(high))
    width = jnp.max(jnp.where(row == 3, radius, 0.5 * (high - low)), axis=0, keepdims=True)

    def over(table, least):
        return least(least(table, axis=1, keepdims=True), axis=0, keepdims=True)

    up, down = powers(1), powers(-1)
    size = over(jnp.where(up >= width, up, F32(2.0**63)), jnp.min)
    inv = over(jnp.where(up >= width, down, F32(2.0**-63)), jnp.max)
    magic = size * F32(1.5 * 2.0**20)
    return inv, (0.5 * (low + high) + magic) - magic


def split_frame(scale):
    return scale[0:1, 0:1], [scale[k : k + 1, 0:1] for k in range(1, 4)]


def split_features(points, centre, inv):
    magic = F32(1.5 * 2.0**16)
    grid, rest = [], []
    for k in range(3):
        u = (points[k] - centre[k]) * inv
        h = cut((u + magic) - magic)
        grid.append(h)
        rest.append(u - h)
    rad = points[3] * inv
    norm = grid[0] * grid[0] + grid[1] * grid[1] + grid[2] * grid[2]
    norm1 = cut(norm)
    norm2 = cut(norm - norm1)
    cross = grid[0] * rest[0] + grid[1] * rest[1] + grid[2] * rest[2]
    extra = 2.0 * cross + (rest[0] * rest[0] + rest[1] * rest[1] + rest[2] * rest[2]) + rad * rad
    extra = extra + ((norm - norm1) - norm2)
    extra1 = cut(extra)
    extra2 = cut(extra - extra1)
    extra3 = (extra - extra1) - extra2
    rest1 = [cut(v) for v in rest]
    rest2 = [v - w for v, w in zip(rest, rest1)]
    neg = lambda vs: [-2.0 * v for v in vs]
    one, zero = jnp.ones_like(rad), jnp.zeros_like(rad)
    left = grid + [norm1, norm2, one, one, zero]
    left += rest1 + [extra1, extra2, zero, zero, zero]
    left += rest2 + [extra3, zero, zero, zero, zero]
    right = neg(grid) + [one, one, norm1, norm2, zero]
    right += neg(rest1) + [zero, zero, extra1, extra2, zero]
    right += neg(rest2) + [zero, zero, extra3, zero, zero]
    return left, right, rad


def products(left, right):
    a, b, c = [left[k : k + 8, :] for k in (0, 8, 16)]
    x, y, z = [right[k : k + 8, :] for k in (0, 8, 16)]
    pairs = [(a, x), (b, x), (a, y), (c, x), (a, z), (b, y), (b, z), (c, y)]
    return [jnp.concatenate(v, axis=0).astype(BF16) for v in zip(*pairs)]


def store_features(ref, rows, first):
    width = rows[0].shape[1]
    for t, piece in enumerate(ref):
        count = piece.shape[0] // ROWS
        for k, row in enumerate(rows):
            at = k * count + first
            piece[at : at + 8, :] = row[:, t * LANES : min(width, (t + 1) * LANES)]


def load_features(ref, index):
    blocks = []
    for piece in ref:
        count = piece.shape[0] // ROWS
        groups = [piece[pl.ds(k * count + index, 8, stride=count), :] for k in range(0, ROWS, 8)]
        blocks.append(jnp.concatenate(groups, axis=0))
    return jnp.concatenate(blocks, axis=1) if len(blocks) > 1 else blocks[0]


def contract(left, right):
    return jnp.dot(left, right, preferred_element_type=F32)


def select_rows(index, value, count):
    row = lax.broadcasted_iota(jnp.int32, (count, index.shape[1]), 0)
    left = jnp.where(row == index, 1.0, 0.0).astype(BF16)
    high = value.astype(BF16)
    rest = value - high.astype(F32)
    mid = rest.astype(BF16)
    low = (rest - mid.astype(F32)).astype(BF16)
    return jnp.dot(
        jnp.concatenate([left] * 3, axis=1),
        jnp.concatenate([high, mid, low], axis=0),
        preferred_element_type=F32,
    )


def upright(row):
    return jnp.broadcast_to(row, (8, row.shape[1])).T[:, :1]


def keep(parts, rows, value):
    high = value.astype(BF16)
    parts[rows, :LANES] = high
    parts[rows, LANES:] = (value - high.astype(F32)).astype(BF16)


def add_columns(table, parts, indices):
    shape = (2 * LANES, table.shape[1])
    lane = lax.broadcasted_iota(jnp.int32, shape, 1)
    picks = [jnp.where(lane == index, 1.0, 0.0).astype(BF16) for index in indices]
    table[...] += jnp.dot(
        jnp.concatenate([p[...] for p in parts], axis=1),
        jnp.concatenate(picks, axis=0),
        preferred_element_type=F32,
    )


def inverse_root(d):
    return lax.rsqrt(d)


def fold(v):
    return jnp.sum(v.reshape(v.shape[0] // 8, 8, v.shape[1]), axis=0)


def distances(left, right, out):
    left, right = products(left, right)
    out[...] = contract(left.T, right)


def staged(spans, *stages):
    held = {}
    for t in range(len(spans) + len(stages) - 1):
        for depth in reversed(range(len(stages))):
            k = t - depth
            if 0 <= k < len(spans):
                held[k] = stages[depth](spans[k], held.get(k))
                if depth == len(stages) - 1:
                    del held[k]


def spans_of(height, step=32):
    step = min(step, height)
    return [slice(r, r + step) for r in range(0, height, step)]


def tile_sums(dist, qrow, qleft, parts):
    q0, q1 = qrow[:, :LANES], qrow[:, LANES:]
    qcol = upright(qleft)
    back = [jnp.zeros((8, LANES), F32), jnp.zeros((8, LANES), F32)]

    def root(rows, _):
        return (
            inverse_root(dist[rows, :LANES]),
            inverse_root(dist[rows, LANES:]),
        )

    def sums(rows, held):
        g0, g1 = held
        back[0] = back[0] + fold(g0 * qcol[rows, :])
        back[1] = back[1] + fold(g1 * qcol[rows, :])
        keep(parts, rows, g0 * q0 + g1 * q1)

    staged(spans_of(dist.shape[0]), root, sums)
    return jnp.concatenate([jnp.sum(b, axis=0, keepdims=True) for b in back], axis=1)


def pipeline(total, begin, finish, table, ring, parts):
    size = len(ring)
    ahead = min(2, size - 1)
    group = min(2, size)

    def body(i, carry):
        indices = []
        for k in range(size):
            begin(i * size + k + ahead, ring[(k + ahead) % size])
            indices.append(finish(i * size + k, ring[k], parts[k % len(parts)]))
            if len(indices) == group:
                done = [parts[(k - n) % len(parts)] for n in reversed(range(group))]
                add_columns(table, done, indices)
                indices = []
        return carry

    for k in range(ahead):
        begin(k, ring[k])
    lax.fori_loop(0, (total + size - 1) // size, body, 0)


def ring_size(total):
    return next(size for size in (16, 8, 4, 2, 1) if total % size == 0)


def assemble(sub, S, L, q, pieces):
    def place(s):
        for shift in range(S):
            owner = (s - shift) % S
            q[:, owner * L : (owner + 1) * L] = pieces[shift][: q.shape[0], :]

    for s in range(S):
        pl.when(sub == s)(functools.partial(place, s))


def pack_kernel(sizes, charges, mask, geo, targets, sources, live, masked, geo_out, *packs):
    C, S, L, slots = sizes
    me, sub = lax.axis_index("clu"), lax.axis_index("sub")
    masked[...] = charges[...] * mask[...].astype(F32)
    geo_out[...] = geo[...]
    lane = lax.broadcasted_iota(jnp.int32, (8, L), 1)
    for shift in range(1, C):
        dest = lax.rem(me + shift, C)
        codes = jnp.full((8, L), -1.0, F32)
        for j in range(slots):
            code = jnp.where(live[dest, j] > 0, sources[dest, j], -1)
            codes = jnp.where(lane == j, code.astype(F32), codes)
        packs[shift - 1][5 * slots :, :] = codes

    def fill(s):
        for shift in range(1, C):
            dest = lax.rem(me + shift, C)
            pack = packs[shift - 1]
            for j in range(slots):
                t = targets[dest, j]
                g = geo[t, :, s * L : (s + 1) * L]
                for k in range(4):
                    pack[k * slots + j : k * slots + j + 1, :] = g[k : k + 1]
                pack[4 * slots + j : 4 * slots + j + 1, :] = masked[pl.ds(t, 1), :]

    for s in range(S):
        pl.when(sub == s)(functools.partial(fill, s))


def remote_kernel(sizes, fb0, fb1, scale, up, *rest):
    C, S, L, slots, clusters, panels = sizes
    pieces = rest[:S]
    packs = rest[S : S + C - 1]
    acc_out = rest[S + C - 1]
    sends = rest[S + C : S + C + C - 1]
    q, tq, acc, fwdt, fa0, order, codes, sems, *work = rest[S + C + C - 1 :]
    fa, fb = (fa0,), (fb0, fb1)
    n = (C - 1) * slots
    copies = [
        pltpu.make_async_copy(packs[k].at[pl.ds(5 * slots, 8), :], codes.at[k], sems.at[k])
        for k in range(C - 1)
    ]
    for copy in copies:
        copy.start()
    assemble(lax.axis_index("sub"), S, L, q, pieces)
    acc[...] = jnp.zeros_like(acc)
    fwdt[...] = jnp.zeros_like(fwdt)
    for copy in copies:
        copy.wait()
    found = jnp.int32(0)
    for shift in range(C - 1):
        for j in range(slots):
            code = codes[shift, 0, j].astype(jnp.int32)
            order[n + 1 + shift * slots + j] = jnp.maximum(code, 0)
            order[found] = shift * slots + j
            found = found + (code >= 0).astype(jnp.int32)
    inv, centre = split_frame(scale)
    for shift in range(C - 1):
        for first in range(0, slots, 8):
            points = [packs[shift][k * slots + first : k * slots + first + 8, :] for k in range(5)]
            left, _, _ = split_features(points, centre, inv)
            store_features(fa, left, shift * slots + first)
            at = shift * slots + first
            tq[at : at + 8, :] = points[4]

    def begin(i, dist):
        slot = order[jnp.minimum(i, jnp.maximum(found - 1, 0))]
        distances(load_features(fa, slot), load_features(fb, order[n + 1 + slot]), dist)

    def finish(i, dist, part):
        ok = i < found
        slot = order[jnp.minimum(i, jnp.maximum(found - 1, 0))]
        source = order[n + 1 + slot]
        back = tile_sums(
            dist, q[pl.ds(source, 1), :], tq[pl.ds(slot, 1), :], part
        )
        acc[pl.ds(source, 1), :] += jnp.where(ok, back, 0.0)
        return jnp.where(ok, slot, -1)

    pipeline(found, begin, finish, fwdt, work[:8], work[8:])
    acc_out[...] = acc[...] * inv
    fwd = (fwdt[...] * inv).T
    rank = up.shape[1]
    for shift in range(C - 1):
        sends[shift][:slots, :] = fwd[shift * slots : (shift + 1) * slots, :]
        sends[shift][slots:, :] = jnp.zeros((up.shape[0], L), F32)
        sends[shift][slots:, :rank] = up[...]


def prepare_kernel(
    geo, masked, basis_far, transfer_far, parent_far,
    fa0, fa1, fb0, fb1, diag, scale, up, basis, transfer, parent, sems
):
    copies = [
        pltpu.make_async_copy(src, dst, sems.at[k])
        for k, (src, dst) in enumerate(
            [(basis_far, basis), (transfer_far, transfer), (parent_far, parent)]
        )
    ]
    for copy in copies:
        copy.start()
    inv, centre = frame(geo)
    scale[...] = jnp.zeros_like(scale)
    scale[0:1, :] = jnp.broadcast_to(inv, (1, LANES))
    for k in range(3):
        scale[k + 1 : k + 2, :] = jnp.broadcast_to(centre[k : k + 1, :], (1, LANES))
    inv, centre = split_frame(scale)
    for first in range(0, geo.shape[0], 8):
        points = [geo[first : first + 8, k, :] for k in range(4)]
        left, right, rad = split_features(points, centre, inv)
        store_features((fa0, fa1), left, first)
        store_features((fb0, fb1), right, first)
        diag[first : first + 8, :] = lax.rsqrt(2.0 * (rad * rad))
    for copy in copies:
        copy.wait()
    up[...] = up_sums(basis, masked, transfer, parent, up.shape[0])


def local_kernel(sizes, pair_rows, pairs, fa0, fa1, fb0, fb1, scale, acc_in, *rest):
    S, L, R, clusters, panels = sizes
    pieces = rest[:S]
    acc_out = rest[S]
    q, acc, pair_sums, *work = rest[S + 1 :]
    ring, sums = work[:16], work[16:]
    fa, fb = (fa0, fa1), (fb0, fb1)
    sub = lax.axis_index("sub")
    assemble(sub, S, L, q, pieces)
    acc[...] = jnp.zeros_like(acc)
    pair_sums[...] = jnp.zeros_like(pair_sums)

    count = pairs.shape[1] // S
    start = sub * count

    def begin(i, dist):
        p = start + jnp.minimum(i, count - 1)
        distances(load_features(fa, pairs[0, p]), load_features(fb, pairs[1, p]), dist)

    def finish(i, dist, part):
        ia, ib = pairs[0, start + i], pairs[1, start + i]
        acc[pl.ds(ib, 1), :] += tile_sums(
            dist, q[pl.ds(ib, 1), :], q[pl.ds(ia, 1), :], part
        )
        return start + i

    pipeline(count, begin, finish, pair_sums, ring[: ring_size(count)], sums)
    width = pair_rows.shape[1]
    total = acc[...] + select_rows(pair_rows[0:1, :], pair_sums[...].T[:width, :], clusters)
    acc_out[...] = acc_in[...] + total * scale[0:1, 0:1]


def self_shares(clusters, S, R):
    base = clusters // R
    unit = base // 4 if R > 1 else 0
    return base, unit


def self_kernel(sizes, fa0, fa1, fb0, fb1, diags, scale, part, *rest):
    S, L, R, clusters, panels = sizes
    pieces = rest[:S]
    out, q, fs, spots, self_sums, *work = rest[S:]
    ring, sums = work[:16], work[16:]
    sub, rep = lax.axis_index("sub"), lax.axis_index("rep")
    assemble(sub, S, L, q, pieces)
    self_sums[...] = jnp.zeros_like(self_sums)

    def place(s):
        t, at = (s * L) // LANES, (s * L) % LANES
        fs[...] = (fa0, fa1)[t][:, at : at + L]
        spots[...] = diags[:, s * L : (s + 1) * L]

    for s in range(S):
        pl.when(sub == s)(functools.partial(place, s))
    base, unit = self_shares(clusters, S, R)
    first = rep * base - jnp.where(rep > 0, unit, 0)
    share = base + jnp.where(rep == R - 1, unit, 0) - jnp.where(rep == 0, unit, 0)

    def begin(i, dist):
        c = first + jnp.minimum(i, share - 1)
        distances(load_features((fs,), c), load_features((fb0, fb1), c), dist)

    def finish(i, dist, parts):
        c = first + i
        qrow = q[pl.ds(c, 1), :]
        diag = upright(spots[pl.ds(c, 1), :])

        def root(span, _):
            shape = (span.stop - span.start, LANES)
            row = lax.broadcasted_iota(jnp.int32, shape, 0) + (sub * L + span.start)
            col = lax.broadcasted_iota(jnp.int32, shape, 1)
            return [
                jnp.where(row == col + t, diag[span, :], inverse_root(dist[span, t : t + LANES]))
                for t in range(0, panels, LANES)
            ]

        def partial(span, held):
            keep(parts, span, sum(g * qrow[:, t * LANES : (t + 1) * LANES] for t, g in enumerate(held)))

        staged(spans_of(L), root, partial)
        return c

    pipeline(share, begin, finish, self_sums, ring[: ring_size(unit or base)], sums)
    out[...] = part[...]
    out[:clusters, :] = part[:clusters, :] + self_sums[...].T * scale[0:1, 0:1]


def merge_kernel(sizes, far_list, targets, near, coupling, transfer, parent, up, *rest):
    C, S, L, slots, clusters = sizes
    sums = rest[: C - 1]
    parts = rest[C - 1 : C - 1 + S]
    parents = rest[-1]
    me, sub = lax.axis_index("clu"), lax.axis_index("sub")
    index = [targets[pl.ds(lax.rem(me + shift, C), 1), :] for shift in range(1, C)]
    got = select_rows(
        jnp.concatenate(index, axis=1), jnp.concatenate([v[:slots, :] for v in sums], axis=0), clusters
    )

    par_dev, far_n, rank = coupling.shape[0], coupling.shape[1], coupling.shape[2]
    parents[pl.ds(pl.multiple_of(me * par_dev, 8), par_dev), :] = up[...]
    for shift in range(1, C):
        owner = lax.rem(me + shift, C)
        parents[pl.ds(pl.multiple_of(owner * par_dev, 8), par_dev), :] = sums[shift - 1][slots:, :rank]
    lane = lax.broadcasted_iota(jnp.int32, (rank, LANES), 1)
    field = jnp.zeros((rank, LANES), F32)
    for p in range(par_dev):
        part = jnp.zeros((rank, rank), F32)
        for k in range(far_n):
            part = part + coupling[p, k] * parents[pl.ds(far_list[k, p], 1), :]
        field = jnp.where(lane == p, jnp.sum(part, axis=1, keepdims=True), field)
    which = lax.broadcasted_iota(jnp.int32, (LANES, clusters), 0)
    onehot = (parent[...] == which).astype(F32)
    down = jnp.dot(field, onehot, precision=HIGHEST, preferred_element_type=F32)
    fields = jnp.concatenate(
        [jnp.sum(transfer[r] * down, axis=0, keepdims=True) for r in range(rank)], axis=0
    )

    def give(s):
        for shift in range(S):
            other = (s + shift) % S
            part = near[:, other * L : (other + 1) * L]
            parts[shift][:clusters, :] = part + got if shift == 0 else part
            for t in range(clusters // L):
                at = clusters + t * rank
                parts[shift][at : at + rank, :] = fields[:, t * L : (t + 1) * L]

    for s in range(S):
        pl.when(sub == s)(functools.partial(give, s))


def up_sums(basis, masked, transfer, parent, count):
    clusters = basis.shape[0]
    rank = basis.shape[1]
    lane = lax.broadcasted_iota(jnp.int32, (rank, clusters), 1)
    leaf = jnp.zeros((rank, clusters), F32)
    for c in range(clusters):
        part = jnp.sum(basis[c] * masked[c : c + 1, :], axis=1, keepdims=True)
        leaf = jnp.where(lane == c, part, leaf)
    lifted = jnp.zeros((rank, clusters), F32)
    for r in range(rank):
        lifted = lifted + transfer[r] * leaf[r : r + 1, :]
    which = lax.broadcasted_iota(jnp.int32, (count, clusters), 0)
    onehot = (parent[...] == which).astype(F32)
    return lax.dot_general(
        onehot, lifted, (((1,), (1,)), ((), ())), precision=HIGHEST, preferred_element_type=F32
    )


def far_kernel(basis, near, out):
    clusters, rank = basis.shape[0], basis.shape[1]
    L = out.shape[1]
    fields = [near[clusters + t * rank : clusters + (t + 1) * rank, :] for t in range(clusters // L)]
    fields = jnp.concatenate(fields, axis=1) if len(fields) > 1 else fields[0]
    for c in range(clusters):
        far = jnp.sum(basis[c] * fields[:, c : c + 1], axis=0, keepdims=True)
        out[c : c + 1, :] = far + near[c : c + 1, :]


def send(value, moves):
    names = tuple(name for name, _ in moves)
    steps = [step for _, step in moves]
    sizes = [lax.axis_size(name) for name in names]
    perm = []

    def flat(coords):
        index = 0
        for size, c in zip(sizes, coords):
            index = index * size + c
        return index

    total = 1
    for size in sizes:
        total *= size
    for index in range(total):
        coords, left = [], index
        for size in reversed(sizes):
            coords.append(left % size)
            left //= size
        coords.reverse()
        perm.append((index, flat([(c + s) % n for c, s, n in zip(coords, steps, sizes)])))
    return lax.ppermute(value, names if len(names) > 1 else names[0], perm)


def on_device(
    charges,
    panel_mask,
    geometry,
    remote_source,
    remote_target,
    remote_live,
    local_pairs,
    basis,
    transfer,
    parent_of,
    far_list,
    coupling,
):
    clusters, L = charges.shape
    panels = geometry.shape[2]
    C, S, R = lax.axis_size("clu"), lax.axis_size("sub"), lax.axis_size("rep")
    slots = remote_source.shape[2]
    par_dev, rank = far_list.shape[0], transfer.shape[1]
    n = (C - 1) * slots
    shape = jax.ShapeDtypeStruct
    targets = remote_target[0]
    basis_t = jnp.transpose(basis, (0, 2, 1))
    transfer_t = jnp.transpose(transfer, (1, 2, 0))
    parent = parent_of[None, :]

    made = pl.pallas_call(
        functools.partial(pack_kernel, (C, S, L, slots)),
        out_shape=[pltpu.VMEM((clusters, L), F32), pltpu.VMEM(geometry.shape, F32)]
        + [pltpu.VMEM((5 * slots + 8, L), F32)] * (C - 1),
        in_specs=[vmem()] * 3 + [smem()] * 3,
        out_specs=[vmem()] * (C + 1),
        compiler_params=limit(60),
        cost_estimate=about(2),
        name="packs",
    )(charges, panel_mask, geometry, targets, remote_source[0], remote_live[0])
    masked, geo, packs = made[0], made[1], made[2:]
    pieces = [masked] + [send(masked, (("sub", d),)) for d in range(1, S)]
    packs = [send(packs[d - 1], (("clu", d),)) for d in range(1, C)]

    *features, up = pl.pallas_call(
        prepare_kernel,
        out_shape=[pltpu.VMEM((clusters * ROWS, LANES), F32)] * 4
        + [
            pltpu.VMEM((clusters, panels), F32),
            pltpu.VMEM((8, LANES), F32),
            pltpu.VMEM((par_dev, rank), F32),
        ],
        in_specs=[vmem()] * 2 + [pl.BlockSpec(memory_space=pltpu.HBM)] * 3,
        out_specs=[vmem()] * 7,
        scratch_shapes=[
            pltpu.VMEM(basis_t.shape, F32),
            pltpu.VMEM(transfer_t.shape, F32),
            pltpu.VMEM(parent.shape, jnp.int32),
            pltpu.SemaphoreType.DMA((3,)),
        ],
        compiler_params=limit(24),
        cost_estimate=about(4),
        name="prepare",
    )(*near_by(geo, masked), *far_off(basis_t, transfer_t, parent))
    *tables, diags, scale = features

    made = pl.pallas_call(
        functools.partial(remote_kernel, (C, S, L, slots, clusters, panels)),
        out_shape=[pltpu.VMEM((clusters, panels), F32)]
        + [pltpu.VMEM((slots + par_dev, L), F32)] * (C - 1),
        in_specs=[vmem()] * (4 + S + C - 1),
        out_specs=[vmem()] * C,
        scratch_shapes=[
            pltpu.VMEM((clusters, panels), F32),
            pltpu.VMEM((n, L), F32),
            pltpu.VMEM((clusters, panels), F32),
            pltpu.VMEM((L, whole(n)), F32),
            pltpu.VMEM((n * ROWS, L), F32),
            pltpu.SMEM((2 * n + 1,), jnp.int32),
            pltpu.SMEM((C - 1, 8, L), F32),
            pltpu.SemaphoreType.DMA((C - 1,)),
        ]
        + [pltpu.VMEM((L, panels), F32)] * 8
        + [pltpu.VMEM((L, 2 * LANES), BF16)] * 4,
        compiler_params=limit(24),
        cost_estimate=about(6),
        name="near_remote",
    )(*near_by(*tables[2:], scale, up, *pieces, *packs))
    acc, sums = made[0], [send(made[d], (("clu", C - d),)) for d in range(1, C)]

    wide = whole(local_pairs.shape[1])
    near = pl.pallas_call(
        functools.partial(local_kernel, (S, L, R, clusters, panels)),
        out_shape=pltpu.VMEM((clusters, panels), F32),
        in_specs=[vmem(), smem()] + [vmem()] * (6 + S),
        out_specs=vmem(),
        scratch_shapes=[
            pltpu.VMEM((clusters, panels), F32),
            pltpu.VMEM((clusters, panels), F32),
            pltpu.VMEM((panels, wide), F32),
        ]
        + [pltpu.VMEM((panels, panels), F32)] * 16
        + [pltpu.VMEM((panels, 2 * LANES), BF16)] * 4,
        compiler_params=limit(24),
        cost_estimate=about(9),
        name="near_local",
    )(*near_by(local_pairs[0].T), local_pairs[0].T, *near_by(*tables, scale, acc, *pieces))

    height = clusters + clusters // L * rank
    parts = pl.pallas_call(
        functools.partial(merge_kernel, (C, S, L, slots, clusters)),
        out_shape=[pltpu.VMEM((height, L), F32)] * S,
        in_specs=[smem()] + [vmem()] * (6 + C - 1),
        out_specs=[vmem()] * S,
        scratch_shapes=[pltpu.VMEM((C * par_dev, rank), F32)],
        compiler_params=limit(16),
        cost_estimate=about(1),
        name="merge",
    )(far_list.T, *near_by(targets, near, coupling, transfer_t, parent, up, *sums))
    others = [send(parts[d], (("sub", d),)) for d in range(1, S)]

    near = pl.pallas_call(
        functools.partial(self_kernel, (S, L, R, clusters, panels)),
        out_shape=pltpu.VMEM((height, L), F32),
        in_specs=[vmem()] * (7 + S),
        out_specs=vmem(),
        scratch_shapes=[
            pltpu.VMEM((clusters, panels), F32),
            pltpu.VMEM((clusters * ROWS, L), F32),
            pltpu.VMEM((clusters, L), F32),
            pltpu.VMEM((L, clusters), F32),
        ]
        + [pltpu.VMEM((L, panels), F32)] * 16
        + [pltpu.VMEM((L, 2 * LANES), BF16)] * 4,
        compiler_params=limit(24),
        cost_estimate=about(4),
        name="near_self",
    )(*near_by(*tables, diags, scale, parts[0], *pieces))
    for other in others:
        near = near + other
    others = [send(near, (("rep", e),)) for e in range(1, R)]

    total = pl.pallas_call(
        far_kernel,
        out_shape=pltpu.VMEM((clusters, L), F32),
        in_specs=[vmem()] * 2,
        out_specs=vmem(),
        compiler_params=limit(16),
        cost_estimate=about(1),
        name="far_down",
    )(*near_by(basis_t, near))
    for other in others:
        total = total + other[:clusters]
    return total * panel_mask.astype(F32)


def solution(mesh):
    placed = (
        P(("grp", "clu"), "sub"),
        P(("grp", "clu"), "sub"),
        P(("grp", "clu"), None, None),
        P(("grp", "clu"), None, "rep"),
        P(("grp", "clu"), None, "rep"),
        P(("grp", "clu"), None, "rep"),
        P(("grp", "clu"), "rep", None),
        P(("grp", "clu"), "sub", None),
        P(("grp", "clu"), None, None),
        P(("grp", "clu")),
        P(("grp", "clu"), None),
        P(("grp", "clu"), None, None, None),
    )
    return jax.shard_map(
        on_device, mesh=mesh, in_specs=placed, out_specs=P(("grp", "clu"), "sub"), check_vma=False
    )
```

```python
import functools

import jax
import jax.numpy as jnp
from jax import lax
from jax.experimental import pallas as pl
from jax.experimental.pallas import tpu as pltpu
from jax.sharding import PartitionSpec as P

F32 = jnp.float32
BF16 = jnp.bfloat16
HIGHEST = lax.Precision.HIGHEST
ROWS = 24
LANES = 128


def limit(mib):
    return pltpu.CompilerParams(vmem_limit_bytes=mib * 1024 * 1024)


def about(us):
    return pl.CostEstimate(flops=0, bytes_accessed=int(us * 3.5e6), transcendentals=0)


def vmem():
    return pl.BlockSpec(memory_space=pltpu.VMEM)


def near_by(*arrays):
    return [pltpu.with_memory_space_constraint(x, pltpu.VMEM) for x in arrays]


def far_off(*arrays):
    return [pltpu.with_memory_space_constraint(x, pltpu.HBM) for x in arrays]


def smem():
    return pl.BlockSpec(memory_space=pltpu.SMEM)


def whole(size):
    return -(-size // LANES) * LANES


def cut(v):
    return v.astype(BF16).astype(F32)


def powers(sign):
    lane = lax.broadcasted_iota(jnp.int32, (8, LANES), 1)
    out = jnp.full((8, LANES), 2.0 ** (-64 * sign), F32)
    for bit in range(7):
        out = out * jnp.where((lane >> bit) & 1 == 1, F32(2.0 ** (sign * 2**bit)), F32(1.0))
    return out


def frame(geo):
    low, high = [None] * 8, [None] * 8
    blocks = [(t, c) for c in range(0, geo.shape[1], 8) for t in range(geo.shape[0])]
    for i, (t, c) in enumerate(blocks):
        g, k = geo[t, c : c + 8, :], i % 8
        low[k] = g if low[k] is None else jnp.minimum(low[k], g)
        high[k] = g if high[k] is None else jnp.maximum(high[k], g)
    low = jnp.min(functools.reduce(jnp.minimum, low), axis=1, keepdims=True)
    high = jnp.max(functools.reduce(jnp.maximum, high), axis=1, keepdims=True)
    low, high = jnp.minimum(low[:4], low[4:]), jnp.maximum(high[:4], high[4:])
    row = lax.broadcasted_iota(jnp.int32, low.shape, 0)
    radius = jnp.maximum(jnp.abs(low), jnp.abs(high))
    width = jnp.max(jnp.where(row == 3, radius, 0.5 * (high - low)), axis=0, keepdims=True)

    def over(table, least):
        return least(least(table, axis=1, keepdims=True), axis=0, keepdims=True)

    up, down = powers(1), powers(-1)
    size = over(jnp.where(up >= width, up, F32(2.0**63)), jnp.min)
    inv = over(jnp.where(up >= width, down, F32(2.0**-63)), jnp.max)
    magic = size * F32(1.5 * 2.0**20)
    return inv, (0.5 * (low + high) + magic) - magic


def split_frame(scale):
    return scale[0:1, 0:1], [scale[k : k + 1, 0:1] for k in range(1, 4)]


def split_features(points, centre, inv):
    magic = F32(1.5 * 2.0**16)
    grid, rest = [], []
    for k in range(3):
        u = (points[k] - centre[k]) * inv
        h = cut((u + magic) - magic)
        grid.append(h)
        rest.append(u - h)
    rad = points[3] * inv
    norm = grid[0] * grid[0] + grid[1] * grid[1] + grid[2] * grid[2]
    norm1 = cut(norm)
    norm2 = cut(norm - norm1)
    cross = grid[0] * rest[0] + grid[1] * rest[1] + grid[2] * rest[2]
    extra = 2.0 * cross + (rest[0] * rest[0] + rest[1] * rest[1] + rest[2] * rest[2]) + rad * rad
    extra = extra + ((norm - norm1) - norm2)
    extra1 = cut(extra)
    extra2 = cut(extra - extra1)
    extra3 = (extra - extra1) - extra2
    rest1 = [cut(v) for v in rest]
    rest2 = [v - w for v, w in zip(rest, rest1)]
    neg = lambda vs: [-2.0 * v for v in vs]
    one, zero = jnp.ones_like(rad), jnp.zeros_like(rad)
    left = grid + [norm1, norm2, one, one, zero]
    left += rest1 + [extra1, extra2, zero, zero, zero]
    left += rest2 + [extra3, zero, zero, zero, zero]
    right = neg(grid) + [one, one, norm1, norm2, zero]
    right += neg(rest1) + [zero, zero, extra1, extra2, zero]
    right += neg(rest2) + [zero, zero, extra3, zero, zero]
    return left, right, rad


def products(left, right):
    a, b, c = [left[k : k + 8, :] for k in (0, 8, 16)]
    x, y, z = [right[k : k + 8, :] for k in (0, 8, 16)]
    pairs = [(a, x), (b, x), (a, y), (c, x), (a, z), (b, y), (b, z), (c, y)]
    return [jnp.concatenate(v, axis=0).astype(BF16) for v in zip(*pairs)]


def store_features(ref, rows, first):
    width = rows[0].shape[1]
    for k, row in enumerate(rows):
        for t in range(ref.shape[0]):
            at = pl.ds(first * ROWS + k, 8, stride=ROWS)
            ref[t, at, :] = row[:, t * LANES : min(width, (t + 1) * LANES)]


def load_features(ref, index, order=None):
    start = pl.multiple_of(index * ROWS, 8)
    order = range(ref.shape[0]) if order is None else order
    blocks = [ref[t, pl.ds(start, ROWS), :] for t in order]
    return jnp.concatenate(blocks, axis=1) if len(blocks) > 1 else blocks[0]


def contract(left, right):
    return jnp.dot(left, right, preferred_element_type=F32)


def select_rows(index, value, count):
    row = lax.broadcasted_iota(jnp.int32, (count, index.shape[1]), 0)
    left = jnp.where(row == index, 1.0, 0.0).astype(BF16)
    high = value.astype(BF16)
    rest = value - high.astype(F32)
    mid = rest.astype(BF16)
    low = (rest - mid.astype(F32)).astype(BF16)
    return jnp.dot(
        jnp.concatenate([left] * 3, axis=1),
        jnp.concatenate([high, mid, low], axis=0),
        preferred_element_type=F32,
    )


def upright(row):
    return jnp.broadcast_to(row, (8, row.shape[1])).T[:, :1]


def keep(parts, rows, value):
    high = value.astype(BF16)
    parts[rows, :LANES] = high
    parts[rows, LANES:] = (value - high.astype(F32)).astype(BF16)


def add_columns(table, parts, indices):
    shape = (2 * LANES, table.shape[1])
    lane = lax.broadcasted_iota(jnp.int32, shape, 1)
    picks = [jnp.where(lane == index, 1.0, 0.0).astype(BF16) for index in indices]
    table[...] += jnp.dot(
        jnp.concatenate([p[...] for p in parts], axis=1),
        jnp.concatenate(picks, axis=0),
        preferred_element_type=F32,
    )


def inverse_root(d):
    return lax.rsqrt(d)


def fold(v):
    return jnp.sum(v.reshape(v.shape[0] // 8, 8, v.shape[1]), axis=0)


def distances(left, right, out):
    left, right = products(left, right)
    out[...] = contract(left.T, right)


def staged(spans, *stages):
    held = {}
    for t in range(len(spans) + len(stages) - 1):
        for depth in reversed(range(len(stages))):
            k = t - depth
            if 0 <= k < len(spans):
                held[k] = stages[depth](spans[k], held.get(k))
                if depth == len(stages) - 1:
                    del held[k]


def spans_of(height, step=32):
    step = min(step, height)
    return [slice(r, r + step) for r in range(0, height, step)]


def tile_sums(dist, qrow, qleft, parts):
    q0, q1 = qrow[:, :LANES], qrow[:, LANES:]
    qcol = upright(qleft)
    back = [jnp.zeros((8, LANES), F32), jnp.zeros((8, LANES), F32)]

    def root(rows, _):
        return (
            inverse_root(dist[rows, :LANES]),
            inverse_root(dist[rows, LANES:]),
        )

    def sums(rows, held):
        g0, g1 = held
        back[0] = back[0] + fold(g0 * qcol[rows, :])
        back[1] = back[1] + fold(g1 * qcol[rows, :])
        keep(parts, rows, g0 * q0 + g1 * q1)

    staged(spans_of(dist.shape[0]), root, sums)
    return jnp.concatenate([jnp.sum(b, axis=0, keepdims=True) for b in back], axis=1)


def pipeline(total, begin, finish, table, ring, parts):
    size = len(ring)
    ahead = min(2, size - 1)
    group = min(2, size)

    def body(i, carry):
        indices = []
        for k in range(size):
            begin(i * size + k + ahead, ring[(k + ahead) % size])
            indices.append(finish(i * size + k, ring[k], parts[k % len(parts)]))
            if len(indices) == group:
                done = [parts[(k - n) % len(parts)] for n in reversed(range(group))]
                add_columns(table, done, indices)
                indices = []
        return carry

    for k in range(ahead):
        begin(k, ring[k])
    lax.fori_loop(0, (total + size - 1) // size, body, 0)


def ring_size(total):
    return next(size for size in (16, 8, 4, 2, 1) if total % size == 0)


def assemble(sub, S, L, q, pieces):
    def place(s):
        for shift in range(S):
            owner = (s - shift) % S
            q[:, owner * L : (owner + 1) * L] = pieces[shift][: q.shape[0], :]

    for s in range(S):
        pl.when(sub == s)(functools.partial(place, s))


def pack_kernel(sizes, charges, mask, geo, targets, sources, live, masked, geo_out, *packs):
    C, S, L, slots = sizes
    me, sub = lax.axis_index("clu"), lax.axis_index("sub")
    masked[...] = charges[...] * mask[...].astype(F32)
    for t in range(geo_out.shape[0]):
        geo_out[t, :, :] = geo[:, :, t * LANES : (t + 1) * LANES].reshape(geo_out.shape[1:])
    lane = lax.broadcasted_iota(jnp.int32, (8, L), 1)
    for shift in range(1, C):
        dest = lax.rem(me + shift, C)
        codes = jnp.full((8, L), -1.0, F32)
        for j in range(slots):
            code = jnp.where(live[dest, j] > 0, sources[dest, j], -1)
            codes = jnp.where(lane == j, code.astype(F32), codes)
        packs[shift - 1][5 * slots :, :] = codes

    def fill(s):
        for shift in range(1, C):
            dest = lax.rem(me + shift, C)
            pack = packs[shift - 1]
            for j in range(slots):
                t = targets[dest, j]
                g = geo[t, :, s * L : (s + 1) * L]
                for k in range(4):
                    pack[k * slots + j : k * slots + j + 1, :] = g[k : k + 1]
                pack[4 * slots + j : 4 * slots + j + 1, :] = masked[pl.ds(t, 1), :]

    for s in range(S):
        pl.when(sub == s)(functools.partial(fill, s))


def remote_kernel(sizes, fb, scale, up, *rest):
    C, S, L, slots, clusters, panels = sizes
    pieces = rest[:S]
    packs = rest[S : S + C - 1]
    acc_out = rest[S + C - 1]
    sends = rest[S + C : S + C + C - 1]
    q, tq, acc, fwdt, fa, order, codes, sems, *work = rest[S + C + C - 1 :]
    n = (C - 1) * slots
    copies = [
        pltpu.make_async_copy(packs[k].at[pl.ds(5 * slots, 8), :], codes.at[k], sems.at[k])
        for k in range(C - 1)
    ]
    for copy in copies:
        copy.start()
    assemble(lax.axis_index("sub"), S, L, q, pieces)
    acc[...] = jnp.zeros_like(acc)
    fwdt[...] = jnp.zeros_like(fwdt)
    for copy in copies:
        copy.wait()
    found = jnp.int32(0)
    for shift in range(C - 1):
        for j in range(slots):
            code = codes[shift, 0, j].astype(jnp.int32)
            order[n + 1 + shift * slots + j] = jnp.maximum(code, 0)
            order[found] = shift * slots + j
            found = found + (code >= 0).astype(jnp.int32)
    inv, centre = split_frame(scale)
    for shift in range(C - 1):
        for first in range(0, slots, 8):
            points = [packs[shift][k * slots + first : k * slots + first + 8, :] for k in range(5)]
            left, _, _ = split_features(points, centre, inv)
            store_features(fa, left, shift * slots + first)
            at = shift * slots + first
            tq[at : at + 8, :] = points[4]

    def begin(i, dist):
        slot = order[jnp.minimum(i, jnp.maximum(found - 1, 0))]
        distances(load_features(fa, slot), load_features(fb, order[n + 1 + slot]), dist)

    def finish(i, dist, part):
        ok = i < found
        slot = order[jnp.minimum(i, jnp.maximum(found - 1, 0))]
        source = order[n + 1 + slot]
        back = tile_sums(
            dist, q[pl.ds(source, 1), :], tq[pl.ds(slot, 1), :], part
        )
        acc[pl.ds(source, 1), :] += jnp.where(ok, back, 0.0)
        return jnp.where(ok, slot, -1)

    pipeline(found, begin, finish, fwdt, work[:8], work[8:])
    acc_out[...] = acc[...] * inv
    fwd = (fwdt[...] * inv).T
    rank = up.shape[1]
    for shift in range(C - 1):
        sends[shift][:slots, :] = fwd[shift * slots : (shift + 1) * slots, :]
        sends[shift][slots:, :] = jnp.zeros((up.shape[0], L), F32)
        sends[shift][slots:, :rank] = up[...]


def prepare_kernel(
    geo, masked, basis_far, transfer_far, parent_far,
    fa, fb, diag, scale, up, basis, transfer, parent, sems
):
    copies = [
        pltpu.make_async_copy(src, dst, sems.at[k])
        for k, (src, dst) in enumerate(
            [(basis_far, basis), (transfer_far, transfer), (parent_far, parent)]
        )
    ]
    for copy in copies:
        copy.start()
    inv, centre = frame(geo)
    scale[...] = jnp.zeros_like(scale)
    scale[0:1, :] = jnp.broadcast_to(inv, (1, LANES))
    for k in range(3):
        scale[k + 1 : k + 2, :] = jnp.broadcast_to(centre[k : k + 1, :], (1, LANES))
    inv, centre = split_frame(scale)
    for first in range(0, diag.shape[0], 8):
        points = [
            jnp.concatenate(
                [geo[t, pl.ds(first * 4 + k, 8, stride=4), :] for t in range(geo.shape[0])], axis=1
            )
            for k in range(4)
        ]
        left, right, rad = split_features(points, centre, inv)
        store_features(fa, left, first)
        store_features(fb, right, first)
        diag[first : first + 8, :] = lax.rsqrt(2.0 * (rad * rad))
    for copy in copies:
        copy.wait()
    up[...] = up_sums(basis, masked, transfer, parent, up.shape[0])


def local_kernel(sizes, pair_rows, pairs, fa, fb, scale, acc_in, *rest):
    S, L, R, clusters, panels = sizes
    pieces = rest[:S]
    acc_out = rest[S]
    q, acc, pair_sums, *work = rest[S + 1 :]
    ring, sums = work[:16], work[16:]
    sub = lax.axis_index("sub")
    assemble(sub, S, L, q, pieces)
    acc[...] = jnp.zeros_like(acc)
    pair_sums[...] = jnp.zeros_like(pair_sums)

    count = pairs.shape[1] // S
    start = sub * count

    def begin(i, dist):
        p = start + jnp.minimum(i, count - 1)
        distances(load_features(fa, pairs[0, p]), load_features(fb, pairs[1, p]), dist)

    def finish(i, dist, part):
        ia, ib = pairs[0, start + i], pairs[1, start + i]
        acc[pl.ds(ib, 1), :] += tile_sums(
            dist, q[pl.ds(ib, 1), :], q[pl.ds(ia, 1), :], part
        )
        return start + i

    pipeline(count, begin, finish, pair_sums, ring[: ring_size(count)], sums)
    width = pair_rows.shape[1]
    total = acc[...] + select_rows(pair_rows[0:1, :], pair_sums[...].T[:width, :], clusters)
    acc_out[...] = acc_in[...] + total * scale[0:1, 0:1]


def self_shares(clusters, S, R):
    base = clusters // R
    unit = base // 4 if R > 1 else 0
    return base, unit


def self_kernel(sizes, fa, fb, diags, scale, part, *rest):
    S, L, R, clusters, panels = sizes
    pieces = rest[:S]
    out, q, fs, spots, self_sums, *work = rest[S:]
    ring, sums = work[:16], work[16:]
    sub, rep = lax.axis_index("sub"), lax.axis_index("rep")
    self_sums[...] = jnp.zeros_like(self_sums)
    blocks = L == LANES
    if blocks:
        order = [lax.rem(sub + S - shift, S) for shift in range(S)]
        for shift in range(S):
            q[:, shift * L : (shift + 1) * L] = pieces[shift][...]
    else:
        order = None
        assemble(sub, S, L, q, pieces)

    def place(s):
        if not blocks:
            t, at = (s * L) // LANES, (s * L) % LANES
            fs[0, :, :] = fa[t, :, at : at + L]
        spots[...] = diags[:, s * L : (s + 1) * L]

    for s in range(S):
        pl.when(sub == s)(functools.partial(place, s))
    base, unit = self_shares(clusters, S, R)
    first = rep * base - jnp.where(rep > 0, unit, 0)
    share = base + jnp.where(rep == R - 1, unit, 0) - jnp.where(rep == 0, unit, 0)

    def begin(i, dist):
        c = first + jnp.minimum(i, share - 1)
        own = load_features(fa, c, order[:1]) if blocks else load_features(fs, c)
        distances(own, load_features(fb, c, order), dist)

    def finish(i, dist, parts):
        c = first + i
        qrow = q[pl.ds(c, 1), :]
        diag = upright(spots[pl.ds(c, 1), :])

        def root(span, _):
            shape = (span.stop - span.start, LANES)
            row = lax.broadcasted_iota(jnp.int32, shape, 0) + span.start
            row = row if blocks else row + sub * L
            col = lax.broadcasted_iota(jnp.int32, shape, 1)
            values = [inverse_root(dist[span, t : t + LANES]) for t in range(0, panels, LANES)]
            for t in range(1 if blocks else len(values)):
                values[t] = jnp.where(row == col + t * LANES, diag[span, :], values[t])
            return values

        def partial(span, held):
            keep(parts, span, sum(g * qrow[:, t * LANES : (t + 1) * LANES] for t, g in enumerate(held)))

        staged(spans_of(L), root, partial)
        return c

    pipeline(share, begin, finish, self_sums, ring[: ring_size(unit or base)], sums)
    out[...] = part[...]
    out[:clusters, :] = part[:clusters, :] + self_sums[...].T * scale[0:1, 0:1]


def merge_kernel(sizes, far_list, targets, near, coupling, transfer, parent, up, *rest):
    C, S, L, slots, clusters = sizes
    sums = rest[: C - 1]
    parts = rest[C - 1 : C - 1 + S]
    parents = rest[-1]
    me, sub = lax.axis_index("clu"), lax.axis_index("sub")
    index = [targets[pl.ds(lax.rem(me + shift, C), 1), :] for shift in range(1, C)]
    got = select_rows(
        jnp.concatenate(index, axis=1), jnp.concatenate([v[:slots, :] for v in sums], axis=0), clusters
    )

    par_dev, far_n, rank = coupling.shape[0], coupling.shape[1], coupling.shape[2]
    parents[pl.ds(pl.multiple_of(me * par_dev, 8), par_dev), :] = up[...]
    for shift in range(1, C):
        owner = lax.rem(me + shift, C)
        parents[pl.ds(pl.multiple_of(owner * par_dev, 8), par_dev), :] = sums[shift - 1][slots:, :rank]
    lane = lax.broadcasted_iota(jnp.int32, (rank, LANES), 1)
    field = jnp.zeros((rank, LANES), F32)
    for p in range(par_dev):
        part = jnp.zeros((rank, rank), F32)
        for k in range(far_n):
            part = part + coupling[p, k] * parents[pl.ds(far_list[k, p], 1), :]
        field = jnp.where(lane == p, jnp.sum(part, axis=1, keepdims=True), field)
    which = lax.broadcasted_iota(jnp.int32, (LANES, clusters), 0)
    onehot = (parent[...] == which).astype(F32)
    down = jnp.dot(field, onehot, precision=HIGHEST, preferred_element_type=F32)
    fields = jnp.concatenate(
        [jnp.sum(transfer[r] * down, axis=0, keepdims=True) for r in range(rank)], axis=0
    )

    def give(s):
        for shift in range(S):
            other = (s + shift) % S
            part = near[:, other * L : (other + 1) * L]
            parts[shift][:clusters, :] = part + got if shift == 0 else part
            for t in range(clusters // L):
                at = clusters + t * rank
                parts[shift][at : at + rank, :] = fields[:, t * L : (t + 1) * L]

    for s in range(S):
        pl.when(sub == s)(functools.partial(give, s))


def up_sums(basis, masked, transfer, parent, count):
    clusters = basis.shape[0]
    rank = basis.shape[1]
    lane = lax.broadcasted_iota(jnp.int32, (rank, clusters), 1)
    leaf = jnp.zeros((rank, clusters), F32)
    for c in range(clusters):
        part = jnp.sum(basis[c] * masked[c : c + 1, :], axis=1, keepdims=True)
        leaf = jnp.where(lane == c, part, leaf)
    lifted = jnp.zeros((rank, clusters), F32)
    for r in range(rank):
        lifted = lifted + transfer[r] * leaf[r : r + 1, :]
    which = lax.broadcasted_iota(jnp.int32, (count, clusters), 0)
    onehot = (parent[...] == which).astype(F32)
    return lax.dot_general(
        onehot, lifted, (((1,), (1,)), ((), ())), precision=HIGHEST, preferred_element_type=F32
    )


def far_kernel(basis, near, out):
    clusters, rank = basis.shape[0], basis.shape[1]
    L = out.shape[1]
    fields = [near[clusters + t * rank : clusters + (t + 1) * rank, :] for t in range(clusters // L)]
    fields = jnp.concatenate(fields, axis=1) if len(fields) > 1 else fields[0]
    for c in range(clusters):
        far = jnp.sum(basis[c] * fields[:, c : c + 1], axis=0, keepdims=True)
        out[c : c + 1, :] = far + near[c : c + 1, :]


def send(value, moves):
    names = tuple(name for name, _ in moves)
    steps = [step for _, step in moves]
    sizes = [lax.axis_size(name) for name in names]
    perm = []

    def flat(coords):
        index = 0
        for size, c in zip(sizes, coords):
            index = index * size + c
        return index

    total = 1
    for size in sizes:
        total *= size
    for index in range(total):
        coords, left = [], index
        for size in reversed(sizes):
            coords.append(left % size)
            left //= size
        coords.reverse()
        perm.append((index, flat([(c + s) % n for c, s, n in zip(coords, steps, sizes)])))
    return lax.ppermute(value, names if len(names) > 1 else names[0], perm)


def on_device(
    charges,
    panel_mask,
    geometry,
    remote_source,
    remote_target,
    remote_live,
    local_pairs,
    basis,
    transfer,
    parent_of,
    far_list,
    coupling,
):
    clusters, L = charges.shape
    panels = geometry.shape[2]
    C, S, R = lax.axis_size("clu"), lax.axis_size("sub"), lax.axis_size("rep")
    slots = remote_source.shape[2]
    par_dev, rank = far_list.shape[0], transfer.shape[1]
    n = (C - 1) * slots
    shape = jax.ShapeDtypeStruct
    targets = remote_target[0]
    basis_t = jnp.transpose(basis, (0, 2, 1))
    transfer_t = jnp.transpose(transfer, (1, 2, 0))
    parent = parent_of[None, :]

    made = pl.pallas_call(
        functools.partial(pack_kernel, (C, S, L, slots)),
        out_shape=[pltpu.VMEM((clusters, L), F32), pltpu.VMEM((panels // LANES, clusters * 4, LANES), F32)]
        + [pltpu.VMEM((5 * slots + 8, L), F32)] * (C - 1),
        in_specs=[vmem()] * 3 + [smem()] * 3,
        out_specs=[vmem()] * (C + 1),
        compiler_params=limit(60),
        cost_estimate=about(2),
        name="packs",
    )(charges, panel_mask, geometry, targets, remote_source[0], remote_live[0])
    masked, geo, packs = made[0], made[1], made[2:]
    pieces = [masked] + [send(masked, (("sub", d),)) for d in range(1, S)]
    packs = [send(packs[d - 1], (("clu", d),)) for d in range(1, C)]

    *features, up = pl.pallas_call(
        prepare_kernel,
        out_shape=[pltpu.VMEM((panels // LANES, clusters * ROWS, LANES), F32)] * 2
        + [
            pltpu.VMEM((clusters, panels), F32),
            pltpu.VMEM((8, LANES), F32),
            pltpu.VMEM((par_dev, rank), F32),
        ],
        in_specs=[vmem()] * 2 + [pl.BlockSpec(memory_space=pltpu.HBM)] * 3,
        out_specs=[vmem()] * 5,
        scratch_shapes=[
            pltpu.VMEM(basis_t.shape, F32),
            pltpu.VMEM(transfer_t.shape, F32),
            pltpu.VMEM(parent.shape, jnp.int32),
            pltpu.SemaphoreType.DMA((3,)),
        ],
        compiler_params=limit(24),
        cost_estimate=about(4),
        name="prepare",
    )(*near_by(geo, masked), *far_off(basis_t, transfer_t, parent))
    *tables, diags, scale = features

    made = pl.pallas_call(
        functools.partial(remote_kernel, (C, S, L, slots, clusters, panels)),
        out_shape=[pltpu.VMEM((clusters, panels), F32)]
        + [pltpu.VMEM((slots + par_dev, L), F32)] * (C - 1),
        in_specs=[vmem()] * (3 + S + C - 1),
        out_specs=[vmem()] * C,
        scratch_shapes=[
            pltpu.VMEM((clusters, panels), F32),
            pltpu.VMEM((n, L), F32),
            pltpu.VMEM((clusters, panels), F32),
            pltpu.VMEM((L, whole(n)), F32),
            pltpu.VMEM((1, n * ROWS, L), F32),
            pltpu.SMEM((2 * n + 1,), jnp.int32),
            pltpu.SMEM((C - 1, 8, L), F32),
            pltpu.SemaphoreType.DMA((C - 1,)),
        ]
        + [pltpu.VMEM((L, panels), F32)] * 8
        + [pltpu.VMEM((L, 2 * LANES), BF16)] * 4,
        compiler_params=limit(24),
        cost_estimate=about(6),
        name="near_remote",
    )(*near_by(tables[1], scale, up, *pieces, *packs))
    acc, sums = made[0], [send(made[d], (("clu", C - d),)) for d in range(1, C)]

    wide = whole(local_pairs.shape[1])
    near = pl.pallas_call(
        functools.partial(local_kernel, (S, L, R, clusters, panels)),
        out_shape=pltpu.VMEM((clusters, panels), F32),
        in_specs=[vmem(), smem()] + [vmem()] * (4 + S),
        out_specs=vmem(),
        scratch_shapes=[
            pltpu.VMEM((clusters, panels), F32),
            pltpu.VMEM((clusters, panels), F32),
            pltpu.VMEM((panels, wide), F32),
        ]
        + [pltpu.VMEM((panels, panels), F32)] * 16
        + [pltpu.VMEM((panels, 2 * LANES), BF16)] * 4,
        compiler_params=limit(24),
        cost_estimate=about(9),
        name="near_local",
    )(*near_by(local_pairs[0].T), local_pairs[0].T, *near_by(*tables, scale, acc, *pieces))

    height = clusters + clusters // L * rank
    parts = pl.pallas_call(
        functools.partial(merge_kernel, (C, S, L, slots, clusters)),
        out_shape=[pltpu.VMEM((height, L), F32)] * S,
        in_specs=[smem()] + [vmem()] * (6 + C - 1),
        out_specs=[vmem()] * S,
        scratch_shapes=[pltpu.VMEM((C * par_dev, rank), F32)],
        compiler_params=limit(16),
        cost_estimate=about(1),
        name="merge",
    )(far_list.T, *near_by(targets, near, coupling, transfer_t, parent, up, *sums))
    others = [send(parts[d], (("sub", d),)) for d in range(1, S)]

    near = pl.pallas_call(
        functools.partial(self_kernel, (S, L, R, clusters, panels)),
        out_shape=pltpu.VMEM((height, L), F32),
        in_specs=[vmem()] * (5 + S),
        out_specs=vmem(),
        scratch_shapes=[
            pltpu.VMEM((clusters, panels), F32),
            pltpu.VMEM((1, 8 if L == LANES else clusters * ROWS, L), F32),
            pltpu.VMEM((clusters, L), F32),
            pltpu.VMEM((L, clusters), F32),
        ]
        + [pltpu.VMEM((L, panels), F32)] * 16
        + [pltpu.VMEM((L, 2 * LANES), BF16)] * 4,
        compiler_params=limit(24),
        cost_estimate=about(4),
        name="near_self",
    )(*near_by(*tables, diags, scale, parts[0], *pieces))
    for other in others:
        near = near + other
    others = [send(near, (("rep", e),)) for e in range(1, R)]

    total = pl.pallas_call(
        far_kernel,
        out_shape=pltpu.VMEM((clusters, L), F32),
        in_specs=[vmem()] * 2,
        out_specs=vmem(),
        compiler_params=limit(16),
        cost_estimate=about(1),
        name="far_down",
    )(*near_by(basis_t, near))
    for other in others:
        total = total + other[:clusters]
    return total * panel_mask.astype(F32)


def solution(mesh):
    placed = (
        P(("grp", "clu"), "sub"),
        P(("grp", "clu"), "sub"),
        P(("grp", "clu"), None, None),
        P(("grp", "clu"), None, "rep"),
        P(("grp", "clu"), None, "rep"),
        P(("grp", "clu"), None, "rep"),
        P(("grp", "clu"), "rep", None),
        P(("grp", "clu"), "sub", None),
        P(("grp", "clu"), None, None),
        P(("grp", "clu")),
        P(("grp", "clu"), None),
        P(("grp", "clu"), None, None, None),
    )
    return jax.shard_map(
        on_device, mesh=mesh, in_specs=placed, out_specs=P(("grp", "clu"), "sub"), check_vma=False
    )
```

```python
import functools

import jax
import jax.numpy as jnp
from jax import lax
from jax.experimental import pallas as pl
from jax.experimental.pallas import tpu as pltpu
from jax.sharding import PartitionSpec as P

F32 = jnp.float32
BF16 = jnp.bfloat16
HIGHEST = lax.Precision.HIGHEST
ROWS = 24
LANES = 128


def limit(mib):
    return pltpu.CompilerParams(vmem_limit_bytes=mib * 1024 * 1024)


def about(us):
    return pl.CostEstimate(flops=0, bytes_accessed=int(us * 3.5e6), transcendentals=0)


def vmem():
    return pl.BlockSpec(memory_space=pltpu.VMEM)


def near_by(*arrays):
    return [pltpu.with_memory_space_constraint(x, pltpu.VMEM) for x in arrays]


def far_off(*arrays):
    return [pltpu.with_memory_space_constraint(x, pltpu.HBM) for x in arrays]


def smem():
    return pl.BlockSpec(memory_space=pltpu.SMEM)


def whole(size):
    return -(-size // LANES) * LANES


def cut(v):
    return v.astype(BF16).astype(F32)


def powers(sign):
    lane = lax.broadcasted_iota(jnp.int32, (8, LANES), 1)
    out = jnp.full((8, LANES), 2.0 ** (-64 * sign), F32)
    for bit in range(7):
        out = out * jnp.where((lane >> bit) & 1 == 1, F32(2.0 ** (sign * 2**bit)), F32(1.0))
    return out


def frame(geo):
    low, high = [None] * 8, [None] * 8
    blocks = [(t, c) for c in range(0, geo.shape[1], 8) for t in range(geo.shape[0])]
    for i, (t, c) in enumerate(blocks):
        g, k = geo[t, c : c + 8, :], i % 8
        low[k] = g if low[k] is None else jnp.minimum(low[k], g)
        high[k] = g if high[k] is None else jnp.maximum(high[k], g)
    low = jnp.min(functools.reduce(jnp.minimum, low), axis=1, keepdims=True)
    high = jnp.max(functools.reduce(jnp.maximum, high), axis=1, keepdims=True)
    low, high = jnp.minimum(low[:4], low[4:]), jnp.maximum(high[:4], high[4:])
    row = lax.broadcasted_iota(jnp.int32, low.shape, 0)
    radius = jnp.maximum(jnp.abs(low), jnp.abs(high))
    width = jnp.max(jnp.where(row == 3, radius, 0.5 * (high - low)), axis=0, keepdims=True)

    def over(table, least):
        return least(least(table, axis=1, keepdims=True), axis=0, keepdims=True)

    up, down = powers(1), powers(-1)
    size = over(jnp.where(up >= width, up, F32(2.0**63)), jnp.min)
    inv = over(jnp.where(up >= width, down, F32(2.0**-63)), jnp.max)
    magic = size * F32(1.5 * 2.0**20)
    return inv, (0.5 * (low + high) + magic) - magic


def split_frame(scale):
    return scale[0:1, 0:1], [scale[k : k + 1, 0:1] for k in range(1, 4)]


def split_features(points, centre, inv):
    magic = F32(1.5 * 2.0**16)
    grid, rest = [], []
    for k in range(3):
        u = (points[k] - centre[k]) * inv
        h = cut((u + magic) - magic)
        grid.append(h)
        rest.append(u - h)
    rad = points[3] * inv
    norm = grid[0] * grid[0] + grid[1] * grid[1] + grid[2] * grid[2]
    norm1 = cut(norm)
    norm2 = cut(norm - norm1)
    cross = grid[0] * rest[0] + grid[1] * rest[1] + grid[2] * rest[2]
    extra = 2.0 * cross + (rest[0] * rest[0] + rest[1] * rest[1] + rest[2] * rest[2]) + rad * rad
    extra = extra + ((norm - norm1) - norm2)
    extra1 = cut(extra)
    extra2 = cut(extra - extra1)
    extra3 = (extra - extra1) - extra2
    rest1 = [cut(v) for v in rest]
    rest2 = [v - w for v, w in zip(rest, rest1)]
    neg = lambda vs: [-2.0 * v for v in vs]
    one, zero = jnp.ones_like(rad), jnp.zeros_like(rad)
    left = grid + [norm1, norm2, one, one, zero]
    left += rest1 + [extra1, extra2, zero, zero, zero]
    left += rest2 + [extra3, zero, zero, zero, zero]
    right = neg(grid) + [one, one, norm1, norm2, zero]
    right += neg(rest1) + [zero, zero, extra1, extra2, zero]
    right += neg(rest2) + [zero, zero, extra3, zero, zero]
    return left, right, rad


def products(left, right):
    a, b, c = [left[k : k + 8, :] for k in (0, 8, 16)]
    x, y, z = [right[k : k + 8, :] for k in (0, 8, 16)]
    pairs = [(a, x), (b, x), (a, y), (c, x), (a, z), (b, y), (b, z), (c, y)]
    return [jnp.concatenate(v, axis=0).astype(BF16) for v in zip(*pairs)]


def store_features(ref, rows, first):
    width = rows[0].shape[1]
    for k, row in enumerate(rows):
        for t in range(ref.shape[0]):
            at = pl.ds(first * ROWS + k, 8, stride=ROWS)
            ref[t, at, :] = row[:, t * LANES : min(width, (t + 1) * LANES)]


def load_features(ref, index, order=None):
    start = pl.multiple_of(index * ROWS, 8)
    order = range(ref.shape[0]) if order is None else order
    blocks = [ref[t, pl.ds(start, ROWS), :] for t in order]
    return jnp.concatenate(blocks, axis=1) if len(blocks) > 1 else blocks[0]


def contract(left, right):
    return jnp.dot(left, right, preferred_element_type=F32)


def select_rows(index, value, count):
    row = lax.broadcasted_iota(jnp.int32, (count, index.shape[1]), 0)
    left = jnp.where(row == index, 1.0, 0.0).astype(BF16)
    high = value.astype(BF16)
    rest = value - high.astype(F32)
    mid = rest.astype(BF16)
    low = (rest - mid.astype(F32)).astype(BF16)
    return jnp.dot(
        jnp.concatenate([left] * 3, axis=1),
        jnp.concatenate([high, mid, low], axis=0),
        preferred_element_type=F32,
    )


def upright(row):
    return jnp.broadcast_to(row, (8, row.shape[1])).T[:, :1]


def keep(parts, rows, value):
    high = value.astype(BF16)
    parts[rows, :LANES] = high
    parts[rows, LANES:] = (value - high.astype(F32)).astype(BF16)


def add_columns(table, parts, indices):
    shape = (2 * LANES, table.shape[1])
    lane = lax.broadcasted_iota(jnp.int32, shape, 1)
    picks = [jnp.where(lane == index, 1.0, 0.0).astype(BF16) for index in indices]
    table[...] += jnp.dot(
        jnp.concatenate([p[...] for p in parts], axis=1),
        jnp.concatenate(picks, axis=0),
        preferred_element_type=F32,
    )


def inverse_root(d):
    return lax.rsqrt(d)


def fold(v):
    return jnp.sum(v.reshape(v.shape[0] // 8, 8, v.shape[1]), axis=0)


def distances(left, right, out):
    left, right = products(left, right)
    out[...] = contract(left.T, right)


def staged(spans, *stages):
    held = {}
    for t in range(len(spans) + len(stages) - 1):
        for depth in reversed(range(len(stages))):
            k = t - depth
            if 0 <= k < len(spans):
                held[k] = stages[depth](spans[k], held.get(k))
                if depth == len(stages) - 1:
                    del held[k]


def spans_of(height, step=32):
    step = min(step, height)
    return [slice(r, r + step) for r in range(0, height, step)]


def tile_sums(dist, qrow, qleft, parts):
    q0, q1 = qrow[:, :LANES], qrow[:, LANES:]
    qcol = upright(qleft)
    back = [jnp.zeros((8, LANES), F32), jnp.zeros((8, LANES), F32)]

    def root(rows, _):
        return (
            inverse_root(dist[rows, :LANES]),
            inverse_root(dist[rows, LANES:]),
        )

    def sums(rows, held):
        g0, g1 = held
        back[0] = back[0] + fold(g0 * qcol[rows, :])
        back[1] = back[1] + fold(g1 * qcol[rows, :])
        keep(parts, rows, g0 * q0 + g1 * q1)

    staged(spans_of(dist.shape[0]), root, sums)
    return jnp.concatenate([jnp.sum(b, axis=0, keepdims=True) for b in back], axis=1)


def pipeline(total, begin, finish, table, ring, parts):
    size = len(ring)
    ahead = min(2, size - 1)
    group = min(2, size)

    def body(i, carry):
        indices = []
        for k in range(size):
            begin(i * size + k + ahead, ring[(k + ahead) % size])
            indices.append(finish(i * size + k, ring[k], parts[k % len(parts)]))
            if len(indices) == group:
                done = [parts[(k - n) % len(parts)] for n in reversed(range(group))]
                add_columns(table, done, indices)
                indices = []
        return carry

    for k in range(ahead):
        begin(k, ring[k])
    lax.fori_loop(0, (total + size - 1) // size, body, 0)


def ring_size(total):
    return next(size for size in (32, 16, 8, 4, 2, 1) if total % size == 0)


def assemble(sub, S, L, q, pieces):
    def place(s):
        for shift in range(S):
            owner = (s - shift) % S
            q[:, owner * L : (owner + 1) * L] = pieces[shift][: q.shape[0], :]

    for s in range(S):
        pl.when(sub == s)(functools.partial(place, s))


def pack_kernel(sizes, charges, mask, geo, targets, sources, live, masked, geo_out, packs):
    C, S, L, slots = sizes
    sub = lax.axis_index("sub")
    masked[...] = charges[...] * mask[...].astype(F32)
    for t in range(geo_out.shape[0]):
        geo_out[t, :, :] = geo[:, :, t * LANES : (t + 1) * LANES].reshape(geo_out.shape[1:])
    lane = lax.broadcasted_iota(jnp.int32, (8, L), 1)
    for dest in range(C):
        codes = jnp.full((8, L), -1.0, F32)
        for j in range(slots):
            code = jnp.where(live[dest, j] > 0, sources[dest, j], -1)
            codes = jnp.where(lane == j, code.astype(F32), codes)
        packs[dest, 5 * slots :, :] = codes

    def fill(s):
        for dest in range(C):
            for j in range(slots):
                t = targets[dest, j]
                g = geo[t, :, s * L : (s + 1) * L]
                for k in range(4):
                    packs[dest, k * slots + j : k * slots + j + 1, :] = g[k : k + 1]
                packs[dest, 4 * slots + j : 4 * slots + j + 1, :] = masked[pl.ds(t, 1), :]

    for s in range(S):
        pl.when(sub == s)(functools.partial(fill, s))


def remote_kernel(sizes, fb, scale, up, *rest):
    C, S, L, slots, clusters, panels = sizes
    pieces = rest[:S]
    packs, acc_out, sends = rest[S : S + 3]
    q, tq, acc, fwdt, fa, order, codes, sems, *work = rest[S + 3 :]
    ring, sums = work[:16], work[16:]
    n = C * slots
    copies = [
        pltpu.make_async_copy(packs.at[k, pl.ds(5 * slots, 8), :], codes.at[k], sems.at[k])
        for k in range(C)
    ]
    for copy in copies:
        copy.start()
    assemble(lax.axis_index("sub"), S, L, q, pieces)
    acc[...] = jnp.zeros_like(acc)
    fwdt[...] = jnp.zeros_like(fwdt)
    for copy in copies:
        copy.wait()
    found = jnp.int32(0)
    for shift in range(C):
        for j in range(slots):
            code = codes[shift, 0, j].astype(jnp.int32)
            order[n + 1 + shift * slots + j] = jnp.maximum(code, 0)
            order[found] = shift * slots + j
            found = found + (code >= 0).astype(jnp.int32)
    inv, centre = split_frame(scale)
    for shift in range(C):
        for first in range(0, slots, 8):
            points = [packs[shift, k * slots + first : k * slots + first + 8, :] for k in range(5)]
            left, _, _ = split_features(points, centre, inv)
            store_features(fa, left, shift * slots + first)
            at = shift * slots + first
            tq[at : at + 8, :] = points[4]

    def begin(i, dist):
        slot = order[jnp.minimum(i, jnp.maximum(found - 1, 0))]
        distances(load_features(fa, slot), load_features(fb, order[n + 1 + slot]), dist)

    def finish(i, dist, part):
        ok = i < found
        slot = order[jnp.minimum(i, jnp.maximum(found - 1, 0))]
        source = order[n + 1 + slot]
        back = tile_sums(
            dist, q[pl.ds(source, 1), :], tq[pl.ds(slot, 1), :], part
        )
        acc[pl.ds(source, 1), :] += jnp.where(ok, back, 0.0)
        return jnp.where(ok, slot, -1)

    pipeline(found, begin, finish, fwdt, ring, sums)
    acc_out[...] = acc[...] * inv
    fwd = (fwdt[...] * inv).T
    rank = up.shape[1]
    for shift in range(C):
        sends[shift, :slots, :] = fwd[shift * slots : (shift + 1) * slots, :]
        sends[shift, slots:, :] = jnp.zeros((up.shape[0], L), F32)
        sends[shift, slots:, :rank] = up[...]


def prepare_kernel(
    geo, masked, basis_far, transfer_far, parent_far,
    fa, fb, diag, scale, up, basis, transfer, parent, sems
):
    copies = [
        pltpu.make_async_copy(src, dst, sems.at[k])
        for k, (src, dst) in enumerate(
            [(basis_far, basis), (transfer_far, transfer), (parent_far, parent)]
        )
    ]
    for copy in copies:
        copy.start()
    inv, centre = frame(geo)
    scale[...] = jnp.zeros_like(scale)
    scale[0:1, :] = jnp.broadcast_to(inv, (1, LANES))
    for k in range(3):
        scale[k + 1 : k + 2, :] = jnp.broadcast_to(centre[k : k + 1, :], (1, LANES))
    inv, centre = split_frame(scale)
    for first in range(0, diag.shape[0], 8):
        points = [
            jnp.concatenate(
                [geo[t, pl.ds(first * 4 + k, 8, stride=4), :] for t in range(geo.shape[0])], axis=1
            )
            for k in range(4)
        ]
        left, right, rad = split_features(points, centre, inv)
        store_features(fa, left, first)
        store_features(fb, right, first)
        diag[first : first + 8, :] = lax.rsqrt(2.0 * (rad * rad))
    for copy in copies:
        copy.wait()
    up[...] = up_sums(basis, masked, transfer, parent, up.shape[0])


def local_kernel(sizes, pair_rows, pairs, fa, fb, scale, acc_in, *rest):
    S, L, R, clusters, panels = sizes
    pieces = rest[:S]
    acc_out = rest[S]
    q, acc, pair_sums, *work = rest[S + 1 :]
    ring, sums = work[:32], work[32:]
    sub = lax.axis_index("sub")
    assemble(sub, S, L, q, pieces)
    acc[...] = jnp.zeros_like(acc)
    pair_sums[...] = jnp.zeros_like(pair_sums)

    count = pairs.shape[1] // S
    start = sub * count

    def begin(i, dist):
        p = start + jnp.minimum(i, count - 1)
        distances(load_features(fa, pairs[0, p]), load_features(fb, pairs[1, p]), dist)

    def finish(i, dist, part):
        ia, ib = pairs[0, start + i], pairs[1, start + i]
        acc[pl.ds(ib, 1), :] += tile_sums(
            dist, q[pl.ds(ib, 1), :], q[pl.ds(ia, 1), :], part
        )
        return start + i

    pipeline(count, begin, finish, pair_sums, ring[: ring_size(count)], sums)
    width = pair_rows.shape[1]
    total = acc[...] + select_rows(pair_rows[0:1, :], pair_sums[...].T[:width, :], clusters)
    acc_out[...] = acc_in[...] + total * scale[0:1, 0:1]


def self_shares(clusters, S, R):
    base = clusters // R
    unit = base // 4 if R > 1 else 0
    return base, unit


def self_kernel(sizes, fa, fb, diags, scale, part, *rest):
    S, L, R, clusters, panels = sizes
    pieces = rest[:S]
    out, q, fs, spots, self_sums, *work = rest[S:]
    ring, sums = work[:16], work[16:]
    sub, rep = lax.axis_index("sub"), lax.axis_index("rep")
    self_sums[...] = jnp.zeros_like(self_sums)
    blocks = L == LANES
    if blocks:
        order = [lax.rem(sub + S - shift, S) for shift in range(S)]
        for shift in range(S):
            q[:, shift * L : (shift + 1) * L] = pieces[shift][...]
    else:
        order = None
        assemble(sub, S, L, q, pieces)

    def place(s):
        if not blocks:
            t, at = (s * L) // LANES, (s * L) % LANES
            fs[0, :, :] = fa[t, :, at : at + L]
        spots[...] = diags[:, s * L : (s + 1) * L]

    for s in range(S):
        pl.when(sub == s)(functools.partial(place, s))
    base, unit = self_shares(clusters, S, R)
    first = rep * base - jnp.where(rep > 0, unit, 0)
    share = base + jnp.where(rep == R - 1, unit, 0) - jnp.where(rep == 0, unit, 0)

    def begin(i, dist):
        c = first + jnp.minimum(i, share - 1)
        own = load_features(fa, c, order[:1]) if blocks else load_features(fs, c)
        distances(own, load_features(fb, c, order), dist)

    def finish(i, dist, parts):
        c = first + i
        qrow = q[pl.ds(c, 1), :]
        diag = upright(spots[pl.ds(c, 1), :])

        def root(span, _):
            shape = (span.stop - span.start, LANES)
            row = lax.broadcasted_iota(jnp.int32, shape, 0) + span.start
            row = row if blocks else row + sub * L
            col = lax.broadcasted_iota(jnp.int32, shape, 1)
            values = [inverse_root(dist[span, t : t + LANES]) for t in range(0, panels, LANES)]
            for t in range(1 if blocks else len(values)):
                values[t] = jnp.where(row == col + t * LANES, diag[span, :], values[t])
            return values

        def partial(span, held):
            keep(parts, span, sum(g * qrow[:, t * LANES : (t + 1) * LANES] for t, g in enumerate(held)))

        staged(spans_of(L), root, partial)
        return c

    pipeline(share, begin, finish, self_sums, ring[: ring_size(unit or base)], sums)
    out[...] = part[...]
    out[:clusters, :] = part[:clusters, :] + self_sums[...].T * scale[0:1, 0:1]


def merge_kernel(sizes, far_list, targets, near, coupling, transfer, parent, sums, *rest):
    C, S, L, slots, clusters = sizes
    parts, parents = rest[:S], rest[S]
    sub = lax.axis_index("sub")
    got = select_rows(
        jnp.concatenate([targets[d : d + 1, :] for d in range(C)], axis=1),
        jnp.concatenate([sums[d, :slots, :] for d in range(C)], axis=0),
        clusters,
    )

    par_dev, far_n, rank = coupling.shape[0], coupling.shape[1], coupling.shape[2]
    for d in range(C):
        parents[d * par_dev : (d + 1) * par_dev, :] = sums[d, slots:, :rank]
    lane = lax.broadcasted_iota(jnp.int32, (rank, LANES), 1)
    field = jnp.zeros((rank, LANES), F32)
    for p in range(par_dev):
        part = jnp.zeros((rank, rank), F32)
        for k in range(far_n):
            part = part + coupling[p, k] * parents[pl.ds(far_list[k, p], 1), :]
        field = jnp.where(lane == p, jnp.sum(part, axis=1, keepdims=True), field)
    which = lax.broadcasted_iota(jnp.int32, (LANES, clusters), 0)
    onehot = (parent[...] == which).astype(F32)
    down = jnp.dot(field, onehot, precision=HIGHEST, preferred_element_type=F32)
    fields = jnp.concatenate(
        [jnp.sum(transfer[r] * down, axis=0, keepdims=True) for r in range(rank)], axis=0
    )

    def give(s):
        for shift in range(S):
            other = (s + shift) % S
            part = near[:, other * L : (other + 1) * L]
            parts[shift][:clusters, :] = part + got if shift == 0 else part
            for t in range(clusters // L):
                at = clusters + t * rank
                parts[shift][at : at + rank, :] = fields[:, t * L : (t + 1) * L]

    for s in range(S):
        pl.when(sub == s)(functools.partial(give, s))


def up_sums(basis, masked, transfer, parent, count):
    clusters = basis.shape[0]
    rank = basis.shape[1]
    lane = lax.broadcasted_iota(jnp.int32, (rank, clusters), 1)
    leaf = jnp.zeros((rank, clusters), F32)
    for c in range(clusters):
        part = jnp.sum(basis[c] * masked[c : c + 1, :], axis=1, keepdims=True)
        leaf = jnp.where(lane == c, part, leaf)
    lifted = jnp.zeros((rank, clusters), F32)
    for r in range(rank):
        lifted = lifted + transfer[r] * leaf[r : r + 1, :]
    which = lax.broadcasted_iota(jnp.int32, (count, clusters), 0)
    onehot = (parent[...] == which).astype(F32)
    return lax.dot_general(
        onehot, lifted, (((1,), (1,)), ((), ())), precision=HIGHEST, preferred_element_type=F32
    )


def far_kernel(basis, near, out):
    clusters, rank = basis.shape[0], basis.shape[1]
    L = out.shape[1]
    fields = [near[clusters + t * rank : clusters + (t + 1) * rank, :] for t in range(clusters // L)]
    fields = jnp.concatenate(fields, axis=1) if len(fields) > 1 else fields[0]
    for c in range(clusters):
        far = jnp.sum(basis[c] * fields[:, c : c + 1], axis=0, keepdims=True)
        out[c : c + 1, :] = far + near[c : c + 1, :]


def send(value, moves):
    names = tuple(name for name, _ in moves)
    steps = [step for _, step in moves]
    sizes = [lax.axis_size(name) for name in names]
    perm = []

    def flat(coords):
        index = 0
        for size, c in zip(sizes, coords):
            index = index * size + c
        return index

    total = 1
    for size in sizes:
        total *= size
    for index in range(total):
        coords, left = [], index
        for size in reversed(sizes):
            coords.append(left % size)
            left //= size
        coords.reverse()
        perm.append((index, flat([(c + s) % n for c, s, n in zip(coords, steps, sizes)])))
    return lax.ppermute(value, names if len(names) > 1 else names[0], perm)


def on_device(
    charges,
    panel_mask,
    geometry,
    remote_source,
    remote_target,
    remote_live,
    local_pairs,
    basis,
    transfer,
    parent_of,
    far_list,
    coupling,
):
    clusters, L = charges.shape
    panels = geometry.shape[2]
    C, S, R = lax.axis_size("clu"), lax.axis_size("sub"), lax.axis_size("rep")
    slots = remote_source.shape[2]
    par_dev, rank = far_list.shape[0], transfer.shape[1]
    n = C * slots
    shape = jax.ShapeDtypeStruct
    targets = remote_target[0]
    basis_t = jnp.transpose(basis, (0, 2, 1))
    transfer_t = jnp.transpose(transfer, (1, 2, 0))
    parent = parent_of[None, :]

    made = pl.pallas_call(
        functools.partial(pack_kernel, (C, S, L, slots)),
        out_shape=[pltpu.VMEM((clusters, L), F32), pltpu.VMEM((panels // LANES, clusters * 4, LANES), F32)]
        + [pltpu.VMEM((C, 5 * slots + 8, L), F32)],
        in_specs=[vmem()] * 3 + [smem()] * 3,
        out_specs=[vmem()] * 3,
        compiler_params=limit(60),
        cost_estimate=about(2),
        name="packs",
    )(charges, panel_mask, geometry, targets, remote_source[0], remote_live[0])
    masked, geo, packs = made
    pieces = [masked] + [send(masked, (("sub", d),)) for d in range(1, S)]
    packs = lax.all_to_all(packs, "clu", split_axis=0, concat_axis=0, tiled=True)

    *features, up = pl.pallas_call(
        prepare_kernel,
        out_shape=[pltpu.VMEM((panels // LANES, clusters * ROWS, LANES), F32)] * 2
        + [
            pltpu.VMEM((clusters, panels), F32),
            pltpu.VMEM((8, LANES), F32),
            pltpu.VMEM((par_dev, rank), F32),
        ],
        in_specs=[vmem()] * 2 + [pl.BlockSpec(memory_space=pltpu.HBM)] * 3,
        out_specs=[vmem()] * 5,
        scratch_shapes=[
            pltpu.VMEM(basis_t.shape, F32),
            pltpu.VMEM(transfer_t.shape, F32),
            pltpu.VMEM(parent.shape, jnp.int32),
            pltpu.SemaphoreType.DMA((3,)),
        ],
        compiler_params=limit(24),
        cost_estimate=about(4),
        name="prepare",
    )(*near_by(geo, masked), *far_off(basis_t, transfer_t, parent))
    *tables, diags, scale = features

    made = pl.pallas_call(
        functools.partial(remote_kernel, (C, S, L, slots, clusters, panels)),
        out_shape=[pltpu.VMEM((clusters, panels), F32)]
        + [pltpu.VMEM((C, slots + par_dev, L), F32)],
        in_specs=[vmem()] * (4 + S),
        out_specs=[vmem()] * 2,
        scratch_shapes=[
            pltpu.VMEM((clusters, panels), F32),
            pltpu.VMEM((n, L), F32),
            pltpu.VMEM((clusters, panels), F32),
            pltpu.VMEM((L, whole(n)), F32),
            pltpu.VMEM((1, n * ROWS, L), F32),
            pltpu.SMEM((2 * n + 1,), jnp.int32),
            pltpu.SMEM((C, 8, L), F32),
            pltpu.SemaphoreType.DMA((C,)),
        ]
        + [pltpu.VMEM((L, panels), F32)] * 16
        + [pltpu.VMEM((L, 2 * LANES), BF16)] * 4,
        compiler_params=limit(24),
        cost_estimate=about(6),
        name="near_remote",
    )(*near_by(tables[1], scale, up, *pieces, packs))
    acc = made[0]
    sums = lax.all_to_all(made[1], "clu", split_axis=0, concat_axis=0, tiled=True)

    wide = whole(local_pairs.shape[1])
    near = pl.pallas_call(
        functools.partial(local_kernel, (S, L, R, clusters, panels)),
        out_shape=pltpu.VMEM((clusters, panels), F32),
        in_specs=[vmem(), smem()] + [vmem()] * (4 + S),
        out_specs=vmem(),
        scratch_shapes=[
            pltpu.VMEM((clusters, panels), F32),
            pltpu.VMEM((clusters, panels), F32),
            pltpu.VMEM((panels, wide), F32),
        ]
        + [pltpu.VMEM((panels, panels), F32)] * 32
        + [pltpu.VMEM((panels, 2 * LANES), BF16)] * 4,
        compiler_params=limit(24),
        cost_estimate=about(9),
        name="near_local",
    )(*near_by(local_pairs[0].T), local_pairs[0].T, *near_by(*tables, scale, acc, *pieces))

    height = clusters + clusters // L * rank
    parts = pl.pallas_call(
        functools.partial(merge_kernel, (C, S, L, slots, clusters)),
        out_shape=[pltpu.VMEM((height, L), F32)] * S,
        in_specs=[smem()] + [vmem()] * 6,
        out_specs=[vmem()] * S,
        scratch_shapes=[pltpu.VMEM((C * par_dev, rank), F32)],
        compiler_params=limit(16),
        cost_estimate=about(1),
        name="merge",
    )(far_list.T, *near_by(targets, near, coupling, transfer_t, parent, sums))
    others = [send(parts[d], (("sub", d),)) for d in range(1, S)]

    near = pl.pallas_call(
        functools.partial(self_kernel, (S, L, R, clusters, panels)),
        out_shape=pltpu.VMEM((height, L), F32),
        in_specs=[vmem()] * (5 + S),
        out_specs=vmem(),
        scratch_shapes=[
            pltpu.VMEM((clusters, panels), F32),
            pltpu.VMEM((1, 8 if L == LANES else clusters * ROWS, L), F32),
            pltpu.VMEM((clusters, L), F32),
            pltpu.VMEM((L, clusters), F32),
        ]
        + [pltpu.VMEM((L, panels), F32)] * 16
        + [pltpu.VMEM((L, 2 * LANES), BF16)] * 4,
        compiler_params=limit(24),
        cost_estimate=about(4),
        name="near_self",
    )(*near_by(*tables, diags, scale, parts[0], *pieces))
    for other in others:
        near = near + other
    others = [send(near, (("rep", e),)) for e in range(1, R)]

    total = pl.pallas_call(
        far_kernel,
        out_shape=pltpu.VMEM((clusters, L), F32),
        in_specs=[vmem()] * 2,
        out_specs=vmem(),
        compiler_params=limit(16),
        cost_estimate=about(1),
        name="far_down",
    )(*near_by(basis_t, near))
    for other in others:
        total = total + other[:clusters]
    return total * panel_mask.astype(F32)


def solution(mesh):
    placed = (
        P(("grp", "clu"), "sub"),
        P(("grp", "clu"), "sub"),
        P(("grp", "clu"), None, None),
        P(("grp", "clu"), None, "rep"),
        P(("grp", "clu"), None, "rep"),
        P(("grp", "clu"), None, "rep"),
        P(("grp", "clu"), "rep", None),
        P(("grp", "clu"), "sub", None),
        P(("grp", "clu"), None, None),
        P(("grp", "clu")),
        P(("grp", "clu"), None),
        P(("grp", "clu"), None, None, None),
    )
    return jax.shard_map(
        on_device, mesh=mesh, in_specs=placed, out_specs=P(("grp", "clu"), "sub"), check_vma=False
    )
```

```python
import functools

import jax
import jax.numpy as jnp
from jax import lax
from jax.experimental import pallas as pl
from jax.experimental.pallas import tpu as pltpu
from jax.sharding import PartitionSpec as P

F32 = jnp.float32
BF16 = jnp.bfloat16
HIGHEST = lax.Precision.HIGHEST
ROWS = 24
LANES = 128


def limit(mib):
    return pltpu.CompilerParams(vmem_limit_bytes=mib * 1024 * 1024)


def about(us):
    return pl.CostEstimate(flops=0, bytes_accessed=int(us * 3.5e6), transcendentals=0)


def vmem():
    return pl.BlockSpec(memory_space=pltpu.VMEM)


def near_by(*arrays):
    return [pltpu.with_memory_space_constraint(x, pltpu.VMEM) for x in arrays]


def far_off(*arrays):
    return [pltpu.with_memory_space_constraint(x, pltpu.HBM) for x in arrays]


def smem():
    return pl.BlockSpec(memory_space=pltpu.SMEM)


def whole(size):
    return -(-size // LANES) * LANES


def cut(v):
    return v.astype(BF16).astype(F32)


def powers(sign):
    lane = lax.broadcasted_iota(jnp.int32, (8, LANES), 1)
    out = jnp.full((8, LANES), 2.0 ** (-64 * sign), F32)
    for bit in range(7):
        out = out * jnp.where((lane >> bit) & 1 == 1, F32(2.0 ** (sign * 2**bit)), F32(1.0))
    return out


def frame(geo):
    low, high = [None] * 8, [None] * 8
    blocks = [(t, c) for c in range(0, geo.shape[1], 8) for t in range(geo.shape[0])]
    for i, (t, c) in enumerate(blocks):
        g, k = geo[t, c : c + 8, :], i % 8
        low[k] = g if low[k] is None else jnp.minimum(low[k], g)
        high[k] = g if high[k] is None else jnp.maximum(high[k], g)
    low = jnp.min(functools.reduce(jnp.minimum, low), axis=1, keepdims=True)
    high = jnp.max(functools.reduce(jnp.maximum, high), axis=1, keepdims=True)
    low, high = jnp.minimum(low[:4], low[4:]), jnp.maximum(high[:4], high[4:])
    row = lax.broadcasted_iota(jnp.int32, low.shape, 0)
    radius = jnp.maximum(jnp.abs(low), jnp.abs(high))
    width = jnp.max(jnp.where(row == 3, radius, 0.5 * (high - low)), axis=0, keepdims=True)

    def over(table, least):
        return least(least(table, axis=1, keepdims=True), axis=0, keepdims=True)

    up, down = powers(1), powers(-1)
    size = over(jnp.where(up >= width, up, F32(2.0**63)), jnp.min)
    inv = over(jnp.where(up >= width, down, F32(2.0**-63)), jnp.max)
    magic = size * F32(1.5 * 2.0**20)
    return inv, (0.5 * (low + high) + magic) - magic


def split_frame(scale):
    return scale[0:1, 0:1], [scale[k : k + 1, 0:1] for k in range(1, 4)]


def split_features(points, centre, inv):
    magic = F32(1.5 * 2.0**16)
    grid, rest = [], []
    for k in range(3):
        u = (points[k] - centre[k]) * inv
        h = cut((u + magic) - magic)
        grid.append(h)
        rest.append(u - h)
    rad = points[3] * inv
    norm = grid[0] * grid[0] + grid[1] * grid[1] + grid[2] * grid[2]
    norm1 = cut(norm)
    norm2 = cut(norm - norm1)
    cross = grid[0] * rest[0] + grid[1] * rest[1] + grid[2] * rest[2]
    extra = 2.0 * cross + (rest[0] * rest[0] + rest[1] * rest[1] + rest[2] * rest[2]) + rad * rad
    extra = extra + ((norm - norm1) - norm2)
    extra1 = cut(extra)
    extra2 = cut(extra - extra1)
    extra3 = (extra - extra1) - extra2
    rest1 = [cut(v) for v in rest]
    rest2 = [v - w for v, w in zip(rest, rest1)]
    neg = lambda vs: [-2.0 * v for v in vs]
    one, zero = jnp.ones_like(rad), jnp.zeros_like(rad)
    left = grid + [norm1, norm2, one, one, zero]
    left += rest1 + [extra1, extra2, zero, zero, zero]
    left += rest2 + [extra3, zero, zero, zero, zero]
    right = neg(grid) + [one, one, norm1, norm2, zero]
    right += neg(rest1) + [zero, zero, extra1, extra2, zero]
    right += neg(rest2) + [zero, zero, extra3, zero, zero]
    return left, right, rad


def products(left, right):
    a, b, c = [left[k : k + 8, :] for k in (0, 8, 16)]
    x, y, z = [right[k : k + 8, :] for k in (0, 8, 16)]
    pairs = [(a, x), (b, x), (a, y), (c, x), (a, z), (b, y), (b, z), (c, y)]
    return [jnp.concatenate(v, axis=0).astype(BF16) for v in zip(*pairs)]


def store_features(ref, rows, first):
    width = rows[0].shape[1]
    for k, row in enumerate(rows):
        for t in range(ref.shape[0]):
            at = pl.ds(first * ROWS + k, 8, stride=ROWS)
            ref[t, at, :] = row[:, t * LANES : min(width, (t + 1) * LANES)]


def load_features(ref, index, order=None):
    start = pl.multiple_of(index * ROWS, 8)
    order = range(ref.shape[0]) if order is None else order
    blocks = [ref[t, pl.ds(start, ROWS), :] for t in order]
    return jnp.concatenate(blocks, axis=1) if len(blocks) > 1 else blocks[0]


def contract(left, right):
    return jnp.dot(left, right, preferred_element_type=F32)


def select_rows(index, value, count):
    row = lax.broadcasted_iota(jnp.int32, (count, index.shape[1]), 0)
    left = jnp.where(row == index, 1.0, 0.0).astype(BF16)
    high = value.astype(BF16)
    rest = value - high.astype(F32)
    mid = rest.astype(BF16)
    low = (rest - mid.astype(F32)).astype(BF16)
    return jnp.dot(
        jnp.concatenate([left] * 3, axis=1),
        jnp.concatenate([high, mid, low], axis=0),
        preferred_element_type=F32,
    )


def upright(row):
    return jnp.broadcast_to(row, (8, row.shape[1])).T[:, :1]


def keep(parts, rows, value):
    high = value.astype(BF16)
    parts[rows, :LANES] = high
    parts[rows, LANES:] = (value - high.astype(F32)).astype(BF16)


def add_columns(table, parts, indices):
    shape = (2 * LANES, table.shape[1])
    lane = lax.broadcasted_iota(jnp.int32, shape, 1)
    picks = [jnp.where(lane == index, 1.0, 0.0).astype(BF16) for index in indices]
    table[...] += jnp.dot(
        jnp.concatenate([p[...] for p in parts], axis=1),
        jnp.concatenate(picks, axis=0),
        preferred_element_type=F32,
    )


def inverse_root(d):
    return lax.rsqrt(d)


def fold(v):
    return jnp.sum(v.reshape(v.shape[0] // 8, 8, v.shape[1]), axis=0)


def distances(left, right, out):
    left, right = products(left, right)
    out[...] = contract(left.T, right)


def staged(spans, *stages):
    held = {}
    for t in range(len(spans) + len(stages) - 1):
        for depth in reversed(range(len(stages))):
            k = t - depth
            if 0 <= k < len(spans):
                held[k] = stages[depth](spans[k], held.get(k))
                if depth == len(stages) - 1:
                    del held[k]


def spans_of(height, step=32):
    step = min(step, height)
    return [slice(r, r + step) for r in range(0, height, step)]


def tile_sums(dist, qrow, qleft, parts):
    q0, q1 = qrow[:, :LANES], qrow[:, LANES:]
    qcol = upright(qleft)
    back = [jnp.zeros((8, LANES), F32), jnp.zeros((8, LANES), F32)]

    def root(rows, _):
        return (
            inverse_root(dist[rows, :LANES]),
            inverse_root(dist[rows, LANES:]),
        )

    def sums(rows, held):
        g0, g1 = held
        back[0] = back[0] + fold(g0 * qcol[rows, :])
        back[1] = back[1] + fold(g1 * qcol[rows, :])
        keep(parts, rows, g0 * q0 + g1 * q1)

    staged(spans_of(dist.shape[0]), root, sums)
    return jnp.concatenate([jnp.sum(b, axis=0, keepdims=True) for b in back], axis=1)


def pipeline(total, begin, finish, table, size, ring, parts):
    ring = ring[: min(len(ring), size)]
    ahead = min(2, len(ring) - 1)
    group = min(2, size)

    def body(i, carry):
        indices = []
        for k in range(size):
            begin(i * size + k + ahead, ring[(k + ahead) % len(ring)])
            indices.append(finish(i * size + k, ring[k % len(ring)], parts[k % len(parts)]))
            if len(indices) == group:
                done = [parts[(k - n) % len(parts)] for n in reversed(range(group))]
                add_columns(table, done, indices)
                indices = []
        return carry

    for k in range(ahead):
        begin(k, ring[k])
    lax.fori_loop(0, (total + size - 1) // size, body, 0)


def body_size(total, most):
    return next(size for size in (32, 16, 8, 4, 2, 1) if size <= most and total % size == 0)


def assemble(sub, S, L, q, pieces):
    def place(s):
        for shift in range(S):
            owner = (s - shift) % S
            q[:, owner * L : (owner + 1) * L] = pieces[shift][: q.shape[0], :]

    for s in range(S):
        pl.when(sub == s)(functools.partial(place, s))


def pack_kernel(sizes, charges, mask, geo, targets, sources, live, masked, geo_out, *packs):
    C, S, L, slots = sizes
    me, sub = lax.axis_index("clu"), lax.axis_index("sub")
    masked[...] = charges[...] * mask[...].astype(F32)
    for t in range(geo_out.shape[0]):
        geo_out[t, :, :] = geo[:, :, t * LANES : (t + 1) * LANES].reshape(geo_out.shape[1:])
    lane = lax.broadcasted_iota(jnp.int32, (8, L), 1)
    for shift in range(1, C):
        dest = lax.rem(me + shift, C)
        codes = jnp.full((8, L), -1.0, F32)
        for j in range(slots):
            code = jnp.where(live[dest, j] > 0, sources[dest, j], -1)
            codes = jnp.where(lane == j, code.astype(F32), codes)
        packs[shift - 1][5 * slots :, :] = codes

    def fill(s):
        for shift in range(1, C):
            dest = lax.rem(me + shift, C)
            pack = packs[shift - 1]
            for j in range(slots):
                t = targets[dest, j]
                g = geo[t, :, s * L : (s + 1) * L]
                for k in range(4):
                    pack[k * slots + j : k * slots + j + 1, :] = g[k : k + 1]
                pack[4 * slots + j : 4 * slots + j + 1, :] = masked[pl.ds(t, 1), :]

    for s in range(S):
        pl.when(sub == s)(functools.partial(fill, s))


def remote_kernel(sizes, fb, scale, up, before, *rest):
    del before
    C, S, L, slots, clusters, panels = sizes
    pieces = rest[:S]
    packs = rest[S : S + C - 1]
    acc_out = rest[S + C - 1]
    sends = rest[S + C : S + C + C - 1]
    q, tq, acc, fwdt, fa, order, codes, sems, *work = rest[S + C + C - 1 :]
    n = (C - 1) * slots
    copies = [
        pltpu.make_async_copy(packs[k].at[pl.ds(5 * slots, 8), :], codes.at[k], sems.at[k])
        for k in range(C - 1)
    ]
    for copy in copies:
        copy.start()
    assemble(lax.axis_index("sub"), S, L, q, pieces)
    acc[...] = jnp.zeros_like(acc)
    fwdt[...] = jnp.zeros_like(fwdt)
    for copy in copies:
        copy.wait()
    found = jnp.int32(0)
    for shift in range(C - 1):
        for j in range(slots):
            code = codes[shift, 0, j].astype(jnp.int32)
            order[n + 1 + shift * slots + j] = jnp.maximum(code, 0)
            order[found] = shift * slots + j
            found = found + (code >= 0).astype(jnp.int32)
    inv, centre = split_frame(scale)
    for shift in range(C - 1):
        for first in range(0, slots, 8):
            points = [packs[shift][k * slots + first : k * slots + first + 8, :] for k in range(5)]
            left, _, _ = split_features(points, centre, inv)
            store_features(fa, left, shift * slots + first)
            at = shift * slots + first
            tq[at : at + 8, :] = points[4]

    def begin(i, dist):
        slot = order[jnp.minimum(i, jnp.maximum(found - 1, 0))]
        distances(load_features(fa, slot), load_features(fb, order[n + 1 + slot]), dist)

    def finish(i, dist, part):
        ok = i < found
        slot = order[jnp.minimum(i, jnp.maximum(found - 1, 0))]
        source = order[n + 1 + slot]
        back = tile_sums(
            dist, q[pl.ds(source, 1), :], tq[pl.ds(slot, 1), :], part
        )
        acc[pl.ds(source, 1), :] += jnp.where(ok, back, 0.0)
        return jnp.where(ok, slot, -1)

    pipeline(found, begin, finish, fwdt, 8, work[:4], work[4:])
    acc_out[...] = acc[...] * inv
    fwd = (fwdt[...] * inv).T
    rank = up.shape[1]
    for shift in range(C - 1):
        sends[shift][:slots, :] = fwd[shift * slots : (shift + 1) * slots, :]
        sends[shift][slots:, :] = jnp.zeros((up.shape[0], L), F32)
        sends[shift][slots:, :rank] = up[...]


def prepare_kernel(
    geo, masked, basis_far, transfer_far, parent_far,
    fa, fb, diag, scale, up, basis, transfer, parent, sems
):
    copies = [
        pltpu.make_async_copy(src, dst, sems.at[k])
        for k, (src, dst) in enumerate(
            [(basis_far, basis), (transfer_far, transfer), (parent_far, parent)]
        )
    ]
    for copy in copies:
        copy.start()
    inv, centre = frame(geo)
    scale[...] = jnp.zeros_like(scale)
    scale[0:1, :] = jnp.broadcast_to(inv, (1, LANES))
    for k in range(3):
        scale[k + 1 : k + 2, :] = jnp.broadcast_to(centre[k : k + 1, :], (1, LANES))
    inv, centre = split_frame(scale)
    for first in range(0, diag.shape[0], 8):
        points = [
            jnp.concatenate(
                [geo[t, pl.ds(first * 4 + k, 8, stride=4), :] for t in range(geo.shape[0])], axis=1
            )
            for k in range(4)
        ]
        left, right, rad = split_features(points, centre, inv)
        store_features(fa, left, first)
        store_features(fb, right, first)
        diag[first : first + 8, :] = lax.rsqrt(2.0 * (rad * rad))
    for copy in copies:
        copy.wait()
    up[...] = up_sums(basis, masked, transfer, parent, up.shape[0])


def local_kernel(sizes, pair_rows, pairs, fa, fb, scale, acc_in, *rest):
    S, L, R, clusters, panels = sizes
    pieces = rest[:S]
    acc_out = rest[S]
    q, acc, pair_sums, *work = rest[S + 1 :]
    ring, sums = work[:8], work[8:]
    sub = lax.axis_index("sub")
    assemble(sub, S, L, q, pieces)
    acc[...] = jnp.zeros_like(acc)
    pair_sums[...] = jnp.zeros_like(pair_sums)

    count = pairs.shape[1] // S
    start = sub * count

    def begin(i, dist):
        p = start + jnp.minimum(i, count - 1)
        distances(load_features(fa, pairs[0, p]), load_features(fb, pairs[1, p]), dist)

    def finish(i, dist, part):
        ia, ib = pairs[0, start + i], pairs[1, start + i]
        acc[pl.ds(ib, 1), :] += tile_sums(
            dist, q[pl.ds(ib, 1), :], q[pl.ds(ia, 1), :], part
        )
        return start + i

    pipeline(count, begin, finish, pair_sums, body_size(count, 32), ring, sums)
    width = pair_rows.shape[1]
    total = acc[...] + select_rows(pair_rows[0:1, :], pair_sums[...].T[:width, :], clusters)
    acc_out[...] = acc_in[...] + total * scale[0:1, 0:1]


def self_kernel(sizes, early, fa, fb, diags, scale, *rest):
    S, L, R, clusters, panels = sizes
    if not early:
        part, before, *rest = rest
    pieces = rest[:S]
    out, q, fs, spots, self_sums, *work = rest[S:]
    ring, sums = work[:8], work[8:]
    sub, rep = lax.axis_index("sub"), lax.axis_index("rep")
    self_sums[...] = jnp.zeros_like(self_sums)
    blocks = L == LANES
    if blocks:
        order = [lax.rem(sub + S - shift, S) for shift in range(S)]
        for shift in range(S):
            q[:, shift * L : (shift + 1) * L] = pieces[shift][...]
    else:
        order = None
        assemble(sub, S, L, q, pieces)

    def place(s):
        if not blocks:
            t, at = (s * L) // LANES, (s * L) % LANES
            fs[0, :, :] = fa[t, :, at : at + L]
        spots[...] = diags[:, s * L : (s + 1) * L]

    for s in range(S):
        pl.when(sub == s)(functools.partial(place, s))
    base = clusters // R
    unit = base // 4
    first = rep * base
    share = base
    if R > 1:
        first = first - jnp.where(rep > 0, unit, 0)
        share = share + jnp.where(rep == R - 1, unit, 0) - jnp.where(rep == 0, unit, 0)
    if early:
        share = unit
    else:
        first, share = first + unit, share - unit

    def begin(i, dist):
        c = first + jnp.minimum(i, share - 1)
        own = load_features(fa, c, order[:1]) if blocks else load_features(fs, c)
        distances(own, load_features(fb, c, order), dist)

    def finish(i, dist, parts):
        c = first + i
        qrow = q[pl.ds(c, 1), :]
        diag = upright(spots[pl.ds(c, 1), :])

        def root(span, _):
            shape = (span.stop - span.start, LANES)
            row = lax.broadcasted_iota(jnp.int32, shape, 0) + span.start
            row = row if blocks else row + sub * L
            col = lax.broadcasted_iota(jnp.int32, shape, 1)
            values = [inverse_root(dist[span, t : t + LANES]) for t in range(0, panels, LANES)]
            for t in range(1 if blocks else len(values)):
                values[t] = jnp.where(row == col + t * LANES, diag[span, :], values[t])
            return values

        def partial(span, held):
            keep(parts, span, sum(g * qrow[:, t * LANES : (t + 1) * LANES] for t, g in enumerate(held)))

        staged(spans_of(L), root, partial)
        return c

    pipeline(share, begin, finish, self_sums, body_size(unit, 16), ring, sums)
    total = self_sums[...].T * scale[0:1, 0:1]
    if early:
        out[...] = total
    else:
        out[...] = part[...]
        out[:clusters, :] = (part[:clusters, :] + before[...]) + total


def merge_kernel(sizes, far_list, targets, near, coupling, transfer, parent, up, *rest):
    C, S, L, slots, clusters = sizes
    sums = rest[: C - 1]
    parts = rest[C - 1 : C - 1 + S]
    parents = rest[-1]
    me, sub = lax.axis_index("clu"), lax.axis_index("sub")
    index = [targets[pl.ds(lax.rem(me + shift, C), 1), :] for shift in range(1, C)]
    got = select_rows(
        jnp.concatenate(index, axis=1), jnp.concatenate([v[:slots, :] for v in sums], axis=0), clusters
    )

    par_dev, far_n, rank = coupling.shape[0], coupling.shape[1], coupling.shape[2]
    parents[pl.ds(pl.multiple_of(me * par_dev, 8), par_dev), :] = up[...]
    for shift in range(1, C):
        owner = lax.rem(me + shift, C)
        parents[pl.ds(pl.multiple_of(owner * par_dev, 8), par_dev), :] = sums[shift - 1][slots:, :rank]
    lane = lax.broadcasted_iota(jnp.int32, (rank, LANES), 1)
    field = jnp.zeros((rank, LANES), F32)
    for p in range(par_dev):
        part = jnp.zeros((rank, rank), F32)
        for k in range(far_n):
            part = part + coupling[p, k] * parents[pl.ds(far_list[k, p], 1), :]
        field = jnp.where(lane == p, jnp.sum(part, axis=1, keepdims=True), field)
    which = lax.broadcasted_iota(jnp.int32, (LANES, clusters), 0)
    onehot = (parent[...] == which).astype(F32)
    down = jnp.dot(field, onehot, precision=HIGHEST, preferred_element_type=F32)
    fields = jnp.concatenate(
        [jnp.sum(transfer[r] * down, axis=0, keepdims=True) for r in range(rank)], axis=0
    )

    def give(s):
        for shift in range(S):
            other = (s + shift) % S
            part = near[:, other * L : (other + 1) * L]
            parts[shift][:clusters, :] = part + got if shift == 0 else part
            for t in range(clusters // L):
                at = clusters + t * rank
                parts[shift][at : at + rank, :] = fields[:, t * L : (t + 1) * L]

    for s in range(S):
        pl.when(sub == s)(functools.partial(give, s))


def up_sums(basis, masked, transfer, parent, count):
    clusters = basis.shape[0]
    rank = basis.shape[1]
    lane = lax.broadcasted_iota(jnp.int32, (rank, clusters), 1)
    leaf = jnp.zeros((rank, clusters), F32)
    for c in range(clusters):
        part = jnp.sum(basis[c] * masked[c : c + 1, :], axis=1, keepdims=True)
        leaf = jnp.where(lane == c, part, leaf)
    lifted = jnp.zeros((rank, clusters), F32)
    for r in range(rank):
        lifted = lifted + transfer[r] * leaf[r : r + 1, :]
    which = lax.broadcasted_iota(jnp.int32, (count, clusters), 0)
    onehot = (parent[...] == which).astype(F32)
    return lax.dot_general(
        onehot, lifted, (((1,), (1,)), ((), ())), precision=HIGHEST, preferred_element_type=F32
    )


def far_kernel(basis, near, out):
    clusters, rank = basis.shape[0], basis.shape[1]
    L = out.shape[1]
    fields = [near[clusters + t * rank : clusters + (t + 1) * rank, :] for t in range(clusters // L)]
    fields = jnp.concatenate(fields, axis=1) if len(fields) > 1 else fields[0]
    for c in range(clusters):
        far = jnp.sum(basis[c] * fields[:, c : c + 1], axis=0, keepdims=True)
        out[c : c + 1, :] = far + near[c : c + 1, :]


def send(value, moves):
    names = tuple(name for name, _ in moves)
    steps = [step for _, step in moves]
    sizes = [lax.axis_size(name) for name in names]
    perm = []

    def flat(coords):
        index = 0
        for size, c in zip(sizes, coords):
            index = index * size + c
        return index

    total = 1
    for size in sizes:
        total *= size
    for index in range(total):
        coords, left = [], index
        for size in reversed(sizes):
            coords.append(left % size)
            left //= size
        coords.reverse()
        perm.append((index, flat([(c + s) % n for c, s, n in zip(coords, steps, sizes)])))
    return lax.ppermute(value, names if len(names) > 1 else names[0], perm)


def on_device(
    charges,
    panel_mask,
    geometry,
    remote_source,
    remote_target,
    remote_live,
    local_pairs,
    basis,
    transfer,
    parent_of,
    far_list,
    coupling,
):
    clusters, L = charges.shape
    panels = geometry.shape[2]
    C, S, R = lax.axis_size("clu"), lax.axis_size("sub"), lax.axis_size("rep")
    slots = remote_source.shape[2]
    par_dev, rank = far_list.shape[0], transfer.shape[1]
    n = (C - 1) * slots
    shape = jax.ShapeDtypeStruct
    targets = remote_target[0]
    basis_t = jnp.transpose(basis, (0, 2, 1))
    transfer_t = jnp.transpose(transfer, (1, 2, 0))
    parent = parent_of[None, :]

    made = pl.pallas_call(
        functools.partial(pack_kernel, (C, S, L, slots)),
        out_shape=[pltpu.VMEM((clusters, L), F32), pltpu.VMEM((panels // LANES, clusters * 4, LANES), F32)]
        + [pltpu.VMEM((5 * slots + 8, L), F32)] * (C - 1),
        in_specs=[vmem()] * 3 + [smem()] * 3,
        out_specs=[vmem()] * (C + 1),
        compiler_params=limit(60),
        cost_estimate=about(2),
        name="packs",
    )(charges, panel_mask, geometry, targets, remote_source[0], remote_live[0])
    masked, geo, packs = made[0], made[1], made[2:]
    pieces = [masked] + [send(masked, (("sub", d),)) for d in range(1, S)]
    packs = [send(packs[d - 1], (("clu", d),)) for d in range(1, C)]

    *features, up = pl.pallas_call(
        prepare_kernel,
        out_shape=[pltpu.VMEM((panels // LANES, clusters * ROWS, LANES), F32)] * 2
        + [
            pltpu.VMEM((clusters, panels), F32),
            pltpu.VMEM((8, LANES), F32),
            pltpu.VMEM((par_dev, rank), F32),
        ],
        in_specs=[vmem()] * 2 + [pl.BlockSpec(memory_space=pltpu.HBM)] * 3,
        out_specs=[vmem()] * 5,
        scratch_shapes=[
            pltpu.VMEM(basis_t.shape, F32),
            pltpu.VMEM(transfer_t.shape, F32),
            pltpu.VMEM(parent.shape, jnp.int32),
            pltpu.SemaphoreType.DMA((3,)),
        ],
        compiler_params=limit(24),
        cost_estimate=about(4),
        name="prepare",
    )(*near_by(geo, masked), *far_off(basis_t, transfer_t, parent))
    *tables, diags, scale = features

    def own_tiles(early, height, *added):
        return pl.pallas_call(
            functools.partial(self_kernel, (S, L, R, clusters, panels), early),
            out_shape=pltpu.VMEM((height, L), F32),
            in_specs=[vmem()] * (4 + len(added) + S),
            out_specs=vmem(),
            scratch_shapes=[
                pltpu.VMEM((clusters, panels), F32),
                pltpu.VMEM((1, 8 if L == LANES else clusters * ROWS, L), F32),
                pltpu.VMEM((clusters, L), F32),
                pltpu.VMEM((L, clusters), F32),
            ]
            + [pltpu.VMEM((L, panels), F32)] * 8
            + [pltpu.VMEM((L, 2 * LANES), BF16)] * 4,
            compiler_params=limit(24),
            cost_estimate=about(2 if early else 4),
            name="near_self_early" if early else "near_self",
        )(*near_by(*tables, diags, scale, *added, *pieces))

    before = own_tiles(True, clusters)

    made = pl.pallas_call(
        functools.partial(remote_kernel, (C, S, L, slots, clusters, panels)),
        out_shape=[pltpu.VMEM((clusters, panels), F32)]
        + [pltpu.VMEM((slots + par_dev, L), F32)] * (C - 1),
        in_specs=[vmem()] * (4 + S + C - 1),
        out_specs=[vmem()] * C,
        scratch_shapes=[
            pltpu.VMEM((clusters, panels), F32),
            pltpu.VMEM((n, L), F32),
            pltpu.VMEM((clusters, panels), F32),
            pltpu.VMEM((L, whole(n)), F32),
            pltpu.VMEM((1, n * ROWS, L), F32),
            pltpu.SMEM((2 * n + 1,), jnp.int32),
            pltpu.SMEM((C - 1, 8, L), F32),
            pltpu.SemaphoreType.DMA((C - 1,)),
        ]
        + [pltpu.VMEM((L, panels), F32)] * 4
        + [pltpu.VMEM((L, 2 * LANES), BF16)] * 4,
        compiler_params=limit(24),
        cost_estimate=about(6),
        name="near_remote",
    )(*near_by(tables[1], scale, up, before, *pieces, *packs))
    acc, sums = made[0], [send(made[d], (("clu", C - d),)) for d in range(1, C)]

    wide = whole(local_pairs.shape[1])
    near = pl.pallas_call(
        functools.partial(local_kernel, (S, L, R, clusters, panels)),
        out_shape=pltpu.VMEM((clusters, panels), F32),
        in_specs=[vmem(), smem()] + [vmem()] * (4 + S),
        out_specs=vmem(),
        scratch_shapes=[
            pltpu.VMEM((clusters, panels), F32),
            pltpu.VMEM((clusters, panels), F32),
            pltpu.VMEM((panels, wide), F32),
        ]
        + [pltpu.VMEM((panels, panels), F32)] * 8
        + [pltpu.VMEM((panels, 2 * LANES), BF16)] * 4,
        compiler_params=limit(24),
        cost_estimate=about(9),
        name="near_local",
    )(*near_by(local_pairs[0].T), local_pairs[0].T, *near_by(*tables, scale, acc, *pieces))

    height = clusters + clusters // L * rank
    parts = pl.pallas_call(
        functools.partial(merge_kernel, (C, S, L, slots, clusters)),
        out_shape=[pltpu.VMEM((height, L), F32)] * S,
        in_specs=[smem()] + [vmem()] * (6 + C - 1),
        out_specs=[vmem()] * S,
        scratch_shapes=[pltpu.VMEM((C * par_dev, rank), F32)],
        compiler_params=limit(16),
        cost_estimate=about(1),
        name="merge",
    )(far_list.T, *near_by(targets, near, coupling, transfer_t, parent, up, *sums))
    others = [send(parts[d], (("sub", d),)) for d in range(1, S)]

    near = own_tiles(False, height, parts[0], before)
    for other in others:
        near = near + other
    others = [send(near, (("rep", e),)) for e in range(1, R)]

    total = pl.pallas_call(
        far_kernel,
        out_shape=pltpu.VMEM((clusters, L), F32),
        in_specs=[vmem()] * 2,
        out_specs=vmem(),
        compiler_params=limit(16),
        cost_estimate=about(1),
        name="far_down",
    )(*near_by(basis_t, near))
    for other in others:
        total = total + other[:clusters]
    return total * panel_mask.astype(F32)


def solution(mesh):
    placed = (
        P(("grp", "clu"), "sub"),
        P(("grp", "clu"), "sub"),
        P(("grp", "clu"), None, None),
        P(("grp", "clu"), None, "rep"),
        P(("grp", "clu"), None, "rep"),
        P(("grp", "clu"), None, "rep"),
        P(("grp", "clu"), "rep", None),
        P(("grp", "clu"), "sub", None),
        P(("grp", "clu"), None, None),
        P(("grp", "clu")),
        P(("grp", "clu"), None),
        P(("grp", "clu"), None, None, None),
    )
    return jax.shard_map(
        on_device, mesh=mesh, in_specs=placed, out_specs=P(("grp", "clu"), "sub"), check_vma=False
    )
```

```python
import functools

import jax
import jax.numpy as jnp
from jax import lax
from jax.experimental import pallas as pl
from jax.experimental.pallas import tpu as pltpu
from jax.sharding import PartitionSpec as P

F32 = jnp.float32
BF16 = jnp.bfloat16
ROWS = 24
LANES = 128


def limit(mib):
    return pltpu.CompilerParams(vmem_limit_bytes=mib * 1024 * 1024)


def about(us):
    return pl.CostEstimate(flops=0, bytes_accessed=int(us * 3.5e6), transcendentals=0)


def vmem():
    return pl.BlockSpec(memory_space=pltpu.VMEM)


def near_by(*arrays):
    return [pltpu.with_memory_space_constraint(x, pltpu.VMEM) for x in arrays]


def far_off(*arrays):
    return [pltpu.with_memory_space_constraint(x, pltpu.HBM) for x in arrays]


def smem():
    return pl.BlockSpec(memory_space=pltpu.SMEM)


def whole(size):
    return -(-size // LANES) * LANES


def cut(v):
    return v.astype(BF16).astype(F32)


def powers(sign):
    lane = lax.broadcasted_iota(jnp.int32, (8, LANES), 1)
    out = jnp.full((8, LANES), 2.0 ** (-64 * sign), F32)
    for bit in range(7):
        out = out * jnp.where((lane >> bit) & 1 == 1, F32(2.0 ** (sign * 2**bit)), F32(1.0))
    return out


def frame(geo):
    low, high = [None] * 8, [None] * 8
    blocks = [(t, c) for c in range(0, geo.shape[1], 8) for t in range(geo.shape[0])]
    for i, (t, c) in enumerate(blocks):
        g, k = geo[t, c : c + 8, :], i % 8
        low[k] = g if low[k] is None else jnp.minimum(low[k], g)
        high[k] = g if high[k] is None else jnp.maximum(high[k], g)
    low = jnp.min(functools.reduce(jnp.minimum, low), axis=1, keepdims=True)
    high = jnp.max(functools.reduce(jnp.maximum, high), axis=1, keepdims=True)
    low, high = jnp.minimum(low[:4], low[4:]), jnp.maximum(high[:4], high[4:])
    row = lax.broadcasted_iota(jnp.int32, low.shape, 0)
    radius = jnp.maximum(jnp.abs(low), jnp.abs(high))
    width = jnp.max(jnp.where(row == 3, radius, 0.5 * (high - low)), axis=0, keepdims=True)

    def over(table, least):
        return least(least(table, axis=1, keepdims=True), axis=0, keepdims=True)

    up, down = powers(1), powers(-1)
    size = over(jnp.where(up >= width, up, F32(2.0**63)), jnp.min)
    inv = over(jnp.where(up >= width, down, F32(2.0**-63)), jnp.max)
    magic = size * F32(1.5 * 2.0**20)
    return inv, (0.5 * (low + high) + magic) - magic


def split_frame(scale):
    return scale[0:1, 0:1], [scale[k : k + 1, 0:1] for k in range(1, 4)]


def split_features(points, centre, inv):
    magic = F32(1.5 * 2.0**16)
    grid, rest = [], []
    for k in range(3):
        u = (points[k] - centre[k]) * inv
        h = cut((u + magic) - magic)
        grid.append(h)
        rest.append(u - h)
    rad = points[3] * inv
    norm = grid[0] * grid[0] + grid[1] * grid[1] + grid[2] * grid[2]
    norm1 = cut(norm)
    norm2 = cut(norm - norm1)
    cross = grid[0] * rest[0] + grid[1] * rest[1] + grid[2] * rest[2]
    extra = 2.0 * cross + (rest[0] * rest[0] + rest[1] * rest[1] + rest[2] * rest[2]) + rad * rad
    extra = extra + ((norm - norm1) - norm2)
    extra1 = cut(extra)
    extra2 = cut(extra - extra1)
    extra3 = (extra - extra1) - extra2
    rest1 = [cut(v) for v in rest]
    rest2 = [v - w for v, w in zip(rest, rest1)]
    neg = lambda vs: [-2.0 * v for v in vs]
    one, zero = jnp.ones_like(rad), jnp.zeros_like(rad)
    left = grid + [norm1, norm2, one, one, zero]
    left += rest1 + [extra1, extra2, zero, zero, zero]
    left += rest2 + [extra3, zero, zero, zero, zero]
    right = neg(grid) + [one, one, norm1, norm2, zero]
    right += neg(rest1) + [zero, zero, extra1, extra2, zero]
    right += neg(rest2) + [zero, zero, extra3, zero, zero]
    return left, right, rad


def products(left, right):
    a, b, c = [left[k : k + 8, :] for k in (0, 8, 16)]
    x, y, z = [right[k : k + 8, :] for k in (0, 8, 16)]
    pairs = [(a, x), (b, x), (a, y), (c, x), (a, z), (b, y)]
    return [jnp.concatenate(v, axis=0).astype(BF16) for v in zip(*pairs)]


def store_features(ref, rows, first):
    width = rows[0].shape[1]
    for k, row in enumerate(rows):
        for t in range(ref.shape[0]):
            at = pl.ds(first * ROWS + k, 8, stride=ROWS)
            ref[t, at, :] = row[:, t * LANES : min(width, (t + 1) * LANES)]


def load_features(ref, index, order=None):
    start = pl.multiple_of(index * ROWS, 8)
    order = range(ref.shape[0]) if order is None else order
    blocks = [ref[t, pl.ds(start, ROWS), :] for t in order]
    return jnp.concatenate(blocks, axis=1) if len(blocks) > 1 else blocks[0]


def contract(left, right):
    return jnp.dot(left, right, preferred_element_type=F32)


def pieces_of(value):
    high = value.astype(BF16)
    rest = value - high.astype(F32)
    mid = rest.astype(BF16)
    return [high, mid, (rest - mid.astype(F32)).astype(BF16)]


def select_rows(index, value, count):
    row = lax.broadcasted_iota(jnp.int32, (count, index.shape[1]), 0)
    left = jnp.where(row == index, 1.0, 0.0).astype(BF16)
    return jnp.dot(
        jnp.concatenate([left] * 3, axis=1),
        jnp.concatenate(pieces_of(value), axis=0),
        preferred_element_type=F32,
    )


def upright(row):
    return jnp.broadcast_to(row, (8, row.shape[1])).T[:, :1]


def keep(parts, rows, value):
    high = value.astype(BF16)
    parts[rows, :LANES] = high
    parts[rows, LANES:] = (value - high.astype(F32)).astype(BF16)


def add_columns(table, parts, indices):
    shape = (2 * LANES, table.shape[1])
    lane = lax.broadcasted_iota(jnp.int32, shape, 1)
    picks = [jnp.where(lane == index, 1.0, 0.0).astype(BF16) for index in indices]
    table[...] += jnp.dot(
        jnp.concatenate([p[...] for p in parts], axis=1),
        jnp.concatenate(picks, axis=0),
        preferred_element_type=F32,
    )


def inverse_root(d):
    return lax.rsqrt(d)


def fold(v):
    return jnp.sum(v.reshape(v.shape[0] // 8, 8, v.shape[1]), axis=0)


def distances(left, right, out):
    left, right = products(left, right)
    out[...] = contract(left.T, right)


def staged(spans, *stages):
    held = {}
    for t in range(len(spans) + len(stages) - 1):
        for depth in reversed(range(len(stages))):
            k = t - depth
            if 0 <= k < len(spans):
                held[k] = stages[depth](spans[k], held.get(k))
                if depth == len(stages) - 1:
                    del held[k]


def spans_of(height, step=32):
    step = min(step, height)
    return [slice(r, r + step) for r in range(0, height, step)]


def tile_sums(dist, qrow, qleft, parts):
    q0, q1 = qrow[:, :LANES], qrow[:, LANES:]
    qcol = upright(qleft)
    back = [jnp.zeros((8, LANES), F32), jnp.zeros((8, LANES), F32)]

    def root(rows, _):
        return (
            inverse_root(dist[rows, :LANES]),
            inverse_root(dist[rows, LANES:]),
        )

    def sums(rows, held):
        g0, g1 = held
        back[0] = back[0] + fold(g0 * qcol[rows, :])
        back[1] = back[1] + fold(g1 * qcol[rows, :])
        keep(parts, rows, g0 * q0 + g1 * q1)

    staged(spans_of(dist.shape[0]), root, sums)
    return jnp.concatenate([jnp.sum(b, axis=0, keepdims=True) for b in back], axis=1)


def pipeline(total, begin, finish, table, size, ring, parts):
    ring = ring[: min(len(ring), size)]
    ahead = min(2, len(ring) - 1)
    group = min(2, size)

    def body(i, carry):
        indices = []
        for k in range(size):
            begin(i * size + k + ahead, ring[(k + ahead) % len(ring)])
            indices.append(finish(i * size + k, ring[k % len(ring)], parts[k % len(parts)]))
            if len(indices) == group:
                done = [parts[(k - n) % len(parts)] for n in reversed(range(group))]
                add_columns(table, done, indices)
                indices = []
        return carry

    for k in range(ahead):
        begin(k, ring[k])
    lax.fori_loop(0, (total + size - 1) // size, body, 0)


def body_size(total, most):
    return next(size for size in (32, 16, 8, 4, 2, 1) if size <= most and total % size == 0)


def assemble(sub, S, L, q, pieces):
    def place(s):
        for shift in range(S):
            owner = (s - shift) % S
            q[:, owner * L : (owner + 1) * L] = pieces[shift][: q.shape[0], :]

    for s in range(S):
        pl.when(sub == s)(functools.partial(place, s))


def pack_kernel(sizes, charges, mask, geo, targets, sources, live, masked, geo_out, *packs):
    C, S, L, slots = sizes
    me, sub = lax.axis_index("clu"), lax.axis_index("sub")
    masked[...] = charges[...] * mask[...].astype(F32)
    for t in range(geo_out.shape[0]):
        geo_out[t, :, :] = geo[:, :, t * LANES : (t + 1) * LANES].reshape(geo_out.shape[1:])
    lane = lax.broadcasted_iota(jnp.int32, (8, L), 1)
    for shift in range(1, C):
        dest = lax.rem(me + shift, C)
        codes = jnp.full((8, L), -1.0, F32)
        for j in range(slots):
            code = jnp.where(live[dest, j] > 0, sources[dest, j], -1)
            codes = jnp.where(lane == j, code.astype(F32), codes)
        packs[shift - 1][5 * slots :, :] = codes

    def fill(s):
        for shift in range(1, C):
            dest = lax.rem(me + shift, C)
            pack = packs[shift - 1]
            for j in range(slots):
                t = targets[dest, j]
                g = geo[t, :, s * L : (s + 1) * L]
                for k in range(4):
                    pack[k * slots + j : k * slots + j + 1, :] = g[k : k + 1]
                pack[4 * slots + j : 4 * slots + j + 1, :] = masked[pl.ds(t, 1), :]

    for s in range(S):
        pl.when(sub == s)(functools.partial(fill, s))


def remote_kernel(sizes, fb, scale, up, before, *rest):
    del before
    C, S, L, slots, clusters, panels = sizes
    pieces = rest[:S]
    packs = rest[S : S + C - 1]
    acc_out = rest[S + C - 1]
    sends = rest[S + C : S + C + C - 1]
    q, tq, acc, fwdt, fa, order, codes, sems, *work = rest[S + C + C - 1 :]
    n = (C - 1) * slots
    copies = [
        pltpu.make_async_copy(packs[k].at[pl.ds(5 * slots, 8), :], codes.at[k], sems.at[k])
        for k in range(C - 1)
    ]
    for copy in copies:
        copy.start()
    assemble(lax.axis_index("sub"), S, L, q, pieces)
    acc[...] = jnp.zeros_like(acc)
    fwdt[...] = jnp.zeros_like(fwdt)
    for copy in copies:
        copy.wait()
    found = jnp.int32(0)
    for shift in range(C - 1):
        for j in range(slots):
            code = codes[shift, 0, j].astype(jnp.int32)
            order[n + 1 + shift * slots + j] = jnp.maximum(code, 0)
            order[found] = shift * slots + j
            found = found + (code >= 0).astype(jnp.int32)
    inv, centre = split_frame(scale)
    for shift in range(C - 1):
        for first in range(0, slots, 8):
            points = [packs[shift][k * slots + first : k * slots + first + 8, :] for k in range(5)]
            left, _, _ = split_features(points, centre, inv)
            store_features(fa, left, shift * slots + first)
            at = shift * slots + first
            tq[at : at + 8, :] = points[4]

    def begin(i, dist):
        slot = order[jnp.minimum(i, jnp.maximum(found - 1, 0))]
        distances(load_features(fa, slot), load_features(fb, order[n + 1 + slot]), dist)

    def finish(i, dist, part):
        ok = i < found
        slot = order[jnp.minimum(i, jnp.maximum(found - 1, 0))]
        source = order[n + 1 + slot]
        back = tile_sums(
            dist, q[pl.ds(source, 1), :], tq[pl.ds(slot, 1), :], part
        )
        acc[pl.ds(source, 1), :] += jnp.where(ok, back, 0.0)
        return jnp.where(ok, slot, -1)

    pipeline(found, begin, finish, fwdt, 8, work[:4], work[4:])
    acc_out[...] = acc[...] * inv
    fwd = (fwdt[...] * inv).T
    rank = up.shape[1]
    for shift in range(C - 1):
        sends[shift][:slots, :] = fwd[shift * slots : (shift + 1) * slots, :]
        sends[shift][slots:, :] = jnp.zeros((up.shape[0], L), F32)
        sends[shift][slots:, :rank] = up[...]


def prepare_kernel(
    geo, masked, basis_far, transfer_far, parent_far,
    fa, fb, diag, scale, up, basis, transfer, parent, sems
):
    copies = [
        pltpu.make_async_copy(src, dst, sems.at[k])
        for k, (src, dst) in enumerate(
            [(basis_far, basis), (transfer_far, transfer), (parent_far, parent)]
        )
    ]
    for copy in copies:
        copy.start()
    inv, centre = frame(geo)
    scale[...] = jnp.zeros_like(scale)
    scale[0:1, :] = jnp.broadcast_to(inv, (1, LANES))
    for k in range(3):
        scale[k + 1 : k + 2, :] = jnp.broadcast_to(centre[k : k + 1, :], (1, LANES))
    inv, centre = split_frame(scale)
    for first in range(0, diag.shape[0], 8):
        points = [
            jnp.concatenate(
                [geo[t, pl.ds(first * 4 + k, 8, stride=4), :] for t in range(geo.shape[0])], axis=1
            )
            for k in range(4)
        ]
        left, right, rad = split_features(points, centre, inv)
        store_features(fa, left, first)
        store_features(fb, right, first)
        diag[first : first + 8, :] = lax.rsqrt(2.0 * (rad * rad))
    for copy in copies:
        copy.wait()
    up[...] = up_sums(basis, masked, transfer, parent, up.shape[0])


def local_kernel(sizes, pair_rows, pairs, fa, fb, scale, acc_in, *rest):
    S, L, R, clusters, panels = sizes
    pieces = rest[:S]
    acc_out = rest[S]
    q, acc, pair_sums, *work = rest[S + 1 :]
    ring, sums = work[:8], work[8:]
    sub = lax.axis_index("sub")
    assemble(sub, S, L, q, pieces)
    acc[...] = jnp.zeros_like(acc)
    pair_sums[...] = jnp.zeros_like(pair_sums)

    count = pairs.shape[1] // S
    start = sub * count

    def begin(i, dist):
        p = start + jnp.minimum(i, count - 1)
        distances(load_features(fa, pairs[0, p]), load_features(fb, pairs[1, p]), dist)

    def finish(i, dist, part):
        ia, ib = pairs[0, start + i], pairs[1, start + i]
        acc[pl.ds(ib, 1), :] += tile_sums(
            dist, q[pl.ds(ib, 1), :], q[pl.ds(ia, 1), :], part
        )
        return start + i

    pipeline(count, begin, finish, pair_sums, body_size(count, 32), ring, sums)
    width = pair_rows.shape[1]
    total = acc[...] + select_rows(pair_rows[0:1, :], pair_sums[...].T[:width, :], clusters)
    acc_out[...] = acc_in[...] + total * scale[0:1, 0:1]


def self_kernel(sizes, early, fa, fb, diags, scale, *rest):
    S, L, R, clusters, panels = sizes
    if not early:
        part, before, *rest = rest
    pieces = rest[:S]
    out, q, fs, spots, self_sums, *work = rest[S:]
    ring, sums = work[:8], work[8:]
    sub, rep = lax.axis_index("sub"), lax.axis_index("rep")
    self_sums[...] = jnp.zeros_like(self_sums)
    blocks = L == LANES
    if blocks:
        order = [lax.rem(sub + S - shift, S) for shift in range(S)]
        for shift in range(S):
            q[:, shift * L : (shift + 1) * L] = pieces[shift][...]
    else:
        order = None
        assemble(sub, S, L, q, pieces)

    def place(s):
        if not blocks:
            t, at = (s * L) // LANES, (s * L) % LANES
            fs[0, :, :] = fa[t, :, at : at + L]
        spots[...] = diags[:, s * L : (s + 1) * L]

    for s in range(S):
        pl.when(sub == s)(functools.partial(place, s))
    base = clusters // R
    unit = base // 4
    first = rep * base
    share = base
    if R > 1:
        first = first - jnp.where(rep > 0, unit, 0)
        share = share + jnp.where(rep == R - 1, unit, 0) - jnp.where(rep == 0, unit, 0)
    if early:
        share = unit
    else:
        first, share = first + unit, share - unit

    def begin(i, dist):
        c = first + jnp.minimum(i, share - 1)
        own = load_features(fa, c, order[:1]) if blocks else load_features(fs, c)
        distances(own, load_features(fb, c, order), dist)

    def finish(i, dist, parts):
        c = first + i
        qrow = q[pl.ds(c, 1), :]
        diag = upright(spots[pl.ds(c, 1), :])

        def root(span, _):
            shape = (span.stop - span.start, LANES)
            row = lax.broadcasted_iota(jnp.int32, shape, 0) + span.start
            row = row if blocks else row + sub * L
            col = lax.broadcasted_iota(jnp.int32, shape, 1)
            values = [inverse_root(dist[span, t : t + LANES]) for t in range(0, panels, LANES)]
            for t in range(1 if blocks else len(values)):
                values[t] = jnp.where(row == col + t * LANES, diag[span, :], values[t])
            return values

        def partial(span, held):
            keep(parts, span, sum(g * qrow[:, t * LANES : (t + 1) * LANES] for t, g in enumerate(held)))

        staged(spans_of(L), root, partial)
        return c

    pipeline(share, begin, finish, self_sums, body_size(unit, 16), ring, sums)
    total = self_sums[...].T * scale[0:1, 0:1]
    if early:
        out[...] = total
    else:
        out[...] = part[...]
        out[:clusters, :] = (part[:clusters, :] + before[...]) + total


def merge_kernel(sizes, far_list, targets, near, coupling, transfer, parent, up, *rest):
    C, S, L, slots, clusters = sizes
    sums = rest[: C - 1]
    parts = rest[C - 1 : C - 1 + S]
    parents = rest[-1]
    me, sub = lax.axis_index("clu"), lax.axis_index("sub")
    index = [targets[pl.ds(lax.rem(me + shift, C), 1), :] for shift in range(1, C)]
    got = select_rows(
        jnp.concatenate(index, axis=1), jnp.concatenate([v[:slots, :] for v in sums], axis=0), clusters
    )

    par_dev, far_n, rank = coupling.shape[0], coupling.shape[1], coupling.shape[2]
    parents[pl.ds(pl.multiple_of(me * par_dev, 8), par_dev), :] = up[...]
    for shift in range(1, C):
        owner = lax.rem(me + shift, C)
        parents[pl.ds(pl.multiple_of(owner * par_dev, 8), par_dev), :] = sums[shift - 1][slots:, :rank]
    lane = lax.broadcasted_iota(jnp.int32, (rank, LANES), 1)
    field = jnp.zeros((rank, LANES), F32)
    for p in range(par_dev):
        part = jnp.zeros((rank, rank), F32)
        for k in range(far_n):
            part = part + coupling[p, k] * parents[pl.ds(far_list[k, p], 1), :]
        field = jnp.where(lane == p, jnp.sum(part, axis=1, keepdims=True), field)
    which = lax.broadcasted_iota(jnp.int32, (LANES, clusters), 0)
    onehot = jnp.where(parent[...] == which, 1.0, 0.0).astype(BF16)
    down = jnp.dot(
        jnp.concatenate(pieces_of(field), axis=1),
        jnp.concatenate([onehot] * 3, axis=0),
        preferred_element_type=F32,
    )
    fields = jnp.concatenate(
        [jnp.sum(transfer[r] * down, axis=0, keepdims=True) for r in range(rank)], axis=0
    )

    def give(s):
        for shift in range(S):
            other = (s + shift) % S
            part = near[:, other * L : (other + 1) * L]
            parts[shift][:clusters, :] = part + got if shift == 0 else part
            for t in range(clusters // L):
                at = clusters + t * rank
                parts[shift][at : at + rank, :] = fields[:, t * L : (t + 1) * L]

    for s in range(S):
        pl.when(sub == s)(functools.partial(give, s))


def up_sums(basis, masked, transfer, parent, count):
    clusters = basis.shape[0]
    rank = basis.shape[1]
    lane = lax.broadcasted_iota(jnp.int32, (rank, clusters), 1)
    leaf = jnp.zeros((rank, clusters), F32)
    for c in range(clusters):
        part = jnp.sum(basis[c] * masked[c : c + 1, :], axis=1, keepdims=True)
        leaf = jnp.where(lane == c, part, leaf)
    lifted = jnp.zeros((rank, clusters), F32)
    for r in range(rank):
        lifted = lifted + transfer[r] * leaf[r : r + 1, :]
    which = lax.broadcasted_iota(jnp.int32, (count, clusters), 0)
    onehot = jnp.where(parent[...] == which, 1.0, 0.0).astype(BF16)
    return lax.dot_general(
        jnp.concatenate([onehot] * 3, axis=1),
        jnp.concatenate(pieces_of(lifted), axis=1),
        (((1,), (1,)), ((), ())),
        preferred_element_type=F32,
    )


def far_kernel(basis, near, out):
    clusters, rank = basis.shape[0], basis.shape[1]
    L = out.shape[1]
    fields = [near[clusters + t * rank : clusters + (t + 1) * rank, :] for t in range(clusters // L)]
    fields = jnp.concatenate(fields, axis=1) if len(fields) > 1 else fields[0]
    for c in range(clusters):
        far = jnp.sum(basis[c] * fields[:, c : c + 1], axis=0, keepdims=True)
        out[c : c + 1, :] = far + near[c : c + 1, :]


def send(value, moves):
    names = tuple(name for name, _ in moves)
    steps = [step for _, step in moves]
    sizes = [lax.axis_size(name) for name in names]
    perm = []

    def flat(coords):
        index = 0
        for size, c in zip(sizes, coords):
            index = index * size + c
        return index

    total = 1
    for size in sizes:
        total *= size
    for index in range(total):
        coords, left = [], index
        for size in reversed(sizes):
            coords.append(left % size)
            left //= size
        coords.reverse()
        perm.append((index, flat([(c + s) % n for c, s, n in zip(coords, steps, sizes)])))
    return lax.ppermute(value, names if len(names) > 1 else names[0], perm)


def on_device(
    charges,
    panel_mask,
    geometry,
    remote_source,
    remote_target,
    remote_live,
    local_pairs,
    basis,
    transfer,
    parent_of,
    far_list,
    coupling,
):
    clusters, L = charges.shape
    panels = geometry.shape[2]
    C, S, R = lax.axis_size("clu"), lax.axis_size("sub"), lax.axis_size("rep")
    slots = remote_source.shape[2]
    par_dev, rank = far_list.shape[0], transfer.shape[1]
    n = (C - 1) * slots
    shape = jax.ShapeDtypeStruct
    targets = remote_target[0]
    basis_t = jnp.transpose(basis, (0, 2, 1))
    transfer_t = jnp.transpose(transfer, (1, 2, 0))
    parent = parent_of[None, :]

    made = pl.pallas_call(
        functools.partial(pack_kernel, (C, S, L, slots)),
        out_shape=[pltpu.VMEM((clusters, L), F32), pltpu.VMEM((panels // LANES, clusters * 4, LANES), F32)]
        + [pltpu.VMEM((5 * slots + 8, L), F32)] * (C - 1),
        in_specs=[vmem()] * 3 + [smem()] * 3,
        out_specs=[vmem()] * (C + 1),
        compiler_params=limit(60),
        cost_estimate=about(2),
        name="packs",
    )(charges, panel_mask, geometry, targets, remote_source[0], remote_live[0])
    masked, geo, packs = made[0], made[1], made[2:]
    pieces = [masked] + [send(masked, (("sub", d),)) for d in range(1, S)]
    packs = [send(packs[d - 1], (("clu", d),)) for d in range(1, C)]

    *features, up = pl.pallas_call(
        prepare_kernel,
        out_shape=[pltpu.VMEM((panels // LANES, clusters * ROWS, LANES), F32)] * 2
        + [
            pltpu.VMEM((clusters, panels), F32),
            pltpu.VMEM((8, LANES), F32),
            pltpu.VMEM((par_dev, rank), F32),
        ],
        in_specs=[vmem()] * 2 + [pl.BlockSpec(memory_space=pltpu.HBM)] * 3,
        out_specs=[vmem()] * 5,
        scratch_shapes=[
            pltpu.VMEM(basis_t.shape, F32),
            pltpu.VMEM(transfer_t.shape, F32),
            pltpu.VMEM(parent.shape, jnp.int32),
            pltpu.SemaphoreType.DMA((3,)),
        ],
        compiler_params=limit(24),
        cost_estimate=about(4),
        name="prepare",
    )(*near_by(geo, masked), *far_off(basis_t, transfer_t, parent))
    *tables, diags, scale = features

    def own_tiles(early, height, *added):
        return pl.pallas_call(
            functools.partial(self_kernel, (S, L, R, clusters, panels), early),
            out_shape=pltpu.VMEM((height, L), F32),
            in_specs=[vmem()] * (4 + len(added) + S),
            out_specs=vmem(),
            scratch_shapes=[
                pltpu.VMEM((clusters, panels), F32),
                pltpu.VMEM((1, 8 if L == LANES else clusters * ROWS, L), F32),
                pltpu.VMEM((clusters, L), F32),
                pltpu.VMEM((L, clusters), F32),
            ]
            + [pltpu.VMEM((L, panels), F32)] * 8
            + [pltpu.VMEM((L, 2 * LANES), BF16)] * 4,
            compiler_params=limit(24),
            cost_estimate=about(2 if early else 4),
            name="near_self_early" if early else "near_self",
        )(*near_by(*tables, diags, scale, *added, *pieces))

    before = own_tiles(True, clusters)

    made = pl.pallas_call(
        functools.partial(remote_kernel, (C, S, L, slots, clusters, panels)),
        out_shape=[pltpu.VMEM((clusters, panels), F32)]
        + [pltpu.VMEM((slots + par_dev, L), F32)] * (C - 1),
        in_specs=[vmem()] * (4 + S + C - 1),
        out_specs=[vmem()] * C,
        scratch_shapes=[
            pltpu.VMEM((clusters, panels), F32),
            pltpu.VMEM((n, L), F32),
            pltpu.VMEM((clusters, panels), F32),
            pltpu.VMEM((L, whole(n)), F32),
            pltpu.VMEM((1, n * ROWS, L), F32),
            pltpu.SMEM((2 * n + 1,), jnp.int32),
            pltpu.SMEM((C - 1, 8, L), F32),
            pltpu.SemaphoreType.DMA((C - 1,)),
        ]
        + [pltpu.VMEM((L, panels), F32)] * 4
        + [pltpu.VMEM((L, 2 * LANES), BF16)] * 4,
        compiler_params=limit(24),
        cost_estimate=about(6),
        name="near_remote",
    )(*near_by(tables[1], scale, up, before, *pieces, *packs))
    acc, sums = made[0], [send(made[d], (("clu", C - d),)) for d in range(1, C)]

    wide = whole(local_pairs.shape[1])
    near = pl.pallas_call(
        functools.partial(local_kernel, (S, L, R, clusters, panels)),
        out_shape=pltpu.VMEM((clusters, panels), F32),
        in_specs=[vmem(), smem()] + [vmem()] * (4 + S),
        out_specs=vmem(),
        scratch_shapes=[
            pltpu.VMEM((clusters, panels), F32),
            pltpu.VMEM((clusters, panels), F32),
            pltpu.VMEM((panels, wide), F32),
        ]
        + [pltpu.VMEM((panels, panels), F32)] * 8
        + [pltpu.VMEM((panels, 2 * LANES), BF16)] * 4,
        compiler_params=limit(24),
        cost_estimate=about(9),
        name="near_local",
    )(*near_by(local_pairs[0].T), local_pairs[0].T, *near_by(*tables, scale, acc, *pieces))

    height = clusters + clusters // L * rank
    parts = pl.pallas_call(
        functools.partial(merge_kernel, (C, S, L, slots, clusters)),
        out_shape=[pltpu.VMEM((height, L), F32)] * S,
        in_specs=[smem()] + [vmem()] * (6 + C - 1),
        out_specs=[vmem()] * S,
        scratch_shapes=[pltpu.VMEM((C * par_dev, rank), F32)],
        compiler_params=limit(16),
        cost_estimate=about(1),
        name="merge",
    )(far_list.T, *near_by(targets, near, coupling, transfer_t, parent, up, *sums))
    others = [send(parts[d], (("sub", d),)) for d in range(1, S)]

    near = own_tiles(False, height, parts[0], before)
    for other in others:
        near = near + other
    others = [send(near, (("rep", e),)) for e in range(1, R)]

    total = pl.pallas_call(
        far_kernel,
        out_shape=pltpu.VMEM((clusters, L), F32),
        in_specs=[vmem()] * 2,
        out_specs=vmem(),
        compiler_params=limit(16),
        cost_estimate=about(1),
        name="far_down",
    )(*near_by(basis_t, near))
    for other in others:
        total = total + other[:clusters]
    return total * panel_mask.astype(F32)


def solution(mesh):
    placed = (
        P(("grp", "clu"), "sub"),
        P(("grp", "clu"), "sub"),
        P(("grp", "clu"), None, None),
        P(("grp", "clu"), None, "rep"),
        P(("grp", "clu"), None, "rep"),
        P(("grp", "clu"), None, "rep"),
        P(("grp", "clu"), "rep", None),
        P(("grp", "clu"), "sub", None),
        P(("grp", "clu"), None, None),
        P(("grp", "clu")),
        P(("grp", "clu"), None),
        P(("grp", "clu"), None, None, None),
    )
    return jax.shard_map(
        on_device, mesh=mesh, in_specs=placed, out_specs=P(("grp", "clu"), "sub"), check_vma=False
    )
```

```python
import functools

import jax
import jax.numpy as jnp
from jax import lax
from jax.experimental import pallas as pl
from jax.experimental.pallas import tpu as pltpu
from jax.sharding import PartitionSpec as P

F32 = jnp.float32
BF16 = jnp.bfloat16
HIGHEST = lax.Precision.HIGHEST
ROWS = 24
LANES = 128


def limit(mib):
    return pltpu.CompilerParams(vmem_limit_bytes=mib * 1024 * 1024)


def about(us):
    return pl.CostEstimate(flops=0, bytes_accessed=int(us * 3.5e6), transcendentals=0)


def vmem():
    return pl.BlockSpec(memory_space=pltpu.VMEM)


def near_by(*arrays):
    return [pltpu.with_memory_space_constraint(x, pltpu.VMEM) for x in arrays]


def far_off(*arrays):
    return [pltpu.with_memory_space_constraint(x, pltpu.HBM) for x in arrays]


def smem():
    return pl.BlockSpec(memory_space=pltpu.SMEM)


def whole(size):
    return -(-size // LANES) * LANES


def cut(v):
    return v.astype(BF16).astype(F32)


def powers(sign):
    lane = lax.broadcasted_iota(jnp.int32, (8, LANES), 1)
    out = jnp.full((8, LANES), 2.0 ** (-64 * sign), F32)
    for bit in range(7):
        out = out * jnp.where((lane >> bit) & 1 == 1, F32(2.0 ** (sign * 2**bit)), F32(1.0))
    return out


def frame(geo):
    low, high = [None] * 8, [None] * 8
    blocks = [(t, c) for c in range(0, geo.shape[1], 8) for t in range(geo.shape[0])]
    for i, (t, c) in enumerate(blocks):
        g, k = geo[t, c : c + 8, :], i % 8
        low[k] = g if low[k] is None else jnp.minimum(low[k], g)
        high[k] = g if high[k] is None else jnp.maximum(high[k], g)
    low = jnp.min(functools.reduce(jnp.minimum, low), axis=1, keepdims=True)
    high = jnp.max(functools.reduce(jnp.maximum, high), axis=1, keepdims=True)
    low, high = jnp.minimum(low[:4], low[4:]), jnp.maximum(high[:4], high[4:])
    row = lax.broadcasted_iota(jnp.int32, low.shape, 0)
    radius = jnp.maximum(jnp.abs(low), jnp.abs(high))
    width = jnp.max(jnp.where(row == 3, radius, 0.5 * (high - low)), axis=0, keepdims=True)

    def over(table, least):
        return least(least(table, axis=1, keepdims=True), axis=0, keepdims=True)

    up, down = powers(1), powers(-1)
    size = over(jnp.where(up >= width, up, F32(2.0**63)), jnp.min)
    inv = over(jnp.where(up >= width, down, F32(2.0**-63)), jnp.max)
    magic = size * F32(1.5 * 2.0**20)
    return inv, (0.5 * (low + high) + magic) - magic


def split_frame(scale):
    return scale[0:1, 0:1], [scale[k : k + 1, 0:1] for k in range(1, 4)]


def split_features(points, centre, inv):
    magic = F32(1.5 * 2.0**16)
    grid, rest = [], []
    for k in range(3):
        u = (points[k] - centre[k]) * inv
        h = cut((u + magic) - magic)
        grid.append(h)
        rest.append(u - h)
    rad = points[3] * inv
    norm = grid[0] * grid[0] + grid[1] * grid[1] + grid[2] * grid[2]
    norm1 = cut(norm)
    norm2 = cut(norm - norm1)
    cross = grid[0] * rest[0] + grid[1] * rest[1] + grid[2] * rest[2]
    extra = 2.0 * cross + (rest[0] * rest[0] + rest[1] * rest[1] + rest[2] * rest[2]) + rad * rad
    extra = extra + ((norm - norm1) - norm2)
    extra1 = cut(extra)
    extra2 = cut(extra - extra1)
    extra3 = (extra - extra1) - extra2
    rest1 = [cut(v) for v in rest]
    rest2 = [v - w for v, w in zip(rest, rest1)]
    neg = lambda vs: [-2.0 * v for v in vs]
    one, zero = jnp.ones_like(rad), jnp.zeros_like(rad)
    left = grid + [norm1, norm2, one, one, zero]
    left += rest1 + [extra1, extra2, zero, zero, zero]
    left += rest2 + [extra3, zero, zero, zero, zero]
    right = neg(grid) + [one, one, norm1, norm2, zero]
    right += neg(rest1) + [zero, zero, extra1, extra2, zero]
    right += neg(rest2) + [zero, zero, extra3, zero, zero]
    return left, right, rad


def products(left, right):
    a, b, c = [left[k : k + 8, :] for k in (0, 8, 16)]
    x, y, z = [right[k : k + 8, :] for k in (0, 8, 16)]
    pairs = [(a, x), (b, x), (a, y), (c, x), (a, z), (b, y), (b, z), (c, y)]
    return [jnp.concatenate(v, axis=0).astype(BF16) for v in zip(*pairs)]


def store_features(ref, rows, first):
    width = rows[0].shape[1]
    for k, row in enumerate(rows):
        for t in range(ref.shape[0]):
            at = pl.ds(first * ROWS + k, 8, stride=ROWS)
            ref[t, at, :] = row[:, t * LANES : min(width, (t + 1) * LANES)]


def load_features(ref, index, order=None):
    start = pl.multiple_of(index * ROWS, 8)
    order = range(ref.shape[0]) if order is None else order
    blocks = [ref[t, pl.ds(start, ROWS), :] for t in order]
    return jnp.concatenate(blocks, axis=1) if len(blocks) > 1 else blocks[0]


def contract(left, right):
    return jnp.dot(left, right, preferred_element_type=F32)


def select_rows(index, value, count):
    row = lax.broadcasted_iota(jnp.int32, (count, index.shape[1]), 0)
    left = jnp.where(row == index, 1.0, 0.0).astype(BF16)
    high = value.astype(BF16)
    rest = value - high.astype(F32)
    mid = rest.astype(BF16)
    low = (rest - mid.astype(F32)).astype(BF16)
    return jnp.dot(
        jnp.concatenate([left] * 3, axis=1),
        jnp.concatenate([high, mid, low], axis=0),
        preferred_element_type=F32,
    )


def upright(row):
    return jnp.broadcast_to(row, (8, row.shape[1])).T[:, :1]


def keep(parts, rows, value):
    high = value.astype(BF16)
    parts[rows, :LANES] = high
    parts[rows, LANES:] = (value - high.astype(F32)).astype(BF16)


def add_columns(table, parts, indices):
    shape = (2 * LANES, table.shape[1])
    lane = lax.broadcasted_iota(jnp.int32, shape, 1)
    picks = [jnp.where(lane == index, 1.0, 0.0).astype(BF16) for index in indices]
    table[...] += jnp.dot(
        jnp.concatenate([p[...] for p in parts], axis=1),
        jnp.concatenate(picks, axis=0),
        preferred_element_type=F32,
    )


def inverse_root(d):
    return lax.rsqrt(d)


def fold(v):
    return jnp.sum(v.reshape(v.shape[0] // 8, 8, v.shape[1]), axis=0)


def distances(left, right, out):
    left, right = products(left, right)
    out[...] = contract(left.T, right)


def staged(spans, *stages):
    held = {}
    for t in range(len(spans) + len(stages) - 1):
        for depth in reversed(range(len(stages))):
            k = t - depth
            if 0 <= k < len(spans):
                held[k] = stages[depth](spans[k], held.get(k))
                if depth == len(stages) - 1:
                    del held[k]


def spans_of(height, step=32):
    step = min(step, height)
    return [slice(r, r + step) for r in range(0, height, step)]


def tile_sums(dist, qrow, qleft, parts):
    q0, q1 = qrow[:, :LANES], qrow[:, LANES:]
    qcol = upright(qleft)
    back = [jnp.zeros((8, LANES), F32), jnp.zeros((8, LANES), F32)]

    def root(rows, _):
        return (
            inverse_root(dist[rows, :LANES]),
            inverse_root(dist[rows, LANES:]),
        )

    def sums(rows, held):
        g0, g1 = held
        back[0] = back[0] + fold(g0 * qcol[rows, :])
        back[1] = back[1] + fold(g1 * qcol[rows, :])
        keep(parts, rows, g0 * q0 + g1 * q1)

    staged(spans_of(dist.shape[0]), root, sums)
    return jnp.concatenate([jnp.sum(b, axis=0, keepdims=True) for b in back], axis=1)


def pipeline(total, begin, finish, table, size, ring, parts):
    ring = ring[: min(len(ring), size)]
    ahead = min(2, len(ring) - 1)
    group = min(2, size)

    def body(i, carry):
        indices = []
        for k in range(size):
            begin(i * size + k + ahead, ring[(k + ahead) % len(ring)])
            indices.append(finish(i * size + k, ring[k % len(ring)], parts[k % len(parts)]))
            if len(indices) == group:
                done = [parts[(k - n) % len(parts)] for n in reversed(range(group))]
                add_columns(table, done, indices)
                indices = []
        return carry

    for k in range(ahead):
        begin(k, ring[k])
    lax.fori_loop(0, (total + size - 1) // size, body, 0)


def body_size(total, most):
    return next(size for size in (32, 16, 8, 4, 2, 1) if size <= most and total % size == 0)


def assemble(sub, S, L, q, pieces):
    def place(s):
        for shift in range(S):
            owner = (s - shift) % S
            q[:, owner * L : (owner + 1) * L] = pieces[shift][: q.shape[0], :]

    for s in range(S):
        pl.when(sub == s)(functools.partial(place, s))


def pack_kernel(sizes, charges, mask, geo, targets, sources, live, masked, geo_out, *packs):
    C, S, L, slots = sizes
    me, sub = lax.axis_index("clu"), lax.axis_index("sub")
    masked[...] = charges[...] * mask[...].astype(F32)
    for t in range(geo_out.shape[0]):
        geo_out[t, :, :] = geo[:, :, t * LANES : (t + 1) * LANES].reshape(geo_out.shape[1:])
    lane = lax.broadcasted_iota(jnp.int32, (8, L), 1)
    for shift in range(1, C):
        dest = lax.rem(me + shift, C)
        codes = jnp.full((8, L), -1.0, F32)
        for j in range(slots):
            code = jnp.where(live[dest, j] > 0, sources[dest, j], -1)
            codes = jnp.where(lane == j, code.astype(F32), codes)
        packs[shift - 1][5 * slots :, :] = codes

    def fill(s):
        for shift in range(1, C):
            dest = lax.rem(me + shift, C)
            pack = packs[shift - 1]
            for j in range(slots):
                t = targets[dest, j]
                g = geo[t, :, s * L : (s + 1) * L]
                for k in range(4):
                    pack[k * slots + j : k * slots + j + 1, :] = g[k : k + 1]
                pack[4 * slots + j : 4 * slots + j + 1, :] = masked[pl.ds(t, 1), :]

    for s in range(S):
        pl.when(sub == s)(functools.partial(fill, s))


def remote_kernel(sizes, fb, scale, up, before, *rest):
    del before
    C, S, L, slots, clusters, panels = sizes
    pieces = rest[:S]
    packs = rest[S : S + C - 1]
    acc_out = rest[S + C - 1]
    sends = rest[S + C : S + C + C - 1]
    q, tq, acc, fwdt, fa, order, codes, sems, *work = rest[S + C + C - 1 :]
    n = (C - 1) * slots
    copies = [
        pltpu.make_async_copy(packs[k].at[pl.ds(5 * slots, 8), :], codes.at[k], sems.at[k])
        for k in range(C - 1)
    ]
    for copy in copies:
        copy.start()
    assemble(lax.axis_index("sub"), S, L, q, pieces)
    acc[...] = jnp.zeros_like(acc)
    fwdt[...] = jnp.zeros_like(fwdt)
    for copy in copies:
        copy.wait()
    found = jnp.int32(0)
    for shift in range(C - 1):
        for j in range(slots):
            code = codes[shift, 0, j].astype(jnp.int32)
            order[n + 1 + shift * slots + j] = jnp.maximum(code, 0)
            order[found] = shift * slots + j
            found = found + (code >= 0).astype(jnp.int32)
    inv, centre = split_frame(scale)
    for shift in range(C - 1):
        for first in range(0, slots, 8):
            points = [packs[shift][k * slots + first : k * slots + first + 8, :] for k in range(5)]
            left, _, _ = split_features(points, centre, inv)
            store_features(fa, left, shift * slots + first)
            at = shift * slots + first
            tq[at : at + 8, :] = points[4]

    def begin(i, dist):
        slot = order[jnp.minimum(i, jnp.maximum(found - 1, 0))]
        distances(load_features(fa, slot), load_features(fb, order[n + 1 + slot]), dist)

    def finish(i, dist, part):
        ok = i < found
        slot = order[jnp.minimum(i, jnp.maximum(found - 1, 0))]
        source = order[n + 1 + slot]
        back = tile_sums(
            dist, q[pl.ds(source, 1), :], tq[pl.ds(slot, 1), :], part
        )
        acc[pl.ds(source, 1), :] += jnp.where(ok, back, 0.0)
        return jnp.where(ok, slot, -1)

    pipeline(found, begin, finish, fwdt, 8, work[:4], work[4:])
    acc_out[...] = acc[...] * inv
    fwd = (fwdt[...] * inv).T
    rank = up.shape[1]
    for shift in range(C - 1):
        sends[shift][:slots, :] = fwd[shift * slots : (shift + 1) * slots, :]
        sends[shift][slots:, :] = jnp.zeros((up.shape[0], L), F32)
        sends[shift][slots:, :rank] = up[...]


def prepare_kernel(
    geo, masked, basis_far, transfer_far, parent_far,
    fa, fb, diag, scale, up, basis, transfer, parent, sems
):
    copies = [
        pltpu.make_async_copy(src, dst, sems.at[k])
        for k, (src, dst) in enumerate(
            [(basis_far, basis), (transfer_far, transfer), (parent_far, parent)]
        )
    ]
    for copy in copies:
        copy.start()
    inv, centre = frame(geo)
    scale[...] = jnp.zeros_like(scale)
    scale[0:1, :] = jnp.broadcast_to(inv, (1, LANES))
    for k in range(3):
        scale[k + 1 : k + 2, :] = jnp.broadcast_to(centre[k : k + 1, :], (1, LANES))
    inv, centre = split_frame(scale)
    for first in range(0, diag.shape[0], 8):
        points = [
            jnp.concatenate(
                [geo[t, pl.ds(first * 4 + k, 8, stride=4), :] for t in range(geo.shape[0])], axis=1
            )
            for k in range(4)
        ]
        left, right, rad = split_features(points, centre, inv)
        store_features(fa, left, first)
        store_features(fb, right, first)
        diag[first : first + 8, :] = lax.rsqrt(2.0 * (rad * rad))
    for copy in copies:
        copy.wait()
    up[...] = up_sums(basis, masked, transfer, parent, up.shape[0])


def local_kernel(sizes, pair_rows, pairs, fa, fb, scale, acc_in, *rest):
    S, L, R, clusters, panels = sizes
    pieces = rest[:S]
    acc_out = rest[S]
    q, acc, pair_sums, *work = rest[S + 1 :]
    ring, sums = work[:8], work[8:]
    sub = lax.axis_index("sub")
    assemble(sub, S, L, q, pieces)
    acc[...] = jnp.zeros_like(acc)
    pair_sums[...] = jnp.zeros_like(pair_sums)

    count = pairs.shape[1] // S
    start = sub * count

    def begin(i, dist):
        p = start + jnp.minimum(i, count - 1)
        distances(load_features(fa, pairs[0, p]), load_features(fb, pairs[1, p]), dist)

    def finish(i, dist, part):
        ia, ib = pairs[0, start + i], pairs[1, start + i]
        acc[pl.ds(ib, 1), :] += tile_sums(
            dist, q[pl.ds(ib, 1), :], q[pl.ds(ia, 1), :], part
        )
        return start + i

    pipeline(count, begin, finish, pair_sums, body_size(count, 32), ring, sums)
    width = pair_rows.shape[1]
    total = acc[...] + select_rows(pair_rows[0:1, :], pair_sums[...].T[:width, :], clusters)
    acc_out[...] = acc_in[...] + total * scale[0:1, 0:1]


def self_kernel(sizes, early, fa, fb, diags, scale, *rest):
    S, L, R, clusters, panels = sizes
    if not early:
        part, before, *rest = rest
    pieces = rest[:S]
    out, q, fs, spots, self_sums, *work = rest[S:]
    ring, sums = work[:8], work[8:]
    sub, rep = lax.axis_index("sub"), lax.axis_index("rep")
    self_sums[...] = jnp.zeros_like(self_sums)
    blocks = L == LANES
    if blocks:
        order = [lax.rem(sub + S - shift, S) for shift in range(S)]
        for shift in range(S):
            q[:, shift * L : (shift + 1) * L] = pieces[shift][...]
    else:
        order = None
        assemble(sub, S, L, q, pieces)

    def place(s):
        if not blocks:
            t, at = (s * L) // LANES, (s * L) % LANES
            fs[0, :, :] = fa[t, :, at : at + L]
        spots[...] = diags[:, s * L : (s + 1) * L]

    for s in range(S):
        pl.when(sub == s)(functools.partial(place, s))
    base = clusters // R
    unit = base // 4
    half = unit // 2
    first = rep * base
    share = base
    ahead = unit
    if R > 1:
        first = first - jnp.where(rep > 0, unit + half, 0)
        more = jnp.where(rep == R - 1, 1, 0) - jnp.where(rep == 0, 1, 0)
        share = share + more * (unit + half)
        ahead = unit + more * half
    if early:
        share = ahead
    else:
        first, share = first + ahead, share - ahead

    def begin(i, dist):
        c = first + jnp.minimum(i, share - 1)
        own = load_features(fa, c, order[:1]) if blocks else load_features(fs, c)
        distances(own, load_features(fb, c, order), dist)

    def finish(i, dist, parts):
        c = first + i
        qrow = q[pl.ds(c, 1), :]
        diag = upright(spots[pl.ds(c, 1), :])

        def root(span, _):
            shape = (span.stop - span.start, LANES)
            row = lax.broadcasted_iota(jnp.int32, shape, 0) + span.start
            row = row if blocks else row + sub * L
            col = lax.broadcasted_iota(jnp.int32, shape, 1)
            values = [inverse_root(dist[span, t : t + LANES]) for t in range(0, panels, LANES)]
            for t in range(1 if blocks else len(values)):
                values[t] = jnp.where(row == col + t * LANES, diag[span, :], values[t])
            return values

        def partial(span, held):
            keep(parts, span, sum(g * qrow[:, t * LANES : (t + 1) * LANES] for t, g in enumerate(held)))

        staged(spans_of(L), root, partial)
        return c

    pipeline(share, begin, finish, self_sums, body_size(half if early else unit, 16), ring, sums)
    total = self_sums[...].T * scale[0:1, 0:1]
    if early:
        out[...] = total
    else:
        out[...] = part[...]
        out[:clusters, :] = (part[:clusters, :] + before[...]) + total


def merge_kernel(sizes, far_list, targets, near, coupling, transfer, parent, up, *rest):
    C, S, L, slots, clusters = sizes
    sums = rest[: C - 1]
    parts = rest[C - 1 : C - 1 + S]
    parents = rest[-1]
    me, sub = lax.axis_index("clu"), lax.axis_index("sub")
    index = [targets[pl.ds(lax.rem(me + shift, C), 1), :] for shift in range(1, C)]
    got = select_rows(
        jnp.concatenate(index, axis=1), jnp.concatenate([v[:slots, :] for v in sums], axis=0), clusters
    )

    par_dev, far_n, rank = coupling.shape[0], coupling.shape[1], coupling.shape[2]
    parents[pl.ds(pl.multiple_of(me * par_dev, 8), par_dev), :] = up[...]
    for shift in range(1, C):
        owner = lax.rem(me + shift, C)
        parents[pl.ds(pl.multiple_of(owner * par_dev, 8), par_dev), :] = sums[shift - 1][slots:, :rank]
    lane = lax.broadcasted_iota(jnp.int32, (rank, LANES), 1)
    field = jnp.zeros((rank, LANES), F32)
    for p in range(par_dev):
        part = jnp.zeros((rank, rank), F32)
        for k in range(far_n):
            part = part + coupling[p, k] * parents[pl.ds(far_list[k, p], 1), :]
        field = jnp.where(lane == p, jnp.sum(part, axis=1, keepdims=True), field)
    which = lax.broadcasted_iota(jnp.int32, (LANES, clusters), 0)
    onehot = (parent[...] == which).astype(F32)
    down = jnp.dot(field, onehot, precision=HIGHEST, preferred_element_type=F32)
    fields = jnp.concatenate(
        [jnp.sum(transfer[r] * down, axis=0, keepdims=True) for r in range(rank)], axis=0
    )

    def give(s):
        for shift in range(S):
            other = (s + shift) % S
            part = near[:, other * L : (other + 1) * L]
            parts[shift][:clusters, :] = part + got if shift == 0 else part
            for t in range(clusters // L):
                at = clusters + t * rank
                parts[shift][at : at + rank, :] = fields[:, t * L : (t + 1) * L]

    for s in range(S):
        pl.when(sub == s)(functools.partial(give, s))


def up_sums(basis, masked, transfer, parent, count):
    clusters = basis.shape[0]
    rank = basis.shape[1]
    lane = lax.broadcasted_iota(jnp.int32, (rank, clusters), 1)
    leaf = jnp.zeros((rank, clusters), F32)
    for c in range(clusters):
        part = jnp.sum(basis[c] * masked[c : c + 1, :], axis=1, keepdims=True)
        leaf = jnp.where(lane == c, part, leaf)
    lifted = jnp.zeros((rank, clusters), F32)
    for r in range(rank):
        lifted = lifted + transfer[r] * leaf[r : r + 1, :]
    which = lax.broadcasted_iota(jnp.int32, (count, clusters), 0)
    onehot = (parent[...] == which).astype(F32)
    return lax.dot_general(
        onehot, lifted, (((1,), (1,)), ((), ())), precision=HIGHEST, preferred_element_type=F32
    )


def far_kernel(basis, near, out):
    clusters, rank = basis.shape[0], basis.shape[1]
    L = out.shape[1]
    fields = [near[clusters + t * rank : clusters + (t + 1) * rank, :] for t in range(clusters // L)]
    fields = jnp.concatenate(fields, axis=1) if len(fields) > 1 else fields[0]
    for c in range(clusters):
        far = jnp.sum(basis[c] * fields[:, c : c + 1], axis=0, keepdims=True)
        out[c : c + 1, :] = far + near[c : c + 1, :]


def send(value, moves):
    names = tuple(name for name, _ in moves)
    steps = [step for _, step in moves]
    sizes = [lax.axis_size(name) for name in names]
    perm = []

    def flat(coords):
        index = 0
        for size, c in zip(sizes, coords):
            index = index * size + c
        return index

    total = 1
    for size in sizes:
        total *= size
    for index in range(total):
        coords, left = [], index
        for size in reversed(sizes):
            coords.append(left % size)
            left //= size
        coords.reverse()
        perm.append((index, flat([(c + s) % n for c, s, n in zip(coords, steps, sizes)])))
    return lax.ppermute(value, names if len(names) > 1 else names[0], perm)


def on_device(
    charges,
    panel_mask,
    geometry,
    remote_source,
    remote_target,
    remote_live,
    local_pairs,
    basis,
    transfer,
    parent_of,
    far_list,
    coupling,
):
    clusters, L = charges.shape
    panels = geometry.shape[2]
    C, S, R = lax.axis_size("clu"), lax.axis_size("sub"), lax.axis_size("rep")
    slots = remote_source.shape[2]
    par_dev, rank = far_list.shape[0], transfer.shape[1]
    n = (C - 1) * slots
    shape = jax.ShapeDtypeStruct
    targets = remote_target[0]
    basis_t = jnp.transpose(basis, (0, 2, 1))
    transfer_t = jnp.transpose(transfer, (1, 2, 0))
    parent = parent_of[None, :]

    made = pl.pallas_call(
        functools.partial(pack_kernel, (C, S, L, slots)),
        out_shape=[pltpu.VMEM((clusters, L), F32), pltpu.VMEM((panels // LANES, clusters * 4, LANES), F32)]
        + [pltpu.VMEM((5 * slots + 8, L), F32)] * (C - 1),
        in_specs=[vmem()] * 3 + [smem()] * 3,
        out_specs=[vmem()] * (C + 1),
        compiler_params=limit(60),
        cost_estimate=about(2),
        name="packs",
    )(charges, panel_mask, geometry, targets, remote_source[0], remote_live[0])
    masked, geo, packs = made[0], made[1], made[2:]
    pieces = [masked] + [send(masked, (("sub", d),)) for d in range(1, S)]
    packs = [send(packs[d - 1], (("clu", d),)) for d in range(1, C)]

    *features, up = pl.pallas_call(
        prepare_kernel,
        out_shape=[pltpu.VMEM((panels // LANES, clusters * ROWS, LANES), F32)] * 2
        + [
            pltpu.VMEM((clusters, panels), F32),
            pltpu.VMEM((8, LANES), F32),
            pltpu.VMEM((par_dev, rank), F32),
        ],
        in_specs=[vmem()] * 2 + [pl.BlockSpec(memory_space=pltpu.HBM)] * 3,
        out_specs=[vmem()] * 5,
        scratch_shapes=[
            pltpu.VMEM(basis_t.shape, F32),
            pltpu.VMEM(transfer_t.shape, F32),
            pltpu.VMEM(parent.shape, jnp.int32),
            pltpu.SemaphoreType.DMA((3,)),
        ],
        compiler_params=limit(24),
        cost_estimate=about(4),
        name="prepare",
    )(*near_by(geo, masked), *far_off(basis_t, transfer_t, parent))
    *tables, diags, scale = features

    def own_tiles(early, height, *added):
        return pl.pallas_call(
            functools.partial(self_kernel, (S, L, R, clusters, panels), early),
            out_shape=pltpu.VMEM((height, L), F32),
            in_specs=[vmem()] * (4 + len(added) + S),
            out_specs=vmem(),
            scratch_shapes=[
                pltpu.VMEM((clusters, panels), F32),
                pltpu.VMEM((1, 8 if L == LANES else clusters * ROWS, L), F32),
                pltpu.VMEM((clusters, L), F32),
                pltpu.VMEM((L, clusters), F32),
            ]
            + [pltpu.VMEM((L, panels), F32)] * 8
            + [pltpu.VMEM((L, 2 * LANES), BF16)] * 4,
            compiler_params=limit(24),
            cost_estimate=about(2 if early else 4),
            name="near_self_early" if early else "near_self",
        )(*near_by(*tables, diags, scale, *added, *pieces))

    before = own_tiles(True, clusters)

    made = pl.pallas_call(
        functools.partial(remote_kernel, (C, S, L, slots, clusters, panels)),
        out_shape=[pltpu.VMEM((clusters, panels), F32)]
        + [pltpu.VMEM((slots + par_dev, L), F32)] * (C - 1),
        in_specs=[vmem()] * (4 + S + C - 1),
        out_specs=[vmem()] * C,
        scratch_shapes=[
            pltpu.VMEM((clusters, panels), F32),
            pltpu.VMEM((n, L), F32),
            pltpu.VMEM((clusters, panels), F32),
            pltpu.VMEM((L, whole(n)), F32),
            pltpu.VMEM((1, n * ROWS, L), F32),
            pltpu.SMEM((2 * n + 1,), jnp.int32),
            pltpu.SMEM((C - 1, 8, L), F32),
            pltpu.SemaphoreType.DMA((C - 1,)),
        ]
        + [pltpu.VMEM((L, panels), F32)] * 4
        + [pltpu.VMEM((L, 2 * LANES), BF16)] * 4,
        compiler_params=limit(24),
        cost_estimate=about(6),
        name="near_remote",
    )(*near_by(tables[1], scale, up, before, *pieces, *packs))
    acc, sums = made[0], [send(made[d], (("clu", C - d),)) for d in range(1, C)]

    wide = whole(local_pairs.shape[1])
    near = pl.pallas_call(
        functools.partial(local_kernel, (S, L, R, clusters, panels)),
        out_shape=pltpu.VMEM((clusters, panels), F32),
        in_specs=[vmem(), smem()] + [vmem()] * (4 + S),
        out_specs=vmem(),
        scratch_shapes=[
            pltpu.VMEM((clusters, panels), F32),
            pltpu.VMEM((clusters, panels), F32),
            pltpu.VMEM((panels, wide), F32),
        ]
        + [pltpu.VMEM((panels, panels), F32)] * 8
        + [pltpu.VMEM((panels, 2 * LANES), BF16)] * 4,
        compiler_params=limit(24),
        cost_estimate=about(9),
        name="near_local",
    )(*near_by(local_pairs[0].T), local_pairs[0].T, *near_by(*tables, scale, acc, *pieces))

    height = clusters + clusters // L * rank
    parts = pl.pallas_call(
        functools.partial(merge_kernel, (C, S, L, slots, clusters)),
        out_shape=[pltpu.VMEM((height, L), F32)] * S,
        in_specs=[smem()] + [vmem()] * (6 + C - 1),
        out_specs=[vmem()] * S,
        scratch_shapes=[pltpu.VMEM((C * par_dev, rank), F32)],
        compiler_params=limit(16),
        cost_estimate=about(1),
        name="merge",
    )(far_list.T, *near_by(targets, near, coupling, transfer_t, parent, up, *sums))
    others = [send(parts[d], (("sub", d),)) for d in range(1, S)]

    near = own_tiles(False, height, parts[0], before)
    for other in others:
        near = near + other
    others = [send(near, (("rep", e),)) for e in range(1, R)]

    total = pl.pallas_call(
        far_kernel,
        out_shape=pltpu.VMEM((clusters, L), F32),
        in_specs=[vmem()] * 2,
        out_specs=vmem(),
        compiler_params=limit(16),
        cost_estimate=about(1),
        name="far_down",
    )(*near_by(basis_t, near))
    for other in others:
        total = total + other[:clusters]
    return total * panel_mask.astype(F32)


def solution(mesh):
    placed = (
        P(("grp", "clu"), "sub"),
        P(("grp", "clu"), "sub"),
        P(("grp", "clu"), None, None),
        P(("grp", "clu"), None, "rep"),
        P(("grp", "clu"), None, "rep"),
        P(("grp", "clu"), None, "rep"),
        P(("grp", "clu"), "rep", None),
        P(("grp", "clu"), "sub", None),
        P(("grp", "clu"), None, None),
        P(("grp", "clu")),
        P(("grp", "clu"), None),
        P(("grp", "clu"), None, None, None),
    )
    return jax.shard_map(
        on_device, mesh=mesh, in_specs=placed, out_specs=P(("grp", "clu"), "sub"), check_vma=False
    )
```

```python
import functools

import jax
import jax.numpy as jnp
from jax import lax
from jax.experimental import pallas as pl
from jax.experimental.pallas import tpu as pltpu
from jax.sharding import PartitionSpec as P

F32 = jnp.float32
BF16 = jnp.bfloat16
HIGHEST = lax.Precision.HIGHEST
ROWS = 24
LANES = 128


def limit(mib):
    return pltpu.CompilerParams(vmem_limit_bytes=mib * 1024 * 1024)


def about(us):
    return pl.CostEstimate(flops=0, bytes_accessed=int(us * 3.5e6), transcendentals=0)


def vmem():
    return pl.BlockSpec(memory_space=pltpu.VMEM)


def near_by(*arrays):
    return [pltpu.with_memory_space_constraint(x, pltpu.VMEM) for x in arrays]


def far_off(*arrays):
    return [pltpu.with_memory_space_constraint(x, pltpu.HBM) for x in arrays]


def smem():
    return pl.BlockSpec(memory_space=pltpu.SMEM)


def whole(size):
    return -(-size // LANES) * LANES


def cut(v):
    return v.astype(BF16).astype(F32)


def powers(sign):
    lane = lax.broadcasted_iota(jnp.int32, (8, LANES), 1)
    out = jnp.full((8, LANES), 2.0 ** (-64 * sign), F32)
    for bit in range(7):
        out = out * jnp.where((lane >> bit) & 1 == 1, F32(2.0 ** (sign * 2**bit)), F32(1.0))
    return out


def frame(geo):
    low, high = [None] * 8, [None] * 8
    blocks = [(t, c) for c in range(0, geo.shape[1], 8) for t in range(geo.shape[0])]
    for i, (t, c) in enumerate(blocks):
        g, k = geo[t, c : c + 8, :], i % 8
        low[k] = g if low[k] is None else jnp.minimum(low[k], g)
        high[k] = g if high[k] is None else jnp.maximum(high[k], g)
    low = jnp.min(functools.reduce(jnp.minimum, low), axis=1, keepdims=True)
    high = jnp.max(functools.reduce(jnp.maximum, high), axis=1, keepdims=True)
    low, high = jnp.minimum(low[:4], low[4:]), jnp.maximum(high[:4], high[4:])
    row = lax.broadcasted_iota(jnp.int32, low.shape, 0)
    radius = jnp.maximum(jnp.abs(low), jnp.abs(high))
    width = jnp.max(jnp.where(row == 3, radius, 0.5 * (high - low)), axis=0, keepdims=True)

    def over(table, least):
        return least(least(table, axis=1, keepdims=True), axis=0, keepdims=True)

    up, down = powers(1), powers(-1)
    size = over(jnp.where(up >= width, up, F32(2.0**63)), jnp.min)
    inv = over(jnp.where(up >= width, down, F32(2.0**-63)), jnp.max)
    magic = size * F32(1.5 * 2.0**20)
    return inv, (0.5 * (low + high) + magic) - magic


def split_frame(scale):
    return scale[0:1, 0:1], [scale[k : k + 1, 0:1] for k in range(1, 4)]


def split_features(points, centre, inv):
    magic = F32(1.5 * 2.0**16)
    grid, rest = [], []
    for k in range(3):
        u = (points[k] - centre[k]) * inv
        h = cut((u + magic) - magic)
        grid.append(h)
        rest.append(u - h)
    rad = points[3] * inv
    norm = grid[0] * grid[0] + grid[1] * grid[1] + grid[2] * grid[2]
    norm1 = cut(norm)
    norm2 = cut(norm - norm1)
    cross = grid[0] * rest[0] + grid[1] * rest[1] + grid[2] * rest[2]
    extra = 2.0 * cross + (rest[0] * rest[0] + rest[1] * rest[1] + rest[2] * rest[2]) + rad * rad
    extra = extra + ((norm - norm1) - norm2)
    extra1 = cut(extra)
    extra2 = cut(extra - extra1)
    extra3 = (extra - extra1) - extra2
    rest1 = [cut(v) for v in rest]
    rest2 = [v - w for v, w in zip(rest, rest1)]
    neg = lambda vs: [-2.0 * v for v in vs]
    one, zero = jnp.ones_like(rad), jnp.zeros_like(rad)
    left = grid + [norm1, norm2, one, one, zero]
    left += rest1 + [extra1, extra2, zero, zero, zero]
    left += rest2 + [extra3, zero, zero, zero, zero]
    right = neg(grid) + [one, one, norm1, norm2, zero]
    right += neg(rest1) + [zero, zero, extra1, extra2, zero]
    right += neg(rest2) + [zero, zero, extra3, zero, zero]
    return left, right, rad


def products(left, right):
    a, b, c = [left[k : k + 8, :] for k in (0, 8, 16)]
    x, y, z = [right[k : k + 8, :] for k in (0, 8, 16)]
    pairs = [(a, x), (b, x), (a, y), (c, x), (a, z), (b, y), (b, z), (c, y)]
    return [jnp.concatenate(v, axis=0).astype(BF16) for v in zip(*pairs)]


def store_features(ref, rows, first):
    width = rows[0].shape[1]
    for k, row in enumerate(rows):
        for t in range(ref.shape[0]):
            at = pl.ds(first * ROWS + k, 8, stride=ROWS)
            ref[t, at, :] = row[:, t * LANES : min(width, (t + 1) * LANES)]


def load_features(ref, index, order=None):
    start = pl.multiple_of(index * ROWS, 8)
    order = range(ref.shape[0]) if order is None else order
    blocks = [ref[t, pl.ds(start, ROWS), :] for t in order]
    return jnp.concatenate(blocks, axis=1) if len(blocks) > 1 else blocks[0]


def contract(left, right):
    return jnp.dot(left, right, preferred_element_type=F32)


def select_rows(index, value, count):
    row = lax.broadcasted_iota(jnp.int32, (count, index.shape[1]), 0)
    left = jnp.where(row == index, 1.0, 0.0).astype(BF16)
    high = value.astype(BF16)
    rest = value - high.astype(F32)
    mid = rest.astype(BF16)
    low = (rest - mid.astype(F32)).astype(BF16)
    return jnp.dot(
        jnp.concatenate([left] * 3, axis=1),
        jnp.concatenate([high, mid, low], axis=0),
        preferred_element_type=F32,
    )


def upright(row):
    return jnp.broadcast_to(row, (8, row.shape[1])).T[:, :1]


def keep(parts, rows, value):
    high = value.astype(BF16)
    parts[rows, :LANES] = high
    parts[rows, LANES:] = (value - high.astype(F32)).astype(BF16)


def add_columns(table, parts, indices):
    shape = (2 * LANES, table.shape[1])
    lane = lax.broadcasted_iota(jnp.int32, shape, 1)
    picks = [jnp.where(lane == index, 1.0, 0.0).astype(BF16) for index in indices]
    table[...] += jnp.dot(
        jnp.concatenate([p[...] for p in parts], axis=1),
        jnp.concatenate(picks, axis=0),
        preferred_element_type=F32,
    )


def inverse_root(d):
    return lax.rsqrt(d)


def fold(v):
    return jnp.sum(v.reshape(v.shape[0] // 8, 8, v.shape[1]), axis=0)


def distances(left, right, out):
    left, right = products(left, right)
    out[...] = contract(left.T, right)


def staged(spans, *stages):
    held = {}
    for t in range(len(spans) + len(stages) - 1):
        for depth in reversed(range(len(stages))):
            k = t - depth
            if 0 <= k < len(spans):
                held[k] = stages[depth](spans[k], held.get(k))
                if depth == len(stages) - 1:
                    del held[k]


def spans_of(height, step=32):
    step = min(step, height)
    return [slice(r, r + step) for r in range(0, height, step)]


def tile_sums(dist, qrow, qleft, parts):
    q0, q1 = qrow[:, :LANES], qrow[:, LANES:]
    qcol = upright(qleft)
    back = [jnp.zeros((8, LANES), F32), jnp.zeros((8, LANES), F32)]

    def root(rows, _):
        return (
            inverse_root(dist[rows, :LANES]),
            inverse_root(dist[rows, LANES:]),
        )

    def sums(rows, held):
        g0, g1 = held
        back[0] = back[0] + fold(g0 * qcol[rows, :])
        back[1] = back[1] + fold(g1 * qcol[rows, :])
        keep(parts, rows, g0 * q0 + g1 * q1)

    staged(spans_of(dist.shape[0]), root, sums)
    return jnp.concatenate([jnp.sum(b, axis=0, keepdims=True) for b in back], axis=1)


def pipeline(total, begin, finish, table, size, ring, parts):
    ring = ring[: min(len(ring), size)]
    ahead = min(2, len(ring) - 1)
    group = min(2, size)

    def body(i, carry):
        indices = []
        for k in range(size):
            begin(i * size + k + ahead, ring[(k + ahead) % len(ring)])
            indices.append(finish(i * size + k, ring[k % len(ring)], parts[k % len(parts)]))
            if len(indices) == group:
                done = [parts[(k - n) % len(parts)] for n in reversed(range(group))]
                add_columns(table, done, indices)
                indices = []
        return carry

    for k in range(ahead):
        begin(k, ring[k])
    lax.fori_loop(0, (total + size - 1) // size, body, 0)


def body_size(total, most):
    return next(size for size in (32, 16, 8, 4, 2, 1) if size <= most and total % size == 0)


def assemble(sub, S, L, q, pieces):
    def place(s):
        for shift in range(S):
            owner = (s - shift) % S
            q[:, owner * L : (owner + 1) * L] = pieces[shift][: q.shape[0], :]

    for s in range(S):
        pl.when(sub == s)(functools.partial(place, s))


def pack_kernel(sizes, charges, mask, geo, targets, sources, live, masked, geo_out, *packs):
    C, S, L, slots = sizes
    me, sub = lax.axis_index("clu"), lax.axis_index("sub")
    masked[...] = charges[...] * mask[...].astype(F32)
    for t in range(geo_out.shape[0]):
        geo_out[t, :, :] = geo[:, :, t * LANES : (t + 1) * LANES].reshape(geo_out.shape[1:])
    lane = lax.broadcasted_iota(jnp.int32, (8, L), 1)
    for shift in range(1, C):
        dest = lax.rem(me + shift, C)
        codes = jnp.full((8, L), -1.0, F32)
        for j in range(slots):
            code = jnp.where(live[dest, j] > 0, sources[dest, j], -1)
            codes = jnp.where(lane == j, code.astype(F32), codes)
        packs[shift - 1][5 * slots :, :] = codes

    def fill(s):
        for shift in range(1, C):
            dest = lax.rem(me + shift, C)
            pack = packs[shift - 1]
            for j in range(slots):
                t = targets[dest, j]
                g = geo[t, :, s * L : (s + 1) * L]
                for k in range(4):
                    pack[k * slots + j : k * slots + j + 1, :] = g[k : k + 1]
                pack[4 * slots + j : 4 * slots + j + 1, :] = masked[pl.ds(t, 1), :]

    for s in range(S):
        pl.when(sub == s)(functools.partial(fill, s))


def remote_kernel(sizes, fb, scale, up, before, *rest):
    del before
    C, S, L, slots, clusters, panels = sizes
    pieces = rest[:S]
    packs = rest[S : S + C - 1]
    acc_out = rest[S + C - 1]
    sends = rest[S + C : S + C + C - 1]
    q, tq, acc, fwdt, fa, order, codes, sems, *work = rest[S + C + C - 1 :]
    n = (C - 1) * slots
    copies = [
        pltpu.make_async_copy(packs[k].at[pl.ds(5 * slots, 8), :], codes.at[k], sems.at[k])
        for k in range(C - 1)
    ]
    for copy in copies:
        copy.start()
    assemble(lax.axis_index("sub"), S, L, q, pieces)
    acc[...] = jnp.zeros_like(acc)
    fwdt[...] = jnp.zeros_like(fwdt)
    for copy in copies:
        copy.wait()
    found = jnp.int32(0)
    for shift in range(C - 1):
        for j in range(slots):
            code = codes[shift, 0, j].astype(jnp.int32)
            order[n + 1 + shift * slots + j] = jnp.maximum(code, 0)
            order[found] = shift * slots + j
            found = found + (code >= 0).astype(jnp.int32)
    inv, centre = split_frame(scale)
    for shift in range(C - 1):
        for first in range(0, slots, 8):
            points = [packs[shift][k * slots + first : k * slots + first + 8, :] for k in range(5)]
            left, _, _ = split_features(points, centre, inv)
            store_features(fa, left, shift * slots + first)
            at = shift * slots + first
            tq[at : at + 8, :] = points[4]

    def begin(i, dist):
        slot = order[jnp.minimum(i, jnp.maximum(found - 1, 0))]
        distances(load_features(fa, slot), load_features(fb, order[n + 1 + slot]), dist)

    def finish(i, dist, part):
        ok = i < found
        slot = order[jnp.minimum(i, jnp.maximum(found - 1, 0))]
        source = order[n + 1 + slot]
        back = tile_sums(
            dist, q[pl.ds(source, 1), :], tq[pl.ds(slot, 1), :], part
        )
        acc[pl.ds(source, 1), :] += jnp.where(ok, back, 0.0)
        return jnp.where(ok, slot, -1)

    pipeline(found, begin, finish, fwdt, 16, work[:4], work[4:])
    acc_out[...] = acc[...] * inv
    fwd = (fwdt[...] * inv).T
    rank = up.shape[1]
    for shift in range(C - 1):
        sends[shift][:slots, :] = fwd[shift * slots : (shift + 1) * slots, :]
        sends[shift][slots:, :] = jnp.zeros((up.shape[0], L), F32)
        sends[shift][slots:, :rank] = up[...]


def prepare_kernel(
    geo, masked, basis_far, transfer_far, parent_far,
    fa, fb, diag, scale, up, basis, transfer, parent, sems
):
    copies = [
        pltpu.make_async_copy(src, dst, sems.at[k])
        for k, (src, dst) in enumerate(
            [(basis_far, basis), (transfer_far, transfer), (parent_far, parent)]
        )
    ]
    for copy in copies:
        copy.start()
    inv, centre = frame(geo)
    scale[...] = jnp.zeros_like(scale)
    scale[0:1, :] = jnp.broadcast_to(inv, (1, LANES))
    for k in range(3):
        scale[k + 1 : k + 2, :] = jnp.broadcast_to(centre[k : k + 1, :], (1, LANES))
    inv, centre = split_frame(scale)
    for first in range(0, diag.shape[0], 8):
        points = [
            jnp.concatenate(
                [geo[t, pl.ds(first * 4 + k, 8, stride=4), :] for t in range(geo.shape[0])], axis=1
            )
            for k in range(4)
        ]
        left, right, rad = split_features(points, centre, inv)
        store_features(fa, left, first)
        store_features(fb, right, first)
        diag[first : first + 8, :] = lax.rsqrt(2.0 * (rad * rad))
    for copy in copies:
        copy.wait()
    up[...] = up_sums(basis, masked, transfer, parent, up.shape[0])


def local_kernel(sizes, pair_rows, pairs, fa, fb, scale, acc_in, *rest):
    S, L, R, clusters, panels = sizes
    pieces = rest[:S]
    acc_out = rest[S]
    q, acc, pair_sums, *work = rest[S + 1 :]
    ring, sums = work[:8], work[8:]
    sub = lax.axis_index("sub")
    assemble(sub, S, L, q, pieces)
    acc[...] = jnp.zeros_like(acc)
    pair_sums[...] = jnp.zeros_like(pair_sums)

    count = pairs.shape[1] // S
    start = sub * count

    def begin(i, dist):
        p = start + jnp.minimum(i, count - 1)
        distances(load_features(fa, pairs[0, p]), load_features(fb, pairs[1, p]), dist)

    def finish(i, dist, part):
        ia, ib = pairs[0, start + i], pairs[1, start + i]
        acc[pl.ds(ib, 1), :] += tile_sums(
            dist, q[pl.ds(ib, 1), :], q[pl.ds(ia, 1), :], part
        )
        return start + i

    pipeline(count, begin, finish, pair_sums, body_size(count, 32), ring, sums)
    width = pair_rows.shape[1]
    total = acc[...] + select_rows(pair_rows[0:1, :], pair_sums[...].T[:width, :], clusters)
    acc_out[...] = acc_in[...] + total * scale[0:1, 0:1]


def self_kernel(sizes, early, fa, fb, diags, scale, *rest):
    S, L, R, clusters, panels = sizes
    if not early:
        part, before, *rest = rest
    pieces = rest[:S]
    out, q, fs, spots, self_sums, *work = rest[S:]
    ring, sums = work[:8], work[8:]
    sub, rep = lax.axis_index("sub"), lax.axis_index("rep")
    self_sums[...] = jnp.zeros_like(self_sums)
    blocks = L == LANES
    if blocks:
        order = [lax.rem(sub + S - shift, S) for shift in range(S)]
        for shift in range(S):
            q[:, shift * L : (shift + 1) * L] = pieces[shift][...]
    else:
        order = None
        assemble(sub, S, L, q, pieces)

    def place(s):
        if not blocks:
            t, at = (s * L) // LANES, (s * L) % LANES
            fs[0, :, :] = fa[t, :, at : at + L]
        spots[...] = diags[:, s * L : (s + 1) * L]

    for s in range(S):
        pl.when(sub == s)(functools.partial(place, s))
    base = clusters // R
    unit = base // 4
    first = rep * base
    share = base
    if R > 1:
        first = first - jnp.where(rep > 0, unit, 0)
        share = share + jnp.where(rep == R - 1, unit, 0) - jnp.where(rep == 0, unit, 0)
    if early:
        share = unit
    else:
        first, share = first + unit, share - unit

    def begin(i, dist):
        c = first + jnp.minimum(i, share - 1)
        own = load_features(fa, c, order[:1]) if blocks else load_features(fs, c)
        distances(own, load_features(fb, c, order), dist)

    def finish(i, dist, parts):
        c = first + i
        qrow = q[pl.ds(c, 1), :]
        diag = upright(spots[pl.ds(c, 1), :])

        def root(span, _):
            shape = (span.stop - span.start, LANES)
            row = lax.broadcasted_iota(jnp.int32, shape, 0) + span.start
            row = row if blocks else row + sub * L
            col = lax.broadcasted_iota(jnp.int32, shape, 1)
            values = [inverse_root(dist[span, t : t + LANES]) for t in range(0, panels, LANES)]
            for t in range(1 if blocks else len(values)):
                values[t] = jnp.where(row == col + t * LANES, diag[span, :], values[t])
            return values

        def partial(span, held):
            keep(parts, span, sum(g * qrow[:, t * LANES : (t + 1) * LANES] for t, g in enumerate(held)))

        staged(spans_of(L), root, partial)
        return c

    pipeline(share, begin, finish, self_sums, body_size(unit, 16), ring, sums)
    total = self_sums[...].T * scale[0:1, 0:1]
    if early:
        out[...] = total
    else:
        out[...] = part[...]
        out[:clusters, :] = (part[:clusters, :] + before[...]) + total


def merge_kernel(sizes, far_list, targets, near, coupling, transfer, parent, up, *rest):
    C, S, L, slots, clusters = sizes
    sums = rest[: C - 1]
    parts = rest[C - 1 : C - 1 + S]
    parents = rest[-1]
    me, sub = lax.axis_index("clu"), lax.axis_index("sub")
    index = [targets[pl.ds(lax.rem(me + shift, C), 1), :] for shift in range(1, C)]
    got = select_rows(
        jnp.concatenate(index, axis=1), jnp.concatenate([v[:slots, :] for v in sums], axis=0), clusters
    )

    par_dev, far_n, rank = coupling.shape[0], coupling.shape[1], coupling.shape[2]
    parents[pl.ds(pl.multiple_of(me * par_dev, 8), par_dev), :] = up[...]
    for shift in range(1, C):
        owner = lax.rem(me + shift, C)
        parents[pl.ds(pl.multiple_of(owner * par_dev, 8), par_dev), :] = sums[shift - 1][slots:, :rank]
    lane = lax.broadcasted_iota(jnp.int32, (rank, LANES), 1)
    field = jnp.zeros((rank, LANES), F32)
    for p in range(par_dev):
        part = jnp.zeros((rank, rank), F32)
        for k in range(far_n):
            part = part + coupling[p, k] * parents[pl.ds(far_list[k, p], 1), :]
        field = jnp.where(lane == p, jnp.sum(part, axis=1, keepdims=True), field)
    which = lax.broadcasted_iota(jnp.int32, (LANES, clusters), 0)
    onehot = (parent[...] == which).astype(F32)
    down = jnp.dot(field, onehot, precision=HIGHEST, preferred_element_type=F32)
    fields = jnp.concatenate(
        [jnp.sum(transfer[r] * down, axis=0, keepdims=True) for r in range(rank)], axis=0
    )

    def give(s):
        for shift in range(S):
            other = (s + shift) % S
            part = near[:, other * L : (other + 1) * L]
            parts[shift][:clusters, :] = part + got if shift == 0 else part
            for t in range(clusters // L):
                at = clusters + t * rank
                parts[shift][at : at + rank, :] = fields[:, t * L : (t + 1) * L]

    for s in range(S):
        pl.when(sub == s)(functools.partial(give, s))


def up_sums(basis, masked, transfer, parent, count):
    clusters = basis.shape[0]
    rank = basis.shape[1]
    lane = lax.broadcasted_iota(jnp.int32, (rank, clusters), 1)
    leaf = jnp.zeros((rank, clusters), F32)
    for c in range(clusters):
        part = jnp.sum(basis[c] * masked[c : c + 1, :], axis=1, keepdims=True)
        leaf = jnp.where(lane == c, part, leaf)
    lifted = jnp.zeros((rank, clusters), F32)
    for r in range(rank):
        lifted = lifted + transfer[r] * leaf[r : r + 1, :]
    which = lax.broadcasted_iota(jnp.int32, (count, clusters), 0)
    onehot = (parent[...] == which).astype(F32)
    return lax.dot_general(
        onehot, lifted, (((1,), (1,)), ((), ())), precision=HIGHEST, preferred_element_type=F32
    )


def far_kernel(basis, near, out):
    clusters, rank = basis.shape[0], basis.shape[1]
    L = out.shape[1]
    fields = [near[clusters + t * rank : clusters + (t + 1) * rank, :] for t in range(clusters // L)]
    fields = jnp.concatenate(fields, axis=1) if len(fields) > 1 else fields[0]
    for c in range(clusters):
        far = jnp.sum(basis[c] * fields[:, c : c + 1], axis=0, keepdims=True)
        out[c : c + 1, :] = far + near[c : c + 1, :]


def send(value, moves):
    names = tuple(name for name, _ in moves)
    steps = [step for _, step in moves]
    sizes = [lax.axis_size(name) for name in names]
    perm = []

    def flat(coords):
        index = 0
        for size, c in zip(sizes, coords):
            index = index * size + c
        return index

    total = 1
    for size in sizes:
        total *= size
    for index in range(total):
        coords, left = [], index
        for size in reversed(sizes):
            coords.append(left % size)
            left //= size
        coords.reverse()
        perm.append((index, flat([(c + s) % n for c, s, n in zip(coords, steps, sizes)])))
    return lax.ppermute(value, names if len(names) > 1 else names[0], perm)


def on_device(
    charges,
    panel_mask,
    geometry,
    remote_source,
    remote_target,
    remote_live,
    local_pairs,
    basis,
    transfer,
    parent_of,
    far_list,
    coupling,
):
    clusters, L = charges.shape
    panels = geometry.shape[2]
    C, S, R = lax.axis_size("clu"), lax.axis_size("sub"), lax.axis_size("rep")
    slots = remote_source.shape[2]
    par_dev, rank = far_list.shape[0], transfer.shape[1]
    n = (C - 1) * slots
    shape = jax.ShapeDtypeStruct
    targets = remote_target[0]
    basis_t = jnp.transpose(basis, (0, 2, 1))
    transfer_t = jnp.transpose(transfer, (1, 2, 0))
    parent = parent_of[None, :]

    made = pl.pallas_call(
        functools.partial(pack_kernel, (C, S, L, slots)),
        out_shape=[pltpu.VMEM((clusters, L), F32), pltpu.VMEM((panels // LANES, clusters * 4, LANES), F32)]
        + [pltpu.VMEM((5 * slots + 8, L), F32)] * (C - 1),
        in_specs=[vmem()] * 3 + [smem()] * 3,
        out_specs=[vmem()] * (C + 1),
        compiler_params=limit(60),
        cost_estimate=about(2),
        name="packs",
    )(charges, panel_mask, geometry, targets, remote_source[0], remote_live[0])
    masked, geo, packs = made[0], made[1], made[2:]
    pieces = [masked] + [send(masked, (("sub", d),)) for d in range(1, S)]
    packs = [send(packs[d - 1], (("clu", d),)) for d in range(1, C)]

    *features, up = pl.pallas_call(
        prepare_kernel,
        out_shape=[pltpu.VMEM((panels // LANES, clusters * ROWS, LANES), F32)] * 2
        + [
            pltpu.VMEM((clusters, panels), F32),
            pltpu.VMEM((8, LANES), F32),
            pltpu.VMEM((par_dev, rank), F32),
        ],
        in_specs=[vmem()] * 2 + [pl.BlockSpec(memory_space=pltpu.HBM)] * 3,
        out_specs=[vmem()] * 5,
        scratch_shapes=[
            pltpu.VMEM(basis_t.shape, F32),
            pltpu.VMEM(transfer_t.shape, F32),
            pltpu.VMEM(parent.shape, jnp.int32),
            pltpu.SemaphoreType.DMA((3,)),
        ],
        compiler_params=limit(24),
        cost_estimate=about(4),
        name="prepare",
    )(*near_by(geo, masked), *far_off(basis_t, transfer_t, parent))
    *tables, diags, scale = features

    def own_tiles(early, height, *added):
        return pl.pallas_call(
            functools.partial(self_kernel, (S, L, R, clusters, panels), early),
            out_shape=pltpu.VMEM((height, L), F32),
            in_specs=[vmem()] * (4 + len(added) + S),
            out_specs=vmem(),
            scratch_shapes=[
                pltpu.VMEM((clusters, panels), F32),
                pltpu.VMEM((1, 8 if L == LANES else clusters * ROWS, L), F32),
                pltpu.VMEM((clusters, L), F32),
                pltpu.VMEM((L, clusters), F32),
            ]
            + [pltpu.VMEM((L, panels), F32)] * 8
            + [pltpu.VMEM((L, 2 * LANES), BF16)] * 4,
            compiler_params=limit(24),
            cost_estimate=about(2 if early else 4),
            name="near_self_early" if early else "near_self",
        )(*near_by(*tables, diags, scale, *added, *pieces))

    before = own_tiles(True, clusters)

    made = pl.pallas_call(
        functools.partial(remote_kernel, (C, S, L, slots, clusters, panels)),
        out_shape=[pltpu.VMEM((clusters, panels), F32)]
        + [pltpu.VMEM((slots + par_dev, L), F32)] * (C - 1),
        in_specs=[vmem()] * (4 + S + C - 1),
        out_specs=[vmem()] * C,
        scratch_shapes=[
            pltpu.VMEM((clusters, panels), F32),
            pltpu.VMEM((n, L), F32),
            pltpu.VMEM((clusters, panels), F32),
            pltpu.VMEM((L, whole(n)), F32),
            pltpu.VMEM((1, n * ROWS, L), F32),
            pltpu.SMEM((2 * n + 1,), jnp.int32),
            pltpu.SMEM((C - 1, 8, L), F32),
            pltpu.SemaphoreType.DMA((C - 1,)),
        ]
        + [pltpu.VMEM((L, panels), F32)] * 4
        + [pltpu.VMEM((L, 2 * LANES), BF16)] * 4,
        compiler_params=limit(24),
        cost_estimate=about(6),
        name="near_remote",
    )(*near_by(tables[1], scale, up, before, *pieces, *packs))
    acc, sums = made[0], [send(made[d], (("clu", C - d),)) for d in range(1, C)]

    wide = whole(local_pairs.shape[1])
    near = pl.pallas_call(
        functools.partial(local_kernel, (S, L, R, clusters, panels)),
        out_shape=pltpu.VMEM((clusters, panels), F32),
        in_specs=[vmem(), smem()] + [vmem()] * (4 + S),
        out_specs=vmem(),
        scratch_shapes=[
            pltpu.VMEM((clusters, panels), F32),
            pltpu.VMEM((clusters, panels), F32),
            pltpu.VMEM((panels, wide), F32),
        ]
        + [pltpu.VMEM((panels, panels), F32)] * 8
        + [pltpu.VMEM((panels, 2 * LANES), BF16)] * 4,
        compiler_params=limit(24),
        cost_estimate=about(9),
        name="near_local",
    )(*near_by(local_pairs[0].T), local_pairs[0].T, *near_by(*tables, scale, acc, *pieces))

    height = clusters + clusters // L * rank
    parts = pl.pallas_call(
        functools.partial(merge_kernel, (C, S, L, slots, clusters)),
        out_shape=[pltpu.VMEM((height, L), F32)] * S,
        in_specs=[smem()] + [vmem()] * (6 + C - 1),
        out_specs=[vmem()] * S,
        scratch_shapes=[pltpu.VMEM((C * par_dev, rank), F32)],
        compiler_params=limit(16),
        cost_estimate=about(1),
        name="merge",
    )(far_list.T, *near_by(targets, near, coupling, transfer_t, parent, up, *sums))
    others = [send(parts[d], (("sub", d),)) for d in range(1, S)]

    near = own_tiles(False, height, parts[0], before)
    for other in others:
        near = near + other
    others = [send(near, (("rep", e),)) for e in range(1, R)]

    total = pl.pallas_call(
        far_kernel,
        out_shape=pltpu.VMEM((clusters, L), F32),
        in_specs=[vmem()] * 2,
        out_specs=vmem(),
        compiler_params=limit(16),
        cost_estimate=about(1),
        name="far_down",
    )(*near_by(basis_t, near))
    for other in others:
        total = total + other[:clusters]
    return total * panel_mask.astype(F32)


def solution(mesh):
    placed = (
        P(("grp", "clu"), "sub"),
        P(("grp", "clu"), "sub"),
        P(("grp", "clu"), None, None),
        P(("grp", "clu"), None, "rep"),
        P(("grp", "clu"), None, "rep"),
        P(("grp", "clu"), None, "rep"),
        P(("grp", "clu"), "rep", None),
        P(("grp", "clu"), "sub", None),
        P(("grp", "clu"), None, None),
        P(("grp", "clu")),
        P(("grp", "clu"), None),
        P(("grp", "clu"), None, None, None),
    )
    return jax.shard_map(
        on_device, mesh=mesh, in_specs=placed, out_specs=P(("grp", "clu"), "sub"), check_vma=False
    )
```
